32 devices in a mesh: grp: 2 (over x), dap: 16 (over z, y, core).
Axes of the slice: x: 2, y: 2, z: 4, core: 2. Of those that a mesh axis runs over, the one named last changes fastest.
Arguments:
- alignment_input: bfloat16 [256, 64, 256], P(('grp', 'dap')), parts along dimension 0, may hold values from -17 to 17
- pair_state_input: bfloat16 [128, 64, 128], P(('grp', 'dap')), parts along dimension 0, may hold values from -17 to 17
- residue_number_index: int32 [128], P('grp'), parts along dimension 0, may hold values from 0 to 63
- chain_label: int32 [128], P('grp'), parts along dimension 0, may hold values from 0 to 3, never falling along the last dimension, each value on 1 to 32 neighbouring positions
- alignment_row_mask: int32 [256], P('grp'), parts along dimension 0, may hold values from 0 to 1
- relative_position_table: bfloat16 [66, 128], replicated, may hold values from -3 to 3
- column_query_weight: bfloat16 [256, 256], replicated, may hold values from -12.625 to 12.625
- column_key_weight: bfloat16 [256, 256], replicated, may hold values from -0.25 to 0.25
- column_value_gate_weight: bfloat16 [256, 512], replicated, may hold values from -0.375 to 0.375
- column_output_weight: bfloat16 [256, 256], replicated, may hold values from -0.375 to 0.375
- alignment_transition_up: bfloat16 [256, 1024], replicated, may hold values from -0.375 to 0.375
- alignment_transition_down: bfloat16 [1024, 256], replicated, may hold values from -0.1875 to 0.1875
- outer_input_weight: bfloat16 [256, 64], replicated, may hold values from -0.375 to 0.375
- outer_output_weight: bfloat16 [1024, 128], replicated, may hold values from -2.5 to 2.5
- outgoing_projection_weight: bfloat16 [128, 512], replicated, may hold values from -0.5 to 0.5
- outgoing_output_gate: bfloat16 [128, 128], replicated, may hold values from -0.5 to 0.5
- outgoing_output_weight: bfloat16 [128, 128], replicated, may hold values from -0.5 to 0.5
- incoming_projection_weight: bfloat16 [128, 512], replicated, may hold values from -0.5 to 0.5
- incoming_output_gate: bfloat16 [128, 128], replicated, may hold values from -0.5 to 0.5
- incoming_output_weight: bfloat16 [128, 128], replicated, may hold values from -0.5 to 0.5
- pair_transition_up: bfloat16 [128, 512], replicated, may hold values from -0.5 to 0.5
- pair_transition_down: bfloat16 [512, 128], replicated, may hold values from -0.25 to 0.25
Outputs:
- alignment_output: bfloat16 [256, 64, 256], P('grp', 'dap'), parts along dimension 0
- pair_state_output: bfloat16 [128, 64, 128], P(('grp', 'dap')), parts along dimension 0
The draws below stay inside these ranges and needn't reach their ends.
There are 2 independent parts, one for each index of `grp`. The reference program is written for one: setup_inputs(seed, part) draws one part's arguments, and reference() takes and returns one part's arrays. A program takes and returns all parts, laid end to end along the dimension named above; an argument that names none is the same for every part. Nothing has to cross between parts.
Inputs may be any that keep to these rules, and one draw needn't show every extreme that they name: `chain_label`: chain ids never fall along the residues.
All inputs are finite; a program needn't handle non-finite values.
Results may differ from the reference program's by a relative error of at most 0.012.
Values may be sent and summed in bfloat16 or wider, within the bound.
No kernel may reach another device: no remote copies, remote signals or barrier semaphores. Data moves between devices by JAX's collectives and lax.ppermute only.
A program may use at most 128 MiB of HBM per device.

```python
import math
import jax
import jax.numpy as jnp
import numpy as np
from jax import lax

CM = 256
CZ = 128
HM = 8
HEAD_SIZE = 32
CO = 32
CT = 128
MAXREL = 32
NBINS = 66
TM = 1024
TZ = 512
S = 128
N = 64


def shared_projection(key):
    return jax.random.truncated_normal(key, -4.0, 4.0, (CM, HM * HEAD_SIZE), jnp.float32) * CM ** (-0.5)


def draw_alignment_input(key, part):
    key = jax.random.fold_in(key, 1)
    first_key = jax.random.fold_in(key, 0)
    values = jax.random.truncated_normal(first_key, -6.0, 6.0, (S, N, CM), jnp.float32)
    return values.astype(jnp.bfloat16)


def draw_pair_state_input(key, part):
    key = jax.random.fold_in(key, 2)
    first_key = jax.random.fold_in(key, 0)
    values = jax.random.truncated_normal(first_key, -6.0, 6.0, (N, N, CZ), jnp.float32)
    return values.astype(jnp.bfloat16)


def draw_column_key_weight(key, part):
    shared = shared_projection(key)
    return shared.astype(jnp.bfloat16)


def draw_column_query_weight(key, part):
    key = jax.random.fold_in(key, 4)
    first_key = jax.random.fold_in(key, 0)
    fresh = jax.random.truncated_normal(first_key, -4.0, 4.0, (CM, HM * HEAD_SIZE), jnp.float32) * CM ** (-0.5)
    values = fresh
    return values.astype(jnp.bfloat16)


def draw_alignment_row_mask(key, part):
    key = jax.random.fold_in(key, 5)
    levels = jax.random.randint(key, (S,), 0, 4)
    marks = (levels > 0).astype(jnp.int32)
    return marks.at[0].set(1)


def place_ends(result, key, low, largest):
    index_at = [jax.random.randint(jax.random.fold_in(key, axis), (), 0, length) for axis, length in enumerate(result.shape)]
    longest = result.shape.index(max(result.shape))
    next_to = index_at[:longest] + [(index_at[longest] + 1) % result.shape[longest]] + index_at[longest + 1:]
    return result.at[tuple(index_at)].set(low).at[tuple(next_to)].set(largest)


def length_profile(count, total, limit, skew):
    loads = [(1 << 20) // math.isqrt(standing ** skew) + 1 for standing in range(2, count + 1)]
    spare, given = total - limit - (count - 1), [1] * (count - 1)
    while spare > 0:
        candidates = [i for i in range(count - 1) if given[i] < limit]
        whole, remaining = sum([loads[i] for i in candidates]), spare
        for i in candidates:
            more = min(limit - given[i], max(1, remaining * loads[i] // whole), spare)
            given[i] = given[i] + more
            spare = spare - more
    return np.array([limit] + given)


def uneven(own_key, amount, total, bound, slope):
    if amount == 2:
        one = jax.random.randint(own_key, (), max(1, total - bound), min(bound, total - 1) + 1)
        return jnp.stack([one, total - one])
    sizes = jnp.asarray(length_profile(amount, total, bound, slope), jnp.int32)
    couples = (amount - 1) // 2
    giver, taker = sizes[1:1 + 2 * couples:2], sizes[2:2 + 2 * couples:2]
    margin = jnp.minimum(giver - 1, bound - taker)
    moved = jax.random.randint(jax.random.fold_in(own_key, 1), (couples,), 0, 1 << 20) % (margin + 1)
    sizes = sizes.at[1:1 + 2 * couples:2].set(giver - moved).at[2:2 + 2 * couples:2].set(taker + moved)
    return sizes[jax.random.permutation(jax.random.fold_in(own_key, 2), amount)]


def bell_draw(key, extent, scale, limit, held_as=jnp.bfloat16):
    result = jax.random.normal(key, extent, jnp.float32) * scale
    return jnp.minimum(jnp.maximum(result, -limit), limit).astype(held_as)


def setup_inputs(seed: int = 0, part: int = 0) -> dict:
    key_list = jax.random.split(jax.random.key(seed), 23)
    part_splits = jax.random.split(jax.random.fold_in(key_list[22], part), 23)
    alignment_input = draw_alignment_input(jax.random.fold_in(jax.random.fold_in(key_list[22], part), 71), part)
    pair_state_input = draw_pair_state_input(jax.random.fold_in(jax.random.fold_in(key_list[22], part), 71), part)
    residue_number_index = place_ends(jax.random.randint(part_splits[2], (N,), 0, 64), jax.random.fold_in(part_splits[2], 1), 0, 63).astype(jnp.int32)
    chain_label = jnp.searchsorted(jnp.cumsum(uneven(part_splits[3], 4, N, N // 2, 0)), jnp.arange(N), side="right").astype(jnp.int32)
    alignment_row_mask = draw_alignment_row_mask(jax.random.fold_in(jax.random.fold_in(key_list[22], part), 71), part)
    relative_position_table = bell_draw(key_list[5], (NBINS, CZ), 0.5, 3.0)
    column_query_weight = draw_column_query_weight(jax.random.fold_in(key_list[22], 71), part)
    column_key_weight = draw_column_key_weight(jax.random.fold_in(key_list[22], 71), part)
    column_value_gate_weight = bell_draw(key_list[8], (CM, 2 * HM * HEAD_SIZE), CM ** -0.5, 0.375)
    column_output_weight = bell_draw(key_list[9], (HM * HEAD_SIZE, CM), (HM * HEAD_SIZE) ** -0.5, 0.375)
    alignment_transition_up = bell_draw(key_list[10], (CM, TM), CM ** -0.5, 0.375)
    alignment_transition_down = bell_draw(key_list[11], (TM, CM), TM ** -0.5, 0.1875)
    outer_input_weight = bell_draw(key_list[12], (CM, 2 * CO), CM ** -0.5, 0.375)
    outer_output_weight = bell_draw(key_list[13], (CO * CO, CZ), (0.5 * S ** 0.5 * CO ** -1), 2.5)
    outgoing_projection_weight = bell_draw(key_list[14], (CZ, 4 * CT), CZ ** -0.5, 0.5)
    outgoing_output_gate = bell_draw(key_list[15], (CZ, CZ), CZ ** -0.5, 0.5)
    outgoing_output_weight = bell_draw(key_list[16], (CT, CZ), CT ** -0.5, 0.5)
    incoming_projection_weight = bell_draw(key_list[17], (CZ, 4 * CT), CZ ** -0.5, 0.5)
    incoming_output_gate = bell_draw(key_list[18], (CZ, CZ), CZ ** -0.5, 0.5)
    incoming_output_weight = bell_draw(key_list[19], (CT, CZ), CT ** -0.5, 0.5)
    pair_transition_up = bell_draw(key_list[20], (CZ, TZ), CZ ** -0.5, 0.5)
    pair_transition_down = bell_draw(key_list[21], (TZ, CZ), TZ ** -0.5, 0.25)
    return {"alignment_input": alignment_input, "pair_state_input": pair_state_input, "residue_number_index": residue_number_index, "chain_label": chain_label, "alignment_row_mask": alignment_row_mask, "relative_position_table": relative_position_table, "column_query_weight": column_query_weight, "column_key_weight": column_key_weight, "column_value_gate_weight": column_value_gate_weight, "column_output_weight": column_output_weight, "alignment_transition_up": alignment_transition_up, "alignment_transition_down": alignment_transition_down, "outer_input_weight": outer_input_weight, "outer_output_weight": outer_output_weight, "outgoing_projection_weight": outgoing_projection_weight, "outgoing_output_gate": outgoing_output_gate, "outgoing_output_weight": outgoing_output_weight, "incoming_projection_weight": incoming_projection_weight, "incoming_output_gate": incoming_output_gate, "incoming_output_weight": incoming_output_weight, "pair_transition_up": pair_transition_up, "pair_transition_down": pair_transition_down}


EPSILON = 1e-05

def layer_normalize(values):
    center = lax.optimization_barrier(jnp.mean(values, axis=-1, keepdims=True))
    shifted = values - center
    spread = lax.optimization_barrier(jnp.mean(shifted * shifted, axis=-1, keepdims=True))
    return shifted * lax.rsqrt(spread + EPSILON)

def project_linear(inputs, weight):
    return jnp.einsum('...c,cf->...f', inputs.astype(jnp.float32), weight.astype(jnp.float32))

def column_attention(query_rows, key_row_block, value_rows, live_rows):

    def one_column(operands):
        query_col, key_col, value_col = operands
        scores = jnp.einsum('shd,thd->hst', query_col.astype(jnp.float32), key_col.astype(jnp.float32))
        scores = jnp.where(live_rows[None, None, :], scores, -1000000000.0)
        row_top = lax.optimization_barrier(jnp.max(scores, axis=-1, keepdims=True))
        raised = jnp.exp(scores - row_top)
        attention = (raised / lax.optimization_barrier(jnp.sum(raised, axis=-1, keepdims=True))).astype(jnp.bfloat16)
        return jnp.einsum('hst,thd->shd', attention.astype(jnp.float32), value_col.astype(jnp.float32))
    return lax.map(one_column, (query_rows, key_row_block, value_rows))

def triangle_inputs(pair_now, weight, gate_weight):
    normed = layer_normalize(pair_now).astype(jnp.bfloat16)
    combined = project_linear(normed, weight)
    hidden_width = weight.shape[1] // 4
    left_side = (jax.nn.sigmoid(combined[..., hidden_width:2 * hidden_width]) * combined[..., :hidden_width]).astype(jnp.bfloat16)
    right_side = (jax.nn.sigmoid(combined[..., 3 * hidden_width:]) * combined[..., 2 * hidden_width:3 * hidden_width]).astype(jnp.bfloat16)
    gating = jax.nn.sigmoid(project_linear(normed, gate_weight))
    return (left_side, right_side, gating)

def triangle_finish(pair_now, product, gating, final_weight):
    product = lax.optimization_barrier(product)
    normed = layer_normalize(product.astype(jnp.float32)).astype(jnp.bfloat16)
    return pair_now + gating * project_linear(normed, final_weight)

def reference(alignment_input, pair_state_input, residue_number_index, chain_label, alignment_row_mask, relative_position_table, column_query_weight, column_key_weight, column_value_gate_weight, column_output_weight, alignment_transition_up, alignment_transition_down, outer_input_weight, outer_output_weight, outgoing_projection_weight, outgoing_output_gate, outgoing_output_weight, incoming_projection_weight, incoming_output_gate, incoming_output_weight, pair_transition_up, pair_transition_down):
    offset = residue_number_index[:, None] - residue_number_index[None, :]
    bin_index = jnp.where(chain_label[:, None] == chain_label[None, :], jnp.clip(offset + MAXREL, 0, 2 * MAXREL), 2 * MAXREL + 1).astype(jnp.int32)
    pair_start = pair_state_input.astype(jnp.float32) + jnp.take(relative_position_table.astype(jnp.float32), bin_index, axis=0)
    live_rows = alignment_row_mask > 0
    live_row_float = live_rows.astype(jnp.float32)
    head_width = HM * HEAD_SIZE
    alignment_normalized = layer_normalize(alignment_input.astype(jnp.float32)).astype(jnp.bfloat16)
    query_rows = (project_linear(alignment_normalized, column_query_weight) * HEAD_SIZE ** (-0.5)).astype(jnp.bfloat16)
    key_row_block = project_linear(alignment_normalized, column_key_weight).astype(jnp.bfloat16)
    value_gate_pair = project_linear(alignment_normalized, column_value_gate_weight)
    value_rows = value_gate_pair[..., :head_width].astype(jnp.bfloat16)

    def by_column(values):
        return values.transpose(1, 0, 2).reshape(N, S, HM, HEAD_SIZE)
    attended = column_attention(by_column(query_rows), by_column(key_row_block), by_column(value_rows), live_rows)
    attended = attended.reshape(N, S, head_width).transpose(1, 0, 2)
    gated_values = (jax.nn.sigmoid(value_gate_pair[..., head_width:]) * attended).astype(jnp.bfloat16)
    alignment_middle = alignment_input.astype(jnp.float32) + project_linear(gated_values, column_output_weight)
    expanded_hidden = jax.nn.relu(project_linear(layer_normalize(alignment_middle).astype(jnp.bfloat16), alignment_transition_up)).astype(jnp.bfloat16)
    alignment_output = (alignment_middle + project_linear(expanded_hidden, alignment_transition_down)).astype(jnp.bfloat16)
    outer_product_input = project_linear(layer_normalize(alignment_output.astype(jnp.float32)).astype(jnp.bfloat16), outer_input_weight) * live_row_float[:, None, None]
    left_part = outer_product_input[..., :CO].astype(jnp.bfloat16)
    right_part = outer_product_input[..., CO:].astype(jnp.bfloat16)
    products = jnp.dot(left_part.reshape(S, N * CO).T, right_part.reshape(S, N * CO), preferred_element_type=jnp.float32)
    products = products.reshape(N, CO, N, CO).transpose(0, 2, 1, 3).astype(jnp.bfloat16).reshape(N, N, CO * CO)
    live_count = jnp.sum(live_row_float)
    pair_mid = pair_start + project_linear(products, outer_output_weight) / live_count
    out_left, out_right, out_gating = triangle_inputs(pair_mid, outgoing_projection_weight, outgoing_output_gate)
    out_product = jnp.einsum('ikc,jkc->ijc', out_left.astype(jnp.float32), out_right.astype(jnp.float32)).astype(jnp.bfloat16)
    pair_after_out = triangle_finish(pair_mid, out_product, out_gating, outgoing_output_weight)
    in_left, in_right, in_gating = triangle_inputs(pair_after_out, incoming_projection_weight, incoming_output_gate)
    in_product = jnp.einsum('kic,kjc->ijc', in_left.astype(jnp.float32), in_right.astype(jnp.float32)).astype(jnp.bfloat16)
    pair_after_in = triangle_finish(pair_after_out, in_product, in_gating, incoming_output_weight)
    pair_expanded = jax.nn.relu(project_linear(layer_normalize(pair_after_in).astype(jnp.bfloat16), pair_transition_up)).astype(jnp.bfloat16)
    pair_state_output = (pair_after_in + project_linear(pair_expanded, pair_transition_down)).astype(jnp.bfloat16)
    return (alignment_output, pair_state_output)
```

```python
import jax
import jax.numpy as jnp
from jax import lax
from jax.sharding import PartitionSpec as P

HM = 8
HEAD_SIZE = 32
CO = 32
MAXREL = 32
NBINS = 66


EPSILON = 1e-05


def layer_normalize(values):
    center = jnp.mean(values, axis=-1, keepdims=True)
    shifted = values - center
    spread = jnp.mean(shifted * shifted, axis=-1, keepdims=True)
    return shifted * lax.rsqrt(spread + EPSILON)


def triangle_inputs(pair_now, weight, gate_weight):
    normed = layer_normalize(pair_now).astype(jnp.bfloat16)
    combined = jnp.einsum("ijc,cf->fij", normed, weight, preferred_element_type=jnp.float32)
    hidden_width = weight.shape[1] // 4
    left_side = (
        jax.nn.sigmoid(combined[hidden_width : 2 * hidden_width]) * combined[:hidden_width]
    ).astype(jnp.bfloat16)
    right_side = (
        jax.nn.sigmoid(combined[3 * hidden_width :]) * combined[2 * hidden_width : 3 * hidden_width]
    ).astype(jnp.bfloat16)
    gating = jax.nn.sigmoid(
        jnp.einsum("ijc,cd->ijd", normed, gate_weight, preferred_element_type=jnp.float32)
    )
    return (left_side, right_side, gating)


def triangle_finish(pair_now, product, gating, final_weight):
    product = lax.optimization_barrier(product)
    normed = layer_normalize(product.transpose(1, 2, 0).astype(jnp.float32)).astype(jnp.bfloat16)
    return pair_now + gating * jnp.einsum(
        "ijc,cd->ijd", normed, final_weight, preferred_element_type=jnp.float32
    )


def by_channels(left_side, right_side, form):
    both = jnp.stack([left_side, right_side])
    both = lax.all_to_all(both, "dap", split_axis=1, concat_axis=2, tiled=True)
    partial_out = jnp.einsum(form, both[0], both[1], preferred_element_type=jnp.float32)
    return lax.all_to_all(
        partial_out.astype(jnp.bfloat16), "dap", split_axis=1, concat_axis=0, tiled=True
    )


def gather_doubling(block):
    shard_pieces = lax.axis_size("dap")
    place = lax.axis_index("dap")
    held = block
    depth = 0
    bit = shard_pieces // 2
    while bit:
        other = lax.ppermute(held, "dap", [(q, q ^ bit) for q in range(shard_pieces)])
        upper = (place & bit) != 0
        first = jnp.where(upper, other, held)
        second = jnp.where(upper, held, other)
        held = jnp.stack([first, second], axis=depth)
        depth += 1
        bit //= 2
    return held.reshape((shard_pieces,) + block.shape)


def local(
    alignment_input,
    pair_state_input,
    residue_number_index,
    chain_label,
    alignment_row_mask,
    relative_position_table,
    column_query_weight,
    column_key_weight,
    column_value_gate_weight,
    column_output_weight,
    alignment_transition_up,
    alignment_transition_down,
    outer_input_weight,
    outer_output_weight,
    outgoing_projection_weight,
    outgoing_output_gate,
    outgoing_output_weight,
    incoming_projection_weight,
    incoming_output_gate,
    incoming_output_weight,
    pair_transition_up,
    pair_transition_down,
):
    shard_pieces = lax.axis_size("dap")
    own_rows = pair_state_input.shape[0]
    residue_count = pair_state_input.shape[1]
    channel_count = alignment_input.shape[2]
    head_width = HM * HEAD_SIZE
    first_row = lax.axis_index("dap") * own_rows
    own_index = lax.dynamic_slice_in_dim(residue_number_index, first_row, own_rows)
    own_chain = lax.dynamic_slice_in_dim(chain_label, first_row, own_rows)
    offset = own_index[:, None] - residue_number_index[None, :]
    bin_index = jnp.where(
        own_chain[:, None] == chain_label[None, :],
        jnp.clip(offset + MAXREL, 0, 2 * MAXREL),
        2 * MAXREL + 1,
    )
    one_hot = (bin_index[:, :, None] == jnp.arange(NBINS, dtype=jnp.int32)[None, None, :]).astype(
        jnp.bfloat16
    )
    pair_start = pair_state_input.astype(jnp.float32) + jnp.einsum(
        "ijb,bc->ijc", one_hot, relative_position_table, preferred_element_type=jnp.float32
    )
    live_rows = alignment_row_mask > 0
    live_row_float = live_rows.astype(jnp.float32)

    def attend_one(operands):
        query_col, key_col, value_col = operands
        scores = jnp.einsum("shd,thd->hst", query_col, key_col, preferred_element_type=jnp.float32)
        scores = jnp.where(live_rows[None, None, :], scores, -1000000000.0)
        row_top = jnp.max(scores, axis=-1, keepdims=True)
        raised = jnp.exp(scores - row_top)
        attention = (raised / jnp.sum(raised, axis=-1, keepdims=True)).astype(jnp.bfloat16)
        return jnp.einsum("hst,thd->shd", attention, value_col, preferred_element_type=jnp.float32)

    blocked_view = alignment_input.reshape(
        alignment_input.shape[0], shard_pieces, residue_count // shard_pieces, channel_count
    )
    block_in = lax.all_to_all(blocked_view, "dap", split_axis=1, concat_axis=0, tiled=True)
    depth_rows = block_in.shape[0]
    count_cols = block_in.shape[2]
    current = block_in.reshape(depth_rows, count_cols, channel_count).astype(jnp.float32)
    normed = layer_normalize(current).astype(jnp.bfloat16)
    query_rows = (
        jnp.einsum("sic,ce->sie", normed, column_query_weight, preferred_element_type=jnp.float32)
        * HEAD_SIZE ** (-0.5)
    ).astype(jnp.bfloat16)
    key_row_block = jnp.einsum(
        "sic,ce->sie", normed, column_key_weight, preferred_element_type=jnp.float32
    ).astype(jnp.bfloat16)
    value_gate_pair = jnp.einsum(
        "sic,ce->sie", normed, column_value_gate_weight, preferred_element_type=jnp.float32
    )
    value_rows = value_gate_pair[..., :head_width].astype(jnp.bfloat16)

    def by_column(values):
        return values.transpose(1, 0, 2).reshape(count_cols, depth_rows, HM, HEAD_SIZE)

    attended = lax.map(
        attend_one, (by_column(query_rows), by_column(key_row_block), by_column(value_rows))
    )
    attended = attended.reshape(count_cols, depth_rows, head_width).transpose(1, 0, 2)
    gated_out = (jax.nn.sigmoid(value_gate_pair[..., head_width:]) * attended).astype(jnp.bfloat16)
    current = current + jnp.einsum(
        "sie,ec->sic", gated_out, column_output_weight, preferred_element_type=jnp.float32
    )
    hidden = jax.nn.relu(
        jnp.einsum(
            "sic,cf->sif",
            layer_normalize(current).astype(jnp.bfloat16),
            alignment_transition_up,
            preferred_element_type=jnp.float32,
        )
    ).astype(jnp.bfloat16)
    current = current + jnp.einsum(
        "sif,fc->sic", hidden, alignment_transition_down, preferred_element_type=jnp.float32
    )
    result = current.astype(jnp.bfloat16)
    outer_product_input = jnp.einsum(
        "sic,cf->sif",
        layer_normalize(result.astype(jnp.float32)).astype(jnp.bfloat16),
        outer_input_weight,
        preferred_element_type=jnp.float32,
    )
    outer_product_input = outer_product_input * live_row_float[:, None, None]
    left_part = outer_product_input[..., :CO].astype(jnp.bfloat16)
    right_part = outer_product_input[..., CO:].astype(jnp.bfloat16)
    all_rows = result.shape[0]
    left_cols = left_part.transpose(1, 0, 2)
    right_cols = right_part.transpose(1, 0, 2).reshape(own_rows, all_rows * CO)
    live_count = jnp.sum(live_row_float)
    right_piece = gather_doubling(right_cols).reshape(-1, all_rows * CO)
    span_rows = right_piece.shape[0]
    products = jnp.einsum(
        "isc,jsd->ijcd",
        left_cols,
        right_piece.reshape(span_rows, all_rows, CO),
        preferred_element_type=jnp.float32,
    )
    products = products.astype(jnp.bfloat16).reshape(own_rows, span_rows, CO * CO)
    outer_mean = (
        jnp.einsum("ijf,fc->ijc", products, outer_output_weight, preferred_element_type=jnp.float32)
        / live_count
    )
    pair_mid = pair_start + outer_mean
    out_left, out_right, out_gating = triangle_inputs(
        pair_mid, outgoing_projection_weight, outgoing_output_gate
    )
    out_product = by_channels(out_left, out_right, "cik,cjk->cij")
    pair_after_out = triangle_finish(pair_mid, out_product, out_gating, outgoing_output_weight)
    in_left, in_right, in_gating = triangle_inputs(
        pair_after_out, incoming_projection_weight, incoming_output_gate
    )
    in_product = by_channels(in_left, in_right, "cki,ckj->cij")
    pair_after_in = triangle_finish(pair_after_out, in_product, in_gating, incoming_output_weight)
    pair_expanded = jax.nn.relu(
        jnp.einsum(
            "ijc,cf->ijf",
            layer_normalize(pair_after_in).astype(jnp.bfloat16),
            pair_transition_up,
            preferred_element_type=jnp.float32,
        )
    ).astype(jnp.bfloat16)
    pair_state_output = (
        pair_after_in
        + jnp.einsum(
            "ijf,fc->ijc", pair_expanded, pair_transition_down, preferred_element_type=jnp.float32
        )
    ).astype(jnp.bfloat16)
    return (result, pair_state_output)


def solution(mesh):
    in_specs = (
        P(("grp", "dap"), None, None),
        P(("grp", "dap"), None, None),
        P("grp"),
        P("grp"),
        P("grp"),
        P(),
        P(),
        P(),
        P(),
        P(),
        P(),
        P(),
        P(),
        P(),
        P(),
        P(),
        P(),
        P(),
        P(),
        P(),
        P(),
        P(),
    )
    out_specs = (P("grp", "dap", None), P(("grp", "dap"), None, None))
    return jax.shard_map(local, mesh=mesh, in_specs=in_specs, out_specs=out_specs, check_vma=False)
```

```python
import jax
import jax.numpy as jnp
from jax import lax
from jax.experimental import pallas as pl
from jax.experimental.pallas import tpu as pltpu
from jax.sharding import PartitionSpec as P

HM = 8
HEAD_SIZE = 32
CO = 32
MAXREL = 32
NBINS = 66


EPSILON = 1e-05


def layer_normalize(values):
    center = jnp.mean(values, axis=-1, keepdims=True)
    shifted = values - center
    spread = jnp.mean(shifted * shifted, axis=-1, keepdims=True)
    return shifted * lax.rsqrt(spread + EPSILON)


def triangle_inputs(pair_now, weight, gate_weight):
    normed = layer_normalize(pair_now).astype(jnp.bfloat16)
    combined = jnp.einsum("ijc,cf->fij", normed, weight, preferred_element_type=jnp.float32)
    hidden_width = weight.shape[1] // 4
    left_side = (
        jax.nn.sigmoid(combined[hidden_width : 2 * hidden_width]) * combined[:hidden_width]
    ).astype(jnp.bfloat16)
    right_side = (
        jax.nn.sigmoid(combined[3 * hidden_width :]) * combined[2 * hidden_width : 3 * hidden_width]
    ).astype(jnp.bfloat16)
    gating = jax.nn.sigmoid(
        jnp.einsum("ijc,cd->ijd", normed, gate_weight, preferred_element_type=jnp.float32)
    )
    return (left_side, right_side, gating)


def triangle_finish(pair_now, product, gating, final_weight):
    product = lax.optimization_barrier(product)
    normed = layer_normalize(product.transpose(1, 2, 0).astype(jnp.float32)).astype(jnp.bfloat16)
    return pair_now + gating * jnp.einsum(
        "ijc,cd->ijd", normed, final_weight, preferred_element_type=jnp.float32
    )


def by_channels(left_side, right_side, form):
    both = jnp.stack([left_side, right_side])
    both = lax.all_to_all(both, "dap", split_axis=1, concat_axis=2, tiled=True)
    partial_out = jnp.einsum(form, both[0], both[1], preferred_element_type=jnp.float32)
    return lax.all_to_all(
        partial_out.astype(jnp.bfloat16), "dap", split_axis=1, concat_axis=0, tiled=True
    )


def gather_doubling(block):
    shard_pieces = lax.axis_size("dap")
    place = lax.axis_index("dap")
    held = block
    depth = 0
    bit = shard_pieces // 2
    while bit:
        other = lax.ppermute(held, "dap", [(q, q ^ bit) for q in range(shard_pieces)])
        upper = (place & bit) != 0
        first = jnp.where(upper, other, held)
        second = jnp.where(upper, held, other)
        held = jnp.stack([first, second], axis=depth)
        depth += 1
        bit //= 2
    return held.reshape((shard_pieces,) + block.shape)


LANES = 128


def gate_curve(values):
    return 0.5 + 0.5 * jnp.tanh(0.5 * values)


def normalize_channels(values):
    center = jnp.mean(values, axis=0, keepdims=True)
    shifted = values - center
    spread = jnp.mean(shifted * shifted, axis=0, keepdims=True)
    return (shifted * lax.rsqrt(spread + EPSILON)).astype(jnp.bfloat16)


def mix(weight, values):
    return jnp.dot(weight, values, preferred_element_type=jnp.float32)


def fold_halves(first_even, second_even, first_odd, second_odd, low_half):
    straight = jnp.where(low_half, first_even, second_odd)
    crossed = jnp.where(low_half, second_even, first_odd)
    return straight + pltpu.roll(crossed, LANES // 2, 1)


def pair_kernel(
    place_ref,
    live_ref,
    parts_ref,
    pair_ref,
    bins_ref,
    table_ref,
    mean_weight_ref,
    out_mix_ref,
    out_gate_ref,
    out_final_ref,
    in_mix_ref,
    in_gate_ref,
    in_final_ref,
    up_ref,
    down_ref,
    result_ref,
    wide_ref,
    right_cols_ref,
    stack_ref,
    pair_now_ref,
    left_ref,
    right_ref,
    product_ref,
    gating_ref,
    chosen_ref,
    own_left_ref,
    own_product_ref,
):
    place = place_ref[0]
    inverse_live = 1.0 / live_ref[0]
    half = LANES // 2
    low_half = lax.broadcasted_iota(jnp.int32, (LANES, LANES), 1) < half
    low_short = lax.broadcasted_iota(jnp.int32, (32, LANES), 1) < half
    channel = lax.broadcasted_iota(jnp.int32, (LANES, LANES), 0)

    for p in range(16):
        wide_ref[p * 128 : (p + 1) * 128, :] = parts_ref[p, 128:256, :].astype(jnp.float32)
    for d in range(0, CO, 2):
        rows = [
            wide_ref[pl.ds(par * CO + d + e, 32, stride=2 * CO), :]
            for e in range(2)
            for par in range(2)
        ]
        right_cols_ref[:, d * half : d * half + LANES] = (
            jnp.concatenate(rows, axis=0).T.astype(jnp.bfloat16)
        )

    def first_chunk(g, carry):
        left_rows = parts_ref[pl.ds(2 * g, 2), 0:128, :].reshape(256, LANES)
        outer = mix(left_rows, right_cols_ref[...]).astype(jnp.bfloat16)
        for i in range(8):
            for d in range(16):
                stack_ref[d * 32 : (d + 1) * 32, i * LANES : (i + 1) * LANES] = outer[
                    i * 32 : (i + 1) * 32, d * LANES : (d + 1) * LANES
                ]
        mixed = mix(mean_weight_ref[...], stack_ref[...])
        slabs = []
        for q in range(4):
            h = 4 * g + q
            even = slice(2 * q * LANES, (2 * q + 1) * LANES)
            odd = slice((2 * q + 1) * LANES, (2 * q + 2) * LANES)
            outer_mean = fold_halves(
                mixed[0:128, even], mixed[0:128, odd], mixed[128:256, even], mixed[128:256, odd], low_half
            )
            one_hot = (channel == bins_ref[pl.ds(h, 1), :]).astype(jnp.float32).astype(jnp.bfloat16)
            start = pair_ref[h].astype(jnp.float32) + mix(table_ref[...], one_hot)
            slab = start + outer_mean * inverse_live
            pair_now_ref[h] = slab
            slabs.append(normalize_channels(slab))
        normed = jnp.concatenate(slabs, axis=1)
        combined = mix(out_mix_ref[...], normed)
        left = gate_curve(combined[128:256]) * combined[0:128]
        right = gate_curve(combined[384:512]) * combined[256:384]
        gating = gate_curve(mix(out_gate_ref[...], normed))
        for q in range(4):
            h = 4 * g + q
            lanes = slice(q * LANES, (q + 1) * LANES)
            left_ref[pl.ds(h * 128, 128), :] = left[:, lanes]
            right_ref[pl.ds(h * 128, 128), :] = right[:, lanes]
            gating_ref[h] = gating[:, lanes]
        return carry

    lax.fori_loop(0, 8, first_chunk, 0)

    def outgoing_channels(block, carry):
        for e in range(8):
            c = block * 8 + e
            left = left_ref[pl.ds(c, 32, stride=128), :].astype(jnp.bfloat16)
            right = right_ref[pl.ds(c, 32, stride=128), :]
            turned = pltpu.roll(right, half, 1)
            spread = jnp.concatenate(
                [
                    jnp.where(low_short, right, 0.0),
                    jnp.where(low_short, turned, 0.0),
                    jnp.where(low_short, 0.0, turned),
                    jnp.where(low_short, 0.0, right),
                ],
                axis=0,
            ).astype(jnp.bfloat16)
            product_ref[pl.ds(c, 32, stride=128), :] = lax.dot_general(
                left, spread, (((1,), (1,)), ((), ())), preferred_element_type=jnp.float32
            )
        return carry

    lax.fori_loop(0, 16, outgoing_channels, 0)

    column = lax.broadcasted_iota(jnp.int32, (1, 256), 1)
    which = column // 32
    own = which % 4
    wanted = half * (which // 4) + 32 * (own % 2) + 2 * place + own // 2
    slab_of = column % 32
    source = lax.broadcasted_iota(jnp.int32, (LANES, 256), 0)
    chosen_ref[...] = jnp.zeros_like(chosen_ref)

    def second_chunk(g, carry):
        products = [
            normalize_channels(product_ref[pl.ds((4 * g + q) * 128, 128), :]) for q in range(4)
        ]
        finished = mix(out_final_ref[...], jnp.concatenate(products, axis=1))
        slabs = []
        picks = []
        for q in range(4):
            h = 4 * g + q
            lanes = slice(q * LANES, (q + 1) * LANES)
            slab = pair_now_ref[h] + gating_ref[h] * finished[:, lanes]
            pair_now_ref[h] = slab
            slabs.append(normalize_channels(slab))
            here = jnp.where(slab_of == h, wanted, -1)
            picks.append((source == here).astype(jnp.float32).astype(jnp.bfloat16))
        normed = jnp.concatenate(slabs, axis=1)
        chosen_ref[...] += mix(normed, jnp.concatenate(picks, axis=0))
        combined = mix(in_mix_ref[256:512, :], normed)
        right = gate_curve(combined[128:256]) * combined[0:128]
        for q in range(4):
            right_ref[pl.ds((4 * g + q) * 128, 128), :] = right[:, q * LANES : (q + 1) * LANES]
        return carry

    lax.fori_loop(0, 8, second_chunk, 0)

    combined = mix(in_mix_ref[0:256, :], chosen_ref[...].astype(jnp.bfloat16))
    own_left = gate_curve(combined[128:256]) * combined[0:128]
    for m in range(8):
        part = own_left[:, (m // 4) * LANES : (m // 4 + 1) * LANES]
        if m % 4:
            part = pltpu.roll(part, LANES - 32 * (m % 4), 1)
        own_left_ref[m * 128 : (m + 1) * 128, :] = part

    def incoming_channels(block, carry):
        for e in range(8):
            c = block * 8 + e
            left = own_left_ref[pl.ds(c, 8, stride=128), :][:, 0:32].astype(jnp.bfloat16)
            right = right_ref[pl.ds(c, 32, stride=128), :].astype(jnp.bfloat16)
            own_product_ref[pl.ds(c, 8, stride=128), :] = mix(left, right)
        return carry

    lax.fori_loop(0, 16, incoming_channels, 0)

    def own_block(m):
        return own_product_ref[m * 128 : (m + 1) * 128, :]

    products = [
        normalize_channels(
            fold_halves(
                own_block(2 * t), own_block(2 * t + 1), own_block(4 + 2 * t), own_block(5 + 2 * t), low_half
            )
        )
        for t in range(2)
    ]
    finished = mix(in_final_ref[...], jnp.concatenate(products, axis=1))
    own_pair = jnp.concatenate([pair_now_ref[2 * place + t] for t in range(2)], axis=1)
    gating = gate_curve(mix(in_gate_ref[...], normalize_channels(own_pair)))
    own_pair = own_pair + gating * finished
    hidden = jnp.maximum(mix(up_ref[...], normalize_channels(own_pair)), 0.0).astype(jnp.bfloat16)
    own_pair = (own_pair + mix(down_ref[...], hidden)).astype(jnp.bfloat16)
    lane = lax.broadcasted_iota(jnp.int32, (LANES, LANES), 1)
    back = half * (channel // half) + 32 * (channel % 2) + (channel % half) // 2
    order = (lane == back).astype(jnp.float32).astype(jnp.bfloat16)
    for t in range(2):
        result_ref[t * 128 : (t + 1) * 128, :] = lax.dot_general(
            order,
            own_pair[:, t * LANES : (t + 1) * LANES],
            (((1,), (1,)), ((), ())),
            preferred_element_type=jnp.float32,
        ).astype(jnp.bfloat16)


def lanes_order(values):
    lead = values.shape[:-1]
    halves = values.reshape(lead + (values.shape[-1] // 2, 2))
    return jnp.swapaxes(halves, -1, -2).reshape(values.shape)


def pair_whole(
    left_part,
    right_part,
    pair_state_input,
    bin_all,
    live_count,
    relative_position_table,
    outer_output_weight,
    outgoing_projection_weight,
    outgoing_output_gate,
    outgoing_output_weight,
    incoming_projection_weight,
    incoming_output_gate,
    incoming_output_weight,
    pair_transition_up,
    pair_transition_down,
):
    width = pair_state_input.shape[2]
    own_pair = lanes_order(pair_state_input.transpose(0, 2, 1))
    own_pair = own_pair.reshape(2, 2, width, 64).transpose(0, 2, 1, 3).reshape(2, width, LANES)
    pair_all = gather_doubling(own_pair).reshape(32, width, LANES)
    parts = jnp.concatenate([left_part.reshape(128, LANES), right_part.reshape(128, LANES)], axis=0)
    parts_all = gather_doubling(parts)
    bins = lanes_order(bin_all).reshape(32, LANES)
    table = jnp.pad(relative_position_table, ((0, LANES - NBINS), (0, 0))).T
    mean_weight = (
        outer_output_weight.reshape(CO, 16, 2, width).transpose(2, 3, 1, 0).reshape(2 * width, 16 * CO)
    )
    place = lax.axis_index("dap").astype(jnp.int32).reshape(1)
    vmem = pl.BlockSpec(memory_space=pltpu.VMEM)
    smem = pl.BlockSpec(memory_space=pltpu.SMEM)
    tall = (32 * 128, LANES)
    result = pl.pallas_call(
        pair_kernel,
        out_shape=jax.ShapeDtypeStruct((256, LANES), jnp.bfloat16),
        in_specs=[smem, smem] + [vmem] * 13,
        out_specs=vmem,
        scratch_shapes=[
            pltpu.VMEM((2048, LANES), jnp.float32),
            pltpu.VMEM((128, 2048), jnp.bfloat16),
            pltpu.VMEM((512, 1024), jnp.bfloat16),
            pltpu.VMEM((32, 128, LANES), jnp.float32),
            pltpu.VMEM(tall, jnp.float32),
            pltpu.VMEM(tall, jnp.float32),
            pltpu.VMEM(tall, jnp.float32),
            pltpu.VMEM((32, 128, LANES), jnp.float32),
            pltpu.VMEM((128, 256), jnp.float32),
            pltpu.VMEM((1024, LANES), jnp.float32),
            pltpu.VMEM((1024, LANES), jnp.float32),
        ],
        compiler_params=pltpu.CompilerParams(vmem_limit_bytes=40 * 1024 * 1024),
        name="pair_whole",
    )(
        place,
        live_count.reshape(1),
        parts_all,
        pair_all,
        bins,
        table,
        mean_weight,
        outgoing_projection_weight.T,
        outgoing_output_gate.T,
        outgoing_output_weight.T,
        incoming_projection_weight.T,
        incoming_output_gate.T,
        incoming_output_weight.T,
        pair_transition_up.T,
        pair_transition_down.T,
    )
    return result.reshape(pair_state_input.shape)


def local(
    alignment_input,
    pair_state_input,
    residue_number_index,
    chain_label,
    alignment_row_mask,
    relative_position_table,
    column_query_weight,
    column_key_weight,
    column_value_gate_weight,
    column_output_weight,
    alignment_transition_up,
    alignment_transition_down,
    outer_input_weight,
    outer_output_weight,
    outgoing_projection_weight,
    outgoing_output_gate,
    outgoing_output_weight,
    incoming_projection_weight,
    incoming_output_gate,
    incoming_output_weight,
    pair_transition_up,
    pair_transition_down,
):
    shard_pieces = lax.axis_size("dap")
    own_rows = pair_state_input.shape[0]
    residue_count = pair_state_input.shape[1]
    channel_count = alignment_input.shape[2]
    head_width = HM * HEAD_SIZE
    first_row = lax.axis_index("dap") * own_rows
    own_index = lax.dynamic_slice_in_dim(residue_number_index, first_row, own_rows)
    own_chain = lax.dynamic_slice_in_dim(chain_label, first_row, own_rows)

    def bins_of(index, chain):
        offset = index[:, None] - residue_number_index[None, :]
        return jnp.where(
            chain[:, None] == chain_label[None, :],
            jnp.clip(offset + MAXREL, 0, 2 * MAXREL),
            2 * MAXREL + 1,
        )

    bin_index = bins_of(own_index, own_chain)
    one_hot = (bin_index[:, :, None] == jnp.arange(NBINS, dtype=jnp.int32)[None, None, :]).astype(
        jnp.bfloat16
    )
    pair_start = pair_state_input.astype(jnp.float32) + jnp.einsum(
        "ijb,bc->ijc", one_hot, relative_position_table, preferred_element_type=jnp.float32
    )
    live_rows = alignment_row_mask > 0
    live_row_float = live_rows.astype(jnp.float32)

    def attend_one(operands):
        query_col, key_col, value_col = operands
        scores = jnp.einsum("shd,thd->hst", query_col, key_col, preferred_element_type=jnp.float32)
        scores = jnp.where(live_rows[None, None, :], scores, -1000000000.0)
        row_top = jnp.max(scores, axis=-1, keepdims=True)
        raised = jnp.exp(scores - row_top)
        attention = (raised / jnp.sum(raised, axis=-1, keepdims=True)).astype(jnp.bfloat16)
        return jnp.einsum("hst,thd->shd", attention, value_col, preferred_element_type=jnp.float32)

    blocked_view = alignment_input.reshape(
        alignment_input.shape[0], shard_pieces, residue_count // shard_pieces, channel_count
    )
    block_in = lax.all_to_all(blocked_view, "dap", split_axis=1, concat_axis=0, tiled=True)
    depth_rows = block_in.shape[0]
    count_cols = block_in.shape[2]
    current = block_in.reshape(depth_rows, count_cols, channel_count).astype(jnp.float32)
    normed = layer_normalize(current).astype(jnp.bfloat16)
    query_rows = (
        jnp.einsum("sic,ce->sie", normed, column_query_weight, preferred_element_type=jnp.float32)
        * HEAD_SIZE ** (-0.5)
    ).astype(jnp.bfloat16)
    key_row_block = jnp.einsum(
        "sic,ce->sie", normed, column_key_weight, preferred_element_type=jnp.float32
    ).astype(jnp.bfloat16)
    value_gate_pair = jnp.einsum(
        "sic,ce->sie", normed, column_value_gate_weight, preferred_element_type=jnp.float32
    )
    value_rows = value_gate_pair[..., :head_width].astype(jnp.bfloat16)

    def by_column(values):
        return values.transpose(1, 0, 2).reshape(count_cols, depth_rows, HM, HEAD_SIZE)

    attended = lax.map(
        attend_one, (by_column(query_rows), by_column(key_row_block), by_column(value_rows))
    )
    attended = attended.reshape(count_cols, depth_rows, head_width).transpose(1, 0, 2)
    gated_out = (jax.nn.sigmoid(value_gate_pair[..., head_width:]) * attended).astype(jnp.bfloat16)
    current = current + jnp.einsum(
        "sie,ec->sic", gated_out, column_output_weight, preferred_element_type=jnp.float32
    )
    hidden = jax.nn.relu(
        jnp.einsum(
            "sic,cf->sif",
            layer_normalize(current).astype(jnp.bfloat16),
            alignment_transition_up,
            preferred_element_type=jnp.float32,
        )
    ).astype(jnp.bfloat16)
    current = current + jnp.einsum(
        "sif,fc->sic", hidden, alignment_transition_down, preferred_element_type=jnp.float32
    )
    result = current.astype(jnp.bfloat16)
    outer_product_input = jnp.einsum(
        "sic,cf->sif",
        layer_normalize(result.astype(jnp.float32)).astype(jnp.bfloat16),
        outer_input_weight,
        preferred_element_type=jnp.float32,
    )
    outer_product_input = outer_product_input * live_row_float[:, None, None]
    left_part = outer_product_input[..., :CO].astype(jnp.bfloat16)
    right_part = outer_product_input[..., CO:].astype(jnp.bfloat16)
    all_rows = result.shape[0]
    if all_rows == LANES and 2 * residue_count == LANES and own_rows == 4:
        return (
            result,
            pair_whole(
                left_part.transpose(1, 2, 0),
                right_part.transpose(1, 2, 0),
                pair_state_input,
                bins_of(residue_number_index, chain_label),
                jnp.sum(live_row_float),
                relative_position_table,
                outer_output_weight,
                outgoing_projection_weight,
                outgoing_output_gate,
                outgoing_output_weight,
                incoming_projection_weight,
                incoming_output_gate,
                incoming_output_weight,
                pair_transition_up,
                pair_transition_down,
            ),
        )
    left_cols = left_part.transpose(1, 0, 2)
    right_cols = right_part.transpose(1, 0, 2).reshape(own_rows, all_rows * CO)
    live_count = jnp.sum(live_row_float)
    right_piece = gather_doubling(right_cols).reshape(-1, all_rows * CO)
    span_rows = right_piece.shape[0]
    products = jnp.einsum(
        "isc,jsd->ijcd",
        left_cols,
        right_piece.reshape(span_rows, all_rows, CO),
        preferred_element_type=jnp.float32,
    )
    products = products.astype(jnp.bfloat16).reshape(own_rows, span_rows, CO * CO)
    outer_mean = (
        jnp.einsum("ijf,fc->ijc", products, outer_output_weight, preferred_element_type=jnp.float32)
        / live_count
    )
    pair_mid = pair_start + outer_mean
    out_left, out_right, out_gating = triangle_inputs(
        pair_mid, outgoing_projection_weight, outgoing_output_gate
    )
    out_product = by_channels(out_left, out_right, "cik,cjk->cij")
    pair_after_out = triangle_finish(pair_mid, out_product, out_gating, outgoing_output_weight)
    in_left, in_right, in_gating = triangle_inputs(
        pair_after_out, incoming_projection_weight, incoming_output_gate
    )
    in_product = by_channels(in_left, in_right, "cki,ckj->cij")
    pair_after_in = triangle_finish(pair_after_out, in_product, in_gating, incoming_output_weight)
    pair_expanded = jax.nn.relu(
        jnp.einsum(
            "ijc,cf->ijf",
            layer_normalize(pair_after_in).astype(jnp.bfloat16),
            pair_transition_up,
            preferred_element_type=jnp.float32,
        )
    ).astype(jnp.bfloat16)
    pair_state_output = (
        pair_after_in
        + jnp.einsum(
            "ijf,fc->ijc", pair_expanded, pair_transition_down, preferred_element_type=jnp.float32
        )
    ).astype(jnp.bfloat16)
    return (result, pair_state_output)


def solution(mesh):
    in_specs = (
        P(("grp", "dap"), None, None),
        P(("grp", "dap"), None, None),
        P("grp"),
        P("grp"),
        P("grp"),
        P(),
        P(),
        P(),
        P(),
        P(),
        P(),
        P(),
        P(),
        P(),
        P(),
        P(),
        P(),
        P(),
        P(),
        P(),
        P(),
        P(),
    )
    out_specs = (P("grp", "dap", None), P(("grp", "dap"), None, None))
    return jax.shard_map(local, mesh=mesh, in_specs=in_specs, out_specs=out_specs, check_vma=False)
```

```python
import jax
import jax.numpy as jnp
from jax import lax
from jax.experimental import pallas as pl
from jax.experimental.pallas import tpu as pltpu
from jax.sharding import PartitionSpec as P

HM = 8
HEAD_SIZE = 32
CO = 32
MAXREL = 32
NBINS = 66


EPSILON = 1e-05


def layer_normalize(values):
    center = jnp.mean(values, axis=-1, keepdims=True)
    shifted = values - center
    spread = jnp.mean(shifted * shifted, axis=-1, keepdims=True)
    return shifted * lax.rsqrt(spread + EPSILON)


def triangle_inputs(pair_now, weight, gate_weight):
    normed = layer_normalize(pair_now).astype(jnp.bfloat16)
    combined = jnp.einsum("ijc,cf->fij", normed, weight, preferred_element_type=jnp.float32)
    hidden_width = weight.shape[1] // 4
    left_side = (
        jax.nn.sigmoid(combined[hidden_width : 2 * hidden_width]) * combined[:hidden_width]
    ).astype(jnp.bfloat16)
    right_side = (
        jax.nn.sigmoid(combined[3 * hidden_width :]) * combined[2 * hidden_width : 3 * hidden_width]
    ).astype(jnp.bfloat16)
    gating = jax.nn.sigmoid(
        jnp.einsum("ijc,cd->ijd", normed, gate_weight, preferred_element_type=jnp.float32)
    )
    return (left_side, right_side, gating)


def triangle_finish(pair_now, product, gating, final_weight):
    product = lax.optimization_barrier(product)
    normed = layer_normalize(product.transpose(1, 2, 0).astype(jnp.float32)).astype(jnp.bfloat16)
    return pair_now + gating * jnp.einsum(
        "ijc,cd->ijd", normed, final_weight, preferred_element_type=jnp.float32
    )


def by_channels(left_side, right_side, form):
    both = jnp.stack([left_side, right_side])
    both = lax.all_to_all(both, "dap", split_axis=1, concat_axis=2, tiled=True)
    partial_out = jnp.einsum(form, both[0], both[1], preferred_element_type=jnp.float32)
    return lax.all_to_all(
        partial_out.astype(jnp.bfloat16), "dap", split_axis=1, concat_axis=0, tiled=True
    )


def gather_doubling(block):
    shard_pieces = lax.axis_size("dap")
    place = lax.axis_index("dap")
    held = block
    depth = 0
    bit = shard_pieces // 2
    while bit:
        other = lax.ppermute(held, "dap", [(q, q ^ bit) for q in range(shard_pieces)])
        upper = (place & bit) != 0
        first = jnp.where(upper, other, held)
        second = jnp.where(upper, held, other)
        held = jnp.stack([first, second], axis=depth)
        depth += 1
        bit //= 2
    return held.reshape((shard_pieces,) + block.shape)


LANES = 128


def gate_curve(values):
    return 0.5 + 0.5 * jnp.tanh(0.5 * values)


def normalize_channels(values):
    center = jnp.mean(values, axis=0, keepdims=True)
    shifted = values - center
    spread = jnp.mean(shifted * shifted, axis=0, keepdims=True)
    return (shifted * lax.rsqrt(spread + EPSILON)).astype(jnp.bfloat16)


def mix(weight, values):
    return jnp.dot(weight, values, preferred_element_type=jnp.float32)


def fold_halves(first_even, second_even, first_odd, second_odd, low_half):
    straight = jnp.where(low_half, first_even, second_odd)
    crossed = jnp.where(low_half, second_even, first_odd)
    return straight + pltpu.roll(crossed, LANES // 2, 1)


def pair_kernel(
    place_ref,
    live_ref,
    parts_ref,
    pair_ref,
    bins_ref,
    table_ref,
    mean_weight_ref,
    out_mix_ref,
    out_gate_ref,
    out_final_ref,
    in_mix_ref,
    in_gate_ref,
    in_final_ref,
    up_ref,
    down_ref,
    result_ref,
    wide_ref,
    right_cols_ref,
    stack_ref,
    pair_now_ref,
    left_ref,
    right_ref,
    product_ref,
    gating_ref,
    chosen_ref,
    own_left_ref,
    own_product_ref,
):
    place = place_ref[0]
    inverse_live = 1.0 / live_ref[0]
    half = LANES // 2
    low_half = lax.broadcasted_iota(jnp.int32, (LANES, LANES), 1) < half
    low_short = lax.broadcasted_iota(jnp.int32, (32, LANES), 1) < half
    channel = lax.broadcasted_iota(jnp.int32, (LANES, LANES), 0)

    def owner_of(m):
        turned = (m & 1) * 8 + (m & 2) * 2 + (m & 4) // 2 + (m & 8) // 8
        return place ^ turned

    for m in range(16):
        wide_ref[pl.ds(pl.multiple_of(owner_of(m) * 128, 128), 128), :] = parts_ref[
            m, 128:256, :
        ].astype(jnp.float32)
    for d in range(0, CO, 2):
        rows = [
            wide_ref[pl.ds(par * CO + d + e, 32, stride=2 * CO), :]
            for e in range(2)
            for par in range(2)
        ]
        right_cols_ref[:, d * half : d * half + LANES] = (
            jnp.concatenate(rows, axis=0).T.astype(jnp.bfloat16)
        )

    def first_chunk(g, carry):
        left_rows = parts_ref[pl.ds(2 * g, 2), 0:128, :].reshape(256, LANES)
        outer = mix(left_rows, right_cols_ref[...]).astype(jnp.bfloat16)
        for i in range(8):
            for d in range(16):
                stack_ref[d * 32 : (d + 1) * 32, i * LANES : (i + 1) * LANES] = outer[
                    i * 32 : (i + 1) * 32, d * LANES : (d + 1) * LANES
                ]
        mixed = mix(mean_weight_ref[...], stack_ref[...])
        slabs = []
        for q in range(4):
            h = 2 * owner_of(2 * g + q // 2) + q % 2
            even = slice(2 * q * LANES, (2 * q + 1) * LANES)
            odd = slice((2 * q + 1) * LANES, (2 * q + 2) * LANES)
            outer_mean = fold_halves(
                mixed[0:128, even], mixed[0:128, odd], mixed[128:256, even], mixed[128:256, odd], low_half
            )
            one_hot = (channel == bins_ref[pl.ds(h, 1), :]).astype(jnp.float32).astype(jnp.bfloat16)
            start = pair_ref[4 * g + q].astype(jnp.float32) + mix(table_ref[...], one_hot)
            slab = start + outer_mean * inverse_live
            pair_now_ref[h] = slab
            slabs.append(normalize_channels(slab))
        normed = jnp.concatenate(slabs, axis=1)
        combined = mix(out_mix_ref[...], normed)
        left = gate_curve(combined[128:256]) * combined[0:128]
        right = gate_curve(combined[384:512]) * combined[256:384]
        gating = gate_curve(mix(out_gate_ref[...], normed))
        for q in range(4):
            h = 2 * owner_of(2 * g + q // 2) + q % 2
            lanes = slice(q * LANES, (q + 1) * LANES)
            left_ref[pl.ds(h * 128, 128), :] = left[:, lanes]
            right_ref[pl.ds(h * 128, 128), :] = right[:, lanes]
            gating_ref[h] = gating[:, lanes]
        return carry

    lax.fori_loop(0, 8, first_chunk, 0)

    def outgoing_channels(block, carry):
        for e in range(8):
            c = block * 8 + e
            left = left_ref[pl.ds(c, 32, stride=128), :].astype(jnp.bfloat16)
            right = right_ref[pl.ds(c, 32, stride=128), :]
            turned = pltpu.roll(right, half, 1)
            spread = jnp.concatenate(
                [
                    jnp.where(low_short, right, 0.0),
                    jnp.where(low_short, turned, 0.0),
                    jnp.where(low_short, 0.0, turned),
                    jnp.where(low_short, 0.0, right),
                ],
                axis=0,
            ).astype(jnp.bfloat16)
            product_ref[pl.ds(c, 32, stride=128), :] = lax.dot_general(
                left, spread, (((1,), (1,)), ((), ())), preferred_element_type=jnp.float32
            )
        return carry

    lax.fori_loop(0, 16, outgoing_channels, 0)

    column = lax.broadcasted_iota(jnp.int32, (1, 256), 1)
    which = column // 32
    own = which % 4
    wanted = half * (which // 4) + 32 * (own % 2) + 2 * place + own // 2
    slab_of = column % 32
    source = lax.broadcasted_iota(jnp.int32, (LANES, 256), 0)
    chosen_ref[...] = jnp.zeros_like(chosen_ref)

    def second_chunk(g, carry):
        products = [
            normalize_channels(product_ref[pl.ds((4 * g + q) * 128, 128), :]) for q in range(4)
        ]
        finished = mix(out_final_ref[...], jnp.concatenate(products, axis=1))
        slabs = []
        picks = []
        for q in range(4):
            h = 4 * g + q
            lanes = slice(q * LANES, (q + 1) * LANES)
            slab = pair_now_ref[h] + gating_ref[h] * finished[:, lanes]
            pair_now_ref[h] = slab
            slabs.append(normalize_channels(slab))
            here = jnp.where(slab_of == h, wanted, -1)
            picks.append((source == here).astype(jnp.float32).astype(jnp.bfloat16))
        normed = jnp.concatenate(slabs, axis=1)
        chosen_ref[...] += mix(normed, jnp.concatenate(picks, axis=0))
        combined = mix(in_mix_ref[256:512, :], normed)
        right = gate_curve(combined[128:256]) * combined[0:128]
        for q in range(4):
            right_ref[pl.ds((4 * g + q) * 128, 128), :] = right[:, q * LANES : (q + 1) * LANES]
        return carry

    lax.fori_loop(0, 8, second_chunk, 0)

    combined = mix(in_mix_ref[0:256, :], chosen_ref[...].astype(jnp.bfloat16))
    own_left = gate_curve(combined[128:256]) * combined[0:128]
    for m in range(8):
        part = own_left[:, (m // 4) * LANES : (m // 4 + 1) * LANES]
        if m % 4:
            part = pltpu.roll(part, LANES - 32 * (m % 4), 1)
        own_left_ref[m * 128 : (m + 1) * 128, :] = part

    def incoming_channels(block, carry):
        for e in range(8):
            c = block * 8 + e
            left = own_left_ref[pl.ds(c, 8, stride=128), :][:, 0:32].astype(jnp.bfloat16)
            right = right_ref[pl.ds(c, 32, stride=128), :].astype(jnp.bfloat16)
            own_product_ref[pl.ds(c, 8, stride=128), :] = mix(left, right)
        return carry

    lax.fori_loop(0, 16, incoming_channels, 0)

    def own_block(m):
        return own_product_ref[m * 128 : (m + 1) * 128, :]

    products = [
        normalize_channels(
            fold_halves(
                own_block(2 * t), own_block(2 * t + 1), own_block(4 + 2 * t), own_block(5 + 2 * t), low_half
            )
        )
        for t in range(2)
    ]
    finished = mix(in_final_ref[...], jnp.concatenate(products, axis=1))
    own_pair = jnp.concatenate([pair_now_ref[2 * place + t] for t in range(2)], axis=1)
    gating = gate_curve(mix(in_gate_ref[...], normalize_channels(own_pair)))
    own_pair = own_pair + gating * finished
    hidden = jnp.maximum(mix(up_ref[...], normalize_channels(own_pair)), 0.0).astype(jnp.bfloat16)
    own_pair = (own_pair + mix(down_ref[...], hidden)).astype(jnp.bfloat16)
    lane = lax.broadcasted_iota(jnp.int32, (LANES, LANES), 1)
    back = half * (channel // half) + 32 * (channel % 2) + (channel % half) // 2
    order = (lane == back).astype(jnp.float32).astype(jnp.bfloat16)
    for t in range(2):
        result_ref[t * 128 : (t + 1) * 128, :] = lax.dot_general(
            order,
            own_pair[:, t * LANES : (t + 1) * LANES],
            (((1,), (1,)), ((), ())),
            preferred_element_type=jnp.float32,
        ).astype(jnp.bfloat16)


def rows_kernel(rows_ref, blocks_ref, wide_ref):
    residues = rows_ref.shape[1]
    count = 8 * residues
    rows = rows_ref[...].astype(jnp.float32).reshape(count, 2 * LANES)
    for e in range(2):
        wide_ref[e * count : (e + 1) * count, :] = rows[:, e * LANES : (e + 1) * LANES]
    for p in range(16):
        for e in range(2):
            block = [
                wide_ref[pl.ds(e * count + 4 * p + i, 8, stride=residues), :] for i in range(4)
            ]
            blocks_ref[p, :, e * LANES : (e + 1) * LANES] = jnp.concatenate(block, axis=0).astype(
                jnp.bfloat16
            )


def normalize_rows(values):
    center = jnp.mean(values, axis=1, keepdims=True)
    shifted = values - center
    spread = jnp.mean(shifted * shifted, axis=1, keepdims=True)
    return (shifted * lax.rsqrt(spread + EPSILON)).astype(jnp.bfloat16)


def contract_last(first, second):
    return lax.dot_general(
        first, second, (((1,), (1,)), ((), ())), preferred_element_type=jnp.float32
    )


def msa_kernel(
    blocks_ref,
    live_ref,
    query_ref,
    key_ref,
    value_gate_ref,
    output_ref,
    up_ref,
    down_ref,
    outer_ref,
    result_ref,
    parts_ref,
    wide_ref,
    final_ref,
):
    for p in range(16):
        block = blocks_ref[p].astype(jnp.float32)
        for i in range(4):
            wide_ref[i * 128 + p * 8 : i * 128 + p * 8 + 8, :] = block[i * 8 : i * 8 + 8, :]
    live = live_ref[...]
    alive = live > 0.0
    width = HM * HEAD_SIZE
    head_of = lax.broadcasted_iota(jnp.int32, (128, width), 1) // HEAD_SIZE
    zero = jnp.zeros((128, width), jnp.bfloat16)
    for i in range(4):
        rows = slice(i * 128, (i + 1) * 128)
        current = wide_ref[rows, :]
        normed = normalize_rows(current)
        query = (mix(normed, query_ref[...]) * HEAD_SIZE ** (-0.5)).astype(jnp.bfloat16)
        key = mix(normed, key_ref[...]).astype(jnp.bfloat16)
        value_gate = mix(normed, value_gate_ref[...])
        value = value_gate[:, :width].astype(jnp.bfloat16)
        keys = jnp.concatenate([jnp.where(head_of == h, key, zero) for h in range(HM)], axis=0)
        values = jnp.concatenate([jnp.where(head_of == h, value, zero) for h in range(HM)], axis=0)
        scores = contract_last(query, keys)
        heads = []
        for h in range(HM):
            score = jnp.where(alive, scores[:, h * 128 : (h + 1) * 128], -1000000000.0)
            raised = jnp.exp(score - jnp.max(score, axis=1, keepdims=True))
            heads.append((raised / jnp.sum(raised, axis=1, keepdims=True)).astype(jnp.bfloat16))
        attended = mix(jnp.concatenate(heads, axis=1), values)
        gated = (gate_curve(value_gate[:, width:]) * attended).astype(jnp.bfloat16)
        current = current + mix(gated, output_ref[...])
        hidden = jnp.maximum(mix(normalize_rows(current), up_ref[...]), 0.0).astype(jnp.bfloat16)
        final = (current + mix(hidden, down_ref[...])).astype(jnp.bfloat16).astype(jnp.float32)
        final_ref[pl.ds(i, 128, stride=4), :] = final[:, :128]
        final_ref[pl.ds(512 + i, 128, stride=4), :] = final[:, 128:]
        outer = (contract_last(outer_ref[...], normalize_rows(final)) * live).astype(jnp.bfloat16)
        parts_ref[i * CO : (i + 1) * CO, :] = outer[:CO, :]
        parts_ref[128 + i * CO : 128 + (i + 1) * CO, :] = outer[CO:, :]
    result_ref[:, :128] = final_ref[:512, :].astype(jnp.bfloat16)
    result_ref[:, 128:] = final_ref[512:, :].astype(jnp.bfloat16)


def msa_whole(
    alignment_input,
    live_row_float,
    column_query_weight,
    column_key_weight,
    column_value_gate_weight,
    column_output_weight,
    alignment_transition_up,
    alignment_transition_down,
    outer_input_weight,
):
    channels = alignment_input.shape[2]
    vmem = pl.BlockSpec(memory_space=pltpu.VMEM)
    blocks = pl.pallas_call(
        rows_kernel,
        out_shape=jax.ShapeDtypeStruct((16, 32, channels), jnp.bfloat16),
        in_specs=[vmem],
        out_specs=vmem,
        scratch_shapes=[pltpu.VMEM((1024, LANES), jnp.float32)],
        compiler_params=pltpu.CompilerParams(vmem_limit_bytes=16 * 1024 * 1024),
        name="rows_by_device",
    )(alignment_input)
    blocks = lax.all_to_all(blocks, "dap", split_axis=0, concat_axis=0, tiled=True)
    result, parts = pl.pallas_call(
        msa_kernel,
        out_shape=(
            jax.ShapeDtypeStruct((512, channels), jnp.bfloat16),
            jax.ShapeDtypeStruct((256, LANES), jnp.bfloat16),
        ),
        in_specs=[vmem] * 9,
        out_specs=(vmem, vmem),
        scratch_shapes=[
            pltpu.VMEM((512, channels), jnp.float32),
            pltpu.VMEM((1024, LANES), jnp.float32),
        ],
        compiler_params=pltpu.CompilerParams(vmem_limit_bytes=32 * 1024 * 1024),
        cost_estimate=pl.CostEstimate(
            flops=1_000_000_000, bytes_accessed=2_500_000, transcendentals=1_000_000
        ),
        name="msa_whole",
    )(
        blocks,
        live_row_float.reshape(1, LANES),
        column_query_weight,
        column_key_weight,
        column_value_gate_weight,
        column_output_weight,
        alignment_transition_up,
        alignment_transition_down,
        outer_input_weight.T,
    )
    return result.reshape(128, 4, channels), parts


def lanes_order(values):
    lead = values.shape[:-1]
    halves = values.reshape(lead + (values.shape[-1] // 2, 2))
    return jnp.swapaxes(halves, -1, -2).reshape(values.shape)


def pair_whole(
    parts,
    pair_state_input,
    bin_all,
    live_count,
    relative_position_table,
    outer_output_weight,
    outgoing_projection_weight,
    outgoing_output_gate,
    outgoing_output_weight,
    incoming_projection_weight,
    incoming_output_gate,
    incoming_output_weight,
    pair_transition_up,
    pair_transition_down,
):
    width = pair_state_input.shape[2]
    own_pair = lanes_order(pair_state_input.transpose(0, 2, 1))
    own_pair = own_pair.reshape(2, 2, width, 64).transpose(0, 2, 1, 3).reshape(2, width, LANES)
    pair_all = gather_exchange(own_pair).reshape(32, width, LANES)
    parts_all = gather_exchange(parts)
    bins = lanes_order(bin_all).reshape(32, LANES)
    table = jnp.pad(relative_position_table, ((0, LANES - NBINS), (0, 0))).T
    mean_weight = (
        outer_output_weight.reshape(CO, 16, 2, width).transpose(2, 3, 1, 0).reshape(2 * width, 16 * CO)
    )
    place = lax.axis_index("dap").astype(jnp.int32).reshape(1)
    vmem = pl.BlockSpec(memory_space=pltpu.VMEM)
    smem = pl.BlockSpec(memory_space=pltpu.SMEM)
    tall = (32 * 128, LANES)
    result = pl.pallas_call(
        pair_kernel,
        out_shape=jax.ShapeDtypeStruct((256, LANES), jnp.bfloat16),
        in_specs=[smem, smem] + [vmem] * 13,
        out_specs=vmem,
        scratch_shapes=[
            pltpu.VMEM((2048, LANES), jnp.float32),
            pltpu.VMEM((128, 2048), jnp.bfloat16),
            pltpu.VMEM((512, 1024), jnp.bfloat16),
            pltpu.VMEM((32, 128, LANES), jnp.float32),
            pltpu.VMEM(tall, jnp.float32),
            pltpu.VMEM(tall, jnp.float32),
            pltpu.VMEM(tall, jnp.float32),
            pltpu.VMEM((32, 128, LANES), jnp.float32),
            pltpu.VMEM((128, 256), jnp.float32),
            pltpu.VMEM((1024, LANES), jnp.float32),
            pltpu.VMEM((1024, LANES), jnp.float32),
        ],
        compiler_params=pltpu.CompilerParams(vmem_limit_bytes=40 * 1024 * 1024),
        name="pair_whole",
    )(
        place,
        live_count.reshape(1),
        parts_all,
        pair_all,
        bins,
        table,
        mean_weight,
        outgoing_projection_weight.T,
        outgoing_output_gate.T,
        outgoing_output_weight.T,
        incoming_projection_weight.T,
        incoming_output_gate.T,
        incoming_output_weight.T,
        pair_transition_up.T,
        pair_transition_down.T,
    )
    return result.reshape(pair_state_input.shape)


def gather_exchange(block):
    shard_pieces = lax.axis_size("dap")
    held = block[None]
    bit = shard_pieces // 2
    while bit:
        other = lax.ppermute(held, "dap", [(q, q ^ bit) for q in range(shard_pieces)])
        held = jnp.concatenate([held, other], axis=0)
        bit //= 2
    return held


def local(
    alignment_input,
    pair_state_input,
    residue_number_index,
    chain_label,
    alignment_row_mask,
    relative_position_table,
    column_query_weight,
    column_key_weight,
    column_value_gate_weight,
    column_output_weight,
    alignment_transition_up,
    alignment_transition_down,
    outer_input_weight,
    outer_output_weight,
    outgoing_projection_weight,
    outgoing_output_gate,
    outgoing_output_weight,
    incoming_projection_weight,
    incoming_output_gate,
    incoming_output_weight,
    pair_transition_up,
    pair_transition_down,
):
    shard_pieces = lax.axis_size("dap")
    own_rows = pair_state_input.shape[0]
    residue_count = pair_state_input.shape[1]
    channel_count = alignment_input.shape[2]
    head_width = HM * HEAD_SIZE
    first_row = lax.axis_index("dap") * own_rows
    own_index = lax.dynamic_slice_in_dim(residue_number_index, first_row, own_rows)
    own_chain = lax.dynamic_slice_in_dim(chain_label, first_row, own_rows)

    def bins_of(index, chain):
        offset = index[:, None] - residue_number_index[None, :]
        return jnp.where(
            chain[:, None] == chain_label[None, :],
            jnp.clip(offset + MAXREL, 0, 2 * MAXREL),
            2 * MAXREL + 1,
        )

    bin_index = bins_of(own_index, own_chain)
    one_hot = (bin_index[:, :, None] == jnp.arange(NBINS, dtype=jnp.int32)[None, None, :]).astype(
        jnp.bfloat16
    )
    pair_start = pair_state_input.astype(jnp.float32) + jnp.einsum(
        "ijb,bc->ijc", one_hot, relative_position_table, preferred_element_type=jnp.float32
    )
    live_rows = alignment_row_mask > 0
    live_row_float = live_rows.astype(jnp.float32)

    if alignment_row_mask.shape[0] == LANES and 2 * residue_count == LANES and own_rows == 4:
        result, parts = msa_whole(
            alignment_input,
            live_row_float,
            column_query_weight,
            column_key_weight,
            column_value_gate_weight,
            column_output_weight,
            alignment_transition_up,
            alignment_transition_down,
            outer_input_weight,
        )
        pair_state_output = pair_whole(
            parts,
            pair_state_input,
            bins_of(residue_number_index, chain_label),
            jnp.sum(live_row_float),
            relative_position_table,
            outer_output_weight,
            outgoing_projection_weight,
            outgoing_output_gate,
            outgoing_output_weight,
            incoming_projection_weight,
            incoming_output_gate,
            incoming_output_weight,
            pair_transition_up,
            pair_transition_down,
        )
        return (result, pair_state_output)

    def attend_one(operands):
        query_col, key_col, value_col = operands
        scores = jnp.einsum("shd,thd->hst", query_col, key_col, preferred_element_type=jnp.float32)
        scores = jnp.where(live_rows[None, None, :], scores, -1000000000.0)
        row_top = jnp.max(scores, axis=-1, keepdims=True)
        raised = jnp.exp(scores - row_top)
        attention = (raised / jnp.sum(raised, axis=-1, keepdims=True)).astype(jnp.bfloat16)
        return jnp.einsum("hst,thd->shd", attention, value_col, preferred_element_type=jnp.float32)

    blocked_view = alignment_input.reshape(
        alignment_input.shape[0], shard_pieces, residue_count // shard_pieces, channel_count
    )
    block_in = lax.all_to_all(blocked_view, "dap", split_axis=1, concat_axis=0, tiled=True)
    depth_rows = block_in.shape[0]
    count_cols = block_in.shape[2]
    current = block_in.reshape(depth_rows, count_cols, channel_count).astype(jnp.float32)
    normed = layer_normalize(current).astype(jnp.bfloat16)
    query_rows = (
        jnp.einsum("sic,ce->sie", normed, column_query_weight, preferred_element_type=jnp.float32)
        * HEAD_SIZE ** (-0.5)
    ).astype(jnp.bfloat16)
    key_row_block = jnp.einsum(
        "sic,ce->sie", normed, column_key_weight, preferred_element_type=jnp.float32
    ).astype(jnp.bfloat16)
    value_gate_pair = jnp.einsum(
        "sic,ce->sie", normed, column_value_gate_weight, preferred_element_type=jnp.float32
    )
    value_rows = value_gate_pair[..., :head_width].astype(jnp.bfloat16)

    def by_column(values):
        return values.transpose(1, 0, 2).reshape(count_cols, depth_rows, HM, HEAD_SIZE)

    attended = lax.map(
        attend_one, (by_column(query_rows), by_column(key_row_block), by_column(value_rows))
    )
    attended = attended.reshape(count_cols, depth_rows, head_width).transpose(1, 0, 2)
    gated_out = (jax.nn.sigmoid(value_gate_pair[..., head_width:]) * attended).astype(jnp.bfloat16)
    current = current + jnp.einsum(
        "sie,ec->sic", gated_out, column_output_weight, preferred_element_type=jnp.float32
    )
    hidden = jax.nn.relu(
        jnp.einsum(
            "sic,cf->sif",
            layer_normalize(current).astype(jnp.bfloat16),
            alignment_transition_up,
            preferred_element_type=jnp.float32,
        )
    ).astype(jnp.bfloat16)
    current = current + jnp.einsum(
        "sif,fc->sic", hidden, alignment_transition_down, preferred_element_type=jnp.float32
    )
    result = current.astype(jnp.bfloat16)
    outer_product_input = jnp.einsum(
        "sic,cf->sif",
        layer_normalize(result.astype(jnp.float32)).astype(jnp.bfloat16),
        outer_input_weight,
        preferred_element_type=jnp.float32,
    )
    outer_product_input = outer_product_input * live_row_float[:, None, None]
    left_part = outer_product_input[..., :CO].astype(jnp.bfloat16)
    right_part = outer_product_input[..., CO:].astype(jnp.bfloat16)
    all_rows = result.shape[0]
    left_cols = left_part.transpose(1, 0, 2)
    right_cols = right_part.transpose(1, 0, 2).reshape(own_rows, all_rows * CO)
    live_count = jnp.sum(live_row_float)
    right_piece = gather_doubling(right_cols).reshape(-1, all_rows * CO)
    span_rows = right_piece.shape[0]
    products = jnp.einsum(
        "isc,jsd->ijcd",
        left_cols,
        right_piece.reshape(span_rows, all_rows, CO),
        preferred_element_type=jnp.float32,
    )
    products = products.astype(jnp.bfloat16).reshape(own_rows, span_rows, CO * CO)
    outer_mean = (
        jnp.einsum("ijf,fc->ijc", products, outer_output_weight, preferred_element_type=jnp.float32)
        / live_count
    )
    pair_mid = pair_start + outer_mean
    out_left, out_right, out_gating = triangle_inputs(
        pair_mid, outgoing_projection_weight, outgoing_output_gate
    )
    out_product = by_channels(out_left, out_right, "cik,cjk->cij")
    pair_after_out = triangle_finish(pair_mid, out_product, out_gating, outgoing_output_weight)
    in_left, in_right, in_gating = triangle_inputs(
        pair_after_out, incoming_projection_weight, incoming_output_gate
    )
    in_product = by_channels(in_left, in_right, "cki,ckj->cij")
    pair_after_in = triangle_finish(pair_after_out, in_product, in_gating, incoming_output_weight)
    pair_expanded = jax.nn.relu(
        jnp.einsum(
            "ijc,cf->ijf",
            layer_normalize(pair_after_in).astype(jnp.bfloat16),
            pair_transition_up,
            preferred_element_type=jnp.float32,
        )
    ).astype(jnp.bfloat16)
    pair_state_output = (
        pair_after_in
        + jnp.einsum(
            "ijf,fc->ijc", pair_expanded, pair_transition_down, preferred_element_type=jnp.float32
        )
    ).astype(jnp.bfloat16)
    return (result, pair_state_output)


def solution(mesh):
    in_specs = (
        P(("grp", "dap"), None, None),
        P(("grp", "dap"), None, None),
        P("grp"),
        P("grp"),
        P("grp"),
        P(),
        P(),
        P(),
        P(),
        P(),
        P(),
        P(),
        P(),
        P(),
        P(),
        P(),
        P(),
        P(),
        P(),
        P(),
        P(),
        P(),
    )
    out_specs = (P("grp", "dap", None), P(("grp", "dap"), None, None))
    return jax.shard_map(local, mesh=mesh, in_specs=in_specs, out_specs=out_specs, check_vma=False)
```

```python
import functools

import jax
import jax.numpy as jnp
from jax import lax
from jax.experimental import pallas as pl
from jax.experimental.pallas import tpu as pltpu
from jax.sharding import PartitionSpec as P

HM = 8
HEAD_SIZE = 32
CO = 32
MAXREL = 32
NBINS = 66


EPSILON = 1e-05


def layer_normalize(values):
    center = jnp.mean(values, axis=-1, keepdims=True)
    shifted = values - center
    spread = jnp.mean(shifted * shifted, axis=-1, keepdims=True)
    return shifted * lax.rsqrt(spread + EPSILON)


def triangle_inputs(pair_now, weight, gate_weight):
    normed = layer_normalize(pair_now).astype(jnp.bfloat16)
    combined = jnp.einsum("ijc,cf->fij", normed, weight, preferred_element_type=jnp.float32)
    hidden_width = weight.shape[1] // 4
    left_side = (
        jax.nn.sigmoid(combined[hidden_width : 2 * hidden_width]) * combined[:hidden_width]
    ).astype(jnp.bfloat16)
    right_side = (
        jax.nn.sigmoid(combined[3 * hidden_width :]) * combined[2 * hidden_width : 3 * hidden_width]
    ).astype(jnp.bfloat16)
    gating = jax.nn.sigmoid(
        jnp.einsum("ijc,cd->ijd", normed, gate_weight, preferred_element_type=jnp.float32)
    )
    return (left_side, right_side, gating)


def triangle_finish(pair_now, product, gating, final_weight):
    product = lax.optimization_barrier(product)
    normed = layer_normalize(product.transpose(1, 2, 0).astype(jnp.float32)).astype(jnp.bfloat16)
    return pair_now + gating * jnp.einsum(
        "ijc,cd->ijd", normed, final_weight, preferred_element_type=jnp.float32
    )


def by_channels(left_side, right_side, form):
    both = jnp.stack([left_side, right_side])
    both = lax.all_to_all(both, "dap", split_axis=1, concat_axis=2, tiled=True)
    partial_out = jnp.einsum(form, both[0], both[1], preferred_element_type=jnp.float32)
    return lax.all_to_all(
        partial_out.astype(jnp.bfloat16), "dap", split_axis=1, concat_axis=0, tiled=True
    )


def gather_doubling(block):
    shard_pieces = lax.axis_size("dap")
    place = lax.axis_index("dap")
    held = block
    depth = 0
    bit = shard_pieces // 2
    while bit:
        other = lax.ppermute(held, "dap", [(q, q ^ bit) for q in range(shard_pieces)])
        upper = (place & bit) != 0
        first = jnp.where(upper, other, held)
        second = jnp.where(upper, held, other)
        held = jnp.stack([first, second], axis=depth)
        depth += 1
        bit //= 2
    return held.reshape((shard_pieces,) + block.shape)


LANES = 128


def gate_curve(values):
    return 0.5 + 0.5 * jnp.tanh(0.5 * values)


def normalize_channels(values):
    center = jnp.mean(values, axis=0, keepdims=True)
    shifted = values - center
    spread = jnp.mean(shifted * shifted, axis=0, keepdims=True)
    return (shifted * lax.rsqrt(spread + EPSILON)).astype(jnp.bfloat16)


def mix(weight, values):
    return jnp.dot(weight, values, preferred_element_type=jnp.float32)


def fold_halves(first_even, second_even, first_odd, second_odd, low_half):
    straight = jnp.where(low_half, first_even, second_odd)
    crossed = jnp.where(low_half, second_even, first_odd)
    return straight + pltpu.roll(crossed, LANES // 2, 1)


def pair_kernel(
    place_ref,
    live_ref,
    *rest,
):
    pair_body(place_ref, live_ref, rest[:4], rest[4:8], *rest[8:])


def pair_body(
    place_ref,
    live_ref,
    part_refs,
    pair_refs,
    embedding_ref,
    mean_weight_ref,
    out_mix_ref,
    out_gate_ref,
    out_final_ref,
    in_mix_ref,
    in_gate_ref,
    in_final_ref,
    up_ref,
    down_ref,
    result_ref,
    wide_ref,
    right_cols_ref,
    stack_ref,
    pair_now_ref,
    left_ref,
    right_ref,
    product_ref,
    gating_ref,
    chosen_ref,
    own_left_ref,
    own_product_ref,
):
    place = place_ref[0]
    inverse_live = 1.0 / live_ref[0]
    half = LANES // 2
    low_half = lax.broadcasted_iota(jnp.int32, (LANES, LANES), 1) < half
    low_short = lax.broadcasted_iota(jnp.int32, (32, LANES), 1) < half

    offsets = (0, 2, 1, 3)

    def owner_of(piece, m):
        return place ^ (offsets[piece] + (m & 1) * 8 + (m & 2) * 2)

    for piece in range(4):
        for m in range(4):
            first = pl.multiple_of(owner_of(piece, m) * 128, 128)
            wide_ref[pl.ds(first, 128), :] = part_refs[piece][m, 128:256, :].astype(jnp.float32)
    for d in range(0, CO, 2):
        rows = [
            wide_ref[pl.ds(par * CO + d + e, 32, stride=2 * CO), :]
            for e in range(2)
            for par in range(2)
        ]
        right_cols_ref[:, d * half : d * half + LANES] = (
            jnp.concatenate(rows, axis=0).T.astype(jnp.bfloat16)
        )

    def first_chunk(piece, g, carry):
        left_rows = part_refs[piece][pl.ds(2 * g, 2), 0:128, :].reshape(256, LANES)
        outer = mix(left_rows, right_cols_ref[...]).astype(jnp.bfloat16)
        for i in range(8):
            for d in range(16):
                stack_ref[d * 32 : (d + 1) * 32, i * LANES : (i + 1) * LANES] = outer[
                    i * 32 : (i + 1) * 32, d * LANES : (d + 1) * LANES
                ]
        mixed = mix(mean_weight_ref[...], stack_ref[...])
        slabs = []
        for q in range(4):
            h = 2 * owner_of(piece, 2 * g + q // 2) + q % 2
            even = slice(2 * q * LANES, (2 * q + 1) * LANES)
            odd = slice((2 * q + 1) * LANES, (2 * q + 2) * LANES)
            outer_mean = fold_halves(
                mixed[0:128, even], mixed[0:128, odd], mixed[128:256, even], mixed[128:256, odd], low_half
            )
            start = pair_refs[piece][2 * g + q // 2, q % 2].astype(jnp.float32)
            start = start + embedding_ref[h].astype(jnp.float32)
            slab = start + outer_mean * inverse_live
            pair_now_ref[h] = slab
            slabs.append(normalize_channels(slab))
        normed = jnp.concatenate(slabs, axis=1)
        combined = mix(out_mix_ref[...], normed)
        left = gate_curve(combined[128:256]) * combined[0:128]
        right = gate_curve(combined[384:512]) * combined[256:384]
        gating = gate_curve(mix(out_gate_ref[...], normed))
        for q in range(4):
            h = 2 * owner_of(piece, 2 * g + q // 2) + q % 2
            lanes = slice(q * LANES, (q + 1) * LANES)
            left_ref[pl.ds(h * 128, 128), :] = left[:, lanes]
            right_ref[pl.ds(h * 128, 128), :] = right[:, lanes]
            gating_ref[h] = gating[:, lanes]
        return carry

    for piece in range(4):
        lax.fori_loop(0, 2, functools.partial(first_chunk, piece), 0)

    def outgoing_channels(block, carry):
        for e in range(8):
            c = block * 8 + e
            left = left_ref[pl.ds(c, 32, stride=128), :].astype(jnp.bfloat16)
            right = right_ref[pl.ds(c, 32, stride=128), :]
            turned = pltpu.roll(right, half, 1)
            spread = jnp.concatenate(
                [
                    jnp.where(low_short, right, 0.0),
                    jnp.where(low_short, turned, 0.0),
                    jnp.where(low_short, 0.0, turned),
                    jnp.where(low_short, 0.0, right),
                ],
                axis=0,
            ).astype(jnp.bfloat16)
            product_ref[pl.ds(c, 32, stride=128), :] = lax.dot_general(
                left, spread, (((1,), (1,)), ((), ())), preferred_element_type=jnp.float32
            )
        return carry

    lax.fori_loop(0, 16, outgoing_channels, 0)

    column = lax.broadcasted_iota(jnp.int32, (1, 256), 1)
    which = column // 32
    own = which % 4
    wanted = half * (which // 4) + 32 * (own % 2) + 2 * place + own // 2
    slab_of = column % 32
    source = lax.broadcasted_iota(jnp.int32, (LANES, 256), 0)
    chosen_ref[...] = jnp.zeros_like(chosen_ref)

    def second_chunk(g, carry):
        products = [
            normalize_channels(product_ref[pl.ds((4 * g + q) * 128, 128), :]) for q in range(4)
        ]
        finished = mix(out_final_ref[...], jnp.concatenate(products, axis=1))
        slabs = []
        picks = []
        for q in range(4):
            h = 4 * g + q
            lanes = slice(q * LANES, (q + 1) * LANES)
            slab = pair_now_ref[h] + gating_ref[h] * finished[:, lanes]
            pair_now_ref[h] = slab
            slabs.append(normalize_channels(slab))
            here = jnp.where(slab_of == h, wanted, -1)
            picks.append((source == here).astype(jnp.float32).astype(jnp.bfloat16))
        normed = jnp.concatenate(slabs, axis=1)
        chosen_ref[...] += mix(normed, jnp.concatenate(picks, axis=0))
        combined = mix(in_mix_ref[256:512, :], normed)
        right = gate_curve(combined[128:256]) * combined[0:128]
        for q in range(4):
            right_ref[pl.ds((4 * g + q) * 128, 128), :] = right[:, q * LANES : (q + 1) * LANES]
        return carry

    lax.fori_loop(0, 8, second_chunk, 0)

    combined = mix(in_mix_ref[0:256, :], chosen_ref[...].astype(jnp.bfloat16))
    own_left = gate_curve(combined[128:256]) * combined[0:128]
    for m in range(8):
        part = own_left[:, (m // 4) * LANES : (m // 4 + 1) * LANES]
        if m % 4:
            part = pltpu.roll(part, LANES - 32 * (m % 4), 1)
        own_left_ref[m * 128 : (m + 1) * 128, :] = part

    def incoming_channels(block, carry):
        for e in range(8):
            c = block * 8 + e
            left = own_left_ref[pl.ds(c, 8, stride=128), :][:, 0:32].astype(jnp.bfloat16)
            right = right_ref[pl.ds(c, 32, stride=128), :].astype(jnp.bfloat16)
            own_product_ref[pl.ds(c, 8, stride=128), :] = mix(left, right)
        return carry

    lax.fori_loop(0, 16, incoming_channels, 0)

    def own_block(m):
        return own_product_ref[m * 128 : (m + 1) * 128, :]

    products = [
        normalize_channels(
            fold_halves(
                own_block(2 * t), own_block(2 * t + 1), own_block(4 + 2 * t), own_block(5 + 2 * t), low_half
            )
        )
        for t in range(2)
    ]
    finished = mix(in_final_ref[...], jnp.concatenate(products, axis=1))
    own_pair = jnp.concatenate([pair_now_ref[2 * place + t] for t in range(2)], axis=1)
    gating = gate_curve(mix(in_gate_ref[...], normalize_channels(own_pair)))
    own_pair = own_pair + gating * finished
    hidden = jnp.maximum(mix(up_ref[...], normalize_channels(own_pair)), 0.0).astype(jnp.bfloat16)
    own_pair = (own_pair + mix(down_ref[...], hidden)).astype(jnp.bfloat16)
    order = lane_order_matrix()
    for t in range(2):
        result_ref[t * 128 : (t + 1) * 128, :] = lax.dot_general(
            order,
            own_pair[:, t * LANES : (t + 1) * LANES],
            (((1,), (1,)), ((), ())),
            preferred_element_type=jnp.float32,
        ).astype(jnp.bfloat16)


def lane_order_matrix():
    half = LANES // 2
    member = lax.broadcasted_iota(jnp.int32, (LANES, LANES), 0)
    lane = lax.broadcasted_iota(jnp.int32, (LANES, LANES), 1)
    back = half * (member // half) + 32 * (member % 2) + (member % half) // 2
    return (lane == back).astype(jnp.float32).astype(jnp.bfloat16)


def contract_first(first, second):
    return lax.dot_general(
        first, second, (((0,), (0,)), ((), ())), preferred_element_type=jnp.float32
    )


def rows_kernel(place_ref, rows_ref, pair_ref, own_pair_ref, *rest):
    block_refs, wide_ref = rest[:-1], rest[-1]
    residues = rows_ref.shape[1]
    count = 8 * residues
    rows = rows_ref[...].astype(jnp.float32).reshape(count, 2 * LANES)
    for e in range(2):
        wide_ref[e * count : (e + 1) * count, :] = rows[:, e * LANES : (e + 1) * LANES]
    for m in range(16):
        first = 4 * (place_ref[0] ^ m)
        for e in range(2):
            block = [
                wide_ref[pl.ds(e * count + first + i, 8, stride=residues), :] for i in range(4)
            ]
            block_refs[m][:, e * LANES : (e + 1) * LANES] = jnp.concatenate(block, axis=0).astype(
                jnp.bfloat16
            )
    order = lane_order_matrix()
    for t in range(2):
        own_pair_ref[t] = contract_first(
            pair_ref[2 * t : 2 * t + 2].reshape(LANES, LANES), order
        ).astype(jnp.bfloat16)


def weights_kernel(
    bins_ref,
    table_ref,
    mean_weight_ref,
    out_mix_ref,
    out_gate_ref,
    out_final_ref,
    in_mix_ref,
    in_gate_ref,
    in_final_ref,
    up_ref,
    down_ref,
    embedding_out,
    mean_weight_out,
    out_mix_out,
    out_gate_out,
    out_final_out,
    in_mix_out,
    in_gate_out,
    in_final_out,
    up_out,
    down_out,
    table_wide_ref,
    mean_wide_ref,
):
    table_wide_ref[...] = jnp.zeros_like(table_wide_ref)
    table_wide_ref[0:NBINS, :] = table_ref[...].astype(jnp.float32)
    table = table_wide_ref[...].T.astype(jnp.bfloat16)
    channel = lax.broadcasted_iota(jnp.int32, (LANES, LANES), 0)

    def embed(g, carry):
        for q in range(4):
            h = 4 * g + q
            one_hot = (channel == bins_ref[pl.ds(h, 1), :]).astype(jnp.float32).astype(jnp.bfloat16)
            embedding_out[h] = mix(table, one_hot).astype(jnp.bfloat16)
        return carry

    lax.fori_loop(0, 8, embed, 0)
    mean_wide_ref[...] = mean_weight_ref[...].astype(jnp.float32)
    for e in range(2):
        for block in range(4):
            rows = [
                mean_wide_ref[pl.ds(2 * (4 * block + k) + e, CO, stride=CO), :] for k in range(4)
            ]
            mean_weight_out[e * LANES : (e + 1) * LANES, block * LANES : (block + 1) * LANES] = (
                jnp.concatenate(rows, axis=0).T.astype(jnp.bfloat16)
            )
    for source, target in (
        (out_mix_ref, out_mix_out),
        (out_gate_ref, out_gate_out),
        (out_final_ref, out_final_out),
        (in_mix_ref, in_mix_out),
        (in_gate_ref, in_gate_out),
        (in_final_ref, in_final_out),
        (up_ref, up_out),
        (down_ref, down_out),
    ):
        rows, columns = source.shape
        for a in range(rows // LANES):
            for b in range(columns // LANES):
                part = source[a * LANES : (a + 1) * LANES, b * LANES : (b + 1) * LANES]
                target[b * LANES : (b + 1) * LANES, a * LANES : (a + 1) * LANES] = (
                    part.astype(jnp.float32).T.astype(jnp.bfloat16)
                )


def normalize_rows(values):
    center = jnp.mean(values, axis=1, keepdims=True)
    shifted = values - center
    spread = jnp.mean(shifted * shifted, axis=1, keepdims=True)
    return (shifted * lax.rsqrt(spread + EPSILON)).astype(jnp.bfloat16)


def contract_last(first, second):
    return lax.dot_general(
        first, second, (((1,), (1,)), ((), ())), preferred_element_type=jnp.float32
    )


def msa_kernel(place_ref, live_ref, *rest):
    block_refs = rest[:16]
    msa_body(place_ref, live_ref, block_refs, *rest[16:])


def msa_body(
    place_ref,
    live_ref,
    block_refs,
    query_ref,
    key_ref,
    value_gate_ref,
    output_ref,
    up_ref,
    down_ref,
    outer_ref,
    result_ref,
    parts_ref,
    wide_ref,
    final_ref,
):
    for m in range(16):
        block = block_refs[m][...].astype(jnp.float32)
        first = (place_ref[0] ^ m) * 8
        for i in range(4):
            wide_ref[pl.ds(pl.multiple_of(i * 128 + first, 8), 8), :] = block[i * 8 : i * 8 + 8, :]
    live = live_ref[...]
    alive = live > 0.0
    width = HM * HEAD_SIZE
    head_of = lax.broadcasted_iota(jnp.int32, (128, width), 1) // HEAD_SIZE
    zero = jnp.zeros((128, width), jnp.bfloat16)
    for i in range(4):
        rows = slice(i * 128, (i + 1) * 128)
        current = wide_ref[rows, :]
        normed = normalize_rows(current)
        query = (mix(normed, query_ref[...]) * HEAD_SIZE ** (-0.5)).astype(jnp.bfloat16)
        key = mix(normed, key_ref[...]).astype(jnp.bfloat16)
        value_gate = mix(normed, value_gate_ref[...])
        value = value_gate[:, :width].astype(jnp.bfloat16)
        keys = jnp.concatenate([jnp.where(head_of == h, key, zero) for h in range(HM)], axis=0)
        values = jnp.concatenate([jnp.where(head_of == h, value, zero) for h in range(HM)], axis=0)
        scores = contract_last(query, keys)
        heads = []
        for h in range(HM):
            score = jnp.where(alive, scores[:, h * 128 : (h + 1) * 128], -1000000000.0)
            raised = jnp.exp(score - jnp.max(score, axis=1, keepdims=True))
            heads.append((raised / jnp.sum(raised, axis=1, keepdims=True)).astype(jnp.bfloat16))
        attended = mix(jnp.concatenate(heads, axis=1), values)
        gated = (gate_curve(value_gate[:, width:]) * attended).astype(jnp.bfloat16)
        current = current + mix(gated, output_ref[...])
        hidden = jnp.maximum(mix(normalize_rows(current), up_ref[...]), 0.0).astype(jnp.bfloat16)
        final = (current + mix(hidden, down_ref[...])).astype(jnp.bfloat16).astype(jnp.float32)
        final_ref[pl.ds(i, 128, stride=4), :] = final[:, :128]
        final_ref[pl.ds(512 + i, 128, stride=4), :] = final[:, 128:]
        outer = (contract_last(outer_ref[...], normalize_rows(final)) * live).astype(jnp.bfloat16)
        parts_ref[i * CO : (i + 1) * CO, :] = outer[:CO, :]
        parts_ref[128 + i * CO : 128 + (i + 1) * CO, :] = outer[CO:, :]
    result_ref[:, :128] = final_ref[:512, :].astype(jnp.bfloat16)
    result_ref[:, 128:] = final_ref[512:, :].astype(jnp.bfloat16)


def exchange(values, offset):
    pieces = lax.axis_size("dap")
    return lax.ppermute(values, "dap", [(q, q ^ offset) for q in range(pieces)])


def whole_block(
    alignment_input,
    pair_state_input,
    bin_all,
    live_row_float,
    relative_position_table,
    column_query_weight,
    column_key_weight,
    column_value_gate_weight,
    column_output_weight,
    alignment_transition_up,
    alignment_transition_down,
    outer_input_weight,
    outer_output_weight,
    *pair_weights,
):
    channels = alignment_input.shape[2]
    width = pair_state_input.shape[2]
    place = lax.axis_index("dap").astype(jnp.int32).reshape(1)
    vmem = pl.BlockSpec(memory_space=pltpu.VMEM)
    smem = pl.BlockSpec(memory_space=pltpu.SMEM)

    def array(*shape):
        return jax.ShapeDtypeStruct(shape, jnp.bfloat16)

    def limit(mebibytes):
        return pltpu.CompilerParams(vmem_limit_bytes=mebibytes * 1024 * 1024)

    own_pair, *blocks = pl.pallas_call(
        rows_kernel,
        out_shape=[array(2, width, LANES)] + [array(32, channels)] * 16,
        in_specs=[smem, vmem, vmem],
        out_specs=[vmem] * 17,
        scratch_shapes=[pltpu.VMEM((1024, LANES), jnp.float32)],
        compiler_params=limit(16),
        name="rows_by_device",
    )(place, alignment_input, pair_state_input)
    blocks = [blocks[0]] + [exchange(blocks[m], m) for m in range(1, 16)]

    pair_far = exchange(own_pair, 8)
    pair_near = [exchange(own_pair, 4), exchange(pair_far, 4)]
    pair_line = jnp.stack([own_pair, pair_far] + pair_near)

    embedding, *turned = pl.pallas_call(
        weights_kernel,
        out_shape=[array(32, width, LANES), array(2 * width, 16 * CO)]
        + [array(*w.shape[::-1]) for w in pair_weights],
        in_specs=[vmem] * 11,
        out_specs=[vmem] * 10,
        scratch_shapes=[
            pltpu.VMEM((LANES, LANES), jnp.float32),
            pltpu.VMEM((1024, LANES), jnp.float32),
        ],
        compiler_params=limit(24),
        cost_estimate=pl.CostEstimate(
            flops=200_000_000, bytes_accessed=4_000_000, transcendentals=0
        ),
        name="turn_weights",
    )(
        lanes_order(bin_all).reshape(32, LANES),
        relative_position_table,
        outer_output_weight,
        *pair_weights,
    )
    blocks, pair_line, turned = lax.optimization_barrier((blocks, pair_line, turned))
    pair_pieces = [pair_line, exchange(pair_line, 2), exchange(pair_line, 1)]

    result, parts = pl.pallas_call(
        msa_kernel,
        out_shape=(array(512, channels), array(256, LANES)),
        in_specs=[smem] + [vmem] * 24,
        out_specs=(vmem, vmem),
        scratch_shapes=[
            pltpu.VMEM((512, channels), jnp.float32),
            pltpu.VMEM((1024, LANES), jnp.float32),
        ],
        compiler_params=limit(32),
        cost_estimate=pl.CostEstimate(
            flops=2_000_000_000, bytes_accessed=10_000_000, transcendentals=1_000_000
        ),
        name="msa_whole",
    )(
        place,
        live_row_float.reshape(1, LANES),
        *blocks,
        column_query_weight,
        column_key_weight,
        column_value_gate_weight,
        column_output_weight,
        alignment_transition_up,
        alignment_transition_down,
        outer_input_weight.T,
    )
    parts, pair_pieces = lax.optimization_barrier((parts, pair_pieces))
    far = exchange(parts, 8)
    near = [exchange(parts, 4), exchange(far, 4)]
    pair_pieces.append(exchange(pair_pieces[1], 1))
    line = jnp.stack([parts, far] + near)
    across = exchange(line, 2)
    pieces = [line, across, exchange(line, 1), exchange(across, 1)]

    tall = (32 * 128, LANES)
    pair_output = pl.pallas_call(
        pair_kernel,
        out_shape=array(256, LANES),
        in_specs=[smem, smem] + [vmem] * 18,
        out_specs=vmem,
        scratch_shapes=[
            pltpu.VMEM((2048, LANES), jnp.float32),
            pltpu.VMEM((128, 2048), jnp.bfloat16),
            pltpu.VMEM((512, 1024), jnp.bfloat16),
            pltpu.VMEM((32, 128, LANES), jnp.float32),
            pltpu.VMEM(tall, jnp.float32),
            pltpu.VMEM(tall, jnp.float32),
            pltpu.VMEM(tall, jnp.float32),
            pltpu.VMEM((32, 128, LANES), jnp.float32),
            pltpu.VMEM((128, 256), jnp.float32),
            pltpu.VMEM((1024, LANES), jnp.float32),
            pltpu.VMEM((1024, LANES), jnp.float32),
        ],
        compiler_params=limit(40),
        name="pair_whole",
    )(place, jnp.sum(live_row_float).reshape(1), *pieces, *pair_pieces, embedding, *turned)
    return result.reshape(128, 4, channels), pair_output.reshape(pair_state_input.shape)


def lanes_order(values):
    lead = values.shape[:-1]
    halves = values.reshape(lead + (values.shape[-1] // 2, 2))
    return jnp.swapaxes(halves, -1, -2).reshape(values.shape)


def local(
    alignment_input,
    pair_state_input,
    residue_number_index,
    chain_label,
    alignment_row_mask,
    relative_position_table,
    column_query_weight,
    column_key_weight,
    column_value_gate_weight,
    column_output_weight,
    alignment_transition_up,
    alignment_transition_down,
    outer_input_weight,
    outer_output_weight,
    outgoing_projection_weight,
    outgoing_output_gate,
    outgoing_output_weight,
    incoming_projection_weight,
    incoming_output_gate,
    incoming_output_weight,
    pair_transition_up,
    pair_transition_down,
):
    shard_pieces = lax.axis_size("dap")
    own_rows = pair_state_input.shape[0]
    residue_count = pair_state_input.shape[1]
    channel_count = alignment_input.shape[2]
    head_width = HM * HEAD_SIZE
    first_row = lax.axis_index("dap") * own_rows
    own_index = lax.dynamic_slice_in_dim(residue_number_index, first_row, own_rows)
    own_chain = lax.dynamic_slice_in_dim(chain_label, first_row, own_rows)

    def bins_of(index, chain):
        offset = index[:, None] - residue_number_index[None, :]
        return jnp.where(
            chain[:, None] == chain_label[None, :],
            jnp.clip(offset + MAXREL, 0, 2 * MAXREL),
            2 * MAXREL + 1,
        )

    bin_index = bins_of(own_index, own_chain)
    one_hot = (bin_index[:, :, None] == jnp.arange(NBINS, dtype=jnp.int32)[None, None, :]).astype(
        jnp.bfloat16
    )
    pair_start = pair_state_input.astype(jnp.float32) + jnp.einsum(
        "ijb,bc->ijc", one_hot, relative_position_table, preferred_element_type=jnp.float32
    )
    live_rows = alignment_row_mask > 0
    live_row_float = live_rows.astype(jnp.float32)

    if alignment_row_mask.shape[0] == LANES and 2 * residue_count == LANES and own_rows == 4:
        return whole_block(
            alignment_input,
            pair_state_input,
            bins_of(residue_number_index, chain_label),
            live_row_float,
            relative_position_table,
            column_query_weight,
            column_key_weight,
            column_value_gate_weight,
            column_output_weight,
            alignment_transition_up,
            alignment_transition_down,
            outer_input_weight,
            outer_output_weight,
            outgoing_projection_weight,
            outgoing_output_gate,
            outgoing_output_weight,
            incoming_projection_weight,
            incoming_output_gate,
            incoming_output_weight,
            pair_transition_up,
            pair_transition_down,
        )

    def attend_one(operands):
        query_col, key_col, value_col = operands
        scores = jnp.einsum("shd,thd->hst", query_col, key_col, preferred_element_type=jnp.float32)
        scores = jnp.where(live_rows[None, None, :], scores, -1000000000.0)
        row_top = jnp.max(scores, axis=-1, keepdims=True)
        raised = jnp.exp(scores - row_top)
        attention = (raised / jnp.sum(raised, axis=-1, keepdims=True)).astype(jnp.bfloat16)
        return jnp.einsum("hst,thd->shd", attention, value_col, preferred_element_type=jnp.float32)

    blocked_view = alignment_input.reshape(
        alignment_input.shape[0], shard_pieces, residue_count // shard_pieces, channel_count
    )
    block_in = lax.all_to_all(blocked_view, "dap", split_axis=1, concat_axis=0, tiled=True)
    depth_rows = block_in.shape[0]
    count_cols = block_in.shape[2]
    current = block_in.reshape(depth_rows, count_cols, channel_count).astype(jnp.float32)
    normed = layer_normalize(current).astype(jnp.bfloat16)
    query_rows = (
        jnp.einsum("sic,ce->sie", normed, column_query_weight, preferred_element_type=jnp.float32)
        * HEAD_SIZE ** (-0.5)
    ).astype(jnp.bfloat16)
    key_row_block = jnp.einsum(
        "sic,ce->sie", normed, column_key_weight, preferred_element_type=jnp.float32
    ).astype(jnp.bfloat16)
    value_gate_pair = jnp.einsum(
        "sic,ce->sie", normed, column_value_gate_weight, preferred_element_type=jnp.float32
    )
    value_rows = value_gate_pair[..., :head_width].astype(jnp.bfloat16)

    def by_column(values):
        return values.transpose(1, 0, 2).reshape(count_cols, depth_rows, HM, HEAD_SIZE)

    attended = lax.map(
        attend_one, (by_column(query_rows), by_column(key_row_block), by_column(value_rows))
    )
    attended = attended.reshape(count_cols, depth_rows, head_width).transpose(1, 0, 2)
    gated_out = (jax.nn.sigmoid(value_gate_pair[..., head_width:]) * attended).astype(jnp.bfloat16)
    current = current + jnp.einsum(
        "sie,ec->sic", gated_out, column_output_weight, preferred_element_type=jnp.float32
    )
    hidden = jax.nn.relu(
        jnp.einsum(
            "sic,cf->sif",
            layer_normalize(current).astype(jnp.bfloat16),
            alignment_transition_up,
            preferred_element_type=jnp.float32,
        )
    ).astype(jnp.bfloat16)
    current = current + jnp.einsum(
        "sif,fc->sic", hidden, alignment_transition_down, preferred_element_type=jnp.float32
    )
    result = current.astype(jnp.bfloat16)
    outer_product_input = jnp.einsum(
        "sic,cf->sif",
        layer_normalize(result.astype(jnp.float32)).astype(jnp.bfloat16),
        outer_input_weight,
        preferred_element_type=jnp.float32,
    )
    outer_product_input = outer_product_input * live_row_float[:, None, None]
    left_part = outer_product_input[..., :CO].astype(jnp.bfloat16)
    right_part = outer_product_input[..., CO:].astype(jnp.bfloat16)
    all_rows = result.shape[0]
    left_cols = left_part.transpose(1, 0, 2)
    right_cols = right_part.transpose(1, 0, 2).reshape(own_rows, all_rows * CO)
    live_count = jnp.sum(live_row_float)
    right_piece = gather_doubling(right_cols).reshape(-1, all_rows * CO)
    span_rows = right_piece.shape[0]
    products = jnp.einsum(
        "isc,jsd->ijcd",
        left_cols,
        right_piece.reshape(span_rows, all_rows, CO),
        preferred_element_type=jnp.float32,
    )
    products = products.astype(jnp.bfloat16).reshape(own_rows, span_rows, CO * CO)
    outer_mean = (
        jnp.einsum("ijf,fc->ijc", products, outer_output_weight, preferred_element_type=jnp.float32)
        / live_count
    )
    pair_mid = pair_start + outer_mean
    out_left, out_right, out_gating = triangle_inputs(
        pair_mid, outgoing_projection_weight, outgoing_output_gate
    )
    out_product = by_channels(out_left, out_right, "cik,cjk->cij")
    pair_after_out = triangle_finish(pair_mid, out_product, out_gating, outgoing_output_weight)
    in_left, in_right, in_gating = triangle_inputs(
        pair_after_out, incoming_projection_weight, incoming_output_gate
    )
    in_product = by_channels(in_left, in_right, "cki,ckj->cij")
    pair_after_in = triangle_finish(pair_after_out, in_product, in_gating, incoming_output_weight)
    pair_expanded = jax.nn.relu(
        jnp.einsum(
            "ijc,cf->ijf",
            layer_normalize(pair_after_in).astype(jnp.bfloat16),
            pair_transition_up,
            preferred_element_type=jnp.float32,
        )
    ).astype(jnp.bfloat16)
    pair_state_output = (
        pair_after_in
        + jnp.einsum(
            "ijf,fc->ijc", pair_expanded, pair_transition_down, preferred_element_type=jnp.float32
        )
    ).astype(jnp.bfloat16)
    return (result, pair_state_output)


def solution(mesh):
    in_specs = (
        P(("grp", "dap"), None, None),
        P(("grp", "dap"), None, None),
        P("grp"),
        P("grp"),
        P("grp"),
        P(),
        P(),
        P(),
        P(),
        P(),
        P(),
        P(),
        P(),
        P(),
        P(),
        P(),
        P(),
        P(),
        P(),
        P(),
        P(),
        P(),
    )
    out_specs = (P("grp", "dap", None), P(("grp", "dap"), None, None))
    return jax.shard_map(local, mesh=mesh, in_specs=in_specs, out_specs=out_specs, check_vma=False)
```

```python
import jax
import jax.numpy as jnp
from jax import lax
from jax.experimental import pallas as pl
from jax.experimental.pallas import tpu as pltpu
from jax.sharding import PartitionSpec as P

HM = 8
HEAD_SIZE = 32
CO = 32
MAXREL = 32
NBINS = 66


EPSILON = 1e-05


def layer_normalize(values):
    center = jnp.mean(values, axis=-1, keepdims=True)
    shifted = values - center
    spread = jnp.mean(shifted * shifted, axis=-1, keepdims=True)
    return shifted * lax.rsqrt(spread + EPSILON)


def triangle_inputs(pair_now, weight, gate_weight):
    normed = layer_normalize(pair_now).astype(jnp.bfloat16)
    combined = jnp.einsum("ijc,cf->fij", normed, weight, preferred_element_type=jnp.float32)
    hidden_width = weight.shape[1] // 4
    left_side = (
        jax.nn.sigmoid(combined[hidden_width : 2 * hidden_width]) * combined[:hidden_width]
    ).astype(jnp.bfloat16)
    right_side = (
        jax.nn.sigmoid(combined[3 * hidden_width :]) * combined[2 * hidden_width : 3 * hidden_width]
    ).astype(jnp.bfloat16)
    gating = jax.nn.sigmoid(
        jnp.einsum("ijc,cd->ijd", normed, gate_weight, preferred_element_type=jnp.float32)
    )
    return (left_side, right_side, gating)


def triangle_finish(pair_now, product, gating, final_weight):
    product = lax.optimization_barrier(product)
    normed = layer_normalize(product.transpose(1, 2, 0).astype(jnp.float32)).astype(jnp.bfloat16)
    return pair_now + gating * jnp.einsum(
        "ijc,cd->ijd", normed, final_weight, preferred_element_type=jnp.float32
    )


def by_channels(left_side, right_side, form):
    both = jnp.stack([left_side, right_side])
    both = lax.all_to_all(both, "dap", split_axis=1, concat_axis=2, tiled=True)
    partial_out = jnp.einsum(form, both[0], both[1], preferred_element_type=jnp.float32)
    return lax.all_to_all(
        partial_out.astype(jnp.bfloat16), "dap", split_axis=1, concat_axis=0, tiled=True
    )


def gather_doubling(block):
    shard_pieces = lax.axis_size("dap")
    place = lax.axis_index("dap")
    held = block
    depth = 0
    bit = shard_pieces // 2
    while bit:
        other = lax.ppermute(held, "dap", [(q, q ^ bit) for q in range(shard_pieces)])
        upper = (place & bit) != 0
        first = jnp.where(upper, other, held)
        second = jnp.where(upper, held, other)
        held = jnp.stack([first, second], axis=depth)
        depth += 1
        bit //= 2
    return held.reshape((shard_pieces,) + block.shape)


LANES = 128


def gate_curve(values):
    return 0.5 + 0.5 * jnp.tanh(0.5 * values)


def normalize_channels(values):
    center = jnp.mean(values, axis=0, keepdims=True)
    shifted = values - center
    spread = jnp.mean(shifted * shifted, axis=0, keepdims=True)
    return (shifted * lax.rsqrt(spread + EPSILON)).astype(jnp.bfloat16)


def mix(weight, values):
    return jnp.dot(weight, values, preferred_element_type=jnp.float32)


def fold_halves(first_even, second_even, first_odd, second_odd, low_half):
    straight = jnp.where(low_half, first_even, second_odd)
    crossed = jnp.where(low_half, second_even, first_odd)
    return straight + pltpu.roll(crossed, LANES // 2, 1)


def turned(ref, name):
    first, last = TURNED[name]
    return ref[first:last, :]


OFFSETS = (0, 8, 4, 12)


def start_kernel(
    place_ref,
    live_ref,
    line_ref,
    across_ref,
    core_line_ref,
    core_across_ref,
    pair_line_ref,
    pair_across_ref,
    embedding_ref,
    turned_ref,
    wide_weight_ref,
    pair_mid_ref,
    left_ref,
    gating_ref,
    right_ref,
    wide_ref,
    right_cols_ref,
    *stack_refs,
):
    place = place_ref[0]
    inverse_live = 1.0 / live_ref[0]
    half = LANES // 2
    low_half = lax.broadcasted_iota(jnp.int32, (LANES, LANES), 1) < half

    for m in range(4):
        for part, device in (
            (line_ref[m, 128:256, :], place ^ OFFSETS[m]),
            (across_ref[m, 128:256, :], place ^ OFFSETS[m] ^ 2),
            (core_line_ref[m], place ^ OFFSETS[m] ^ 1),
            (core_across_ref[m], place ^ OFFSETS[m] ^ 3),
        ):
            wide_ref[pl.ds(pl.multiple_of(device * 128, 128), 128), :] = part.astype(jnp.float32)
    for d in range(0, CO, 2):
        rows = [
            wide_ref[pl.ds(par * CO + d + e, 32, stride=2 * CO), :]
            for e in range(2)
            for par in range(2)
        ]
        right_cols_ref[:, d * half : d * half + LANES] = (
            jnp.concatenate(rows, axis=0).T.astype(jnp.bfloat16)
        )

    for g in range(4):
        parts_ref = (line_ref, across_ref)[g // 2]
        pair_ref = (pair_line_ref, pair_across_ref)[g // 2]
        stack_ref = stack_refs[g % 2]
        first = 2 * (g % 2)
        left_rows = parts_ref[first : first + 2, 0:128, :].reshape(256, LANES)
        outer = mix(left_rows, right_cols_ref[...]).astype(jnp.bfloat16)
        for i in range(8):
            for d in range(16):
                stack_ref[d * 32 : (d + 1) * 32, i * LANES : (i + 1) * LANES] = outer[
                    i * 32 : (i + 1) * 32, d * LANES : (d + 1) * LANES
                ]
        mixed = mix(wide_weight_ref[0:256, :], stack_ref[...])
        slabs = []
        places = []
        for q in range(4):
            m = first + q // 2
            device = place ^ OFFSETS[m] ^ (2 * (g // 2))
            here = 2 * (device // 2) + q % 2
            even = slice(2 * q * LANES, (2 * q + 1) * LANES)
            odd = slice((2 * q + 1) * LANES, (2 * q + 2) * LANES)
            outer_mean = fold_halves(
                mixed[0:128, even], mixed[0:128, odd], mixed[128:256, even], mixed[128:256, odd], low_half
            )
            start = pair_ref[m, q % 2].astype(jnp.float32)
            start = start + embedding_ref[2 * device + q % 2].astype(jnp.float32)
            slab = start + outer_mean * inverse_live
            pair_mid_ref[here] = slab
            slabs.append(normalize_channels(slab))
            places.append(here)
        normed = jnp.concatenate(slabs, axis=1)
        combined = mix(turned(turned_ref, "out_mix"), normed)
        left = gate_curve(combined[128:256]) * combined[0:128]
        right = gate_curve(combined[384:512]) * combined[256:384]
        gating = gate_curve(mix(turned(turned_ref, "out_gate"), normed))
        for q in range(4):
            lanes = slice(q * LANES, (q + 1) * LANES)
            rows = pl.ds(pl.multiple_of(places[q] * 128, 128), 128)
            left_ref[rows, :] = left[:, lanes]
            right_ref[rows, :] = right[:, lanes].astype(jnp.bfloat16)
            gating_ref[places[q]] = gating[:, lanes]


def triangle_kernel(
    place_ref,
    pair_mid_ref,
    left_ref,
    gating_ref,
    right_own_ref,
    right_other_ref,
    turned_ref,
    own_pair_ref,
    own_part_ref,
    other_part_ref,
    right_ref,
    product_ref,
    pair_now_ref,
    chosen_ref,
    own_left_ref,
    own_product_ref,
):
    place = place_ref[0]
    core = place % 2
    half = LANES // 2
    low_half = lax.broadcasted_iota(jnp.int32, (LANES, LANES), 1) < half
    low_short = lax.broadcasted_iota(jnp.int32, (32, LANES), 1) < half
    for chip in range(8):
        for source, side in ((right_own_ref, core), (right_other_ref, 1 - core)):
            rows = pl.ds(pl.multiple_of((4 * chip + 2 * side) * 128, 256), 256)
            right_ref[rows, :] = source[chip * 256 : (chip + 1) * 256, :].astype(jnp.float32)

    def outgoing_channels(block, carry):
        for e in range(8):
            c = block * 8 + e
            left = left_ref[pl.ds(c, 16, stride=128), :].astype(jnp.bfloat16)
            right = right_ref[pl.ds(c, 32, stride=128), :]
            moved = pltpu.roll(right, half, 1)
            spread = jnp.concatenate(
                [
                    jnp.where(low_short, right, 0.0),
                    jnp.where(low_short, moved, 0.0),
                    jnp.where(low_short, 0.0, moved),
                    jnp.where(low_short, 0.0, right),
                ],
                axis=0,
            ).astype(jnp.bfloat16)
            product_ref[pl.ds(c, 16, stride=128), :] = contract_last(left, spread)
        return carry

    lax.fori_loop(0, 16, outgoing_channels, 0)

    column = lax.broadcasted_iota(jnp.int32, (1, 256), 1)
    which = column // 16
    residue = which % 4
    device = place ^ ((which // 4) % 2)
    wanted = half * (which // 8) + 32 * (residue % 2) + 2 * device + residue // 2
    slab_of = column % 16
    source_lane = lax.broadcasted_iota(jnp.int32, (LANES, 256), 0)
    for g in range(4):
        products = [
            normalize_channels(product_ref[(4 * g + q) * 128 : (4 * g + q + 1) * 128, :])
            for q in range(4)
        ]
        finished = mix(turned(turned_ref, "out_final"), jnp.concatenate(products, axis=1))
        slabs = []
        picks = []
        for q in range(4):
            h = 4 * g + q
            lanes = slice(q * LANES, (q + 1) * LANES)
            slab = pair_mid_ref[h] + gating_ref[h] * finished[:, lanes]
            pair_now_ref[h] = slab
            slabs.append(normalize_channels(slab))
            here = jnp.where(slab_of == h, wanted, -1)
            picks.append((source_lane == here).astype(jnp.float32).astype(jnp.bfloat16))
        normed = jnp.concatenate(slabs, axis=1)
        chosen = mix(normed, jnp.concatenate(picks, axis=0))
        if g:
            chosen_ref[...] += chosen
        else:
            chosen_ref[...] = chosen
        combined = mix(turned(turned_ref, "in_mix")[256:512, :], normed)
        right = gate_curve(combined[128:256]) * combined[0:128]
        for q in range(4):
            right_ref[(4 * g + q) * 128 : (4 * g + q + 1) * 128, :] = right[
                :, q * LANES : (q + 1) * LANES
            ]
    for t in range(2):
        own_pair_ref[t] = pair_now_ref[2 * (place // 2) + t]

    combined = mix(turned(turned_ref, "in_mix")[0:256, :], chosen_ref[...].astype(jnp.bfloat16))
    own_left = gate_curve(combined[128:256]) * combined[0:128]
    for m in range(16):
        part = own_left[:, (m // 8) * LANES : (m // 8 + 1) * LANES]
        if m % 8:
            part = pltpu.roll(part, LANES - 16 * (m % 8), 1)
        own_left_ref[m * 128 : (m + 1) * 128, :] = part

    def incoming_channels(block, carry):
        for e in range(8):
            c = block * 8 + e
            left = own_left_ref[pl.ds(c, 16, stride=128), :][:, 0:16].astype(jnp.bfloat16)
            right = right_ref[pl.ds(c, 16, stride=128), :].astype(jnp.bfloat16)
            own_product_ref[pl.ds(c, 16, stride=128), :] = mix(left, right)
        return carry

    lax.fori_loop(0, 16, incoming_channels, 0)

    def block_of(b, e, residue):
        m = 8 * b + 4 * e + residue
        return own_product_ref[m * 128 : (m + 1) * 128, :]

    for e, target in ((0, own_part_ref), (1, other_part_ref)):
        for t in range(2):
            target[t] = fold_halves(
                block_of(0, e, 2 * t),
                block_of(0, e, 2 * t + 1),
                block_of(1, e, 2 * t),
                block_of(1, e, 2 * t + 1),
                low_half,
            )


def finish_kernel(own_pair_ref, own_part_ref, other_part_ref, turned_ref, wide_weight_ref, result_ref):
    products = [normalize_channels(own_part_ref[t] + other_part_ref[t]) for t in range(2)]
    finished = mix(turned(turned_ref, "in_final"), jnp.concatenate(products, axis=1))
    own_pair = jnp.concatenate([own_pair_ref[t] for t in range(2)], axis=1)
    gating = gate_curve(mix(turned(turned_ref, "in_gate"), normalize_channels(own_pair)))
    own_pair = own_pair + gating * finished
    hidden = jnp.maximum(mix(turned(turned_ref, "up"), normalize_channels(own_pair)), 0.0)
    own_pair = own_pair + mix(wide_weight_ref[256:384, :], hidden.astype(jnp.bfloat16))
    own_pair = own_pair.astype(jnp.bfloat16)
    order = lane_order_matrix()
    for t in range(2):
        result_ref[t * 128 : (t + 1) * 128, :] = contract_last(
            order, own_pair[:, t * LANES : (t + 1) * LANES]
        ).astype(jnp.bfloat16)


def lane_order_matrix():
    half = LANES // 2
    member = lax.broadcasted_iota(jnp.int32, (LANES, LANES), 0)
    lane = lax.broadcasted_iota(jnp.int32, (LANES, LANES), 1)
    back = half * (member // half) + 32 * (member % 2) + (member % half) // 2
    return (lane == back).astype(jnp.float32).astype(jnp.bfloat16)


def contract_first(first, second):
    return lax.dot_general(
        first, second, (((0,), (0,)), ((), ())), preferred_element_type=jnp.float32
    )


def rows_kernel(rows_ref, pair_ref, blocks_ref, own_pair_ref, wide_ref):
    residues = rows_ref.shape[1]
    count = 8 * residues
    rows = rows_ref[...].astype(jnp.float32).reshape(count, 2 * LANES)
    for e in range(2):
        wide_ref[e * count : (e + 1) * count, :] = rows[:, e * LANES : (e + 1) * LANES]
    for p in range(16):
        for e in range(2):
            block = [
                wide_ref[pl.ds(e * count + 4 * p + i, 8, stride=residues), :] for i in range(4)
            ]
            blocks_ref[p, :, e * LANES : (e + 1) * LANES] = jnp.concatenate(block, axis=0).astype(
                jnp.bfloat16
            )
    order = lane_order_matrix()
    for t in range(2):
        own_pair_ref[t] = contract_first(
            pair_ref[2 * t : 2 * t + 2].reshape(LANES, LANES), order
        ).astype(jnp.bfloat16)


TURNED = {
    "out_mix": (0, 512),
    "out_gate": (512, 640),
    "out_final": (640, 768),
    "in_mix": (768, 1280),
    "in_gate": (1280, 1408),
    "in_final": (1408, 1536),
    "up": (1536, 2048),
}


def weights_kernel(
    bins_ref,
    table_ref,
    *rest,
):
    sources, (embedding_out, turned_out, wide_out) = rest[:9], rest[9:12]
    landed, (table_wide_ref, mean_wide_ref, arrived) = rest[12:21], rest[21:]
    copies = [
        pltpu.make_async_copy(sources[k], landed[k], arrived.at[k]) for k in range(len(sources))
    ]
    for copy in copies:
        copy.start()
    table_wide_ref[...] = jnp.zeros_like(table_wide_ref)
    table_wide_ref[0:NBINS, :] = table_ref[...].astype(jnp.float32)
    table = table_wide_ref[...].T.astype(jnp.bfloat16)
    channel = lax.broadcasted_iota(jnp.int32, (LANES, LANES), 0)

    def embed(g, carry):
        for q in range(4):
            h = 4 * g + q
            one_hot = (channel == bins_ref[pl.ds(h, 1), :]).astype(jnp.float32).astype(jnp.bfloat16)
            embedding_out[h] = mix(table, one_hot).astype(jnp.bfloat16)
        return carry

    lax.fori_loop(0, 8, embed, 0)
    for copy in copies:
        copy.wait()
    mean_wide_ref[...] = landed[0][...].astype(jnp.float32)
    for e in range(2):
        for block in range(4):
            rows = [
                mean_wide_ref[pl.ds(2 * (4 * block + k) + e, CO, stride=CO), :] for k in range(4)
            ]
            wide_out[e * LANES : (e + 1) * LANES, block * LANES : (block + 1) * LANES] = (
                jnp.concatenate(rows, axis=0).T.astype(jnp.bfloat16)
            )
    first = 0
    for source in landed[1:8]:
        for b in range(source.shape[1] // LANES):
            part = source[:, b * LANES : (b + 1) * LANES].astype(jnp.float32)
            turned_out[first : first + LANES, :] = part.T.astype(jnp.bfloat16)
            first += LANES
    for a in range(4):
        part = landed[8][a * LANES : (a + 1) * LANES, :].astype(jnp.float32)
        wide_out[256:384, a * LANES : (a + 1) * LANES] = part.T.astype(jnp.bfloat16)


def normalize_rows(values):
    center = jnp.mean(values, axis=1, keepdims=True)
    shifted = values - center
    spread = jnp.mean(shifted * shifted, axis=1, keepdims=True)
    return (shifted * lax.rsqrt(spread + EPSILON)).astype(jnp.bfloat16)


def contract_last(first, second):
    return lax.dot_general(
        first, second, (((1,), (1,)), ((), ())), preferred_element_type=jnp.float32
    )


def msa_kernel(
    live_ref,
    blocks_ref,
    query_ref,
    key_ref,
    value_gate_ref,
    output_ref,
    up_ref,
    down_ref,
    outer_ref,
    result_ref,
    parts_ref,
    wide_ref,
    final_ref,
):
    for p in range(16):
        block = blocks_ref[p].astype(jnp.float32)
        for i in range(4):
            wide_ref[i * 128 + p * 8 : i * 128 + p * 8 + 8, :] = block[i * 8 : i * 8 + 8, :]
    live = live_ref[...]
    alive = live > 0.0
    width = HM * HEAD_SIZE
    head_of = lax.broadcasted_iota(jnp.int32, (128, width), 1) // HEAD_SIZE
    zero = jnp.zeros((128, width), jnp.bfloat16)
    for i in range(4):
        rows = slice(i * 128, (i + 1) * 128)
        current = wide_ref[rows, :]
        normed = normalize_rows(current)
        query = (mix(normed, query_ref[...]) * HEAD_SIZE ** (-0.5)).astype(jnp.bfloat16)
        key = mix(normed, key_ref[...]).astype(jnp.bfloat16)
        value_gate = mix(normed, value_gate_ref[...])
        value = value_gate[:, :width].astype(jnp.bfloat16)
        keys = jnp.concatenate([jnp.where(head_of == h, key, zero) for h in range(HM)], axis=0)
        values = jnp.concatenate([jnp.where(head_of == h, value, zero) for h in range(HM)], axis=0)
        scores = contract_last(query, keys)
        heads = []
        for h in range(HM):
            score = jnp.where(alive, scores[:, h * 128 : (h + 1) * 128], -1000000000.0)
            raised = jnp.exp(score - jnp.max(score, axis=1, keepdims=True))
            heads.append((raised / jnp.sum(raised, axis=1, keepdims=True)).astype(jnp.bfloat16))
        attended = mix(jnp.concatenate(heads, axis=1), values)
        gated = (gate_curve(value_gate[:, width:]) * attended).astype(jnp.bfloat16)
        current = current + mix(gated, output_ref[...])
        hidden = jnp.maximum(mix(normalize_rows(current), up_ref[...]), 0.0).astype(jnp.bfloat16)
        final = (current + mix(hidden, down_ref[...])).astype(jnp.bfloat16).astype(jnp.float32)
        final_ref[pl.ds(i, 128, stride=4), :] = final[:, :128]
        final_ref[pl.ds(512 + i, 128, stride=4), :] = final[:, 128:]
        outer = (contract_last(outer_ref[...], normalize_rows(final)) * live).astype(jnp.bfloat16)
        parts_ref[i * CO : (i + 1) * CO, :] = outer[:CO, :]
        parts_ref[128 + i * CO : 128 + (i + 1) * CO, :] = outer[CO:, :]
    result_ref[:, :128] = final_ref[:512, :].astype(jnp.bfloat16)
    result_ref[:, 128:] = final_ref[512:, :].astype(jnp.bfloat16)


def exchange(values, offset):
    pieces = lax.axis_size("dap")
    return lax.ppermute(values, "dap", [(q, q ^ offset) for q in range(pieces)])


def whole_block(
    alignment_input,
    pair_state_input,
    bin_all,
    live_row_float,
    relative_position_table,
    column_query_weight,
    column_key_weight,
    column_value_gate_weight,
    column_output_weight,
    alignment_transition_up,
    alignment_transition_down,
    outer_input_weight,
    *pair_weights,
):
    channels = alignment_input.shape[2]
    width = pair_state_input.shape[2]
    place = lax.axis_index("dap").astype(jnp.int32).reshape(1)
    vmem = pl.BlockSpec(memory_space=pltpu.VMEM)
    smem = pl.BlockSpec(memory_space=pltpu.SMEM)
    hbm = pl.BlockSpec(memory_space=pltpu.HBM)

    def array(*shape, dtype=jnp.bfloat16):
        return jax.ShapeDtypeStruct(shape, dtype)

    def wide(*shape):
        return jax.ShapeDtypeStruct(shape, jnp.float32)

    def limit(mebibytes):
        return pltpu.CompilerParams(vmem_limit_bytes=mebibytes * 1024 * 1024)

    blocks, own_pair = pl.pallas_call(
        rows_kernel,
        out_shape=[array(16, 32, channels), array(2, width, LANES)],
        in_specs=[vmem, vmem],
        out_specs=[vmem, vmem],
        scratch_shapes=[pltpu.VMEM((1024, LANES), jnp.float32)],
        compiler_params=limit(16),
        name="rows_by_device",
    )(alignment_input, pair_state_input)
    blocks = lax.all_to_all(blocks, "dap", split_axis=0, concat_axis=0, tiled=True)

    pair_far = exchange(own_pair, 8)
    pair_near = exchange(jnp.stack([own_pair, pair_far]), 4)
    pair_line = jnp.concatenate([jnp.stack([own_pair, pair_far]), pair_near])

    embedding, turned_weights, wide_weights = pl.pallas_call(
        weights_kernel,
        out_shape=[array(32, width, LANES), array(2048, LANES), array(384, 512)],
        in_specs=[vmem] * 2 + [hbm] * 9,
        out_specs=[vmem] * 3,
        scratch_shapes=[pltpu.VMEM(w.shape, jnp.bfloat16) for w in pair_weights]
        + [
            pltpu.VMEM((LANES, LANES), jnp.float32),
            pltpu.VMEM((1024, LANES), jnp.float32),
            pltpu.SemaphoreType.DMA((9,)),
        ],
        compiler_params=limit(24),
        cost_estimate=pl.CostEstimate(
            flops=200_000_000, bytes_accessed=8_000_000, transcendentals=0
        ),
        name="turn_weights",
    )(
        lanes_order(bin_all).reshape(32, LANES),
        relative_position_table,
        *pair_weights,
    )
    blocks, pair_line = lax.optimization_barrier((blocks, pair_line))
    pair_across = exchange(pair_line, 2)

    result, parts = pl.pallas_call(
        msa_kernel,
        out_shape=(array(512, channels), array(256, LANES)),
        in_specs=[vmem] * 9,
        out_specs=(vmem, vmem),
        scratch_shapes=[
            pltpu.VMEM((512, channels), jnp.float32),
            pltpu.VMEM((1024, LANES), jnp.float32),
        ],
        compiler_params=limit(32),
        cost_estimate=pl.CostEstimate(
            flops=2_000_000_000, bytes_accessed=10_000_000, transcendentals=1_000_000
        ),
        name="msa_whole",
    )(
        live_row_float.reshape(1, LANES),
        blocks,
        column_query_weight,
        column_key_weight,
        column_value_gate_weight,
        column_output_weight,
        alignment_transition_up,
        alignment_transition_down,
        outer_input_weight.T,
    )
    parts, pair_across = lax.optimization_barrier((parts, pair_across))
    far = exchange(parts, 8)
    near = [exchange(parts, 4), exchange(far, 4)]
    line = jnp.stack([parts, far] + near)
    across = exchange(line, 2)
    core_line = exchange(jnp.stack([part[128:256] for part in (parts, far, *near)]), 1)
    core_across = exchange(across[:, 128:256, :], 1)

    slabs = (16, 128, LANES)
    tall = (16 * 128, LANES)
    pair_mid, left, gating, right = pl.pallas_call(
        start_kernel,
        out_shape=[wide(*slabs), wide(*tall), wide(*slabs), array(*tall)],
        in_specs=[smem, smem] + [vmem] * 9,
        out_specs=[vmem] * 4,
        scratch_shapes=[
            pltpu.VMEM((2048, LANES), jnp.float32),
            pltpu.VMEM((128, 2048), jnp.bfloat16),
            pltpu.VMEM((512, 1024), jnp.bfloat16),
            pltpu.VMEM((512, 1024), jnp.bfloat16),
        ],
        compiler_params=limit(32),
        name="pair_start",
    )(
        place,
        jnp.sum(live_row_float).reshape(1),
        line,
        across,
        core_line,
        core_across,
        pair_line,
        pair_across,
        embedding,
        turned_weights,
        wide_weights,
    )
    own_pair, own_part, other_part = pl.pallas_call(
        triangle_kernel,
        out_shape=[wide(2, 128, LANES)] * 3,
        in_specs=[smem] + [vmem] * 6,
        out_specs=[vmem] * 3,
        scratch_shapes=[
            pltpu.VMEM((32 * 128, LANES), jnp.float32),
            pltpu.VMEM(tall, jnp.float32),
            pltpu.VMEM(slabs, jnp.float32),
            pltpu.VMEM((128, 256), jnp.float32),
            pltpu.VMEM(tall, jnp.float32),
            pltpu.VMEM(tall, jnp.float32),
        ],
        compiler_params=limit(32),
        name="pair_triangles",
    )(place, pair_mid, left, gating, right, exchange(right, 1), turned_weights)
    pair_output = pl.pallas_call(
        finish_kernel,
        out_shape=array(256, LANES),
        in_specs=[vmem] * 5,
        out_specs=vmem,
        compiler_params=limit(16),
        name="pair_finish",
    )(own_pair, own_part, exchange(other_part, 1), turned_weights, wide_weights)
    return result.reshape(128, 4, channels), pair_output.reshape(pair_state_input.shape)


def lanes_order(values):
    lead = values.shape[:-1]
    halves = values.reshape(lead + (values.shape[-1] // 2, 2))
    return jnp.swapaxes(halves, -1, -2).reshape(values.shape)


def local(
    alignment_input,
    pair_state_input,
    residue_number_index,
    chain_label,
    alignment_row_mask,
    relative_position_table,
    column_query_weight,
    column_key_weight,
    column_value_gate_weight,
    column_output_weight,
    alignment_transition_up,
    alignment_transition_down,
    outer_input_weight,
    outer_output_weight,
    outgoing_projection_weight,
    outgoing_output_gate,
    outgoing_output_weight,
    incoming_projection_weight,
    incoming_output_gate,
    incoming_output_weight,
    pair_transition_up,
    pair_transition_down,
):
    shard_pieces = lax.axis_size("dap")
    own_rows = pair_state_input.shape[0]
    residue_count = pair_state_input.shape[1]
    channel_count = alignment_input.shape[2]
    head_width = HM * HEAD_SIZE
    first_row = lax.axis_index("dap") * own_rows
    own_index = lax.dynamic_slice_in_dim(residue_number_index, first_row, own_rows)
    own_chain = lax.dynamic_slice_in_dim(chain_label, first_row, own_rows)

    def bins_of(index, chain):
        offset = index[:, None] - residue_number_index[None, :]
        return jnp.where(
            chain[:, None] == chain_label[None, :],
            jnp.clip(offset + MAXREL, 0, 2 * MAXREL),
            2 * MAXREL + 1,
        )

    bin_index = bins_of(own_index, own_chain)
    one_hot = (bin_index[:, :, None] == jnp.arange(NBINS, dtype=jnp.int32)[None, None, :]).astype(
        jnp.bfloat16
    )
    pair_start = pair_state_input.astype(jnp.float32) + jnp.einsum(
        "ijb,bc->ijc", one_hot, relative_position_table, preferred_element_type=jnp.float32
    )
    live_rows = alignment_row_mask > 0
    live_row_float = live_rows.astype(jnp.float32)

    if alignment_row_mask.shape[0] == LANES and 2 * residue_count == LANES and own_rows == 4:
        return whole_block(
            alignment_input,
            pair_state_input,
            bins_of(residue_number_index, chain_label),
            live_row_float,
            relative_position_table,
            column_query_weight,
            column_key_weight,
            column_value_gate_weight,
            column_output_weight,
            alignment_transition_up,
            alignment_transition_down,
            outer_input_weight,
            outer_output_weight,
            outgoing_projection_weight,
            outgoing_output_gate,
            outgoing_output_weight,
            incoming_projection_weight,
            incoming_output_gate,
            incoming_output_weight,
            pair_transition_up,
            pair_transition_down,
        )

    def attend_one(operands):
        query_col, key_col, value_col = operands
        scores = jnp.einsum("shd,thd->hst", query_col, key_col, preferred_element_type=jnp.float32)
        scores = jnp.where(live_rows[None, None, :], scores, -1000000000.0)
        row_top = jnp.max(scores, axis=-1, keepdims=True)
        raised = jnp.exp(scores - row_top)
        attention = (raised / jnp.sum(raised, axis=-1, keepdims=True)).astype(jnp.bfloat16)
        return jnp.einsum("hst,thd->shd", attention, value_col, preferred_element_type=jnp.float32)

    blocked_view = alignment_input.reshape(
        alignment_input.shape[0], shard_pieces, residue_count // shard_pieces, channel_count
    )
    block_in = lax.all_to_all(blocked_view, "dap", split_axis=1, concat_axis=0, tiled=True)
    depth_rows = block_in.shape[0]
    count_cols = block_in.shape[2]
    current = block_in.reshape(depth_rows, count_cols, channel_count).astype(jnp.float32)
    normed = layer_normalize(current).astype(jnp.bfloat16)
    query_rows = (
        jnp.einsum("sic,ce->sie", normed, column_query_weight, preferred_element_type=jnp.float32)
        * HEAD_SIZE ** (-0.5)
    ).astype(jnp.bfloat16)
    key_row_block = jnp.einsum(
        "sic,ce->sie", normed, column_key_weight, preferred_element_type=jnp.float32
    ).astype(jnp.bfloat16)
    value_gate_pair = jnp.einsum(
        "sic,ce->sie", normed, column_value_gate_weight, preferred_element_type=jnp.float32
    )
    value_rows = value_gate_pair[..., :head_width].astype(jnp.bfloat16)

    def by_column(values):
        return values.transpose(1, 0, 2).reshape(count_cols, depth_rows, HM, HEAD_SIZE)

    attended = lax.map(
        attend_one, (by_column(query_rows), by_column(key_row_block), by_column(value_rows))
    )
    attended = attended.reshape(count_cols, depth_rows, head_width).transpose(1, 0, 2)
    gated_out = (jax.nn.sigmoid(value_gate_pair[..., head_width:]) * attended).astype(jnp.bfloat16)
    current = current + jnp.einsum(
        "sie,ec->sic", gated_out, column_output_weight, preferred_element_type=jnp.float32
    )
    hidden = jax.nn.relu(
        jnp.einsum(
            "sic,cf->sif",
            layer_normalize(current).astype(jnp.bfloat16),
            alignment_transition_up,
            preferred_element_type=jnp.float32,
        )
    ).astype(jnp.bfloat16)
    current = current + jnp.einsum(
        "sif,fc->sic", hidden, alignment_transition_down, preferred_element_type=jnp.float32
    )
    result = current.astype(jnp.bfloat16)
    outer_product_input = jnp.einsum(
        "sic,cf->sif",
        layer_normalize(result.astype(jnp.float32)).astype(jnp.bfloat16),
        outer_input_weight,
        preferred_element_type=jnp.float32,
    )
    outer_product_input = outer_product_input * live_row_float[:, None, None]
    left_part = outer_product_input[..., :CO].astype(jnp.bfloat16)
    right_part = outer_product_input[..., CO:].astype(jnp.bfloat16)
    all_rows = result.shape[0]
    left_cols = left_part.transpose(1, 0, 2)
    right_cols = right_part.transpose(1, 0, 2).reshape(own_rows, all_rows * CO)
    live_count = jnp.sum(live_row_float)
    right_piece = gather_doubling(right_cols).reshape(-1, all_rows * CO)
    span_rows = right_piece.shape[0]
    products = jnp.einsum(
        "isc,jsd->ijcd",
        left_cols,
        right_piece.reshape(span_rows, all_rows, CO),
        preferred_element_type=jnp.float32,
    )
    products = products.astype(jnp.bfloat16).reshape(own_rows, span_rows, CO * CO)
    outer_mean = (
        jnp.einsum("ijf,fc->ijc", products, outer_output_weight, preferred_element_type=jnp.float32)
        / live_count
    )
    pair_mid = pair_start + outer_mean
    out_left, out_right, out_gating = triangle_inputs(
        pair_mid, outgoing_projection_weight, outgoing_output_gate
    )
    out_product = by_channels(out_left, out_right, "cik,cjk->cij")
    pair_after_out = triangle_finish(pair_mid, out_product, out_gating, outgoing_output_weight)
    in_left, in_right, in_gating = triangle_inputs(
        pair_after_out, incoming_projection_weight, incoming_output_gate
    )
    in_product = by_channels(in_left, in_right, "cki,ckj->cij")
    pair_after_in = triangle_finish(pair_after_out, in_product, in_gating, incoming_output_weight)
    pair_expanded = jax.nn.relu(
        jnp.einsum(
            "ijc,cf->ijf",
            layer_normalize(pair_after_in).astype(jnp.bfloat16),
            pair_transition_up,
            preferred_element_type=jnp.float32,
        )
    ).astype(jnp.bfloat16)
    pair_state_output = (
        pair_after_in
        + jnp.einsum(
            "ijf,fc->ijc", pair_expanded, pair_transition_down, preferred_element_type=jnp.float32
        )
    ).astype(jnp.bfloat16)
    return (result, pair_state_output)


def solution(mesh):
    in_specs = (
        P(("grp", "dap"), None, None),
        P(("grp", "dap"), None, None),
        P("grp"),
        P("grp"),
        P("grp"),
        P(),
        P(),
        P(),
        P(),
        P(),
        P(),
        P(),
        P(),
        P(),
        P(),
        P(),
        P(),
        P(),
        P(),
        P(),
        P(),
        P(),
    )
    out_specs = (P("grp", "dap", None), P(("grp", "dap"), None, None))
    return jax.shard_map(local, mesh=mesh, in_specs=in_specs, out_specs=out_specs, check_vma=False)
```

```python
import jax
import jax.numpy as jnp
from jax import lax
from jax.experimental import pallas as pl
from jax.experimental.pallas import tpu as pltpu
from jax.sharding import PartitionSpec as P

HM = 8
HEAD_SIZE = 32
CO = 32
MAXREL = 32
NBINS = 66


EPSILON = 1e-05


def layer_normalize(values):
    center = jnp.mean(values, axis=-1, keepdims=True)
    shifted = values - center
    spread = jnp.mean(shifted * shifted, axis=-1, keepdims=True)
    return shifted * lax.rsqrt(spread + EPSILON)


def triangle_inputs(pair_now, weight, gate_weight):
    normed = layer_normalize(pair_now).astype(jnp.bfloat16)
    combined = jnp.einsum("ijc,cf->fij", normed, weight, preferred_element_type=jnp.float32)
    hidden_width = weight.shape[1] // 4
    left_side = (
        jax.nn.sigmoid(combined[hidden_width : 2 * hidden_width]) * combined[:hidden_width]
    ).astype(jnp.bfloat16)
    right_side = (
        jax.nn.sigmoid(combined[3 * hidden_width :]) * combined[2 * hidden_width : 3 * hidden_width]
    ).astype(jnp.bfloat16)
    gating = jax.nn.sigmoid(
        jnp.einsum("ijc,cd->ijd", normed, gate_weight, preferred_element_type=jnp.float32)
    )
    return (left_side, right_side, gating)


def triangle_finish(pair_now, product, gating, final_weight):
    product = lax.optimization_barrier(product)
    normed = layer_normalize(product.transpose(1, 2, 0).astype(jnp.float32)).astype(jnp.bfloat16)
    return pair_now + gating * jnp.einsum(
        "ijc,cd->ijd", normed, final_weight, preferred_element_type=jnp.float32
    )


def by_channels(left_side, right_side, form):
    both = jnp.stack([left_side, right_side])
    both = lax.all_to_all(both, "dap", split_axis=1, concat_axis=2, tiled=True)
    partial_out = jnp.einsum(form, both[0], both[1], preferred_element_type=jnp.float32)
    return lax.all_to_all(
        partial_out.astype(jnp.bfloat16), "dap", split_axis=1, concat_axis=0, tiled=True
    )


def gather_doubling(block):
    shard_pieces = lax.axis_size("dap")
    place = lax.axis_index("dap")
    held = block
    depth = 0
    bit = shard_pieces // 2
    while bit:
        other = lax.ppermute(held, "dap", [(q, q ^ bit) for q in range(shard_pieces)])
        upper = (place & bit) != 0
        first = jnp.where(upper, other, held)
        second = jnp.where(upper, held, other)
        held = jnp.stack([first, second], axis=depth)
        depth += 1
        bit //= 2
    return held.reshape((shard_pieces,) + block.shape)


LANES = 128


def gate_curve(values):
    return 0.5 + 0.5 * jnp.tanh(0.5 * values)


def normalize_channels(values):
    center = jnp.mean(values, axis=0, keepdims=True)
    shifted = values - center
    spread = jnp.mean(shifted * shifted, axis=0, keepdims=True)
    return (shifted * lax.rsqrt(spread + EPSILON)).astype(jnp.bfloat16)


def mix(weight, values):
    return jnp.dot(weight, values, preferred_element_type=jnp.float32)


def fold_halves(first_even, second_even, first_odd, second_odd, low_half):
    straight = jnp.where(low_half, first_even, second_odd)
    crossed = jnp.where(low_half, second_even, first_odd)
    return straight + pltpu.roll(crossed, LANES // 2, 1)


def turned(ref, name):
    first, last = TURNED[name]
    return ref[first:last, :]


OFFSETS = (0, 8, 4, 12)


def start_kernel(
    place_ref,
    live_ref,
    line_ref,
    across_ref,
    core_line_ref,
    core_across_ref,
    pair_line_ref,
    pair_across_ref,
    embedding_ref,
    turned_ref,
    wide_weight_ref,
    pair_mid_ref,
    left_ref,
    gating_ref,
    right_ref,
    wide_ref,
    right_cols_ref,
    *stack_refs,
):
    place = place_ref[0]
    inverse_live = 1.0 / jnp.sum(live_ref[...], axis=1, keepdims=True)
    half = LANES // 2
    low_half = lax.broadcasted_iota(jnp.int32, (LANES, LANES), 1) < half

    for m in range(4):
        for part, device in (
            (line_ref[m, 128:256, :], place ^ OFFSETS[m]),
            (across_ref[m, 128:256, :], place ^ OFFSETS[m] ^ 2),
            (core_line_ref[m], place ^ OFFSETS[m] ^ 1),
            (core_across_ref[m], place ^ OFFSETS[m] ^ 3),
        ):
            wide_ref[pl.ds(pl.multiple_of(device * 128, 128), 128), :] = part.astype(jnp.float32)
    for d in range(0, CO, 2):
        rows = [
            wide_ref[pl.ds(par * CO + d + e, 32, stride=2 * CO), :]
            for e in range(2)
            for par in range(2)
        ]
        right_cols_ref[:, d * half : d * half + LANES] = (
            jnp.concatenate(rows, axis=0).T.astype(jnp.bfloat16)
        )

    for g in range(4):
        parts_ref = (line_ref, across_ref)[g // 2]
        pair_ref = (pair_line_ref, pair_across_ref)[g // 2]
        stack_ref = stack_refs[g % 2]
        first = 2 * (g % 2)
        left_rows = parts_ref[first : first + 2, 0:128, :].reshape(256, LANES)
        outer = mix(left_rows, right_cols_ref[...]).astype(jnp.bfloat16)
        for i in range(8):
            for d in range(16):
                stack_ref[d * 32 : (d + 1) * 32, i * LANES : (i + 1) * LANES] = outer[
                    i * 32 : (i + 1) * 32, d * LANES : (d + 1) * LANES
                ]
        mixed = mix(wide_weight_ref[0:256, :], stack_ref[...])
        slabs = []
        places = []
        for q in range(4):
            m = first + q // 2
            device = place ^ OFFSETS[m] ^ (2 * (g // 2))
            here = 2 * (device // 2) + q % 2
            even = slice(2 * q * LANES, (2 * q + 1) * LANES)
            odd = slice((2 * q + 1) * LANES, (2 * q + 2) * LANES)
            outer_mean = fold_halves(
                mixed[0:128, even], mixed[0:128, odd], mixed[128:256, even], mixed[128:256, odd], low_half
            )
            start = pair_ref[m, q % 2].astype(jnp.float32)
            start = start + embedding_ref[2 * device + q % 2].astype(jnp.float32)
            slab = start + outer_mean * inverse_live
            pair_mid_ref[here] = slab
            slabs.append(normalize_channels(slab))
            places.append(here)
        normed = jnp.concatenate(slabs, axis=1)
        combined = mix(turned(turned_ref, "out_mix"), normed)
        left = gate_curve(combined[128:256]) * combined[0:128]
        right = gate_curve(combined[384:512]) * combined[256:384]
        gating = gate_curve(mix(turned(turned_ref, "out_gate"), normed))
        for q in range(4):
            lanes = slice(q * LANES, (q + 1) * LANES)
            rows = pl.ds(pl.multiple_of(places[q] * 128, 128), 128)
            left_ref[rows, :] = left[:, lanes]
            right_ref[rows, :] = right[:, lanes].astype(jnp.bfloat16)
            gating_ref[places[q]] = gating[:, lanes]


def triangle_kernel(
    place_ref,
    pair_mid_ref,
    left_ref,
    gating_ref,
    right_own_ref,
    right_other_ref,
    turned_ref,
    own_pair_ref,
    own_part_ref,
    other_part_ref,
    right_ref,
    product_ref,
    pair_now_ref,
    chosen_ref,
    own_left_ref,
    own_product_ref,
):
    place = place_ref[0]
    core = place % 2
    half = LANES // 2
    low_half = lax.broadcasted_iota(jnp.int32, (LANES, LANES), 1) < half
    low_short = lax.broadcasted_iota(jnp.int32, (32, LANES), 1) < half
    for chip in range(8):
        for source, side in ((right_own_ref, core), (right_other_ref, 1 - core)):
            rows = pl.ds(pl.multiple_of((4 * chip + 2 * side) * 128, 256), 256)
            right_ref[rows, :] = source[chip * 256 : (chip + 1) * 256, :].astype(jnp.float32)

    nothing = jnp.zeros((32, LANES), jnp.bfloat16)

    def outgoing_channels(block, carry):
        for e in range(32):
            c = block * 32 + e
            left = left_ref[pl.ds(c, 16, stride=128), :].astype(jnp.bfloat16)
            right = right_ref[pl.ds(c, 32, stride=128), :]
            moved = pltpu.roll(right, half, 1).astype(jnp.bfloat16)
            right = right.astype(jnp.bfloat16)
            spread = jnp.concatenate(
                [
                    jnp.where(low_short, right, nothing),
                    jnp.where(low_short, moved, nothing),
                    jnp.where(low_short, nothing, moved),
                    jnp.where(low_short, nothing, right),
                ],
                axis=0,
            )
            product_ref[pl.ds(c, 16, stride=128), :] = contract_last(left, spread)
        return carry

    lax.fori_loop(0, 4, outgoing_channels, 0)

    column = lax.broadcasted_iota(jnp.int32, (1, 256), 1)
    which = column // 16
    residue = which % 4
    device = place ^ ((which // 4) % 2)
    wanted = half * (which // 8) + 32 * (residue % 2) + 2 * device + residue // 2
    slab_of = column % 16
    source_lane = lax.broadcasted_iota(jnp.int32, (LANES, 256), 0)
    for g in range(4):
        products = [
            normalize_channels(product_ref[(4 * g + q) * 128 : (4 * g + q + 1) * 128, :])
            for q in range(4)
        ]
        finished = mix(turned(turned_ref, "out_final"), jnp.concatenate(products, axis=1))
        slabs = []
        picks = []
        for q in range(4):
            h = 4 * g + q
            lanes = slice(q * LANES, (q + 1) * LANES)
            slab = pair_mid_ref[h] + gating_ref[h] * finished[:, lanes]
            pair_now_ref[h] = slab
            slabs.append(normalize_channels(slab))
            here = jnp.where(slab_of == h, wanted, -1)
            picks.append((source_lane == here).astype(jnp.float32).astype(jnp.bfloat16))
        normed = jnp.concatenate(slabs, axis=1)
        chosen = mix(normed, jnp.concatenate(picks, axis=0))
        if g:
            chosen_ref[...] += chosen
        else:
            chosen_ref[...] = chosen
        combined = mix(turned(turned_ref, "in_mix")[256:512, :], normed)
        right = gate_curve(combined[128:256]) * combined[0:128]
        for q in range(4):
            right_ref[(4 * g + q) * 128 : (4 * g + q + 1) * 128, :] = right[
                :, q * LANES : (q + 1) * LANES
            ]
    for t in range(2):
        own_pair_ref[t] = pair_now_ref[2 * (place // 2) + t]

    combined = mix(turned(turned_ref, "in_mix")[0:256, :], chosen_ref[...].astype(jnp.bfloat16))
    own_left = gate_curve(combined[128:256]) * combined[0:128]
    for m in range(16):
        part = own_left[:, (m // 8) * LANES : (m // 8 + 1) * LANES]
        if m % 8:
            part = pltpu.roll(part, LANES - 16 * (m % 8), 1)
        own_left_ref[m * 128 : (m + 1) * 128, :] = part

    def incoming_channels(block, carry):
        for e in range(32):
            c = block * 32 + e
            left = own_left_ref[pl.ds(c, 16, stride=128), :][:, 0:16].astype(jnp.bfloat16)
            right = right_ref[pl.ds(c, 16, stride=128), :].astype(jnp.bfloat16)
            own_product_ref[pl.ds(c, 16, stride=128), :] = mix(left, right)
        return carry

    lax.fori_loop(0, 4, incoming_channels, 0)

    def block_of(b, e, residue):
        m = 8 * b + 4 * e + residue
        return own_product_ref[m * 128 : (m + 1) * 128, :]

    for e, target in ((0, own_part_ref), (1, other_part_ref)):
        for t in range(2):
            target[t] = fold_halves(
                block_of(0, e, 2 * t),
                block_of(0, e, 2 * t + 1),
                block_of(1, e, 2 * t),
                block_of(1, e, 2 * t + 1),
                low_half,
            )


def finish_kernel(own_pair_ref, own_part_ref, other_part_ref, turned_ref, wide_weight_ref, result_ref):
    products = [normalize_channels(own_part_ref[t] + other_part_ref[t]) for t in range(2)]
    finished = mix(turned(turned_ref, "in_final"), jnp.concatenate(products, axis=1))
    own_pair = jnp.concatenate([own_pair_ref[t] for t in range(2)], axis=1)
    gating = gate_curve(mix(turned(turned_ref, "in_gate"), normalize_channels(own_pair)))
    own_pair = own_pair + gating * finished
    hidden = jnp.maximum(mix(turned(turned_ref, "up"), normalize_channels(own_pair)), 0.0)
    own_pair = own_pair + mix(wide_weight_ref[256:384, :], hidden.astype(jnp.bfloat16))
    own_pair = own_pair.astype(jnp.bfloat16)
    order = lane_order_matrix()
    for t in range(2):
        result_ref[t * 128 : (t + 1) * 128, :] = contract_last(
            order, own_pair[:, t * LANES : (t + 1) * LANES]
        ).astype(jnp.bfloat16)


def lane_order_matrix():
    half = LANES // 2
    member = lax.broadcasted_iota(jnp.int32, (LANES, LANES), 0)
    lane = lax.broadcasted_iota(jnp.int32, (LANES, LANES), 1)
    back = half * (member // half) + 32 * (member % 2) + (member % half) // 2
    return (lane == back).astype(jnp.float32).astype(jnp.bfloat16)


def contract_first(first, second):
    return lax.dot_general(
        first, second, (((0,), (0,)), ((), ())), preferred_element_type=jnp.float32
    )


def rows_kernel(
    rows_source, pair_source, blocks_ref, own_pair_ref, rows_ref, pair_ref, wide_ref, arrived
):
    rows_copy = pltpu.make_async_copy(rows_source, rows_ref, arrived.at[0])
    pair_copy = pltpu.make_async_copy(pair_source, pair_ref, arrived.at[1])
    pair_copy.start()
    rows_copy.start()
    pair_copy.wait()
    order = lane_order_matrix()
    for t in range(2):
        own_pair_ref[t] = contract_first(
            pair_ref[2 * t : 2 * t + 2].reshape(LANES, LANES), order
        ).astype(jnp.bfloat16)
    rows_copy.wait()
    residues = rows_ref.shape[1]
    count = 8 * residues
    rows = rows_ref[...].astype(jnp.float32).reshape(count, 2 * LANES)
    for e in range(2):
        wide_ref[e * count : (e + 1) * count, :] = rows[:, e * LANES : (e + 1) * LANES]
    for p in range(16):
        for e in range(2):
            block = [
                wide_ref[pl.ds(e * count + 4 * p + i, 8, stride=residues), :] for i in range(4)
            ]
            blocks_ref[p, :, e * LANES : (e + 1) * LANES] = jnp.concatenate(block, axis=0).astype(
                jnp.bfloat16
            )


TURNED = {
    "out_mix": (0, 512),
    "out_gate": (512, 640),
    "out_final": (640, 768),
    "in_mix": (768, 1280),
    "in_gate": (1280, 1408),
    "in_final": (1408, 1536),
    "up": (1536, 2048),
}


def weights_kernel(
    bins_ref,
    table_ref,
    *rest,
):
    sources, (embedding_out, turned_out, wide_out, ready_out) = rest[:9], rest[9:13]
    landed, (table_wide_ref, mean_wide_ref, arrived) = rest[13:22], rest[22:]
    ready_out[...] = jnp.zeros_like(ready_out)
    copies = [
        pltpu.make_async_copy(sources[k], landed[k], arrived.at[k]) for k in range(len(sources))
    ]
    for copy in copies:
        copy.start()
    table_wide_ref[...] = jnp.zeros_like(table_wide_ref)
    table_wide_ref[0:NBINS, :] = table_ref[...].astype(jnp.float32)
    table = table_wide_ref[...].T.astype(jnp.bfloat16)
    channel = lax.broadcasted_iota(jnp.int32, (LANES, LANES), 0)

    def embed(g, carry):
        for q in range(4):
            h = 4 * g + q
            one_hot = (channel == bins_ref[pl.ds(h, 1), :]).astype(jnp.float32).astype(jnp.bfloat16)
            embedding_out[h] = mix(table, one_hot).astype(jnp.bfloat16)
        return carry

    lax.fori_loop(0, 8, embed, 0)
    for copy in copies:
        copy.wait()
    mean_wide_ref[...] = landed[0][...].astype(jnp.float32)
    for e in range(2):
        for block in range(4):
            rows = [
                mean_wide_ref[pl.ds(2 * (4 * block + k) + e, CO, stride=CO), :] for k in range(4)
            ]
            wide_out[e * LANES : (e + 1) * LANES, block * LANES : (block + 1) * LANES] = (
                jnp.concatenate(rows, axis=0).T.astype(jnp.bfloat16)
            )
    first = 0
    for source in landed[1:8]:
        for b in range(source.shape[1] // LANES):
            part = source[:, b * LANES : (b + 1) * LANES].astype(jnp.float32)
            turned_out[first : first + LANES, :] = part.T.astype(jnp.bfloat16)
            first += LANES
    for a in range(4):
        part = landed[8][a * LANES : (a + 1) * LANES, :].astype(jnp.float32)
        wide_out[256:384, a * LANES : (a + 1) * LANES] = part.T.astype(jnp.bfloat16)


def normalize_rows(values):
    center = jnp.mean(values, axis=1, keepdims=True)
    shifted = values - center
    spread = jnp.mean(shifted * shifted, axis=1, keepdims=True)
    return (shifted * lax.rsqrt(spread + EPSILON)).astype(jnp.bfloat16)


def contract_last(first, second):
    return lax.dot_general(
        first, second, (((1,), (1,)), ((), ())), preferred_element_type=jnp.float32
    )


def msa_kernel(
    live_ref,
    blocks_ref,
    query_ref,
    key_ref,
    value_gate_ref,
    output_ref,
    up_ref,
    down_ref,
    outer_ref,
    ready_ref,
    result_ref,
    parts_ref,
    wide_ref,
    attended_ref,
    final_ref,
):
    for p in range(16):
        block = blocks_ref[p].astype(jnp.float32)
        for i in range(4):
            wide_ref[i * 128 + p * 8 : i * 128 + p * 8 + 8, :] = block[i * 8 : i * 8 + 8, :]
    live = live_ref[...]
    alive = live > 0.0
    width = HM * HEAD_SIZE
    head_of = lax.broadcasted_iota(jnp.int32, (128, width), 1) // HEAD_SIZE
    zero = jnp.zeros((128, width), jnp.bfloat16)
    one = jnp.ones((128, width), jnp.bfloat16)

    def by_head(values):
        return jnp.concatenate([jnp.where(head_of == h, values, zero) for h in range(HM)], axis=0)

    heads = by_head(one)
    normed = normalize_rows(wide_ref[...])
    query = (mix(normed, query_ref[...]) * HEAD_SIZE ** (-0.5)).astype(jnp.bfloat16)
    key = mix(normed, key_ref[...]).astype(jnp.bfloat16)
    value_gate = mix(normed, value_gate_ref[...])
    value = value_gate[:, :width].astype(jnp.bfloat16)
    for i in range(4):
        rows = slice(i * 128, (i + 1) * 128)
        scores = contract_last(query[rows], by_head(key[rows]))
        raised = []
        for h in range(HM):
            score = jnp.where(alive, scores[:, h * 128 : (h + 1) * 128], -1000000000.0)
            raised.append(jnp.exp(score - jnp.max(score, axis=1, keepdims=True)).astype(jnp.bfloat16))
        raised = jnp.concatenate(raised, axis=1)
        attended_ref[rows, :] = mix(raised, by_head(value[rows])) / mix(raised, heads)
    gated = (gate_curve(value_gate[:, width:]) * attended_ref[...]).astype(jnp.bfloat16)
    current = wide_ref[...] + mix(gated, output_ref[...])
    hidden = jnp.maximum(mix(normalize_rows(current), up_ref[...]), 0.0).astype(jnp.bfloat16)
    final = (current + mix(hidden, down_ref[...])).astype(jnp.bfloat16).astype(jnp.float32)
    outer = contract_last(outer_ref[...], normalize_rows(final))
    for i in range(4):
        rows = slice(i * 128, (i + 1) * 128)
        part = (outer[:, rows] * live).astype(jnp.bfloat16)
        parts_ref[i * CO : (i + 1) * CO, :] = part[:CO, :]
        parts_ref[128 + i * CO : 128 + (i + 1) * CO, :] = part[CO:, :]
        final_ref[pl.ds(i, 128, stride=4), :] = final[rows, :128]
        final_ref[pl.ds(512 + i, 128, stride=4), :] = final[rows, 128:]
    result_ref[:, :128] = final_ref[:512, :].astype(jnp.bfloat16)
    result_ref[:, 128:] = final_ref[512:, :].astype(jnp.bfloat16)


def exchange(values, offset):
    pieces = lax.axis_size("dap")
    return lax.ppermute(values, "dap", [(q, q ^ offset) for q in range(pieces)])


def whole_block(
    alignment_input,
    pair_state_input,
    bin_all,
    live_row_float,
    relative_position_table,
    column_query_weight,
    column_key_weight,
    column_value_gate_weight,
    column_output_weight,
    alignment_transition_up,
    alignment_transition_down,
    outer_input_weight,
    *pair_weights,
):
    channels = alignment_input.shape[2]
    width = pair_state_input.shape[2]
    place = lax.axis_index("dap").astype(jnp.int32).reshape(1)
    vmem = pl.BlockSpec(memory_space=pltpu.VMEM)
    smem = pl.BlockSpec(memory_space=pltpu.SMEM)
    hbm = pl.BlockSpec(memory_space=pltpu.HBM)

    def array(*shape, dtype=jnp.bfloat16):
        return jax.ShapeDtypeStruct(shape, dtype)

    def wide(*shape):
        return jax.ShapeDtypeStruct(shape, jnp.float32)

    def limit(mebibytes):
        return pltpu.CompilerParams(vmem_limit_bytes=mebibytes * 1024 * 1024)

    blocks, own_pair = pl.pallas_call(
        rows_kernel,
        out_shape=[array(16, 32, channels), array(2, width, LANES)],
        in_specs=[hbm, hbm],
        out_specs=[vmem, vmem],
        scratch_shapes=[
            pltpu.VMEM(alignment_input.shape, jnp.bfloat16),
            pltpu.VMEM(pair_state_input.shape, jnp.bfloat16),
            pltpu.VMEM((1024, LANES), jnp.float32),
            pltpu.SemaphoreType.DMA((2,)),
        ],
        compiler_params=limit(16),
        name="rows_by_device",
    )(alignment_input, pair_state_input)
    blocks = lax.all_to_all(blocks, "dap", split_axis=0, concat_axis=0, tiled=True)

    pair_far = exchange(own_pair, 8)
    pair_near = exchange(jnp.stack([own_pair, pair_far]), 4)
    pair_line = jnp.concatenate([jnp.stack([own_pair, pair_far]), pair_near])

    embedding, turned_weights, wide_weights, ready = pl.pallas_call(
        weights_kernel,
        out_shape=[array(32, width, LANES), array(2048, LANES), array(384, 512), wide(8, LANES)],
        in_specs=[vmem] * 2 + [hbm] * 9,
        out_specs=[vmem] * 4,
        scratch_shapes=[pltpu.VMEM(w.shape, jnp.bfloat16) for w in pair_weights]
        + [
            pltpu.VMEM((LANES, LANES), jnp.float32),
            pltpu.VMEM((1024, LANES), jnp.float32),
            pltpu.SemaphoreType.DMA((9,)),
        ],
        compiler_params=limit(24),
        cost_estimate=pl.CostEstimate(
            flops=200_000_000, bytes_accessed=8_000_000, transcendentals=0
        ),
        name="turn_weights",
    )(
        lanes_order(bin_all).reshape(32, LANES),
        relative_position_table,
        *pair_weights,
    )
    blocks, pair_line = lax.optimization_barrier((blocks, pair_line))
    pair_across = exchange(pair_line, 2)

    result, parts = pl.pallas_call(
        msa_kernel,
        out_shape=(array(512, channels), array(256, LANES)),
        in_specs=[vmem] * 10,
        out_specs=(vmem, vmem),
        scratch_shapes=[
            pltpu.VMEM((512, channels), jnp.float32),
            pltpu.VMEM((512, channels), jnp.float32),
            pltpu.VMEM((1024, LANES), jnp.float32),
        ],
        compiler_params=limit(32),
        cost_estimate=pl.CostEstimate(
            flops=2_000_000_000, bytes_accessed=10_000_000, transcendentals=1_000_000
        ),
        name="msa_whole",
    )(
        live_row_float.reshape(1, LANES),
        blocks,
        column_query_weight,
        column_key_weight,
        column_value_gate_weight,
        column_output_weight,
        alignment_transition_up,
        alignment_transition_down,
        outer_input_weight.T,
        ready,
    )
    parts, pair_across = lax.optimization_barrier((parts, pair_across))
    far = exchange(parts, 8)
    near = [exchange(parts, 4), exchange(far, 4)]
    line = jnp.stack([parts, far] + near)
    across = exchange(line, 2)
    core_line = exchange(jnp.stack([part[128:256] for part in (parts, far, *near)]), 1)
    core_across = exchange(across[:, 128:256, :], 1)

    slabs = (16, 128, LANES)
    tall = (16 * 128, LANES)
    pair_mid, left, gating, right = pl.pallas_call(
        start_kernel,
        out_shape=[wide(*slabs), wide(*tall), wide(*slabs), array(*tall)],
        in_specs=[smem] + [vmem] * 10,
        out_specs=[vmem] * 4,
        scratch_shapes=[
            pltpu.VMEM((2048, LANES), jnp.float32),
            pltpu.VMEM((128, 2048), jnp.bfloat16),
            pltpu.VMEM((512, 1024), jnp.bfloat16),
            pltpu.VMEM((512, 1024), jnp.bfloat16),
        ],
        compiler_params=limit(32),
        name="pair_start",
    )(
        place,
        live_row_float.reshape(1, LANES),
        line,
        across,
        core_line,
        core_across,
        pair_line,
        pair_across,
        embedding,
        turned_weights,
        wide_weights,
    )
    own_pair, own_part, other_part = pl.pallas_call(
        triangle_kernel,
        out_shape=[wide(2, 128, LANES)] * 3,
        in_specs=[smem] + [vmem] * 6,
        out_specs=[vmem] * 3,
        scratch_shapes=[
            pltpu.VMEM((32 * 128, LANES), jnp.float32),
            pltpu.VMEM(tall, jnp.float32),
            pltpu.VMEM(slabs, jnp.float32),
            pltpu.VMEM((128, 256), jnp.float32),
            pltpu.VMEM(tall, jnp.float32),
            pltpu.VMEM(tall, jnp.float32),
        ],
        compiler_params=limit(32),
        name="pair_triangles",
    )(place, pair_mid, left, gating, right, exchange(right, 1), turned_weights)
    pair_output = pl.pallas_call(
        finish_kernel,
        out_shape=array(256, LANES),
        in_specs=[vmem] * 5,
        out_specs=vmem,
        compiler_params=limit(16),
        name="pair_finish",
    )(own_pair, own_part, exchange(other_part, 1), turned_weights, wide_weights)
    return result.reshape(128, 4, channels), pair_output.reshape(pair_state_input.shape)


def lanes_order(values):
    lead = values.shape[:-1]
    halves = values.reshape(lead + (values.shape[-1] // 2, 2))
    return jnp.swapaxes(halves, -1, -2).reshape(values.shape)


def local(
    alignment_input,
    pair_state_input,
    residue_number_index,
    chain_label,
    alignment_row_mask,
    relative_position_table,
    column_query_weight,
    column_key_weight,
    column_value_gate_weight,
    column_output_weight,
    alignment_transition_up,
    alignment_transition_down,
    outer_input_weight,
    outer_output_weight,
    outgoing_projection_weight,
    outgoing_output_gate,
    outgoing_output_weight,
    incoming_projection_weight,
    incoming_output_gate,
    incoming_output_weight,
    pair_transition_up,
    pair_transition_down,
):
    shard_pieces = lax.axis_size("dap")
    own_rows = pair_state_input.shape[0]
    residue_count = pair_state_input.shape[1]
    channel_count = alignment_input.shape[2]
    head_width = HM * HEAD_SIZE
    first_row = lax.axis_index("dap") * own_rows
    own_index = lax.dynamic_slice_in_dim(residue_number_index, first_row, own_rows)
    own_chain = lax.dynamic_slice_in_dim(chain_label, first_row, own_rows)

    def bins_of(index, chain):
        offset = index[:, None] - residue_number_index[None, :]
        return jnp.where(
            chain[:, None] == chain_label[None, :],
            jnp.clip(offset + MAXREL, 0, 2 * MAXREL),
            2 * MAXREL + 1,
        )

    bin_index = bins_of(own_index, own_chain)
    one_hot = (bin_index[:, :, None] == jnp.arange(NBINS, dtype=jnp.int32)[None, None, :]).astype(
        jnp.bfloat16
    )
    pair_start = pair_state_input.astype(jnp.float32) + jnp.einsum(
        "ijb,bc->ijc", one_hot, relative_position_table, preferred_element_type=jnp.float32
    )
    live_rows = alignment_row_mask > 0
    live_row_float = live_rows.astype(jnp.float32)

    if alignment_row_mask.shape[0] == LANES and 2 * residue_count == LANES and own_rows == 4:
        return whole_block(
            alignment_input,
            pair_state_input,
            bins_of(residue_number_index, chain_label),
            live_row_float,
            relative_position_table,
            column_query_weight,
            column_key_weight,
            column_value_gate_weight,
            column_output_weight,
            alignment_transition_up,
            alignment_transition_down,
            outer_input_weight,
            outer_output_weight,
            outgoing_projection_weight,
            outgoing_output_gate,
            outgoing_output_weight,
            incoming_projection_weight,
            incoming_output_gate,
            incoming_output_weight,
            pair_transition_up,
            pair_transition_down,
        )

    def attend_one(operands):
        query_col, key_col, value_col = operands
        scores = jnp.einsum("shd,thd->hst", query_col, key_col, preferred_element_type=jnp.float32)
        scores = jnp.where(live_rows[None, None, :], scores, -1000000000.0)
        row_top = jnp.max(scores, axis=-1, keepdims=True)
        raised = jnp.exp(scores - row_top)
        attention = (raised / jnp.sum(raised, axis=-1, keepdims=True)).astype(jnp.bfloat16)
        return jnp.einsum("hst,thd->shd", attention, value_col, preferred_element_type=jnp.float32)

    blocked_view = alignment_input.reshape(
        alignment_input.shape[0], shard_pieces, residue_count // shard_pieces, channel_count
    )
    block_in = lax.all_to_all(blocked_view, "dap", split_axis=1, concat_axis=0, tiled=True)
    depth_rows = block_in.shape[0]
    count_cols = block_in.shape[2]
    current = block_in.reshape(depth_rows, count_cols, channel_count).astype(jnp.float32)
    normed = layer_normalize(current).astype(jnp.bfloat16)
    query_rows = (
        jnp.einsum("sic,ce->sie", normed, column_query_weight, preferred_element_type=jnp.float32)
        * HEAD_SIZE ** (-0.5)
    ).astype(jnp.bfloat16)
    key_row_block = jnp.einsum(
        "sic,ce->sie", normed, column_key_weight, preferred_element_type=jnp.float32
    ).astype(jnp.bfloat16)
    value_gate_pair = jnp.einsum(
        "sic,ce->sie", normed, column_value_gate_weight, preferred_element_type=jnp.float32
    )
    value_rows = value_gate_pair[..., :head_width].astype(jnp.bfloat16)

    def by_column(values):
        return values.transpose(1, 0, 2).reshape(count_cols, depth_rows, HM, HEAD_SIZE)

    attended = lax.map(
        attend_one, (by_column(query_rows), by_column(key_row_block), by_column(value_rows))
    )
    attended = attended.reshape(count_cols, depth_rows, head_width).transpose(1, 0, 2)
    gated_out = (jax.nn.sigmoid(value_gate_pair[..., head_width:]) * attended).astype(jnp.bfloat16)
    current = current + jnp.einsum(
        "sie,ec->sic", gated_out, column_output_weight, preferred_element_type=jnp.float32
    )
    hidden = jax.nn.relu(
        jnp.einsum(
            "sic,cf->sif",
            layer_normalize(current).astype(jnp.bfloat16),
            alignment_transition_up,
            preferred_element_type=jnp.float32,
        )
    ).astype(jnp.bfloat16)
    current = current + jnp.einsum(
        "sif,fc->sic", hidden, alignment_transition_down, preferred_element_type=jnp.float32
    )
    result = current.astype(jnp.bfloat16)
    outer_product_input = jnp.einsum(
        "sic,cf->sif",
        layer_normalize(result.astype(jnp.float32)).astype(jnp.bfloat16),
        outer_input_weight,
        preferred_element_type=jnp.float32,
    )
    outer_product_input = outer_product_input * live_row_float[:, None, None]
    left_part = outer_product_input[..., :CO].astype(jnp.bfloat16)
    right_part = outer_product_input[..., CO:].astype(jnp.bfloat16)
    all_rows = result.shape[0]
    left_cols = left_part.transpose(1, 0, 2)
    right_cols = right_part.transpose(1, 0, 2).reshape(own_rows, all_rows * CO)
    live_count = jnp.sum(live_row_float)
    right_piece = gather_doubling(right_cols).reshape(-1, all_rows * CO)
    span_rows = right_piece.shape[0]
    products = jnp.einsum(
        "isc,jsd->ijcd",
        left_cols,
        right_piece.reshape(span_rows, all_rows, CO),
        preferred_element_type=jnp.float32,
    )
    products = products.astype(jnp.bfloat16).reshape(own_rows, span_rows, CO * CO)
    outer_mean = (
        jnp.einsum("ijf,fc->ijc", products, outer_output_weight, preferred_element_type=jnp.float32)
        / live_count
    )
    pair_mid = pair_start + outer_mean
    out_left, out_right, out_gating = triangle_inputs(
        pair_mid, outgoing_projection_weight, outgoing_output_gate
    )
    out_product = by_channels(out_left, out_right, "cik,cjk->cij")
    pair_after_out = triangle_finish(pair_mid, out_product, out_gating, outgoing_output_weight)
    in_left, in_right, in_gating = triangle_inputs(
        pair_after_out, incoming_projection_weight, incoming_output_gate
    )
    in_product = by_channels(in_left, in_right, "cki,ckj->cij")
    pair_after_in = triangle_finish(pair_after_out, in_product, in_gating, incoming_output_weight)
    pair_expanded = jax.nn.relu(
        jnp.einsum(
            "ijc,cf->ijf",
            layer_normalize(pair_after_in).astype(jnp.bfloat16),
            pair_transition_up,
            preferred_element_type=jnp.float32,
        )
    ).astype(jnp.bfloat16)
    pair_state_output = (
        pair_after_in
        + jnp.einsum(
            "ijf,fc->ijc", pair_expanded, pair_transition_down, preferred_element_type=jnp.float32
        )
    ).astype(jnp.bfloat16)
    return (result, pair_state_output)


def solution(mesh):
    in_specs = (
        P(("grp", "dap"), None, None),
        P(("grp", "dap"), None, None),
        P("grp"),
        P("grp"),
        P("grp"),
        P(),
        P(),
        P(),
        P(),
        P(),
        P(),
        P(),
        P(),
        P(),
        P(),
        P(),
        P(),
        P(),
        P(),
        P(),
        P(),
        P(),
    )
    out_specs = (P("grp", "dap", None), P(("grp", "dap"), None, None))
    return jax.shard_map(local, mesh=mesh, in_specs=in_specs, out_specs=out_specs, check_vma=False)
```

```python
import jax
import jax.numpy as jnp
from jax import lax
from jax.experimental import pallas as pl
from jax.experimental.pallas import tpu as pltpu
from jax.sharding import PartitionSpec as P

HM = 8
HEAD_SIZE = 32
CO = 32
MAXREL = 32
NBINS = 66


EPSILON = 1e-05


def layer_normalize(values):
    center = jnp.mean(values, axis=-1, keepdims=True)
    shifted = values - center
    spread = jnp.mean(shifted * shifted, axis=-1, keepdims=True)
    return shifted * lax.rsqrt(spread + EPSILON)


def triangle_inputs(pair_now, weight, gate_weight):
    normed = layer_normalize(pair_now).astype(jnp.bfloat16)
    combined = jnp.einsum("ijc,cf->fij", normed, weight, preferred_element_type=jnp.float32)
    hidden_width = weight.shape[1] // 4
    left_side = (
        jax.nn.sigmoid(combined[hidden_width : 2 * hidden_width]) * combined[:hidden_width]
    ).astype(jnp.bfloat16)
    right_side = (
        jax.nn.sigmoid(combined[3 * hidden_width :]) * combined[2 * hidden_width : 3 * hidden_width]
    ).astype(jnp.bfloat16)
    gating = jax.nn.sigmoid(
        jnp.einsum("ijc,cd->ijd", normed, gate_weight, preferred_element_type=jnp.float32)
    )
    return (left_side, right_side, gating)


def triangle_finish(pair_now, product, gating, final_weight):
    product = lax.optimization_barrier(product)
    normed = layer_normalize(product.transpose(1, 2, 0).astype(jnp.float32)).astype(jnp.bfloat16)
    return pair_now + gating * jnp.einsum(
        "ijc,cd->ijd", normed, final_weight, preferred_element_type=jnp.float32
    )


def by_channels(left_side, right_side, form):
    both = jnp.stack([left_side, right_side])
    both = lax.all_to_all(both, "dap", split_axis=1, concat_axis=2, tiled=True)
    partial_out = jnp.einsum(form, both[0], both[1], preferred_element_type=jnp.float32)
    return lax.all_to_all(
        partial_out.astype(jnp.bfloat16), "dap", split_axis=1, concat_axis=0, tiled=True
    )


def gather_doubling(block):
    shard_pieces = lax.axis_size("dap")
    place = lax.axis_index("dap")
    held = block
    depth = 0
    bit = shard_pieces // 2
    while bit:
        other = lax.ppermute(held, "dap", [(q, q ^ bit) for q in range(shard_pieces)])
        upper = (place & bit) != 0
        first = jnp.where(upper, other, held)
        second = jnp.where(upper, held, other)
        held = jnp.stack([first, second], axis=depth)
        depth += 1
        bit //= 2
    return held.reshape((shard_pieces,) + block.shape)


LANES = 128


def gate_curve(values):
    return 0.5 + 0.5 * jnp.tanh(0.5 * values)


def normalize_channels(values):
    center = jnp.mean(values, axis=0, keepdims=True)
    shifted = values - center
    spread = jnp.mean(shifted * shifted, axis=0, keepdims=True)
    return (shifted * lax.rsqrt(spread + EPSILON)).astype(jnp.bfloat16)


def mix(weight, values):
    return jnp.dot(weight, values, preferred_element_type=jnp.float32)


def fold_halves(first_even, second_even, first_odd, second_odd, low_half):
    straight = jnp.where(low_half, first_even, second_odd)
    crossed = jnp.where(low_half, second_even, first_odd)
    return straight + pltpu.roll(crossed, LANES // 2, 1)


def turned(ref, name):
    first, last = TURNED[name]
    return ref[first:last, :]


OFFSETS = (0, 8, 4, 12)


def start_kernel(
    place_ref,
    live_ref,
    line_ref,
    across_ref,
    core_line_ref,
    core_across_ref,
    pair_line_ref,
    pair_across_ref,
    embedding_ref,
    turned_ref,
    wide_weight_ref,
    pair_mid_ref,
    left_ref,
    gating_ref,
    right_ref,
    wide_ref,
    right_cols_ref,
    *stack_refs,
):
    place = place_ref[0]
    inverse_live = 1.0 / jnp.sum(live_ref[...], axis=1, keepdims=True)
    half = LANES // 2
    low_half = lax.broadcasted_iota(jnp.int32, (LANES, LANES), 1) < half

    for m in range(4):
        for part, device in (
            (line_ref[m, 128:256, :], place ^ OFFSETS[m]),
            (across_ref[m, 128:256, :], place ^ OFFSETS[m] ^ 2),
            (core_line_ref[m, 128:256, :], place ^ OFFSETS[m] ^ 1),
            (core_across_ref[m, 128:256, :], place ^ OFFSETS[m] ^ 3),
        ):
            wide_ref[pl.ds(pl.multiple_of(device * 128, 128), 128), :] = part.astype(jnp.float32)
    for d in range(0, CO, 2):
        rows = [
            wide_ref[pl.ds(par * CO + d + e, 32, stride=2 * CO), :]
            for e in range(2)
            for par in range(2)
        ]
        right_cols_ref[:, d * half : d * half + LANES] = (
            jnp.concatenate(rows, axis=0).T.astype(jnp.bfloat16)
        )

    for g in range(4):
        parts_ref = (line_ref, across_ref)[g // 2]
        pair_ref = (pair_line_ref, pair_across_ref)[g // 2]
        stack_ref = stack_refs[g % 2]
        first = 2 * (g % 2)
        left_rows = parts_ref[first : first + 2, 0:128, :].reshape(256, LANES)
        outer = mix(left_rows, right_cols_ref[...]).astype(jnp.bfloat16)
        for i in range(8):
            for d in range(16):
                stack_ref[d * 32 : (d + 1) * 32, i * LANES : (i + 1) * LANES] = outer[
                    i * 32 : (i + 1) * 32, d * LANES : (d + 1) * LANES
                ]
        mixed = mix(wide_weight_ref[0:256, :], stack_ref[...])
        slabs = []
        places = []
        for q in range(4):
            m = first + q // 2
            device = place ^ OFFSETS[m] ^ (2 * (g // 2))
            here = 2 * (device // 2) + q % 2
            even = slice(2 * q * LANES, (2 * q + 1) * LANES)
            odd = slice((2 * q + 1) * LANES, (2 * q + 2) * LANES)
            outer_mean = fold_halves(
                mixed[0:128, even], mixed[0:128, odd], mixed[128:256, even], mixed[128:256, odd], low_half
            )
            start = pair_ref[m, q % 2].astype(jnp.float32)
            start = start + embedding_ref[2 * device + q % 2].astype(jnp.float32)
            slab = start + outer_mean * inverse_live
            pair_mid_ref[here] = slab
            slabs.append(normalize_channels(slab))
            places.append(here)
        normed = jnp.concatenate(slabs, axis=1)
        combined = mix(turned(turned_ref, "out_mix"), normed)
        left = gate_curve(combined[128:256]) * combined[0:128]
        right = gate_curve(combined[384:512]) * combined[256:384]
        gating = gate_curve(mix(turned(turned_ref, "out_gate"), normed))
        for q in range(4):
            lanes = slice(q * LANES, (q + 1) * LANES)
            rows = pl.ds(pl.multiple_of(places[q] * 128, 128), 128)
            left_ref[rows, :] = left[:, lanes]
            right_ref[rows, :] = right[:, lanes].astype(jnp.bfloat16)
            gating_ref[places[q]] = gating[:, lanes]


def triangle_kernel(
    place_ref,
    pair_mid_ref,
    left_ref,
    gating_ref,
    right_own_ref,
    right_other_ref,
    turned_ref,
    own_pair_ref,
    own_part_ref,
    other_part_ref,
    right_ref,
    product_ref,
    pair_now_ref,
    chosen_ref,
    own_left_ref,
    own_product_ref,
):
    place = place_ref[0]
    core = place % 2
    half = LANES // 2
    low_half = lax.broadcasted_iota(jnp.int32, (LANES, LANES), 1) < half
    low_short = lax.broadcasted_iota(jnp.int32, (32, LANES), 1) < half
    for chip in range(8):
        for source, side in ((right_own_ref, core), (right_other_ref, 1 - core)):
            rows = pl.ds(pl.multiple_of((4 * chip + 2 * side) * 128, 256), 256)
            right_ref[rows, :] = source[chip * 256 : (chip + 1) * 256, :].astype(jnp.float32)

    nothing = jnp.zeros((32, LANES), jnp.bfloat16)

    def outgoing_channels(block, carry):
        for e in range(32):
            c = block * 32 + e
            left = left_ref[pl.ds(c, 16, stride=128), :].astype(jnp.bfloat16)
            right = right_ref[pl.ds(c, 32, stride=128), :]
            moved = pltpu.roll(right, half, 1).astype(jnp.bfloat16)
            right = right.astype(jnp.bfloat16)
            spread = jnp.concatenate(
                [
                    jnp.where(low_short, right, nothing),
                    jnp.where(low_short, moved, nothing),
                    jnp.where(low_short, nothing, moved),
                    jnp.where(low_short, nothing, right),
                ],
                axis=0,
            )
            product_ref[pl.ds(c, 16, stride=128), :] = contract_last(left, spread)
        return carry

    lax.fori_loop(0, 4, outgoing_channels, 0)

    column = lax.broadcasted_iota(jnp.int32, (1, 256), 1)
    which = column // 16
    residue = which % 4
    device = place ^ ((which // 4) % 2)
    wanted = half * (which // 8) + 32 * (residue % 2) + 2 * device + residue // 2
    slab_of = column % 16
    source_lane = lax.broadcasted_iota(jnp.int32, (LANES, 256), 0)
    for g in range(4):
        products = [
            normalize_channels(product_ref[(4 * g + q) * 128 : (4 * g + q + 1) * 128, :])
            for q in range(4)
        ]
        finished = mix(turned(turned_ref, "out_final"), jnp.concatenate(products, axis=1))
        slabs = []
        picks = []
        for q in range(4):
            h = 4 * g + q
            lanes = slice(q * LANES, (q + 1) * LANES)
            slab = pair_mid_ref[h] + gating_ref[h] * finished[:, lanes]
            pair_now_ref[h] = slab
            slabs.append(normalize_channels(slab))
            here = jnp.where(slab_of == h, wanted, -1)
            picks.append((source_lane == here).astype(jnp.float32).astype(jnp.bfloat16))
        normed = jnp.concatenate(slabs, axis=1)
        chosen = mix(normed, jnp.concatenate(picks, axis=0))
        if g:
            chosen_ref[...] += chosen
        else:
            chosen_ref[...] = chosen
        combined = mix(turned(turned_ref, "in_mix")[256:512, :], normed)
        right = gate_curve(combined[128:256]) * combined[0:128]
        for q in range(4):
            right_ref[(4 * g + q) * 128 : (4 * g + q + 1) * 128, :] = right[
                :, q * LANES : (q + 1) * LANES
            ]
    for t in range(2):
        own_pair_ref[t] = pair_now_ref[2 * (place // 2) + t]

    combined = mix(turned(turned_ref, "in_mix")[0:256, :], chosen_ref[...].astype(jnp.bfloat16))
    own_left = gate_curve(combined[128:256]) * combined[0:128]
    for m in range(16):
        part = own_left[:, (m // 8) * LANES : (m // 8 + 1) * LANES]
        if m % 8:
            part = pltpu.roll(part, LANES - 16 * (m % 8), 1)
        own_left_ref[m * 128 : (m + 1) * 128, :] = part

    def incoming_channels(block, carry):
        for e in range(32):
            c = block * 32 + e
            left = own_left_ref[pl.ds(c, 16, stride=128), :][:, 0:16].astype(jnp.bfloat16)
            right = right_ref[pl.ds(c, 16, stride=128), :].astype(jnp.bfloat16)
            own_product_ref[pl.ds(c, 16, stride=128), :] = mix(left, right)
        return carry

    lax.fori_loop(0, 4, incoming_channels, 0)

    def block_of(b, e, residue):
        m = 8 * b + 4 * e + residue
        return own_product_ref[m * 128 : (m + 1) * 128, :]

    for e, target in ((0, own_part_ref), (1, other_part_ref)):
        for t in range(2):
            target[t] = fold_halves(
                block_of(0, e, 2 * t),
                block_of(0, e, 2 * t + 1),
                block_of(1, e, 2 * t),
                block_of(1, e, 2 * t + 1),
                low_half,
            )


def finish_kernel(own_pair_ref, own_part_ref, other_part_ref, turned_ref, wide_weight_ref, result_ref):
    products = [normalize_channels(own_part_ref[t] + other_part_ref[t]) for t in range(2)]
    finished = mix(turned(turned_ref, "in_final"), jnp.concatenate(products, axis=1))
    own_pair = jnp.concatenate([own_pair_ref[t] for t in range(2)], axis=1)
    gating = gate_curve(mix(turned(turned_ref, "in_gate"), normalize_channels(own_pair)))
    own_pair = own_pair + gating * finished
    hidden = jnp.maximum(mix(turned(turned_ref, "up"), normalize_channels(own_pair)), 0.0)
    own_pair = own_pair + mix(wide_weight_ref[256:384, :], hidden.astype(jnp.bfloat16))
    own_pair = own_pair.astype(jnp.bfloat16)
    order = lane_order_matrix()
    for t in range(2):
        result_ref[t * 128 : (t + 1) * 128, :] = contract_last(
            order, own_pair[:, t * LANES : (t + 1) * LANES]
        ).astype(jnp.bfloat16)


def lane_order_matrix():
    half = LANES // 2
    member = lax.broadcasted_iota(jnp.int32, (LANES, LANES), 0)
    lane = lax.broadcasted_iota(jnp.int32, (LANES, LANES), 1)
    back = half * (member // half) + 32 * (member % 2) + (member % half) // 2
    return (lane == back).astype(jnp.float32).astype(jnp.bfloat16)


def contract_first(first, second):
    return lax.dot_general(
        first, second, (((0,), (0,)), ((), ())), preferred_element_type=jnp.float32
    )


def rows_kernel(
    rows_source, pair_source, blocks_ref, own_pair_ref, rows_ref, pair_ref, wide_ref, arrived
):
    rows_copy = pltpu.make_async_copy(rows_source, rows_ref, arrived.at[0])
    pair_copy = pltpu.make_async_copy(pair_source, pair_ref, arrived.at[1])
    pair_copy.start()
    rows_copy.start()
    pair_copy.wait()
    order = lane_order_matrix()
    for t in range(2):
        own_pair_ref[t] = contract_first(
            pair_ref[2 * t : 2 * t + 2].reshape(LANES, LANES), order
        ).astype(jnp.bfloat16)
    rows_copy.wait()
    residues = rows_ref.shape[1]
    count = 8 * residues
    rows = rows_ref[...].astype(jnp.float32).reshape(count, 2 * LANES)
    for e in range(2):
        wide_ref[e * count : (e + 1) * count, :] = rows[:, e * LANES : (e + 1) * LANES]
    for p in range(16):
        for e in range(2):
            block = [
                wide_ref[pl.ds(e * count + 4 * p + i, 8, stride=residues), :] for i in range(4)
            ]
            blocks_ref[p, :, e * LANES : (e + 1) * LANES] = jnp.concatenate(block, axis=0).astype(
                jnp.bfloat16
            )


TURNED = {
    "out_mix": (0, 512),
    "out_gate": (512, 640),
    "out_final": (640, 768),
    "in_mix": (768, 1280),
    "in_gate": (1280, 1408),
    "in_final": (1408, 1536),
    "up": (1536, 2048),
}


def weights_kernel(
    bins_ref,
    table_ref,
    own_pair_ref,
    far_pair_ref,
    *rest,
):
    sources, (embedding_out, turned_out, wide_out, both_out) = rest[:9], rest[9:13]
    landed, (table_wide_ref, mean_wide_ref, arrived) = rest[13:22], rest[22:]
    both_out[0] = own_pair_ref[...]
    both_out[1] = far_pair_ref[...]
    copies = [
        pltpu.make_async_copy(sources[k], landed[k], arrived.at[k]) for k in range(len(sources))
    ]
    for copy in copies:
        copy.start()
    table_wide_ref[...] = jnp.zeros_like(table_wide_ref)
    table_wide_ref[0:NBINS, :] = table_ref[...].astype(jnp.float32)
    table = table_wide_ref[...].T.astype(jnp.bfloat16)
    channel = lax.broadcasted_iota(jnp.int32, (LANES, LANES), 0)

    def embed(g, carry):
        for q in range(4):
            h = 4 * g + q
            one_hot = (channel == bins_ref[pl.ds(h, 1), :]).astype(jnp.float32).astype(jnp.bfloat16)
            embedding_out[h] = mix(table, one_hot).astype(jnp.bfloat16)
        return carry

    lax.fori_loop(0, 8, embed, 0)
    for copy in copies:
        copy.wait()
    mean_wide_ref[...] = landed[0][...].astype(jnp.float32)
    for e in range(2):
        for block in range(4):
            rows = [
                mean_wide_ref[pl.ds(2 * (4 * block + k) + e, CO, stride=CO), :] for k in range(4)
            ]
            wide_out[e * LANES : (e + 1) * LANES, block * LANES : (block + 1) * LANES] = (
                jnp.concatenate(rows, axis=0).T.astype(jnp.bfloat16)
            )
    first = 0
    for source in landed[1:8]:
        for b in range(source.shape[1] // LANES):
            part = source[:, b * LANES : (b + 1) * LANES].astype(jnp.float32)
            turned_out[first : first + LANES, :] = part.T.astype(jnp.bfloat16)
            first += LANES
    for a in range(4):
        part = landed[8][a * LANES : (a + 1) * LANES, :].astype(jnp.float32)
        wide_out[256:384, a * LANES : (a + 1) * LANES] = part.T.astype(jnp.bfloat16)


def normalize_rows(values):
    center = jnp.mean(values, axis=1, keepdims=True)
    shifted = values - center
    spread = jnp.mean(shifted * shifted, axis=1, keepdims=True)
    return (shifted * lax.rsqrt(spread + EPSILON)).astype(jnp.bfloat16)


def contract_last(first, second):
    return lax.dot_general(
        first, second, (((1,), (1,)), ((), ())), preferred_element_type=jnp.float32
    )


def msa_kernel(
    live_ref,
    blocks_ref,
    query_ref,
    key_ref,
    value_gate_ref,
    output_ref,
    up_ref,
    down_ref,
    outer_ref,
    result_ref,
    parts_ref,
    wide_ref,
    attended_ref,
    final_ref,
    *landed,
):
    arrived = landed[-1]
    sources = (query_ref, key_ref, value_gate_ref, output_ref, up_ref, down_ref)
    copies = [
        pltpu.make_async_copy(source, landed[k], arrived.at[k]) for k, source in enumerate(sources)
    ]
    for copy in copies:
        copy.start()
    query_ref, key_ref, value_gate_ref, output_ref, up_ref, down_ref = landed[:6]
    for p in range(16):
        block = blocks_ref[p].astype(jnp.float32)
        for i in range(4):
            wide_ref[i * 128 + p * 8 : i * 128 + p * 8 + 8, :] = block[i * 8 : i * 8 + 8, :]
    live = live_ref[...]
    alive = live > 0.0
    width = HM * HEAD_SIZE
    head_of = lax.broadcasted_iota(jnp.int32, (128, width), 1) // HEAD_SIZE
    zero = jnp.zeros((128, width), jnp.bfloat16)
    one = jnp.ones((128, width), jnp.bfloat16)

    def by_head(values):
        return jnp.concatenate([jnp.where(head_of == h, values, zero) for h in range(HM)], axis=0)

    heads = by_head(one)
    normed = normalize_rows(wide_ref[...])
    for copy in copies[:3]:
        copy.wait()
    query = (mix(normed, query_ref[...]) * HEAD_SIZE ** (-0.5)).astype(jnp.bfloat16)
    key = mix(normed, key_ref[...]).astype(jnp.bfloat16)
    value_gate = mix(normed, value_gate_ref[...])
    value = value_gate[:, :width].astype(jnp.bfloat16)
    for i in range(4):
        rows = slice(i * 128, (i + 1) * 128)
        scores = contract_last(query[rows], by_head(key[rows]))
        raised = []
        for h in range(HM):
            score = jnp.where(alive, scores[:, h * 128 : (h + 1) * 128], -1000000000.0)
            raised.append(jnp.exp(score - jnp.max(score, axis=1, keepdims=True)).astype(jnp.bfloat16))
        raised = jnp.concatenate(raised, axis=1)
        attended_ref[rows, :] = mix(raised, by_head(value[rows])) / mix(raised, heads)
    gated = (gate_curve(value_gate[:, width:]) * attended_ref[...]).astype(jnp.bfloat16)
    for copy in copies[3:]:
        copy.wait()
    current = wide_ref[...] + mix(gated, output_ref[...])
    hidden = jnp.maximum(mix(normalize_rows(current), up_ref[...]), 0.0).astype(jnp.bfloat16)
    final = (current + mix(hidden, down_ref[...])).astype(jnp.bfloat16).astype(jnp.float32)
    outer = contract_last(outer_ref[...], normalize_rows(final))
    for i in range(4):
        rows = slice(i * 128, (i + 1) * 128)
        part = (outer[:, rows] * live).astype(jnp.bfloat16)
        parts_ref[i * CO : (i + 1) * CO, :] = part[:CO, :]
        parts_ref[128 + i * CO : 128 + (i + 1) * CO, :] = part[CO:, :]
        final_ref[pl.ds(i, 128, stride=4), :] = final[rows, :128]
        final_ref[pl.ds(512 + i, 128, stride=4), :] = final[rows, 128:]
    result_ref[:, :128] = final_ref[:512, :].astype(jnp.bfloat16)
    result_ref[:, 128:] = final_ref[512:, :].astype(jnp.bfloat16)


def exchange(values, offset):
    pieces = lax.axis_size("dap")
    return lax.ppermute(values, "dap", [(q, q ^ offset) for q in range(pieces)])


def whole_block(
    alignment_input,
    pair_state_input,
    bin_all,
    live_row_float,
    relative_position_table,
    column_query_weight,
    column_key_weight,
    column_value_gate_weight,
    column_output_weight,
    alignment_transition_up,
    alignment_transition_down,
    outer_input_weight,
    *pair_weights,
):
    channels = alignment_input.shape[2]
    width = pair_state_input.shape[2]
    place = lax.axis_index("dap").astype(jnp.int32).reshape(1)
    vmem = pl.BlockSpec(memory_space=pltpu.VMEM)
    smem = pl.BlockSpec(memory_space=pltpu.SMEM)
    hbm = pl.BlockSpec(memory_space=pltpu.HBM)

    def array(*shape, dtype=jnp.bfloat16):
        return jax.ShapeDtypeStruct(shape, dtype)

    def wide(*shape):
        return jax.ShapeDtypeStruct(shape, jnp.float32)

    def limit(mebibytes):
        return pltpu.CompilerParams(vmem_limit_bytes=mebibytes * 1024 * 1024)

    blocks, own_pair = pl.pallas_call(
        rows_kernel,
        out_shape=[array(16, 32, channels), array(2, width, LANES)],
        in_specs=[hbm, hbm],
        out_specs=[vmem, vmem],
        scratch_shapes=[
            pltpu.VMEM(alignment_input.shape, jnp.bfloat16),
            pltpu.VMEM(pair_state_input.shape, jnp.bfloat16),
            pltpu.VMEM((1024, LANES), jnp.float32),
            pltpu.SemaphoreType.DMA((2,)),
        ],
        compiler_params=limit(56),
        name="rows_by_device",
    )(alignment_input, pair_state_input)
    blocks = lax.all_to_all(blocks, "dap", split_axis=0, concat_axis=0, tiled=True)

    pair_far = exchange(own_pair, 8)
    embedding, turned_weights, wide_weights, pair_both = pl.pallas_call(
        weights_kernel,
        out_shape=[array(32, width, LANES), array(2048, LANES), array(384, 512), array(2, 2, width, LANES)],
        in_specs=[vmem] * 4 + [hbm] * 9,
        out_specs=[vmem] * 4,
        scratch_shapes=[pltpu.VMEM(w.shape, jnp.bfloat16) for w in pair_weights]
        + [
            pltpu.VMEM((LANES, LANES), jnp.float32),
            pltpu.VMEM((1024, LANES), jnp.float32),
            pltpu.SemaphoreType.DMA((9,)),
        ],
        compiler_params=limit(56),
        cost_estimate=pl.CostEstimate(
            flops=200_000_000, bytes_accessed=8_000_000, transcendentals=0
        ),
        name="turn_weights",
    )(
        lanes_order(bin_all).reshape(32, LANES),
        relative_position_table,
        own_pair,
        pair_far,
        *pair_weights,
    )
    pair_line = jnp.concatenate([pair_both, exchange(pair_both, 4)])
    blocks, pair_line = lax.optimization_barrier((blocks, pair_line))
    pair_across = exchange(pair_line, 2)

    result, parts = pl.pallas_call(
        msa_kernel,
        out_shape=(array(512, channels), array(256, LANES)),
        in_specs=[vmem] * 2 + [hbm] * 6 + [vmem],
        out_specs=(vmem, vmem),
        scratch_shapes=[
            pltpu.VMEM((512, channels), jnp.float32),
            pltpu.VMEM((512, channels), jnp.float32),
            pltpu.VMEM((1024, LANES), jnp.float32),
        ]
        + [
            pltpu.VMEM(w.shape, jnp.bfloat16)
            for w in (
                column_query_weight,
                column_key_weight,
                column_value_gate_weight,
                column_output_weight,
                alignment_transition_up,
                alignment_transition_down,
            )
        ]
        + [pltpu.SemaphoreType.DMA((6,))],
        compiler_params=limit(56),
        cost_estimate=pl.CostEstimate(
            flops=2_000_000_000, bytes_accessed=10_000_000, transcendentals=1_000_000
        ),
        name="msa_whole",
    )(
        live_row_float.reshape(1, LANES),
        blocks,
        column_query_weight,
        column_key_weight,
        column_value_gate_weight,
        column_output_weight,
        alignment_transition_up,
        alignment_transition_down,
        outer_input_weight.T,
    )
    far = exchange(parts, 8)
    near = [exchange(parts, 4), exchange(far, 4)]
    line = jnp.stack([parts, far] + near)
    across = exchange(line, 2)
    core_line = exchange(line, 1)
    core_across = exchange(across, 1)

    slabs = (16, 128, LANES)
    tall = (16 * 128, LANES)
    pair_mid, left, gating, right = pl.pallas_call(
        start_kernel,
        out_shape=[wide(*slabs), wide(*tall), wide(*slabs), array(*tall)],
        in_specs=[smem] + [vmem] * 10,
        out_specs=[vmem] * 4,
        scratch_shapes=[
            pltpu.VMEM((2048, LANES), jnp.float32),
            pltpu.VMEM((128, 2048), jnp.bfloat16),
            pltpu.VMEM((512, 1024), jnp.bfloat16),
            pltpu.VMEM((512, 1024), jnp.bfloat16),
        ],
        compiler_params=limit(32),
        name="pair_start",
    )(
        place,
        live_row_float.reshape(1, LANES),
        line,
        across,
        core_line,
        core_across,
        pair_line,
        pair_across,
        embedding,
        turned_weights,
        wide_weights,
    )
    own_pair, own_part, other_part = pl.pallas_call(
        triangle_kernel,
        out_shape=[wide(2, 128, LANES)] * 3,
        in_specs=[smem] + [vmem] * 6,
        out_specs=[vmem] * 3,
        scratch_shapes=[
            pltpu.VMEM((32 * 128, LANES), jnp.float32),
            pltpu.VMEM(tall, jnp.float32),
            pltpu.VMEM(slabs, jnp.float32),
            pltpu.VMEM((128, 256), jnp.float32),
            pltpu.VMEM(tall, jnp.float32),
            pltpu.VMEM(tall, jnp.float32),
        ],
        compiler_params=limit(32),
        name="pair_triangles",
    )(place, pair_mid, left, gating, right, exchange(right, 1), turned_weights)
    pair_output = pl.pallas_call(
        finish_kernel,
        out_shape=array(256, LANES),
        in_specs=[vmem] * 5,
        out_specs=vmem,
        compiler_params=limit(16),
        name="pair_finish",
    )(own_pair, own_part, exchange(other_part, 1), turned_weights, wide_weights)
    return result.reshape(128, 4, channels), pair_output.reshape(pair_state_input.shape)


def lanes_order(values):
    lead = values.shape[:-1]
    halves = values.reshape(lead + (values.shape[-1] // 2, 2))
    return jnp.swapaxes(halves, -1, -2).reshape(values.shape)


def local(
    alignment_input,
    pair_state_input,
    residue_number_index,
    chain_label,
    alignment_row_mask,
    relative_position_table,
    column_query_weight,
    column_key_weight,
    column_value_gate_weight,
    column_output_weight,
    alignment_transition_up,
    alignment_transition_down,
    outer_input_weight,
    outer_output_weight,
    outgoing_projection_weight,
    outgoing_output_gate,
    outgoing_output_weight,
    incoming_projection_weight,
    incoming_output_gate,
    incoming_output_weight,
    pair_transition_up,
    pair_transition_down,
):
    shard_pieces = lax.axis_size("dap")
    own_rows = pair_state_input.shape[0]
    residue_count = pair_state_input.shape[1]
    channel_count = alignment_input.shape[2]
    head_width = HM * HEAD_SIZE
    first_row = lax.axis_index("dap") * own_rows
    own_index = lax.dynamic_slice_in_dim(residue_number_index, first_row, own_rows)
    own_chain = lax.dynamic_slice_in_dim(chain_label, first_row, own_rows)

    def bins_of(index, chain):
        offset = index[:, None] - residue_number_index[None, :]
        return jnp.where(
            chain[:, None] == chain_label[None, :],
            jnp.clip(offset + MAXREL, 0, 2 * MAXREL),
            2 * MAXREL + 1,
        )

    bin_index = bins_of(own_index, own_chain)
    one_hot = (bin_index[:, :, None] == jnp.arange(NBINS, dtype=jnp.int32)[None, None, :]).astype(
        jnp.bfloat16
    )
    pair_start = pair_state_input.astype(jnp.float32) + jnp.einsum(
        "ijb,bc->ijc", one_hot, relative_position_table, preferred_element_type=jnp.float32
    )
    live_rows = alignment_row_mask > 0
    live_row_float = live_rows.astype(jnp.float32)

    if alignment_row_mask.shape[0] == LANES and 2 * residue_count == LANES and own_rows == 4:
        return whole_block(
            alignment_input,
            pair_state_input,
            bins_of(residue_number_index, chain_label),
            live_row_float,
            relative_position_table,
            column_query_weight,
            column_key_weight,
            column_value_gate_weight,
            column_output_weight,
            alignment_transition_up,
            alignment_transition_down,
            outer_input_weight,
            outer_output_weight,
            outgoing_projection_weight,
            outgoing_output_gate,
            outgoing_output_weight,
            incoming_projection_weight,
            incoming_output_gate,
            incoming_output_weight,
            pair_transition_up,
            pair_transition_down,
        )

    def attend_one(operands):
        query_col, key_col, value_col = operands
        scores = jnp.einsum("shd,thd->hst", query_col, key_col, preferred_element_type=jnp.float32)
        scores = jnp.where(live_rows[None, None, :], scores, -1000000000.0)
        row_top = jnp.max(scores, axis=-1, keepdims=True)
        raised = jnp.exp(scores - row_top)
        attention = (raised / jnp.sum(raised, axis=-1, keepdims=True)).astype(jnp.bfloat16)
        return jnp.einsum("hst,thd->shd", attention, value_col, preferred_element_type=jnp.float32)

    blocked_view = alignment_input.reshape(
        alignment_input.shape[0], shard_pieces, residue_count // shard_pieces, channel_count
    )
    block_in = lax.all_to_all(blocked_view, "dap", split_axis=1, concat_axis=0, tiled=True)
    depth_rows = block_in.shape[0]
    count_cols = block_in.shape[2]
    current = block_in.reshape(depth_rows, count_cols, channel_count).astype(jnp.float32)
    normed = layer_normalize(current).astype(jnp.bfloat16)
    query_rows = (
        jnp.einsum("sic,ce->sie", normed, column_query_weight, preferred_element_type=jnp.float32)
        * HEAD_SIZE ** (-0.5)
    ).astype(jnp.bfloat16)
    key_row_block = jnp.einsum(
        "sic,ce->sie", normed, column_key_weight, preferred_element_type=jnp.float32
    ).astype(jnp.bfloat16)
    value_gate_pair = jnp.einsum(
        "sic,ce->sie", normed, column_value_gate_weight, preferred_element_type=jnp.float32
    )
    value_rows = value_gate_pair[..., :head_width].astype(jnp.bfloat16)

    def by_column(values):
        return values.transpose(1, 0, 2).reshape(count_cols, depth_rows, HM, HEAD_SIZE)

    attended = lax.map(
        attend_one, (by_column(query_rows), by_column(key_row_block), by_column(value_rows))
    )
    attended = attended.reshape(count_cols, depth_rows, head_width).transpose(1, 0, 2)
    gated_out = (jax.nn.sigmoid(value_gate_pair[..., head_width:]) * attended).astype(jnp.bfloat16)
    current = current + jnp.einsum(
        "sie,ec->sic", gated_out, column_output_weight, preferred_element_type=jnp.float32
    )
    hidden = jax.nn.relu(
        jnp.einsum(
            "sic,cf->sif",
            layer_normalize(current).astype(jnp.bfloat16),
            alignment_transition_up,
            preferred_element_type=jnp.float32,
        )
    ).astype(jnp.bfloat16)
    current = current + jnp.einsum(
        "sif,fc->sic", hidden, alignment_transition_down, preferred_element_type=jnp.float32
    )
    result = current.astype(jnp.bfloat16)
    outer_product_input = jnp.einsum(
        "sic,cf->sif",
        layer_normalize(result.astype(jnp.float32)).astype(jnp.bfloat16),
        outer_input_weight,
        preferred_element_type=jnp.float32,
    )
    outer_product_input = outer_product_input * live_row_float[:, None, None]
    left_part = outer_product_input[..., :CO].astype(jnp.bfloat16)
    right_part = outer_product_input[..., CO:].astype(jnp.bfloat16)
    all_rows = result.shape[0]
    left_cols = left_part.transpose(1, 0, 2)
    right_cols = right_part.transpose(1, 0, 2).reshape(own_rows, all_rows * CO)
    live_count = jnp.sum(live_row_float)
    right_piece = gather_doubling(right_cols).reshape(-1, all_rows * CO)
    span_rows = right_piece.shape[0]
    products = jnp.einsum(
        "isc,jsd->ijcd",
        left_cols,
        right_piece.reshape(span_rows, all_rows, CO),
        preferred_element_type=jnp.float32,
    )
    products = products.astype(jnp.bfloat16).reshape(own_rows, span_rows, CO * CO)
    outer_mean = (
        jnp.einsum("ijf,fc->ijc", products, outer_output_weight, preferred_element_type=jnp.float32)
        / live_count
    )
    pair_mid = pair_start + outer_mean
    out_left, out_right, out_gating = triangle_inputs(
        pair_mid, outgoing_projection_weight, outgoing_output_gate
    )
    out_product = by_channels(out_left, out_right, "cik,cjk->cij")
    pair_after_out = triangle_finish(pair_mid, out_product, out_gating, outgoing_output_weight)
    in_left, in_right, in_gating = triangle_inputs(
        pair_after_out, incoming_projection_weight, incoming_output_gate
    )
    in_product = by_channels(in_left, in_right, "cki,ckj->cij")
    pair_after_in = triangle_finish(pair_after_out, in_product, in_gating, incoming_output_weight)
    pair_expanded = jax.nn.relu(
        jnp.einsum(
            "ijc,cf->ijf",
            layer_normalize(pair_after_in).astype(jnp.bfloat16),
            pair_transition_up,
            preferred_element_type=jnp.float32,
        )
    ).astype(jnp.bfloat16)
    pair_state_output = (
        pair_after_in
        + jnp.einsum(
            "ijf,fc->ijc", pair_expanded, pair_transition_down, preferred_element_type=jnp.float32
        )
    ).astype(jnp.bfloat16)
    return (result, pair_state_output)


def solution(mesh):
    in_specs = (
        P(("grp", "dap"), None, None),
        P(("grp", "dap"), None, None),
        P("grp"),
        P("grp"),
        P("grp"),
        P(),
        P(),
        P(),
        P(),
        P(),
        P(),
        P(),
        P(),
        P(),
        P(),
        P(),
        P(),
        P(),
        P(),
        P(),
        P(),
        P(),
    )
    out_specs = (P("grp", "dap", None), P(("grp", "dap"), None, None))
    return jax.shard_map(local, mesh=mesh, in_specs=in_specs, out_specs=out_specs, check_vma=False)
```

```python
import jax
import jax.numpy as jnp
from jax import lax
from jax.experimental import pallas as pl
from jax.experimental.pallas import tpu as pltpu
from jax.sharding import PartitionSpec as P

HM = 8
HEAD_SIZE = 32
CO = 32
MAXREL = 32
NBINS = 66


EPSILON = 1e-05


def layer_normalize(values):
    center = jnp.mean(values, axis=-1, keepdims=True)
    shifted = values - center
    spread = jnp.mean(shifted * shifted, axis=-1, keepdims=True)
    return shifted * lax.rsqrt(spread + EPSILON)


def triangle_inputs(pair_now, weight, gate_weight):
    normed = layer_normalize(pair_now).astype(jnp.bfloat16)
    combined = jnp.einsum("ijc,cf->fij", normed, weight, preferred_element_type=jnp.float32)
    hidden_width = weight.shape[1] // 4
    left_side = (
        jax.nn.sigmoid(combined[hidden_width : 2 * hidden_width]) * combined[:hidden_width]
    ).astype(jnp.bfloat16)
    right_side = (
        jax.nn.sigmoid(combined[3 * hidden_width :]) * combined[2 * hidden_width : 3 * hidden_width]
    ).astype(jnp.bfloat16)
    gating = jax.nn.sigmoid(
        jnp.einsum("ijc,cd->ijd", normed, gate_weight, preferred_element_type=jnp.float32)
    )
    return (left_side, right_side, gating)


def triangle_finish(pair_now, product, gating, final_weight):
    product = lax.optimization_barrier(product)
    normed = layer_normalize(product.transpose(1, 2, 0).astype(jnp.float32)).astype(jnp.bfloat16)
    return pair_now + gating * jnp.einsum(
        "ijc,cd->ijd", normed, final_weight, preferred_element_type=jnp.float32
    )


def by_channels(left_side, right_side, form):
    both = jnp.stack([left_side, right_side])
    both = lax.all_to_all(both, "dap", split_axis=1, concat_axis=2, tiled=True)
    partial_out = jnp.einsum(form, both[0], both[1], preferred_element_type=jnp.float32)
    return lax.all_to_all(
        partial_out.astype(jnp.bfloat16), "dap", split_axis=1, concat_axis=0, tiled=True
    )


def gather_doubling(block):
    shard_pieces = lax.axis_size("dap")
    place = lax.axis_index("dap")
    held = block
    depth = 0
    bit = shard_pieces // 2
    while bit:
        other = lax.ppermute(held, "dap", [(q, q ^ bit) for q in range(shard_pieces)])
        upper = (place & bit) != 0
        first = jnp.where(upper, other, held)
        second = jnp.where(upper, held, other)
        held = jnp.stack([first, second], axis=depth)
        depth += 1
        bit //= 2
    return held.reshape((shard_pieces,) + block.shape)


LANES = 128


def gate_curve(values):
    return 0.5 + 0.5 * jnp.tanh(0.5 * values)


def normalize_channels(values):
    center = jnp.mean(values, axis=0, keepdims=True)
    shifted = values - center
    spread = jnp.mean(shifted * shifted, axis=0, keepdims=True)
    return (shifted * lax.rsqrt(spread + EPSILON)).astype(jnp.bfloat16)


def mix(weight, values):
    return jnp.dot(weight, values, preferred_element_type=jnp.float32)


def fold_halves(first_even, second_even, first_odd, second_odd, low_half):
    straight = jnp.where(low_half, first_even, second_odd)
    crossed = jnp.where(low_half, second_even, first_odd)
    return straight + pltpu.roll(crossed, LANES // 2, 1)


def transpose_blocks(ref):
    rows, columns = ref.shape
    return jnp.concatenate(
        [
            jnp.concatenate(
                [
                    ref[a : a + LANES, b : b + LANES].astype(jnp.float32).T.astype(jnp.bfloat16)
                    for a in range(0, rows, LANES)
                ],
                axis=1,
            )
            for b in range(0, columns, LANES)
        ],
        axis=0,
    )


def start_copies(sources, landed, arrived):
    copies = [
        pltpu.make_async_copy(source, landed[k], arrived.at[k]) for k, source in enumerate(sources)
    ]
    for copy in copies:
        copy.start()
    return copies


FIRSTS = (0, 4, 2, 6)


def start_kernel(place_ref, live_ref, bins_ref, table_ref, *rest):
    part_refs, core_refs, pair_refs, sources = rest[:4], rest[4:8], rest[8:12], rest[12:15]
    pair_mid_ref, left_ref, gating_ref, right_ref = rest[15:19]
    wide_ref, right_cols_ref, mean_wide_ref, mean_weight_ref, table_wide_ref = rest[19:24]
    stack_refs, landed, arrived = rest[24:26], rest[26:29], rest[29]
    copies = start_copies(sources, landed, arrived)
    place = place_ref[0]
    inverse_live = 1.0 / jnp.sum(live_ref[...], axis=1, keepdims=True)
    half = LANES // 2
    channel = lax.broadcasted_iota(jnp.int32, (LANES, LANES), 0)
    table_wide_ref[...] = jnp.zeros_like(table_wide_ref)
    table_wide_ref[0:NBINS, :] = table_ref[...].astype(jnp.float32)
    table = table_wide_ref[...].T.astype(jnp.bfloat16)
    low_half = lax.broadcasted_iota(jnp.int32, (LANES, LANES), 1) < half

    for g in range(4):
        for m in range(2):
            device = place ^ FIRSTS[g] ^ (8 * m)
            for part, owner in ((part_refs[g], device), (core_refs[g], device ^ 1)):
                wide_ref[pl.ds(pl.multiple_of(owner * 128, 128), 128), :] = part[
                    m, 128:256, :
                ].astype(jnp.float32)
    for d in range(0, CO, 2):
        rows = [
            wide_ref[pl.ds(par * CO + d + e, 32, stride=2 * CO), :]
            for e in range(2)
            for par in range(2)
        ]
        right_cols_ref[:, d * half : d * half + LANES] = (
            jnp.concatenate(rows, axis=0).T.astype(jnp.bfloat16)
        )

    for copy in copies:
        copy.wait()
    mean_wide_ref[...] = landed[0][...].astype(jnp.float32)
    for e in range(2):
        for block in range(4):
            rows = [
                mean_wide_ref[pl.ds(2 * (4 * block + k) + e, CO, stride=CO), :] for k in range(4)
            ]
            mean_weight_ref[e * LANES : (e + 1) * LANES, block * LANES : (block + 1) * LANES] = (
                jnp.concatenate(rows, axis=0).T.astype(jnp.bfloat16)
            )
    out_mix = transpose_blocks(landed[1])
    out_gate = transpose_blocks(landed[2])

    for g in range(4):
        stack_ref = stack_refs[g % 2]
        left_rows = part_refs[g][:, 0:128, :].reshape(256, LANES)
        outer = mix(left_rows, right_cols_ref[...]).astype(jnp.bfloat16)
        for i in range(8):
            for d in range(16):
                stack_ref[d * 32 : (d + 1) * 32, i * LANES : (i + 1) * LANES] = outer[
                    i * 32 : (i + 1) * 32, d * LANES : (d + 1) * LANES
                ]
        mixed = mix(mean_weight_ref[...], stack_ref[...])
        slabs = []
        places = []
        devices = [place ^ FIRSTS[g] ^ (8 * m) for m in range(2)]
        one_hot = [
            (channel == bins_ref[pl.ds(2 * devices[q // 2] + q % 2, 1), :]).astype(jnp.float32)
            for q in range(4)
        ]
        embedding = mix(table, jnp.concatenate(one_hot, axis=1).astype(jnp.bfloat16))
        for q in range(4):
            device = devices[q // 2]
            here = 2 * (device // 2) + q % 2
            even = slice(2 * q * LANES, (2 * q + 1) * LANES)
            odd = slice((2 * q + 1) * LANES, (2 * q + 2) * LANES)
            outer_mean = fold_halves(
                mixed[0:128, even], mixed[0:128, odd], mixed[128:256, even], mixed[128:256, odd], low_half
            )
            start = pair_refs[g][q // 2, q % 2].astype(jnp.float32)
            start = start + embedding[:, q * LANES : (q + 1) * LANES]
            slab = start + outer_mean * inverse_live
            pair_mid_ref[here] = slab
            slabs.append(normalize_channels(slab))
            places.append(here)
        normed = jnp.concatenate(slabs, axis=1)
        combined = mix(out_mix, normed)
        left = gate_curve(combined[128:256]) * combined[0:128]
        right = gate_curve(combined[384:512]) * combined[256:384]
        gating = gate_curve(mix(out_gate, normed))
        for q in range(4):
            lanes = slice(q * LANES, (q + 1) * LANES)
            rows = pl.ds(pl.multiple_of(places[q] * 128, 128), 128)
            left_ref[rows, :] = left[:, lanes]
            right_ref[rows, :] = right[:, lanes].astype(jnp.bfloat16)
            gating_ref[places[q]] = gating[:, lanes]


def triangle_kernel(
    place_ref,
    pair_mid_ref,
    left_ref,
    gating_ref,
    right_own_ref,
    right_other_ref,
    *rest,
):
    sources, (own_pair_ref, own_part_ref, other_part_ref) = rest[:6], rest[6:9]
    narrow_ref, wide_out_ref = rest[9:11]
    right_ref, product_ref, pair_now_ref, chosen_ref, own_left_ref, own_product_ref = rest[11:17]
    landed, arrived = rest[17:23], rest[23]
    copies = start_copies(sources, landed, arrived)
    place = place_ref[0]
    core = place % 2
    half = LANES // 2
    low_half = lax.broadcasted_iota(jnp.int32, (LANES, LANES), 1) < half
    low_short = lax.broadcasted_iota(jnp.int32, (32, LANES), 1) < half
    for chip in range(8):
        for source, side in ((right_own_ref, core), (right_other_ref, 1 - core)):
            rows = pl.ds(pl.multiple_of((4 * chip + 2 * side) * 128, 256), 256)
            right_ref[rows, :] = source[chip * 256 : (chip + 1) * 256, :].astype(jnp.float32)

    nothing = jnp.zeros((32, LANES), jnp.bfloat16)

    def outgoing_channels(block, carry):
        for e in range(32):
            c = block * 32 + e
            left = left_ref[pl.ds(c, 16, stride=128), :].astype(jnp.bfloat16)
            right = right_ref[pl.ds(c, 32, stride=128), :]
            moved = pltpu.roll(right, half, 1).astype(jnp.bfloat16)
            right = right.astype(jnp.bfloat16)
            spread = jnp.concatenate(
                [
                    jnp.where(low_short, right, nothing),
                    jnp.where(low_short, moved, nothing),
                    jnp.where(low_short, nothing, moved),
                    jnp.where(low_short, nothing, right),
                ],
                axis=0,
            )
            product_ref[pl.ds(c, 16, stride=128), :] = contract_last(left, spread)
        return carry

    lax.fori_loop(0, 4, outgoing_channels, 0)

    for copy in copies:
        copy.wait()
    out_final = transpose_blocks(landed[0])
    in_mix = transpose_blocks(landed[1])
    narrow_ref[0:128, :] = transpose_blocks(landed[3])
    narrow_ref[128:256, :] = transpose_blocks(landed[2])
    narrow_ref[256:768, :] = transpose_blocks(landed[4])
    wide_out_ref[...] = transpose_blocks(landed[5])

    column = lax.broadcasted_iota(jnp.int32, (1, 256), 1)
    which = column // 16
    residue = which % 4
    device = place ^ ((which // 4) % 2)
    wanted = half * (which // 8) + 32 * (residue % 2) + 2 * device + residue // 2
    slab_of = column % 16
    source_lane = lax.broadcasted_iota(jnp.int32, (LANES, 256), 0)
    for g in range(4):
        products = [
            normalize_channels(product_ref[(4 * g + q) * 128 : (4 * g + q + 1) * 128, :])
            for q in range(4)
        ]
        finished = mix(out_final, jnp.concatenate(products, axis=1))
        slabs = []
        picks = []
        for q in range(4):
            h = 4 * g + q
            lanes = slice(q * LANES, (q + 1) * LANES)
            slab = pair_mid_ref[h] + gating_ref[h] * finished[:, lanes]
            pair_now_ref[h] = slab
            slabs.append(normalize_channels(slab))
            here = jnp.where(slab_of == h, wanted, -1)
            picks.append((source_lane == here).astype(jnp.float32).astype(jnp.bfloat16))
        normed = jnp.concatenate(slabs, axis=1)
        chosen = mix(normed, jnp.concatenate(picks, axis=0))
        if g:
            chosen_ref[...] += chosen
        else:
            chosen_ref[...] = chosen
        combined = mix(in_mix[256:512], normed)
        right = gate_curve(combined[128:256]) * combined[0:128]
        for q in range(4):
            right_ref[(4 * g + q) * 128 : (4 * g + q + 1) * 128, :] = right[
                :, q * LANES : (q + 1) * LANES
            ]
    for t in range(2):
        own_pair_ref[t] = pair_now_ref[2 * (place // 2) + t]

    combined = mix(in_mix[0:256], chosen_ref[...].astype(jnp.bfloat16))
    own_left = gate_curve(combined[128:256]) * combined[0:128]
    for m in range(16):
        part = own_left[:, (m // 8) * LANES : (m // 8 + 1) * LANES]
        if m % 8:
            part = pltpu.roll(part, LANES - 16 * (m % 8), 1)
        own_left_ref[m * 128 : (m + 1) * 128, :] = part

    def incoming_channels(block, carry):
        for e in range(32):
            c = block * 32 + e
            left = own_left_ref[pl.ds(c, 16, stride=128), :][:, 0:16].astype(jnp.bfloat16)
            right = right_ref[pl.ds(c, 16, stride=128), :].astype(jnp.bfloat16)
            own_product_ref[pl.ds(c, 16, stride=128), :] = mix(left, right)
        return carry

    lax.fori_loop(0, 4, incoming_channels, 0)

    def block_of(b, e, residue):
        m = 8 * b + 4 * e + residue
        return own_product_ref[m * 128 : (m + 1) * 128, :]

    for e, target in ((0, own_part_ref), (1, other_part_ref)):
        for t in range(2):
            target[t] = fold_halves(
                block_of(0, e, 2 * t),
                block_of(0, e, 2 * t + 1),
                block_of(1, e, 2 * t),
                block_of(1, e, 2 * t + 1),
                low_half,
            )


def finish_kernel(own_pair_ref, own_part_ref, other_part_ref, narrow_ref, down_ref, result_ref):
    products = [normalize_channels(own_part_ref[t] + other_part_ref[t]) for t in range(2)]
    finished = mix(narrow_ref[0:128, :], jnp.concatenate(products, axis=1))
    own_pair = jnp.concatenate([own_pair_ref[t] for t in range(2)], axis=1)
    gating = gate_curve(mix(narrow_ref[128:256, :], normalize_channels(own_pair)))
    own_pair = own_pair + gating * finished
    hidden = jnp.maximum(mix(narrow_ref[256:768, :], normalize_channels(own_pair)), 0.0)
    own_pair = own_pair + mix(down_ref[...], hidden.astype(jnp.bfloat16))
    own_pair = own_pair.astype(jnp.bfloat16)
    order = lane_order_matrix()
    for t in range(2):
        result_ref[t * 128 : (t + 1) * 128, :] = contract_last(
            order, own_pair[:, t * LANES : (t + 1) * LANES]
        ).astype(jnp.bfloat16)


def lane_order_matrix():
    half = LANES // 2
    member = lax.broadcasted_iota(jnp.int32, (LANES, LANES), 0)
    lane = lax.broadcasted_iota(jnp.int32, (LANES, LANES), 1)
    back = half * (member // half) + 32 * (member % 2) + (member % half) // 2
    return (lane == back).astype(jnp.float32).astype(jnp.bfloat16)


def contract_first(first, second):
    return lax.dot_general(
        first, second, (((0,), (0,)), ((), ())), preferred_element_type=jnp.float32
    )


def rows_kernel(
    rows_source, pair_source, blocks_ref, own_pair_ref, rows_ref, pair_ref, wide_ref, arrived
):
    rows_copy = pltpu.make_async_copy(rows_source, rows_ref, arrived.at[0])
    pair_copy = pltpu.make_async_copy(pair_source, pair_ref, arrived.at[1])
    pair_copy.start()
    rows_copy.start()
    pair_copy.wait()
    order = lane_order_matrix()
    for t in range(2):
        own_pair_ref[t] = contract_first(
            pair_ref[2 * t : 2 * t + 2].reshape(LANES, LANES), order
        ).astype(jnp.bfloat16)
    rows_copy.wait()
    residues = rows_ref.shape[1]
    count = 8 * residues
    rows = rows_ref[...].astype(jnp.float32).reshape(count, 2 * LANES)
    for e in range(2):
        wide_ref[e * count : (e + 1) * count, :] = rows[:, e * LANES : (e + 1) * LANES]
    for p in range(16):
        for e in range(2):
            block = [
                wide_ref[pl.ds(e * count + 4 * p + i, 8, stride=residues), :] for i in range(4)
            ]
            blocks_ref[p, :, e * LANES : (e + 1) * LANES] = jnp.concatenate(block, axis=0).astype(
                jnp.bfloat16
            )


def normalize_rows(values):
    center = jnp.mean(values, axis=1, keepdims=True)
    shifted = values - center
    spread = jnp.mean(shifted * shifted, axis=1, keepdims=True)
    return (shifted * lax.rsqrt(spread + EPSILON)).astype(jnp.bfloat16)


def contract_last(first, second):
    return lax.dot_general(
        first, second, (((1,), (1,)), ((), ())), preferred_element_type=jnp.float32
    )


def msa_kernel(
    live_ref,
    blocks_ref,
    query_ref,
    key_ref,
    value_gate_ref,
    output_ref,
    up_ref,
    down_ref,
    outer_ref,
    result_ref,
    parts_ref,
    wide_ref,
    attended_ref,
    final_ref,
):
    for p in range(16):
        block = blocks_ref[p].astype(jnp.float32)
        for i in range(4):
            wide_ref[i * 128 + p * 8 : i * 128 + p * 8 + 8, :] = block[i * 8 : i * 8 + 8, :]
    live = live_ref[...]
    alive = live > 0.0
    width = HM * HEAD_SIZE
    head_of = lax.broadcasted_iota(jnp.int32, (128, width), 1) // HEAD_SIZE
    zero = jnp.zeros((128, width), jnp.bfloat16)
    one = jnp.ones((128, width), jnp.bfloat16)

    def by_head(values):
        return jnp.concatenate([jnp.where(head_of == h, values, zero) for h in range(HM)], axis=0)

    heads = by_head(one)
    normed = normalize_rows(wide_ref[...])
    query = (mix(normed, query_ref[...]) * HEAD_SIZE ** (-0.5)).astype(jnp.bfloat16)
    key = mix(normed, key_ref[...]).astype(jnp.bfloat16)
    value_gate = mix(normed, value_gate_ref[...])
    value = value_gate[:, :width].astype(jnp.bfloat16)
    for i in range(4):
        rows = slice(i * 128, (i + 1) * 128)
        scores = contract_last(query[rows], by_head(key[rows]))
        raised = []
        for h in range(HM):
            score = jnp.where(alive, scores[:, h * 128 : (h + 1) * 128], -1000000000.0)
            raised.append(jnp.exp(score - jnp.max(score, axis=1, keepdims=True)).astype(jnp.bfloat16))
        raised = jnp.concatenate(raised, axis=1)
        attended_ref[rows, :] = mix(raised, by_head(value[rows])) / mix(raised, heads)
    gated = (gate_curve(value_gate[:, width:]) * attended_ref[...]).astype(jnp.bfloat16)
    current = wide_ref[...] + mix(gated, output_ref[...])
    hidden = jnp.maximum(mix(normalize_rows(current), up_ref[...]), 0.0).astype(jnp.bfloat16)
    final = (current + mix(hidden, down_ref[...])).astype(jnp.bfloat16).astype(jnp.float32)
    outer = contract_last(outer_ref[...], normalize_rows(final))
    for i in range(4):
        rows = slice(i * 128, (i + 1) * 128)
        part = (outer[:, rows] * live).astype(jnp.bfloat16)
        parts_ref[i * CO : (i + 1) * CO, :] = part[:CO, :]
        parts_ref[128 + i * CO : 128 + (i + 1) * CO, :] = part[CO:, :]
        final_ref[pl.ds(i, 128, stride=4), :] = final[rows, :128]
        final_ref[pl.ds(512 + i, 128, stride=4), :] = final[rows, 128:]
    result_ref[:, :128] = final_ref[:512, :].astype(jnp.bfloat16)
    result_ref[:, 128:] = final_ref[512:, :].astype(jnp.bfloat16)


def exchange(values, offset):
    pieces = lax.axis_size("dap")
    return lax.ppermute(values, "dap", [(q, q ^ offset) for q in range(pieces)])


def whole_block(
    alignment_input,
    pair_state_input,
    bin_all,
    live_row_float,
    relative_position_table,
    column_query_weight,
    column_key_weight,
    column_value_gate_weight,
    column_output_weight,
    alignment_transition_up,
    alignment_transition_down,
    outer_input_weight,
    *pair_weights,
):
    channels = alignment_input.shape[2]
    width = pair_state_input.shape[2]
    place = lax.axis_index("dap").astype(jnp.int32).reshape(1)
    vmem = pl.BlockSpec(memory_space=pltpu.VMEM)
    smem = pl.BlockSpec(memory_space=pltpu.SMEM)
    hbm = pl.BlockSpec(memory_space=pltpu.HBM)

    def array(*shape, dtype=jnp.bfloat16):
        return jax.ShapeDtypeStruct(shape, dtype)

    def wide(*shape):
        return jax.ShapeDtypeStruct(shape, jnp.float32)

    def limit(mebibytes):
        return pltpu.CompilerParams(vmem_limit_bytes=mebibytes * 1024 * 1024)

    blocks, own_pair = pl.pallas_call(
        rows_kernel,
        out_shape=[array(16, 32, channels), array(2, width, LANES)],
        in_specs=[hbm, hbm],
        out_specs=[vmem, vmem],
        scratch_shapes=[
            pltpu.VMEM(alignment_input.shape, jnp.bfloat16),
            pltpu.VMEM(pair_state_input.shape, jnp.bfloat16),
            pltpu.VMEM((1024, LANES), jnp.float32),
            pltpu.SemaphoreType.DMA((2,)),
        ],
        compiler_params=limit(56),
        name="rows_by_device",
    )(alignment_input, pair_state_input)
    blocks = lax.all_to_all(blocks, "dap", split_axis=0, concat_axis=0, tiled=True)

    pair_first = jnp.stack([own_pair, exchange(own_pair, 8)])
    pair_second = exchange(pair_first, 4)
    blocks, pair_first, pair_second = lax.optimization_barrier((blocks, pair_first, pair_second))
    pair_pieces = [pair_first, pair_second, exchange(pair_first, 2), exchange(pair_second, 2)]

    result, parts = pl.pallas_call(
        msa_kernel,
        out_shape=(array(512, channels), array(256, LANES)),
        in_specs=[vmem] * 9,
        out_specs=(vmem, vmem),
        scratch_shapes=[
            pltpu.VMEM((512, channels), jnp.float32),
            pltpu.VMEM((512, channels), jnp.float32),
            pltpu.VMEM((1024, LANES), jnp.float32),
        ],
        compiler_params=limit(32),
        cost_estimate=pl.CostEstimate(
            flops=2_000_000_000, bytes_accessed=10_000_000, transcendentals=1_000_000
        ),
        name="msa_whole",
    )(
        live_row_float.reshape(1, LANES),
        blocks,
        column_query_weight,
        column_key_weight,
        column_value_gate_weight,
        column_output_weight,
        alignment_transition_up,
        alignment_transition_down,
        outer_input_weight.T,
    )
    first = jnp.stack([parts, exchange(parts, 8)])
    second = exchange(first, 4)
    pieces = [first, second, exchange(first, 2), exchange(second, 2)]
    core_pieces = [exchange(piece, 1) for piece in pieces]

    slabs = (16, 128, LANES)
    tall = (16 * 128, LANES)
    pair_mid, left, gating, right = pl.pallas_call(
        start_kernel,
        out_shape=[wide(*slabs), wide(*tall), wide(*slabs), array(*tall)],
        in_specs=[smem] + [vmem] * 15 + [hbm] * 3,
        out_specs=[vmem] * 4,
        scratch_shapes=[
            pltpu.VMEM((2048, LANES), jnp.float32),
            pltpu.VMEM((128, 2048), jnp.bfloat16),
            pltpu.VMEM((1024, LANES), jnp.float32),
            pltpu.VMEM((256, 512), jnp.bfloat16),
            pltpu.VMEM((LANES, LANES), jnp.float32),
            pltpu.VMEM((512, 1024), jnp.bfloat16),
            pltpu.VMEM((512, 1024), jnp.bfloat16),
        ]
        + [pltpu.VMEM(w.shape, jnp.bfloat16) for w in pair_weights[:3]]
        + [pltpu.SemaphoreType.DMA((3,))],
        compiler_params=limit(48),
        name="pair_start",
    )(
        place,
        live_row_float.reshape(1, LANES),
        lanes_order(bin_all).reshape(32, LANES),
        relative_position_table,
        *pieces,
        *core_pieces,
        *pair_pieces,
        *pair_weights[:3],
    )
    own_pair, own_part, other_part, narrow_weights, down_weight = pl.pallas_call(
        triangle_kernel,
        out_shape=[wide(2, 128, LANES)] * 3 + [array(768, LANES), array(128, 512)],
        in_specs=[smem] + [vmem] * 5 + [hbm] * 6,
        out_specs=[vmem] * 5,
        scratch_shapes=[
            pltpu.VMEM((32 * 128, LANES), jnp.float32),
            pltpu.VMEM(tall, jnp.float32),
            pltpu.VMEM(slabs, jnp.float32),
            pltpu.VMEM((128, 256), jnp.float32),
            pltpu.VMEM(tall, jnp.float32),
            pltpu.VMEM(tall, jnp.float32),
        ]
        + [pltpu.VMEM(w.shape, jnp.bfloat16) for w in pair_weights[3:]]
        + [pltpu.SemaphoreType.DMA((6,))],
        compiler_params=limit(48),
        name="pair_triangles",
    )(place, pair_mid, left, gating, right, exchange(right, 1), *pair_weights[3:])
    pair_output = pl.pallas_call(
        finish_kernel,
        out_shape=array(256, LANES),
        in_specs=[vmem] * 5,
        out_specs=vmem,
        compiler_params=limit(16),
        name="pair_finish",
    )(own_pair, own_part, exchange(other_part, 1), narrow_weights, down_weight)
    return result.reshape(128, 4, channels), pair_output.reshape(pair_state_input.shape)


def lanes_order(values):
    lead = values.shape[:-1]
    halves = values.reshape(lead + (values.shape[-1] // 2, 2))
    return jnp.swapaxes(halves, -1, -2).reshape(values.shape)


def local(
    alignment_input,
    pair_state_input,
    residue_number_index,
    chain_label,
    alignment_row_mask,
    relative_position_table,
    column_query_weight,
    column_key_weight,
    column_value_gate_weight,
    column_output_weight,
    alignment_transition_up,
    alignment_transition_down,
    outer_input_weight,
    outer_output_weight,
    outgoing_projection_weight,
    outgoing_output_gate,
    outgoing_output_weight,
    incoming_projection_weight,
    incoming_output_gate,
    incoming_output_weight,
    pair_transition_up,
    pair_transition_down,
):
    shard_pieces = lax.axis_size("dap")
    own_rows = pair_state_input.shape[0]
    residue_count = pair_state_input.shape[1]
    channel_count = alignment_input.shape[2]
    head_width = HM * HEAD_SIZE
    first_row = lax.axis_index("dap") * own_rows
    own_index = lax.dynamic_slice_in_dim(residue_number_index, first_row, own_rows)
    own_chain = lax.dynamic_slice_in_dim(chain_label, first_row, own_rows)

    def bins_of(index, chain):
        offset = index[:, None] - residue_number_index[None, :]
        return jnp.where(
            chain[:, None] == chain_label[None, :],
            jnp.clip(offset + MAXREL, 0, 2 * MAXREL),
            2 * MAXREL + 1,
        )

    bin_index = bins_of(own_index, own_chain)
    one_hot = (bin_index[:, :, None] == jnp.arange(NBINS, dtype=jnp.int32)[None, None, :]).astype(
        jnp.bfloat16
    )
    pair_start = pair_state_input.astype(jnp.float32) + jnp.einsum(
        "ijb,bc->ijc", one_hot, relative_position_table, preferred_element_type=jnp.float32
    )
    live_rows = alignment_row_mask > 0
    live_row_float = live_rows.astype(jnp.float32)

    if alignment_row_mask.shape[0] == LANES and 2 * residue_count == LANES and own_rows == 4:
        return whole_block(
            alignment_input,
            pair_state_input,
            bins_of(residue_number_index, chain_label),
            live_row_float,
            relative_position_table,
            column_query_weight,
            column_key_weight,
            column_value_gate_weight,
            column_output_weight,
            alignment_transition_up,
            alignment_transition_down,
            outer_input_weight,
            outer_output_weight,
            outgoing_projection_weight,
            outgoing_output_gate,
            outgoing_output_weight,
            incoming_projection_weight,
            incoming_output_gate,
            incoming_output_weight,
            pair_transition_up,
            pair_transition_down,
        )

    def attend_one(operands):
        query_col, key_col, value_col = operands
        scores = jnp.einsum("shd,thd->hst", query_col, key_col, preferred_element_type=jnp.float32)
        scores = jnp.where(live_rows[None, None, :], scores, -1000000000.0)
        row_top = jnp.max(scores, axis=-1, keepdims=True)
        raised = jnp.exp(scores - row_top)
        attention = (raised / jnp.sum(raised, axis=-1, keepdims=True)).astype(jnp.bfloat16)
        return jnp.einsum("hst,thd->shd", attention, value_col, preferred_element_type=jnp.float32)

    blocked_view = alignment_input.reshape(
        alignment_input.shape[0], shard_pieces, residue_count // shard_pieces, channel_count
    )
    block_in = lax.all_to_all(blocked_view, "dap", split_axis=1, concat_axis=0, tiled=True)
    depth_rows = block_in.shape[0]
    count_cols = block_in.shape[2]
    current = block_in.reshape(depth_rows, count_cols, channel_count).astype(jnp.float32)
    normed = layer_normalize(current).astype(jnp.bfloat16)
    query_rows = (
        jnp.einsum("sic,ce->sie", normed, column_query_weight, preferred_element_type=jnp.float32)
        * HEAD_SIZE ** (-0.5)
    ).astype(jnp.bfloat16)
    key_row_block = jnp.einsum(
        "sic,ce->sie", normed, column_key_weight, preferred_element_type=jnp.float32
    ).astype(jnp.bfloat16)
    value_gate_pair = jnp.einsum(
        "sic,ce->sie", normed, column_value_gate_weight, preferred_element_type=jnp.float32
    )
    value_rows = value_gate_pair[..., :head_width].astype(jnp.bfloat16)

    def by_column(values):
        return values.transpose(1, 0, 2).reshape(count_cols, depth_rows, HM, HEAD_SIZE)

    attended = lax.map(
        attend_one, (by_column(query_rows), by_column(key_row_block), by_column(value_rows))
    )
    attended = attended.reshape(count_cols, depth_rows, head_width).transpose(1, 0, 2)
    gated_out = (jax.nn.sigmoid(value_gate_pair[..., head_width:]) * attended).astype(jnp.bfloat16)
    current = current + jnp.einsum(
        "sie,ec->sic", gated_out, column_output_weight, preferred_element_type=jnp.float32
    )
    hidden = jax.nn.relu(
        jnp.einsum(
            "sic,cf->sif",
            layer_normalize(current).astype(jnp.bfloat16),
            alignment_transition_up,
            preferred_element_type=jnp.float32,
        )
    ).astype(jnp.bfloat16)
    current = current + jnp.einsum(
        "sif,fc->sic", hidden, alignment_transition_down, preferred_element_type=jnp.float32
    )
    result = current.astype(jnp.bfloat16)
    outer_product_input = jnp.einsum(
        "sic,cf->sif",
        layer_normalize(result.astype(jnp.float32)).astype(jnp.bfloat16),
        outer_input_weight,
        preferred_element_type=jnp.float32,
    )
    outer_product_input = outer_product_input * live_row_float[:, None, None]
    left_part = outer_product_input[..., :CO].astype(jnp.bfloat16)
    right_part = outer_product_input[..., CO:].astype(jnp.bfloat16)
    all_rows = result.shape[0]
    left_cols = left_part.transpose(1, 0, 2)
    right_cols = right_part.transpose(1, 0, 2).reshape(own_rows, all_rows * CO)
    live_count = jnp.sum(live_row_float)
    right_piece = gather_doubling(right_cols).reshape(-1, all_rows * CO)
    span_rows = right_piece.shape[0]
    products = jnp.einsum(
        "isc,jsd->ijcd",
        left_cols,
        right_piece.reshape(span_rows, all_rows, CO),
        preferred_element_type=jnp.float32,
    )
    products = products.astype(jnp.bfloat16).reshape(own_rows, span_rows, CO * CO)
    outer_mean = (
        jnp.einsum("ijf,fc->ijc", products, outer_output_weight, preferred_element_type=jnp.float32)
        / live_count
    )
    pair_mid = pair_start + outer_mean
    out_left, out_right, out_gating = triangle_inputs(
        pair_mid, outgoing_projection_weight, outgoing_output_gate
    )
    out_product = by_channels(out_left, out_right, "cik,cjk->cij")
    pair_after_out = triangle_finish(pair_mid, out_product, out_gating, outgoing_output_weight)
    in_left, in_right, in_gating = triangle_inputs(
        pair_after_out, incoming_projection_weight, incoming_output_gate
    )
    in_product = by_channels(in_left, in_right, "cki,ckj->cij")
    pair_after_in = triangle_finish(pair_after_out, in_product, in_gating, incoming_output_weight)
    pair_expanded = jax.nn.relu(
        jnp.einsum(
            "ijc,cf->ijf",
            layer_normalize(pair_after_in).astype(jnp.bfloat16),
            pair_transition_up,
            preferred_element_type=jnp.float32,
        )
    ).astype(jnp.bfloat16)
    pair_state_output = (
        pair_after_in
        + jnp.einsum(
            "ijf,fc->ijc", pair_expanded, pair_transition_down, preferred_element_type=jnp.float32
        )
    ).astype(jnp.bfloat16)
    return (result, pair_state_output)


def solution(mesh):
    in_specs = (
        P(("grp", "dap"), None, None),
        P(("grp", "dap"), None, None),
        P("grp"),
        P("grp"),
        P("grp"),
        P(),
        P(),
        P(),
        P(),
        P(),
        P(),
        P(),
        P(),
        P(),
        P(),
        P(),
        P(),
        P(),
        P(),
        P(),
        P(),
        P(),
    )
    out_specs = (P("grp", "dap", None), P(("grp", "dap"), None, None))
    return jax.shard_map(local, mesh=mesh, in_specs=in_specs, out_specs=out_specs, check_vma=False)
```

```python
import jax
import jax.numpy as jnp
from jax import lax
from jax.experimental import pallas as pl
from jax.experimental.pallas import tpu as pltpu
from jax.sharding import PartitionSpec as P

HM = 8
HEAD_SIZE = 32
CO = 32
MAXREL = 32
NBINS = 66


EPSILON = 1e-05


def layer_normalize(values):
    center = jnp.mean(values, axis=-1, keepdims=True)
    shifted = values - center
    spread = jnp.mean(shifted * shifted, axis=-1, keepdims=True)
    return shifted * lax.rsqrt(spread + EPSILON)


def triangle_inputs(pair_now, weight, gate_weight):
    normed = layer_normalize(pair_now).astype(jnp.bfloat16)
    combined = jnp.einsum("ijc,cf->fij", normed, weight, preferred_element_type=jnp.float32)
    hidden_width = weight.shape[1] // 4
    left_side = (
        jax.nn.sigmoid(combined[hidden_width : 2 * hidden_width]) * combined[:hidden_width]
    ).astype(jnp.bfloat16)
    right_side = (
        jax.nn.sigmoid(combined[3 * hidden_width :]) * combined[2 * hidden_width : 3 * hidden_width]
    ).astype(jnp.bfloat16)
    gating = jax.nn.sigmoid(
        jnp.einsum("ijc,cd->ijd", normed, gate_weight, preferred_element_type=jnp.float32)
    )
    return (left_side, right_side, gating)


def triangle_finish(pair_now, product, gating, final_weight):
    product = lax.optimization_barrier(product)
    normed = layer_normalize(product.transpose(1, 2, 0).astype(jnp.float32)).astype(jnp.bfloat16)
    return pair_now + gating * jnp.einsum(
        "ijc,cd->ijd", normed, final_weight, preferred_element_type=jnp.float32
    )


def by_channels(left_side, right_side, form):
    both = jnp.stack([left_side, right_side])
    both = lax.all_to_all(both, "dap", split_axis=1, concat_axis=2, tiled=True)
    partial_out = jnp.einsum(form, both[0], both[1], preferred_element_type=jnp.float32)
    return lax.all_to_all(
        partial_out.astype(jnp.bfloat16), "dap", split_axis=1, concat_axis=0, tiled=True
    )


def gather_doubling(block):
    shard_pieces = lax.axis_size("dap")
    place = lax.axis_index("dap")
    held = block
    depth = 0
    bit = shard_pieces // 2
    while bit:
        other = lax.ppermute(held, "dap", [(q, q ^ bit) for q in range(shard_pieces)])
        upper = (place & bit) != 0
        first = jnp.where(upper, other, held)
        second = jnp.where(upper, held, other)
        held = jnp.stack([first, second], axis=depth)
        depth += 1
        bit //= 2
    return held.reshape((shard_pieces,) + block.shape)


LANES = 128


def gate_curve(values):
    return 0.5 + 0.5 * jnp.tanh(0.5 * values)


def normalize_channels(values):
    center = jnp.mean(values, axis=0, keepdims=True)
    shifted = values - center
    spread = jnp.mean(shifted * shifted, axis=0, keepdims=True)
    return (shifted * lax.rsqrt(spread + EPSILON)).astype(jnp.bfloat16)


def mix(weight, values):
    return jnp.dot(weight, values, preferred_element_type=jnp.float32)


def fold_halves(first_even, second_even, first_odd, second_odd, low_half):
    straight = jnp.where(low_half, first_even, second_odd)
    crossed = jnp.where(low_half, second_even, first_odd)
    return straight + pltpu.roll(crossed, LANES // 2, 1)


def transpose_blocks(ref):
    rows, columns = ref.shape
    return jnp.concatenate(
        [
            jnp.concatenate(
                [
                    ref[a : a + LANES, b : b + LANES].astype(jnp.float32).T.astype(jnp.bfloat16)
                    for a in range(0, rows, LANES)
                ],
                axis=1,
            )
            for b in range(0, columns, LANES)
        ],
        axis=0,
    )


def start_copies(sources, landed, arrived):
    copies = [
        pltpu.make_async_copy(source, landed[k], arrived.at[k]) for k, source in enumerate(sources)
    ]
    for copy in copies:
        copy.start()
    return copies


FIRSTS = (0, 4, 2, 6)


def start_kernel(place_ref, live_ref, bins_ref, table_ref, *rest):
    part_refs, core_refs, pair_refs, sources = rest[:4], rest[4:8], rest[8:12], rest[12:15]
    pair_mid_ref, left_ref, gating_ref, right_ref = rest[15:19]
    wide_ref, right_cols_ref, mean_wide_ref, mean_weight_ref, table_wide_ref = rest[19:24]
    stack_refs, landed, arrived = rest[24:26], rest[26:29], rest[29]
    copies = start_copies(sources, landed, arrived)
    place = place_ref[0]
    inverse_live = 1.0 / jnp.sum(live_ref[...], axis=1, keepdims=True)
    half = LANES // 2
    channel = lax.broadcasted_iota(jnp.int32, (LANES, LANES), 0)
    table_wide_ref[...] = jnp.zeros_like(table_wide_ref)
    table_wide_ref[0:NBINS, :] = table_ref[...].astype(jnp.float32)
    table = table_wide_ref[...].T.astype(jnp.bfloat16)
    low_half = lax.broadcasted_iota(jnp.int32, (LANES, LANES), 1) < half

    for g in range(4):
        for m in range(2):
            device = place ^ FIRSTS[g] ^ (8 * m)
            for part, owner in ((part_refs[g], device), (core_refs[g], device ^ 1)):
                wide_ref[pl.ds(pl.multiple_of(owner * 128, 128), 128), :] = part[
                    m, 128:256, :
                ].astype(jnp.float32)
    for d in range(0, CO, 2):
        rows = [
            wide_ref[pl.ds(par * CO + d + e, 32, stride=2 * CO), :]
            for e in range(2)
            for par in range(2)
        ]
        right_cols_ref[:, d * half : d * half + LANES] = (
            jnp.concatenate(rows, axis=0).T.astype(jnp.bfloat16)
        )

    for copy in copies:
        copy.wait()
    mean_wide_ref[...] = landed[0][...].astype(jnp.float32)
    for e in range(2):
        for block in range(4):
            rows = [
                mean_wide_ref[pl.ds(2 * (4 * block + k) + e, CO, stride=CO), :] for k in range(4)
            ]
            mean_weight_ref[e * LANES : (e + 1) * LANES, block * LANES : (block + 1) * LANES] = (
                jnp.concatenate(rows, axis=0).T.astype(jnp.bfloat16)
            )
    out_mix = transpose_blocks(landed[1])
    out_gate = transpose_blocks(landed[2])

    for g in range(4):
        stack_ref = stack_refs[g % 2]
        left_rows = part_refs[g][:, 0:128, :].reshape(256, LANES)
        outer = mix(left_rows, right_cols_ref[...]).astype(jnp.bfloat16)
        for i in range(8):
            for d in range(16):
                stack_ref[d * 32 : (d + 1) * 32, i * LANES : (i + 1) * LANES] = outer[
                    i * 32 : (i + 1) * 32, d * LANES : (d + 1) * LANES
                ]
        mixed = mix(mean_weight_ref[...], stack_ref[...])
        slabs = []
        places = []
        devices = [place ^ FIRSTS[g] ^ (8 * m) for m in range(2)]
        one_hot = [
            (channel == bins_ref[pl.ds(2 * devices[q // 2] + q % 2, 1), :]).astype(jnp.float32)
            for q in range(4)
        ]
        embedding = mix(table, jnp.concatenate(one_hot, axis=1).astype(jnp.bfloat16))
        for q in range(4):
            device = devices[q // 2]
            here = 2 * (device // 2) + q % 2
            even = slice(2 * q * LANES, (2 * q + 1) * LANES)
            odd = slice((2 * q + 1) * LANES, (2 * q + 2) * LANES)
            outer_mean = fold_halves(
                mixed[0:128, even], mixed[0:128, odd], mixed[128:256, even], mixed[128:256, odd], low_half
            )
            start = pair_refs[g][q // 2, q % 2].astype(jnp.float32)
            start = start + embedding[:, q * LANES : (q + 1) * LANES]
            slab = start + outer_mean * inverse_live
            pair_mid_ref[here] = slab
            slabs.append(normalize_channels(slab))
            places.append(here)
        normed = jnp.concatenate(slabs, axis=1)
        combined = mix(out_mix, normed)
        left = gate_curve(combined[128:256]) * combined[0:128]
        right = gate_curve(combined[384:512]) * combined[256:384]
        gating = gate_curve(mix(out_gate, normed))
        for q in range(4):
            lanes = slice(q * LANES, (q + 1) * LANES)
            rows = pl.ds(pl.multiple_of(places[q] * 128, 128), 128)
            left_ref[rows, :] = left[:, lanes]
            right_ref[rows, :] = right[:, lanes].astype(jnp.bfloat16)
            gating_ref[places[q]] = gating[:, lanes]


def triangle_kernel(
    place_ref,
    pair_mid_ref,
    left_ref,
    gating_ref,
    right_own_ref,
    right_other_ref,
    *rest,
):
    sources, (own_pair_ref, own_part_ref, other_part_ref) = rest[:6], rest[6:9]
    narrow_ref, wide_out_ref = rest[9:11]
    right_ref, product_ref, pair_now_ref, chosen_ref, own_left_ref, own_product_ref = rest[11:17]
    landed, arrived = rest[17:23], rest[23]
    copies = start_copies(sources, landed, arrived)
    place = place_ref[0]
    core = place % 2
    half = LANES // 2
    low_half = lax.broadcasted_iota(jnp.int32, (LANES, LANES), 1) < half
    low_short = lax.broadcasted_iota(jnp.int32, (32, LANES), 1) < half
    for chip in range(8):
        for source, side in ((right_own_ref, core), (right_other_ref, 1 - core)):
            rows = pl.ds(pl.multiple_of((4 * chip + 2 * side) * 128, 256), 256)
            right_ref[rows, :] = source[chip * 256 : (chip + 1) * 256, :].astype(jnp.float32)

    nothing = jnp.zeros((32, LANES), jnp.bfloat16)

    def outgoing_channels(block, carry):
        for e in range(32):
            c = block * 32 + e
            left = left_ref[pl.ds(c, 16, stride=128), :].astype(jnp.bfloat16)
            right = right_ref[pl.ds(c, 32, stride=128), :]
            moved = pltpu.roll(right, half, 1).astype(jnp.bfloat16)
            right = right.astype(jnp.bfloat16)
            spread = jnp.concatenate(
                [
                    jnp.where(low_short, right, nothing),
                    jnp.where(low_short, moved, nothing),
                    jnp.where(low_short, nothing, moved),
                    jnp.where(low_short, nothing, right),
                ],
                axis=0,
            )
            product_ref[pl.ds(c, 16, stride=128), :] = contract_last(left, spread)
        return carry

    lax.fori_loop(0, 4, outgoing_channels, 0)

    for copy in copies:
        copy.wait()
    out_final = transpose_blocks(landed[0])
    in_mix = transpose_blocks(landed[1])
    narrow_ref[0:128, :] = transpose_blocks(landed[3])
    narrow_ref[128:256, :] = transpose_blocks(landed[2])
    narrow_ref[256:768, :] = transpose_blocks(landed[4])
    wide_out_ref[...] = transpose_blocks(landed[5])

    column = lax.broadcasted_iota(jnp.int32, (1, 256), 1)
    which = column // 16
    residue = which % 4
    device = place ^ ((which // 4) % 2)
    wanted = half * (which // 8) + 32 * (residue % 2) + 2 * device + residue // 2
    slab_of = column % 16
    source_lane = lax.broadcasted_iota(jnp.int32, (LANES, 256), 0)
    for g in range(4):
        products = [
            normalize_channels(product_ref[(4 * g + q) * 128 : (4 * g + q + 1) * 128, :])
            for q in range(4)
        ]
        finished = mix(out_final, jnp.concatenate(products, axis=1))
        slabs = []
        picks = []
        for q in range(4):
            h = 4 * g + q
            lanes = slice(q * LANES, (q + 1) * LANES)
            slab = pair_mid_ref[h] + gating_ref[h] * finished[:, lanes]
            pair_now_ref[h] = slab
            slabs.append(normalize_channels(slab))
            here = jnp.where(slab_of == h, wanted, -1)
            picks.append((source_lane == here).astype(jnp.float32).astype(jnp.bfloat16))
        normed = jnp.concatenate(slabs, axis=1)
        chosen = mix(normed, jnp.concatenate(picks, axis=0))
        if g:
            chosen_ref[...] += chosen
        else:
            chosen_ref[...] = chosen
        combined = mix(in_mix[256:512], normed)
        right = gate_curve(combined[128:256]) * combined[0:128]
        for q in range(4):
            right_ref[(4 * g + q) * 128 : (4 * g + q + 1) * 128, :] = right[
                :, q * LANES : (q + 1) * LANES
            ]
    for t in range(2):
        own_pair_ref[t] = pair_now_ref[2 * (place // 2) + t]

    combined = mix(in_mix[0:256], chosen_ref[...].astype(jnp.bfloat16))
    own_left = gate_curve(combined[128:256]) * combined[0:128]
    for m in range(16):
        part = own_left[:, (m // 8) * LANES : (m // 8 + 1) * LANES]
        if m % 8:
            part = pltpu.roll(part, LANES - 16 * (m % 8), 1)
        own_left_ref[m * 128 : (m + 1) * 128, :] = part

    def incoming_channels(block, carry):
        for e in range(32):
            c = block * 32 + e
            left = own_left_ref[pl.ds(c, 16, stride=128), :][:, 0:16].astype(jnp.bfloat16)
            right = right_ref[pl.ds(c, 16, stride=128), :].astype(jnp.bfloat16)
            own_product_ref[pl.ds(c, 16, stride=128), :] = mix(left, right)
        return carry

    lax.fori_loop(0, 4, incoming_channels, 0)

    def block_of(b, e, residue):
        m = 8 * b + 4 * e + residue
        return own_product_ref[m * 128 : (m + 1) * 128, :]

    for e, target in ((0, own_part_ref), (1, other_part_ref)):
        for t in range(2):
            target[t] = fold_halves(
                block_of(0, e, 2 * t),
                block_of(0, e, 2 * t + 1),
                block_of(1, e, 2 * t),
                block_of(1, e, 2 * t + 1),
                low_half,
            )


def finish_kernel(own_pair_ref, own_part_ref, other_part_ref, narrow_ref, down_ref, result_ref):
    products = [normalize_channels(own_part_ref[t] + other_part_ref[t]) for t in range(2)]
    finished = mix(narrow_ref[0:128, :], jnp.concatenate(products, axis=1))
    own_pair = jnp.concatenate([own_pair_ref[t] for t in range(2)], axis=1)
    gating = gate_curve(mix(narrow_ref[128:256, :], normalize_channels(own_pair)))
    own_pair = own_pair + gating * finished
    hidden = jnp.maximum(mix(narrow_ref[256:768, :], normalize_channels(own_pair)), 0.0)
    own_pair = own_pair + mix(down_ref[...], hidden.astype(jnp.bfloat16))
    own_pair = own_pair.astype(jnp.bfloat16)
    order = lane_order_matrix()
    for t in range(2):
        result_ref[t * 128 : (t + 1) * 128, :] = contract_last(
            order, own_pair[:, t * LANES : (t + 1) * LANES]
        ).astype(jnp.bfloat16)


def lane_order_matrix():
    half = LANES // 2
    member = lax.broadcasted_iota(jnp.int32, (LANES, LANES), 0)
    lane = lax.broadcasted_iota(jnp.int32, (LANES, LANES), 1)
    back = half * (member // half) + 32 * (member % 2) + (member % half) // 2
    return (lane == back).astype(jnp.float32).astype(jnp.bfloat16)


def contract_first(first, second):
    return lax.dot_general(
        first, second, (((0,), (0,)), ((), ())), preferred_element_type=jnp.float32
    )


def rows_kernel(rows_ref, pair_ref, blocks_ref, own_pair_ref, wide_ref):
    order = lane_order_matrix()
    for t in range(2):
        own_pair_ref[t] = contract_first(
            pair_ref[2 * t : 2 * t + 2].reshape(LANES, LANES), order
        ).astype(jnp.bfloat16)
    residues = rows_ref.shape[1]
    count = 8 * residues
    rows = rows_ref[...].astype(jnp.float32).reshape(count, 2 * LANES)
    for e in range(2):
        wide_ref[e * count : (e + 1) * count, :] = rows[:, e * LANES : (e + 1) * LANES]
    for p in range(16):
        for e in range(2):
            block = [
                wide_ref[pl.ds(e * count + 4 * p + i, 8, stride=residues), :] for i in range(4)
            ]
            blocks_ref[p, :, e * LANES : (e + 1) * LANES] = jnp.concatenate(block, axis=0).astype(
                jnp.bfloat16
            )


def normalize_rows(values):
    center = jnp.mean(values, axis=1, keepdims=True)
    shifted = values - center
    spread = jnp.mean(shifted * shifted, axis=1, keepdims=True)
    return (shifted * lax.rsqrt(spread + EPSILON)).astype(jnp.bfloat16)


def contract_last(first, second):
    return lax.dot_general(
        first, second, (((1,), (1,)), ((), ())), preferred_element_type=jnp.float32
    )


def msa_kernel(
    live_ref,
    blocks_ref,
    query_ref,
    key_ref,
    value_gate_ref,
    output_ref,
    up_ref,
    down_ref,
    outer_ref,
    result_ref,
    parts_ref,
    wide_ref,
    attended_ref,
    final_ref,
):
    for p in range(16):
        block = blocks_ref[p].astype(jnp.float32)
        for i in range(4):
            wide_ref[i * 128 + p * 8 : i * 128 + p * 8 + 8, :] = block[i * 8 : i * 8 + 8, :]
    live = live_ref[...]
    alive = live > 0.0
    width = HM * HEAD_SIZE
    head_of = lax.broadcasted_iota(jnp.int32, (128, width), 1) // HEAD_SIZE
    zero = jnp.zeros((128, width), jnp.bfloat16)
    one = jnp.ones((128, width), jnp.bfloat16)

    def by_head(values):
        return jnp.concatenate([jnp.where(head_of == h, values, zero) for h in range(HM)], axis=0)

    heads = by_head(one)
    normed = normalize_rows(wide_ref[...])
    query = (mix(normed, query_ref[...]) * HEAD_SIZE ** (-0.5)).astype(jnp.bfloat16)
    key = mix(normed, key_ref[...]).astype(jnp.bfloat16)
    value_gate = mix(normed, value_gate_ref[...])
    value = value_gate[:, :width].astype(jnp.bfloat16)
    for i in range(4):
        rows = slice(i * 128, (i + 1) * 128)
        scores = contract_last(query[rows], by_head(key[rows]))
        raised = []
        for h in range(HM):
            score = jnp.where(alive, scores[:, h * 128 : (h + 1) * 128], -1000000000.0)
            raised.append(jnp.exp(score - jnp.max(score, axis=1, keepdims=True)).astype(jnp.bfloat16))
        raised = jnp.concatenate(raised, axis=1)
        attended_ref[rows, :] = mix(raised, by_head(value[rows])) / mix(raised, heads)
    gated = (gate_curve(value_gate[:, width:]) * attended_ref[...]).astype(jnp.bfloat16)
    current = wide_ref[...] + mix(gated, output_ref[...])
    hidden = jnp.maximum(mix(normalize_rows(current), up_ref[...]), 0.0).astype(jnp.bfloat16)
    final = (current + mix(hidden, down_ref[...])).astype(jnp.bfloat16).astype(jnp.float32)
    outer = contract_last(outer_ref[...], normalize_rows(final))
    for i in range(4):
        rows = slice(i * 128, (i + 1) * 128)
        part = (outer[:, rows] * live).astype(jnp.bfloat16)
        parts_ref[i * CO : (i + 1) * CO, :] = part[:CO, :]
        parts_ref[128 + i * CO : 128 + (i + 1) * CO, :] = part[CO:, :]
        final_ref[pl.ds(i, 128, stride=4), :] = final[rows, :128]
        final_ref[pl.ds(512 + i, 128, stride=4), :] = final[rows, 128:]
    result_ref[:, :128] = final_ref[:512, :].astype(jnp.bfloat16)
    result_ref[:, 128:] = final_ref[512:, :].astype(jnp.bfloat16)


def exchange(values, offset):
    pieces = lax.axis_size("dap")
    return lax.ppermute(values, "dap", [(q, q ^ offset) for q in range(pieces)])


def whole_block(
    alignment_input,
    pair_state_input,
    bin_all,
    live_row_float,
    relative_position_table,
    column_query_weight,
    column_key_weight,
    column_value_gate_weight,
    column_output_weight,
    alignment_transition_up,
    alignment_transition_down,
    outer_input_weight,
    *pair_weights,
):
    channels = alignment_input.shape[2]
    width = pair_state_input.shape[2]
    place = lax.axis_index("dap").astype(jnp.int32).reshape(1)
    vmem = pl.BlockSpec(memory_space=pltpu.VMEM)
    smem = pl.BlockSpec(memory_space=pltpu.SMEM)
    hbm = pl.BlockSpec(memory_space=pltpu.HBM)

    def array(*shape, dtype=jnp.bfloat16):
        return jax.ShapeDtypeStruct(shape, dtype)

    def wide(*shape):
        return jax.ShapeDtypeStruct(shape, jnp.float32)

    def limit(mebibytes):
        return pltpu.CompilerParams(vmem_limit_bytes=mebibytes * 1024 * 1024)

    blocks, own_pair = pl.pallas_call(
        rows_kernel,
        out_shape=[array(16, 32, channels), array(2, width, LANES)],
        in_specs=[vmem, vmem],
        out_specs=[vmem, vmem],
        scratch_shapes=[pltpu.VMEM((1024, LANES), jnp.float32)],
        compiler_params=limit(16),
        name="rows_by_device",
    )(alignment_input, pair_state_input)
    blocks = lax.all_to_all(blocks, "dap", split_axis=0, concat_axis=0, tiled=True)

    pair_first = jnp.stack([own_pair, exchange(own_pair, 8)])
    pair_second = exchange(pair_first, 4)
    blocks, pair_first, pair_second = lax.optimization_barrier((blocks, pair_first, pair_second))
    pair_pieces = [pair_first, pair_second, exchange(pair_first, 2), exchange(pair_second, 2)]

    result, parts = pl.pallas_call(
        msa_kernel,
        out_shape=(array(512, channels), array(256, LANES)),
        in_specs=[vmem] * 9,
        out_specs=(vmem, vmem),
        scratch_shapes=[
            pltpu.VMEM((512, channels), jnp.float32),
            pltpu.VMEM((512, channels), jnp.float32),
            pltpu.VMEM((1024, LANES), jnp.float32),
        ],
        compiler_params=limit(32),
        cost_estimate=pl.CostEstimate(
            flops=2_000_000_000, bytes_accessed=10_000_000, transcendentals=1_000_000
        ),
        name="msa_whole",
    )(
        live_row_float.reshape(1, LANES),
        blocks,
        column_query_weight,
        column_key_weight,
        column_value_gate_weight,
        column_output_weight,
        alignment_transition_up,
        alignment_transition_down,
        outer_input_weight.T,
    )
    first = jnp.stack([parts, exchange(parts, 8)])
    second = exchange(first, 4)
    pieces = [first, second, exchange(first, 2), exchange(second, 2)]
    core_pieces = [exchange(piece, 1) for piece in pieces]

    slabs = (16, 128, LANES)
    tall = (16 * 128, LANES)
    pair_mid, left, gating, right = pl.pallas_call(
        start_kernel,
        out_shape=[wide(*slabs), wide(*tall), wide(*slabs), array(*tall)],
        in_specs=[smem] + [vmem] * 15 + [hbm] * 3,
        out_specs=[vmem] * 4,
        scratch_shapes=[
            pltpu.VMEM((2048, LANES), jnp.float32),
            pltpu.VMEM((128, 2048), jnp.bfloat16),
            pltpu.VMEM((1024, LANES), jnp.float32),
            pltpu.VMEM((256, 512), jnp.bfloat16),
            pltpu.VMEM((LANES, LANES), jnp.float32),
            pltpu.VMEM((512, 1024), jnp.bfloat16),
            pltpu.VMEM((512, 1024), jnp.bfloat16),
        ]
        + [pltpu.VMEM(w.shape, jnp.bfloat16) for w in pair_weights[:3]]
        + [pltpu.SemaphoreType.DMA((3,))],
        compiler_params=limit(48),
        name="pair_start",
    )(
        place,
        live_row_float.reshape(1, LANES),
        lanes_order(bin_all).reshape(32, LANES),
        relative_position_table,
        *pieces,
        *core_pieces,
        *pair_pieces,
        *pair_weights[:3],
    )
    own_pair, own_part, other_part, narrow_weights, down_weight = pl.pallas_call(
        triangle_kernel,
        out_shape=[wide(2, 128, LANES)] * 3 + [array(768, LANES), array(128, 512)],
        in_specs=[smem] + [vmem] * 5 + [hbm] * 6,
        out_specs=[vmem] * 5,
        scratch_shapes=[
            pltpu.VMEM((32 * 128, LANES), jnp.float32),
            pltpu.VMEM(tall, jnp.float32),
            pltpu.VMEM(slabs, jnp.float32),
            pltpu.VMEM((128, 256), jnp.float32),
            pltpu.VMEM(tall, jnp.float32),
            pltpu.VMEM(tall, jnp.float32),
        ]
        + [pltpu.VMEM(w.shape, jnp.bfloat16) for w in pair_weights[3:]]
        + [pltpu.SemaphoreType.DMA((6,))],
        compiler_params=limit(48),
        name="pair_triangles",
    )(place, pair_mid, left, gating, right, exchange(right, 1), *pair_weights[3:])
    pair_output = pl.pallas_call(
        finish_kernel,
        out_shape=array(256, LANES),
        in_specs=[vmem] * 5,
        out_specs=vmem,
        compiler_params=limit(16),
        name="pair_finish",
    )(own_pair, own_part, exchange(other_part, 1), narrow_weights, down_weight)
    return result.reshape(128, 4, channels), pair_output.reshape(pair_state_input.shape)


def lanes_order(values):
    lead = values.shape[:-1]
    halves = values.reshape(lead + (values.shape[-1] // 2, 2))
    return jnp.swapaxes(halves, -1, -2).reshape(values.shape)


def local(
    alignment_input,
    pair_state_input,
    residue_number_index,
    chain_label,
    alignment_row_mask,
    relative_position_table,
    column_query_weight,
    column_key_weight,
    column_value_gate_weight,
    column_output_weight,
    alignment_transition_up,
    alignment_transition_down,
    outer_input_weight,
    outer_output_weight,
    outgoing_projection_weight,
    outgoing_output_gate,
    outgoing_output_weight,
    incoming_projection_weight,
    incoming_output_gate,
    incoming_output_weight,
    pair_transition_up,
    pair_transition_down,
):
    shard_pieces = lax.axis_size("dap")
    own_rows = pair_state_input.shape[0]
    residue_count = pair_state_input.shape[1]
    channel_count = alignment_input.shape[2]
    head_width = HM * HEAD_SIZE
    first_row = lax.axis_index("dap") * own_rows
    own_index = lax.dynamic_slice_in_dim(residue_number_index, first_row, own_rows)
    own_chain = lax.dynamic_slice_in_dim(chain_label, first_row, own_rows)

    def bins_of(index, chain):
        offset = index[:, None] - residue_number_index[None, :]
        return jnp.where(
            chain[:, None] == chain_label[None, :],
            jnp.clip(offset + MAXREL, 0, 2 * MAXREL),
            2 * MAXREL + 1,
        )

    bin_index = bins_of(own_index, own_chain)
    one_hot = (bin_index[:, :, None] == jnp.arange(NBINS, dtype=jnp.int32)[None, None, :]).astype(
        jnp.bfloat16
    )
    pair_start = pair_state_input.astype(jnp.float32) + jnp.einsum(
        "ijb,bc->ijc", one_hot, relative_position_table, preferred_element_type=jnp.float32
    )
    live_rows = alignment_row_mask > 0
    live_row_float = live_rows.astype(jnp.float32)

    if alignment_row_mask.shape[0] == LANES and 2 * residue_count == LANES and own_rows == 4:
        return whole_block(
            alignment_input,
            pair_state_input,
            bins_of(residue_number_index, chain_label),
            live_row_float,
            relative_position_table,
            column_query_weight,
            column_key_weight,
            column_value_gate_weight,
            column_output_weight,
            alignment_transition_up,
            alignment_transition_down,
            outer_input_weight,
            outer_output_weight,
            outgoing_projection_weight,
            outgoing_output_gate,
            outgoing_output_weight,
            incoming_projection_weight,
            incoming_output_gate,
            incoming_output_weight,
            pair_transition_up,
            pair_transition_down,
        )

    def attend_one(operands):
        query_col, key_col, value_col = operands
        scores = jnp.einsum("shd,thd->hst", query_col, key_col, preferred_element_type=jnp.float32)
        scores = jnp.where(live_rows[None, None, :], scores, -1000000000.0)
        row_top = jnp.max(scores, axis=-1, keepdims=True)
        raised = jnp.exp(scores - row_top)
        attention = (raised / jnp.sum(raised, axis=-1, keepdims=True)).astype(jnp.bfloat16)
        return jnp.einsum("hst,thd->shd", attention, value_col, preferred_element_type=jnp.float32)

    blocked_view = alignment_input.reshape(
        alignment_input.shape[0], shard_pieces, residue_count // shard_pieces, channel_count
    )
    block_in = lax.all_to_all(blocked_view, "dap", split_axis=1, concat_axis=0, tiled=True)
    depth_rows = block_in.shape[0]
    count_cols = block_in.shape[2]
    current = block_in.reshape(depth_rows, count_cols, channel_count).astype(jnp.float32)
    normed = layer_normalize(current).astype(jnp.bfloat16)
    query_rows = (
        jnp.einsum("sic,ce->sie", normed, column_query_weight, preferred_element_type=jnp.float32)
        * HEAD_SIZE ** (-0.5)
    ).astype(jnp.bfloat16)
    key_row_block = jnp.einsum(
        "sic,ce->sie", normed, column_key_weight, preferred_element_type=jnp.float32
    ).astype(jnp.bfloat16)
    value_gate_pair = jnp.einsum(
        "sic,ce->sie", normed, column_value_gate_weight, preferred_element_type=jnp.float32
    )
    value_rows = value_gate_pair[..., :head_width].astype(jnp.bfloat16)

    def by_column(values):
        return values.transpose(1, 0, 2).reshape(count_cols, depth_rows, HM, HEAD_SIZE)

    attended = lax.map(
        attend_one, (by_column(query_rows), by_column(key_row_block), by_column(value_rows))
    )
    attended = attended.reshape(count_cols, depth_rows, head_width).transpose(1, 0, 2)
    gated_out = (jax.nn.sigmoid(value_gate_pair[..., head_width:]) * attended).astype(jnp.bfloat16)
    current = current + jnp.einsum(
        "sie,ec->sic", gated_out, column_output_weight, preferred_element_type=jnp.float32
    )
    hidden = jax.nn.relu(
        jnp.einsum(
            "sic,cf->sif",
            layer_normalize(current).astype(jnp.bfloat16),
            alignment_transition_up,
            preferred_element_type=jnp.float32,
        )
    ).astype(jnp.bfloat16)
    current = current + jnp.einsum(
        "sif,fc->sic", hidden, alignment_transition_down, preferred_element_type=jnp.float32
    )
    result = current.astype(jnp.bfloat16)
    outer_product_input = jnp.einsum(
        "sic,cf->sif",
        layer_normalize(result.astype(jnp.float32)).astype(jnp.bfloat16),
        outer_input_weight,
        preferred_element_type=jnp.float32,
    )
    outer_product_input = outer_product_input * live_row_float[:, None, None]
    left_part = outer_product_input[..., :CO].astype(jnp.bfloat16)
    right_part = outer_product_input[..., CO:].astype(jnp.bfloat16)
    all_rows = result.shape[0]
    left_cols = left_part.transpose(1, 0, 2)
    right_cols = right_part.transpose(1, 0, 2).reshape(own_rows, all_rows * CO)
    live_count = jnp.sum(live_row_float)
    right_piece = gather_doubling(right_cols).reshape(-1, all_rows * CO)
    span_rows = right_piece.shape[0]
    products = jnp.einsum(
        "isc,jsd->ijcd",
        left_cols,
        right_piece.reshape(span_rows, all_rows, CO),
        preferred_element_type=jnp.float32,
    )
    products = products.astype(jnp.bfloat16).reshape(own_rows, span_rows, CO * CO)
    outer_mean = (
        jnp.einsum("ijf,fc->ijc", products, outer_output_weight, preferred_element_type=jnp.float32)
        / live_count
    )
    pair_mid = pair_start + outer_mean
    out_left, out_right, out_gating = triangle_inputs(
        pair_mid, outgoing_projection_weight, outgoing_output_gate
    )
    out_product = by_channels(out_left, out_right, "cik,cjk->cij")
    pair_after_out = triangle_finish(pair_mid, out_product, out_gating, outgoing_output_weight)
    in_left, in_right, in_gating = triangle_inputs(
        pair_after_out, incoming_projection_weight, incoming_output_gate
    )
    in_product = by_channels(in_left, in_right, "cki,ckj->cij")
    pair_after_in = triangle_finish(pair_after_out, in_product, in_gating, incoming_output_weight)
    pair_expanded = jax.nn.relu(
        jnp.einsum(
            "ijc,cf->ijf",
            layer_normalize(pair_after_in).astype(jnp.bfloat16),
            pair_transition_up,
            preferred_element_type=jnp.float32,
        )
    ).astype(jnp.bfloat16)
    pair_state_output = (
        pair_after_in
        + jnp.einsum(
            "ijf,fc->ijc", pair_expanded, pair_transition_down, preferred_element_type=jnp.float32
        )
    ).astype(jnp.bfloat16)
    return (result, pair_state_output)


def solution(mesh):
    in_specs = (
        P(("grp", "dap"), None, None),
        P(("grp", "dap"), None, None),
        P("grp"),
        P("grp"),
        P("grp"),
        P(),
        P(),
        P(),
        P(),
        P(),
        P(),
        P(),
        P(),
        P(),
        P(),
        P(),
        P(),
        P(),
        P(),
        P(),
        P(),
        P(),
    )
    out_specs = (P("grp", "dap", None), P(("grp", "dap"), None, None))
    return jax.shard_map(local, mesh=mesh, in_specs=in_specs, out_specs=out_specs, check_vma=False)
```

```python
import jax
import jax.numpy as jnp
from jax import lax
from jax.experimental import pallas as pl
from jax.experimental.pallas import tpu as pltpu
from jax.sharding import PartitionSpec as P

HM = 8
HEAD_SIZE = 32
CO = 32
MAXREL = 32
NBINS = 66


EPSILON = 1e-05


def layer_normalize(values):
    center = jnp.mean(values, axis=-1, keepdims=True)
    shifted = values - center
    spread = jnp.mean(shifted * shifted, axis=-1, keepdims=True)
    return shifted * lax.rsqrt(spread + EPSILON)


def triangle_inputs(pair_now, weight, gate_weight):
    normed = layer_normalize(pair_now).astype(jnp.bfloat16)
    combined = jnp.einsum("ijc,cf->fij", normed, weight, preferred_element_type=jnp.float32)
    hidden_width = weight.shape[1] // 4
    left_side = (
        jax.nn.sigmoid(combined[hidden_width : 2 * hidden_width]) * combined[:hidden_width]
    ).astype(jnp.bfloat16)
    right_side = (
        jax.nn.sigmoid(combined[3 * hidden_width :]) * combined[2 * hidden_width : 3 * hidden_width]
    ).astype(jnp.bfloat16)
    gating = jax.nn.sigmoid(
        jnp.einsum("ijc,cd->ijd", normed, gate_weight, preferred_element_type=jnp.float32)
    )
    return (left_side, right_side, gating)


def triangle_finish(pair_now, product, gating, final_weight):
    product = lax.optimization_barrier(product)
    normed = layer_normalize(product.transpose(1, 2, 0).astype(jnp.float32)).astype(jnp.bfloat16)
    return pair_now + gating * jnp.einsum(
        "ijc,cd->ijd", normed, final_weight, preferred_element_type=jnp.float32
    )


def by_channels(left_side, right_side, form):
    both = jnp.stack([left_side, right_side])
    both = lax.all_to_all(both, "dap", split_axis=1, concat_axis=2, tiled=True)
    partial_out = jnp.einsum(form, both[0], both[1], preferred_element_type=jnp.float32)
    return lax.all_to_all(
        partial_out.astype(jnp.bfloat16), "dap", split_axis=1, concat_axis=0, tiled=True
    )


def gather_doubling(block):
    shard_pieces = lax.axis_size("dap")
    place = lax.axis_index("dap")
    held = block
    depth = 0
    bit = shard_pieces // 2
    while bit:
        other = lax.ppermute(held, "dap", [(q, q ^ bit) for q in range(shard_pieces)])
        upper = (place & bit) != 0
        first = jnp.where(upper, other, held)
        second = jnp.where(upper, held, other)
        held = jnp.stack([first, second], axis=depth)
        depth += 1
        bit //= 2
    return held.reshape((shard_pieces,) + block.shape)


LANES = 128


def gate_curve(values):
    return 0.5 + 0.5 * jnp.tanh(0.5 * values)


def normalize_channels(values):
    center = jnp.mean(values, axis=0, keepdims=True)
    shifted = values - center
    spread = jnp.mean(shifted * shifted, axis=0, keepdims=True)
    return (shifted * lax.rsqrt(spread + EPSILON)).astype(jnp.bfloat16)


def mix(weight, values):
    return jnp.dot(weight, values, preferred_element_type=jnp.float32)


def fold_halves(first_even, second_even, first_odd, second_odd, low_half):
    straight = jnp.where(low_half, first_even, second_odd)
    crossed = jnp.where(low_half, second_even, first_odd)
    return straight + pltpu.roll(crossed, LANES // 2, 1)


def transpose_blocks(ref):
    rows, columns = ref.shape
    return jnp.concatenate(
        [
            jnp.concatenate(
                [
                    ref[a : a + LANES, b : b + LANES].astype(jnp.float32).T.astype(jnp.bfloat16)
                    for a in range(0, rows, LANES)
                ],
                axis=1,
            )
            for b in range(0, columns, LANES)
        ],
        axis=0,
    )


def start_copies(sources, landed, arrived):
    copies = [
        pltpu.make_async_copy(source, landed[k], arrived.at[k]) for k, source in enumerate(sources)
    ]
    for copy in copies:
        copy.start()
    return copies


FIRSTS = (0, 4, 2, 6)


def start_kernel(place_ref, live_ref, bins_ref, table_ref, *rest):
    part_refs, core_refs, pair_refs, sources = rest[:4], rest[4:8], rest[8:12], rest[12:15]
    pair_mid_ref, left_ref, gating_ref, right_ref = rest[15:19]
    wide_ref, right_cols_ref, mean_wide_ref, mean_weight_ref, table_wide_ref = rest[19:24]
    stack_refs, landed, arrived = rest[24:26], rest[26:29], rest[29]
    copies = start_copies(sources, landed, arrived)
    place = place_ref[0]
    inverse_live = 1.0 / jnp.sum(live_ref[...], axis=1, keepdims=True)
    half = LANES // 2
    channel = lax.broadcasted_iota(jnp.int32, (LANES, LANES), 0)
    table_wide_ref[...] = jnp.zeros_like(table_wide_ref)
    table_wide_ref[0:NBINS, :] = table_ref[...].astype(jnp.float32)
    table = table_wide_ref[...].T.astype(jnp.bfloat16)
    low_half = lax.broadcasted_iota(jnp.int32, (LANES, LANES), 1) < half

    for g in range(4):
        for m in range(2):
            device = place ^ FIRSTS[g] ^ (8 * m)
            for part, owner in ((part_refs[g], device), (core_refs[g], device ^ 1)):
                wide_ref[pl.ds(pl.multiple_of(owner * 128, 128), 128), :] = part[
                    m, 128:256, :
                ].astype(jnp.float32)
    for d in range(0, CO, 2):
        rows = [
            wide_ref[pl.ds(par * CO + d + e, 32, stride=2 * CO), :]
            for e in range(2)
            for par in range(2)
        ]
        right_cols_ref[:, d * half : d * half + LANES] = (
            jnp.concatenate(rows, axis=0).T.astype(jnp.bfloat16)
        )

    for copy in copies:
        copy.wait()
    mean_wide_ref[...] = landed[0][...].astype(jnp.float32)
    for e in range(2):
        for block in range(4):
            rows = [
                mean_wide_ref[pl.ds(2 * (4 * block + k) + e, CO, stride=CO), :] for k in range(4)
            ]
            mean_weight_ref[e * LANES : (e + 1) * LANES, block * LANES : (block + 1) * LANES] = (
                jnp.concatenate(rows, axis=0).T.astype(jnp.bfloat16)
            )
    out_mix = transpose_blocks(landed[1])
    out_gate = transpose_blocks(landed[2])

    for g in range(4):
        stack_ref = stack_refs[g % 2]
        left_rows = part_refs[g][:, 0:128, :].reshape(256, LANES)
        outer = mix(left_rows, right_cols_ref[...]).astype(jnp.bfloat16)
        for i in range(8):
            for d in range(16):
                stack_ref[d * 32 : (d + 1) * 32, i * LANES : (i + 1) * LANES] = outer[
                    i * 32 : (i + 1) * 32, d * LANES : (d + 1) * LANES
                ]
        mixed = mix(mean_weight_ref[...], stack_ref[...])
        slabs = []
        places = []
        devices = [place ^ FIRSTS[g] ^ (8 * m) for m in range(2)]
        one_hot = [
            (channel == bins_ref[pl.ds(2 * devices[q // 2] + q % 2, 1), :]).astype(jnp.float32)
            for q in range(4)
        ]
        embedding = mix(table, jnp.concatenate(one_hot, axis=1).astype(jnp.bfloat16))
        for q in range(4):
            device = devices[q // 2]
            here = 2 * (device // 2) + q % 2
            even = slice(2 * q * LANES, (2 * q + 1) * LANES)
            odd = slice((2 * q + 1) * LANES, (2 * q + 2) * LANES)
            outer_mean = fold_halves(
                mixed[0:128, even], mixed[0:128, odd], mixed[128:256, even], mixed[128:256, odd], low_half
            )
            start = pair_refs[g][q // 2, q % 2].astype(jnp.float32)
            start = start + embedding[:, q * LANES : (q + 1) * LANES]
            slab = start + outer_mean * inverse_live
            pair_mid_ref[here] = slab
            slabs.append(normalize_channels(slab))
            places.append(here)
        normed = jnp.concatenate(slabs, axis=1)
        combined = mix(out_mix, normed)
        left = gate_curve(combined[128:256]) * combined[0:128]
        right = gate_curve(combined[384:512]) * combined[256:384]
        gating = gate_curve(mix(out_gate, normed))
        for q in range(4):
            lanes = slice(q * LANES, (q + 1) * LANES)
            rows = pl.ds(pl.multiple_of(places[q] * 128, 128), 128)
            left_ref[rows, :] = left[:, lanes]
            right_ref[rows, :] = right[:, lanes].astype(jnp.bfloat16)
            gating_ref[places[q]] = gating[:, lanes]


def triangle_kernel(
    place_ref,
    pair_mid_ref,
    left_ref,
    gating_ref,
    right_own_ref,
    right_other_ref,
    *rest,
):
    sources, (own_pair_ref, own_part_ref, other_part_ref) = rest[:6], rest[6:9]
    narrow_ref, wide_out_ref = rest[9:11]
    right_ref, product_ref, pair_now_ref, chosen_ref, own_left_ref, own_product_ref = rest[11:17]
    landed, arrived = rest[17:23], rest[23]
    copies = start_copies(sources, landed, arrived)
    place = place_ref[0]
    core = place % 2
    half = LANES // 2
    low_half = lax.broadcasted_iota(jnp.int32, (LANES, LANES), 1) < half
    low_short = lax.broadcasted_iota(jnp.int32, (32, LANES), 1) < half
    for chip in range(8):
        for source, side in ((right_own_ref, core), (right_other_ref, 1 - core)):
            rows = pl.ds(pl.multiple_of((4 * chip + 2 * side) * 128, 256), 256)
            right_ref[rows, :] = source[chip * 256 : (chip + 1) * 256, :].astype(jnp.float32)

    nothing = jnp.zeros((32, LANES), jnp.bfloat16)

    def outgoing_channels(block, carry):
        for e in range(32):
            c = block * 32 + e
            left = left_ref[pl.ds(c, 16, stride=128), :].astype(jnp.bfloat16)
            right = right_ref[pl.ds(c, 32, stride=128), :]
            moved = pltpu.roll(right, half, 1).astype(jnp.bfloat16)
            right = right.astype(jnp.bfloat16)
            spread = jnp.concatenate(
                [
                    jnp.where(low_short, right, nothing),
                    jnp.where(low_short, moved, nothing),
                    jnp.where(low_short, nothing, moved),
                    jnp.where(low_short, nothing, right),
                ],
                axis=0,
            )
            product_ref[pl.ds(c, 16, stride=128), :] = contract_last(left, spread)
        return carry

    lax.fori_loop(0, 4, outgoing_channels, 0)

    for copy in copies:
        copy.wait()
    out_final = transpose_blocks(landed[0])
    in_mix = transpose_blocks(landed[1])
    narrow_ref[0:128, :] = transpose_blocks(landed[3])
    narrow_ref[128:256, :] = transpose_blocks(landed[2])
    narrow_ref[256:768, :] = transpose_blocks(landed[4])
    wide_out_ref[...] = transpose_blocks(landed[5])

    column = lax.broadcasted_iota(jnp.int32, (1, 256), 1)
    which = column // 16
    residue = which % 4
    device = place ^ ((which // 4) % 2)
    wanted = half * (which // 8) + 32 * (residue % 2) + 2 * device + residue // 2
    slab_of = column % 16
    source_lane = lax.broadcasted_iota(jnp.int32, (LANES, 256), 0)
    for g in range(4):
        products = [
            normalize_channels(product_ref[(4 * g + q) * 128 : (4 * g + q + 1) * 128, :])
            for q in range(4)
        ]
        finished = mix(out_final, jnp.concatenate(products, axis=1))
        slabs = []
        picks = []
        for q in range(4):
            h = 4 * g + q
            lanes = slice(q * LANES, (q + 1) * LANES)
            slab = pair_mid_ref[h] + gating_ref[h] * finished[:, lanes]
            pair_now_ref[h] = slab
            slabs.append(normalize_channels(slab))
            here = jnp.where(slab_of == h, wanted, -1)
            picks.append((source_lane == here).astype(jnp.float32).astype(jnp.bfloat16))
        normed = jnp.concatenate(slabs, axis=1)
        chosen = mix(normed, jnp.concatenate(picks, axis=0))
        if g:
            chosen_ref[...] += chosen
        else:
            chosen_ref[...] = chosen
        combined = mix(in_mix[256:512], normed)
        right = gate_curve(combined[128:256]) * combined[0:128]
        for q in range(4):
            right_ref[(4 * g + q) * 128 : (4 * g + q + 1) * 128, :] = right[
                :, q * LANES : (q + 1) * LANES
            ]
    for t in range(2):
        own_pair_ref[t] = pair_now_ref[2 * (place // 2) + t]

    combined = mix(in_mix[0:256], chosen_ref[...].astype(jnp.bfloat16))
    own_left = gate_curve(combined[128:256]) * combined[0:128]
    for m in range(16):
        part = own_left[:, (m // 8) * LANES : (m // 8 + 1) * LANES]
        if m % 8:
            part = pltpu.roll(part, LANES - 16 * (m % 8), 1)
        own_left_ref[m * 128 : (m + 1) * 128, :] = part

    def incoming_channels(block, carry):
        for e in range(32):
            c = block * 32 + e
            left = own_left_ref[pl.ds(c, 16, stride=128), :][:, 0:16].astype(jnp.bfloat16)
            right = right_ref[pl.ds(c, 16, stride=128), :].astype(jnp.bfloat16)
            own_product_ref[pl.ds(c, 16, stride=128), :] = mix(left, right)
        return carry

    lax.fori_loop(0, 4, incoming_channels, 0)

    def block_of(b, e, residue):
        m = 8 * b + 4 * e + residue
        return own_product_ref[m * 128 : (m + 1) * 128, :]

    for e, target in ((0, own_part_ref), (1, other_part_ref)):
        for t in range(2):
            target[t] = fold_halves(
                block_of(0, e, 2 * t),
                block_of(0, e, 2 * t + 1),
                block_of(1, e, 2 * t),
                block_of(1, e, 2 * t + 1),
                low_half,
            )


def finish_kernel(own_pair_ref, own_part_ref, other_part_ref, narrow_ref, down_ref, result_ref):
    products = [normalize_channels(own_part_ref[t] + other_part_ref[t]) for t in range(2)]
    finished = mix(narrow_ref[0:128, :], jnp.concatenate(products, axis=1))
    own_pair = jnp.concatenate([own_pair_ref[t] for t in range(2)], axis=1)
    gating = gate_curve(mix(narrow_ref[128:256, :], normalize_channels(own_pair)))
    own_pair = own_pair + gating * finished
    hidden = jnp.maximum(mix(narrow_ref[256:768, :], normalize_channels(own_pair)), 0.0)
    own_pair = own_pair + mix(down_ref[...], hidden.astype(jnp.bfloat16))
    own_pair = own_pair.astype(jnp.bfloat16)
    order = lane_order_matrix()
    for t in range(2):
        result_ref[t * 128 : (t + 1) * 128, :] = contract_last(
            order, own_pair[:, t * LANES : (t + 1) * LANES]
        ).astype(jnp.bfloat16)


def lane_order_matrix():
    half = LANES // 2
    member = lax.broadcasted_iota(jnp.int32, (LANES, LANES), 0)
    lane = lax.broadcasted_iota(jnp.int32, (LANES, LANES), 1)
    back = half * (member // half) + 32 * (member % 2) + (member % half) // 2
    return (lane == back).astype(jnp.float32).astype(jnp.bfloat16)


def contract_first(first, second):
    return lax.dot_general(
        first, second, (((0,), (0,)), ((), ())), preferred_element_type=jnp.float32
    )


def rows_kernel(rows_ref, pair_ref, blocks_ref, own_pair_ref, wide_ref):
    order = lane_order_matrix()
    for t in range(2):
        own_pair_ref[t] = contract_first(
            pair_ref[2 * t : 2 * t + 2].reshape(LANES, LANES), order
        ).astype(jnp.bfloat16)
    residues = rows_ref.shape[1]
    count = 8 * residues
    rows = rows_ref[...].astype(jnp.float32).reshape(count, 2 * LANES)
    for e in range(2):
        wide_ref[e * count : (e + 1) * count, :] = rows[:, e * LANES : (e + 1) * LANES]
    for p in range(16):
        for e in range(2):
            block = [
                wide_ref[pl.ds(e * count + 4 * p + i, 8, stride=residues), :] for i in range(4)
            ]
            blocks_ref[p, :, e * LANES : (e + 1) * LANES] = jnp.concatenate(block, axis=0).astype(
                jnp.bfloat16
            )


def normalize_rows(values):
    center = jnp.mean(values, axis=1, keepdims=True)
    shifted = values - center
    spread = jnp.mean(shifted * shifted, axis=1, keepdims=True)
    return (shifted * lax.rsqrt(spread + EPSILON)).astype(jnp.bfloat16)


def contract_last(first, second):
    return lax.dot_general(
        first, second, (((1,), (1,)), ((), ())), preferred_element_type=jnp.float32
    )


def msa_kernel(
    live_ref,
    blocks_ref,
    query_ref,
    key_ref,
    value_gate_ref,
    output_ref,
    up_ref,
    down_ref,
    outer_ref,
    result_ref,
    parts_ref,
    wide_ref,
    attended_ref,
    final_ref,
    *landed,
):
    copies = start_copies((output_ref, up_ref, down_ref), landed, landed[3])
    output_ref, up_ref, down_ref = landed[:3]
    for p in range(16):
        block = blocks_ref[p].astype(jnp.float32)
        for i in range(4):
            wide_ref[i * 128 + p * 8 : i * 128 + p * 8 + 8, :] = block[i * 8 : i * 8 + 8, :]
    live = live_ref[...]
    alive = live > 0.0
    width = HM * HEAD_SIZE
    head_of = lax.broadcasted_iota(jnp.int32, (128, width), 1) // HEAD_SIZE
    zero = jnp.zeros((128, width), jnp.bfloat16)
    one = jnp.ones((128, width), jnp.bfloat16)

    def by_head(values):
        return jnp.concatenate([jnp.where(head_of == h, values, zero) for h in range(HM)], axis=0)

    heads = by_head(one)
    normed = normalize_rows(wide_ref[...])
    query = (mix(normed, query_ref[...]) * HEAD_SIZE ** (-0.5)).astype(jnp.bfloat16)
    key = mix(normed, key_ref[...]).astype(jnp.bfloat16)
    value_gate = mix(normed, value_gate_ref[...])
    value = value_gate[:, :width].astype(jnp.bfloat16)
    for i in range(4):
        rows = slice(i * 128, (i + 1) * 128)
        scores = contract_last(query[rows], by_head(key[rows]))
        raised = []
        for h in range(HM):
            score = jnp.where(alive, scores[:, h * 128 : (h + 1) * 128], -1000000000.0)
            raised.append(jnp.exp(score - jnp.max(score, axis=1, keepdims=True)).astype(jnp.bfloat16))
        raised = jnp.concatenate(raised, axis=1)
        attended_ref[rows, :] = mix(raised, by_head(value[rows])) / mix(raised, heads)
    gated = (gate_curve(value_gate[:, width:]) * attended_ref[...]).astype(jnp.bfloat16)
    for copy in copies:
        copy.wait()
    current = wide_ref[...] + mix(gated, output_ref[...])
    hidden = jnp.maximum(mix(normalize_rows(current), up_ref[...]), 0.0).astype(jnp.bfloat16)
    final = (current + mix(hidden, down_ref[...])).astype(jnp.bfloat16).astype(jnp.float32)
    outer = contract_last(outer_ref[...], normalize_rows(final))
    for i in range(4):
        rows = slice(i * 128, (i + 1) * 128)
        part = (outer[:, rows] * live).astype(jnp.bfloat16)
        parts_ref[i * CO : (i + 1) * CO, :] = part[:CO, :]
        parts_ref[128 + i * CO : 128 + (i + 1) * CO, :] = part[CO:, :]
        final_ref[pl.ds(i, 128, stride=4), :] = final[rows, :128]
        final_ref[pl.ds(512 + i, 128, stride=4), :] = final[rows, 128:]
    result_ref[:, :128] = final_ref[:512, :].astype(jnp.bfloat16)
    result_ref[:, 128:] = final_ref[512:, :].astype(jnp.bfloat16)


def exchange(values, offset):
    pieces = lax.axis_size("dap")
    return lax.ppermute(values, "dap", [(q, q ^ offset) for q in range(pieces)])


def whole_block(
    alignment_input,
    pair_state_input,
    bin_all,
    live_row_float,
    relative_position_table,
    column_query_weight,
    column_key_weight,
    column_value_gate_weight,
    column_output_weight,
    alignment_transition_up,
    alignment_transition_down,
    outer_input_weight,
    *pair_weights,
):
    channels = alignment_input.shape[2]
    width = pair_state_input.shape[2]
    place = lax.axis_index("dap").astype(jnp.int32).reshape(1)
    vmem = pl.BlockSpec(memory_space=pltpu.VMEM)
    smem = pl.BlockSpec(memory_space=pltpu.SMEM)
    hbm = pl.BlockSpec(memory_space=pltpu.HBM)

    def array(*shape, dtype=jnp.bfloat16):
        return jax.ShapeDtypeStruct(shape, dtype)

    def wide(*shape):
        return jax.ShapeDtypeStruct(shape, jnp.float32)

    def limit(mebibytes):
        return pltpu.CompilerParams(vmem_limit_bytes=mebibytes * 1024 * 1024)

    blocks, own_pair = pl.pallas_call(
        rows_kernel,
        out_shape=[array(16, 32, channels), array(2, width, LANES)],
        in_specs=[vmem, vmem],
        out_specs=[vmem, vmem],
        scratch_shapes=[pltpu.VMEM((1024, LANES), jnp.float32)],
        compiler_params=limit(16),
        name="rows_by_device",
    )(alignment_input, pair_state_input)
    blocks = lax.all_to_all(blocks, "dap", split_axis=0, concat_axis=0, tiled=True)

    pair_first = jnp.stack([own_pair, exchange(own_pair, 8)])
    pair_second = exchange(pair_first, 4)
    blocks, pair_first, pair_second = lax.optimization_barrier((blocks, pair_first, pair_second))
    pair_pieces = [pair_first, pair_second, exchange(pair_first, 2), exchange(pair_second, 2)]

    result, parts = pl.pallas_call(
        msa_kernel,
        out_shape=(array(512, channels), array(256, LANES)),
        in_specs=[vmem] * 5 + [hbm] * 3 + [vmem],
        out_specs=(vmem, vmem),
        scratch_shapes=[
            pltpu.VMEM((512, channels), jnp.float32),
            pltpu.VMEM((512, channels), jnp.float32),
            pltpu.VMEM((1024, LANES), jnp.float32),
            pltpu.VMEM(column_output_weight.shape, jnp.bfloat16),
            pltpu.VMEM(alignment_transition_up.shape, jnp.bfloat16),
            pltpu.VMEM(alignment_transition_down.shape, jnp.bfloat16),
            pltpu.SemaphoreType.DMA((3,)),
        ],
        compiler_params=limit(54),
        cost_estimate=pl.CostEstimate(
            flops=2_000_000_000, bytes_accessed=10_000_000, transcendentals=1_000_000
        ),
        name="msa_whole",
    )(
        live_row_float.reshape(1, LANES),
        blocks,
        column_query_weight,
        column_key_weight,
        column_value_gate_weight,
        column_output_weight,
        alignment_transition_up,
        alignment_transition_down,
        outer_input_weight.T,
    )
    parts, pair_pieces = lax.optimization_barrier((parts, pair_pieces))
    first = jnp.stack([parts, exchange(parts, 8)])
    second = exchange(first, 4)
    pieces = [first, second, exchange(first, 2), exchange(second, 2)]
    core_pieces = [exchange(piece, 1) for piece in pieces]

    slabs = (16, 128, LANES)
    tall = (16 * 128, LANES)
    pair_mid, left, gating, right = pl.pallas_call(
        start_kernel,
        out_shape=[wide(*slabs), wide(*tall), wide(*slabs), array(*tall)],
        in_specs=[smem] + [vmem] * 15 + [hbm] * 3,
        out_specs=[vmem] * 4,
        scratch_shapes=[
            pltpu.VMEM((2048, LANES), jnp.float32),
            pltpu.VMEM((128, 2048), jnp.bfloat16),
            pltpu.VMEM((1024, LANES), jnp.float32),
            pltpu.VMEM((256, 512), jnp.bfloat16),
            pltpu.VMEM((LANES, LANES), jnp.float32),
            pltpu.VMEM((512, 1024), jnp.bfloat16),
            pltpu.VMEM((512, 1024), jnp.bfloat16),
        ]
        + [pltpu.VMEM(w.shape, jnp.bfloat16) for w in pair_weights[:3]]
        + [pltpu.SemaphoreType.DMA((3,))],
        compiler_params=limit(48),
        name="pair_start",
    )(
        place,
        live_row_float.reshape(1, LANES),
        lanes_order(bin_all).reshape(32, LANES),
        relative_position_table,
        *pieces,
        *core_pieces,
        *pair_pieces,
        *pair_weights[:3],
    )
    own_pair, own_part, other_part, narrow_weights, down_weight = pl.pallas_call(
        triangle_kernel,
        out_shape=[wide(2, 128, LANES)] * 3 + [array(768, LANES), array(128, 512)],
        in_specs=[smem] + [vmem] * 5 + [hbm] * 6,
        out_specs=[vmem] * 5,
        scratch_shapes=[
            pltpu.VMEM((32 * 128, LANES), jnp.float32),
            pltpu.VMEM(tall, jnp.float32),
            pltpu.VMEM(slabs, jnp.float32),
            pltpu.VMEM((128, 256), jnp.float32),
            pltpu.VMEM(tall, jnp.float32),
            pltpu.VMEM(tall, jnp.float32),
        ]
        + [pltpu.VMEM(w.shape, jnp.bfloat16) for w in pair_weights[3:]]
        + [pltpu.SemaphoreType.DMA((6,))],
        compiler_params=limit(48),
        name="pair_triangles",
    )(place, pair_mid, left, gating, right, exchange(right, 1), *pair_weights[3:])
    pair_output = pl.pallas_call(
        finish_kernel,
        out_shape=array(256, LANES),
        in_specs=[vmem] * 5,
        out_specs=vmem,
        compiler_params=limit(16),
        name="pair_finish",
    )(own_pair, own_part, exchange(other_part, 1), narrow_weights, down_weight)
    return result.reshape(128, 4, channels), pair_output.reshape(pair_state_input.shape)


def lanes_order(values):
    lead = values.shape[:-1]
    halves = values.reshape(lead + (values.shape[-1] // 2, 2))
    return jnp.swapaxes(halves, -1, -2).reshape(values.shape)


def local(
    alignment_input,
    pair_state_input,
    residue_number_index,
    chain_label,
    alignment_row_mask,
    relative_position_table,
    column_query_weight,
    column_key_weight,
    column_value_gate_weight,
    column_output_weight,
    alignment_transition_up,
    alignment_transition_down,
    outer_input_weight,
    outer_output_weight,
    outgoing_projection_weight,
    outgoing_output_gate,
    outgoing_output_weight,
    incoming_projection_weight,
    incoming_output_gate,
    incoming_output_weight,
    pair_transition_up,
    pair_transition_down,
):
    shard_pieces = lax.axis_size("dap")
    own_rows = pair_state_input.shape[0]
    residue_count = pair_state_input.shape[1]
    channel_count = alignment_input.shape[2]
    head_width = HM * HEAD_SIZE
    first_row = lax.axis_index("dap") * own_rows
    own_index = lax.dynamic_slice_in_dim(residue_number_index, first_row, own_rows)
    own_chain = lax.dynamic_slice_in_dim(chain_label, first_row, own_rows)

    def bins_of(index, chain):
        offset = index[:, None] - residue_number_index[None, :]
        return jnp.where(
            chain[:, None] == chain_label[None, :],
            jnp.clip(offset + MAXREL, 0, 2 * MAXREL),
            2 * MAXREL + 1,
        )

    bin_index = bins_of(own_index, own_chain)
    one_hot = (bin_index[:, :, None] == jnp.arange(NBINS, dtype=jnp.int32)[None, None, :]).astype(
        jnp.bfloat16
    )
    pair_start = pair_state_input.astype(jnp.float32) + jnp.einsum(
        "ijb,bc->ijc", one_hot, relative_position_table, preferred_element_type=jnp.float32
    )
    live_rows = alignment_row_mask > 0
    live_row_float = live_rows.astype(jnp.float32)

    if alignment_row_mask.shape[0] == LANES and 2 * residue_count == LANES and own_rows == 4:
        return whole_block(
            alignment_input,
            pair_state_input,
            bins_of(residue_number_index, chain_label),
            live_row_float,
            relative_position_table,
            column_query_weight,
            column_key_weight,
            column_value_gate_weight,
            column_output_weight,
            alignment_transition_up,
            alignment_transition_down,
            outer_input_weight,
            outer_output_weight,
            outgoing_projection_weight,
            outgoing_output_gate,
            outgoing_output_weight,
            incoming_projection_weight,
            incoming_output_gate,
            incoming_output_weight,
            pair_transition_up,
            pair_transition_down,
        )

    def attend_one(operands):
        query_col, key_col, value_col = operands
        scores = jnp.einsum("shd,thd->hst", query_col, key_col, preferred_element_type=jnp.float32)
        scores = jnp.where(live_rows[None, None, :], scores, -1000000000.0)
        row_top = jnp.max(scores, axis=-1, keepdims=True)
        raised = jnp.exp(scores - row_top)
        attention = (raised / jnp.sum(raised, axis=-1, keepdims=True)).astype(jnp.bfloat16)
        return jnp.einsum("hst,thd->shd", attention, value_col, preferred_element_type=jnp.float32)

    blocked_view = alignment_input.reshape(
        alignment_input.shape[0], shard_pieces, residue_count // shard_pieces, channel_count
    )
    block_in = lax.all_to_all(blocked_view, "dap", split_axis=1, concat_axis=0, tiled=True)
    depth_rows = block_in.shape[0]
    count_cols = block_in.shape[2]
    current = block_in.reshape(depth_rows, count_cols, channel_count).astype(jnp.float32)
    normed = layer_normalize(current).astype(jnp.bfloat16)
    query_rows = (
        jnp.einsum("sic,ce->sie", normed, column_query_weight, preferred_element_type=jnp.float32)
        * HEAD_SIZE ** (-0.5)
    ).astype(jnp.bfloat16)
    key_row_block = jnp.einsum(
        "sic,ce->sie", normed, column_key_weight, preferred_element_type=jnp.float32
    ).astype(jnp.bfloat16)
    value_gate_pair = jnp.einsum(
        "sic,ce->sie", normed, column_value_gate_weight, preferred_element_type=jnp.float32
    )
    value_rows = value_gate_pair[..., :head_width].astype(jnp.bfloat16)

    def by_column(values):
        return values.transpose(1, 0, 2).reshape(count_cols, depth_rows, HM, HEAD_SIZE)

    attended = lax.map(
        attend_one, (by_column(query_rows), by_column(key_row_block), by_column(value_rows))
    )
    attended = attended.reshape(count_cols, depth_rows, head_width).transpose(1, 0, 2)
    gated_out = (jax.nn.sigmoid(value_gate_pair[..., head_width:]) * attended).astype(jnp.bfloat16)
    current = current + jnp.einsum(
        "sie,ec->sic", gated_out, column_output_weight, preferred_element_type=jnp.float32
    )
    hidden = jax.nn.relu(
        jnp.einsum(
            "sic,cf->sif",
            layer_normalize(current).astype(jnp.bfloat16),
            alignment_transition_up,
            preferred_element_type=jnp.float32,
        )
    ).astype(jnp.bfloat16)
    current = current + jnp.einsum(
        "sif,fc->sic", hidden, alignment_transition_down, preferred_element_type=jnp.float32
    )
    result = current.astype(jnp.bfloat16)
    outer_product_input = jnp.einsum(
        "sic,cf->sif",
        layer_normalize(result.astype(jnp.float32)).astype(jnp.bfloat16),
        outer_input_weight,
        preferred_element_type=jnp.float32,
    )
    outer_product_input = outer_product_input * live_row_float[:, None, None]
    left_part = outer_product_input[..., :CO].astype(jnp.bfloat16)
    right_part = outer_product_input[..., CO:].astype(jnp.bfloat16)
    all_rows = result.shape[0]
    left_cols = left_part.transpose(1, 0, 2)
    right_cols = right_part.transpose(1, 0, 2).reshape(own_rows, all_rows * CO)
    live_count = jnp.sum(live_row_float)
    right_piece = gather_doubling(right_cols).reshape(-1, all_rows * CO)
    span_rows = right_piece.shape[0]
    products = jnp.einsum(
        "isc,jsd->ijcd",
        left_cols,
        right_piece.reshape(span_rows, all_rows, CO),
        preferred_element_type=jnp.float32,
    )
    products = products.astype(jnp.bfloat16).reshape(own_rows, span_rows, CO * CO)
    outer_mean = (
        jnp.einsum("ijf,fc->ijc", products, outer_output_weight, preferred_element_type=jnp.float32)
        / live_count
    )
    pair_mid = pair_start + outer_mean
    out_left, out_right, out_gating = triangle_inputs(
        pair_mid, outgoing_projection_weight, outgoing_output_gate
    )
    out_product = by_channels(out_left, out_right, "cik,cjk->cij")
    pair_after_out = triangle_finish(pair_mid, out_product, out_gating, outgoing_output_weight)
    in_left, in_right, in_gating = triangle_inputs(
        pair_after_out, incoming_projection_weight, incoming_output_gate
    )
    in_product = by_channels(in_left, in_right, "cki,ckj->cij")
    pair_after_in = triangle_finish(pair_after_out, in_product, in_gating, incoming_output_weight)
    pair_expanded = jax.nn.relu(
        jnp.einsum(
            "ijc,cf->ijf",
            layer_normalize(pair_after_in).astype(jnp.bfloat16),
            pair_transition_up,
            preferred_element_type=jnp.float32,
        )
    ).astype(jnp.bfloat16)
    pair_state_output = (
        pair_after_in
        + jnp.einsum(
            "ijf,fc->ijc", pair_expanded, pair_transition_down, preferred_element_type=jnp.float32
        )
    ).astype(jnp.bfloat16)
    return (result, pair_state_output)


def solution(mesh):
    in_specs = (
        P(("grp", "dap"), None, None),
        P(("grp", "dap"), None, None),
        P("grp"),
        P("grp"),
        P("grp"),
        P(),
        P(),
        P(),
        P(),
        P(),
        P(),
        P(),
        P(),
        P(),
        P(),
        P(),
        P(),
        P(),
        P(),
        P(),
        P(),
        P(),
    )
    out_specs = (P("grp", "dap", None), P(("grp", "dap"), None, None))
    return jax.shard_map(local, mesh=mesh, in_specs=in_specs, out_specs=out_specs, check_vma=False)
```

```python
import jax
import jax.numpy as jnp
from jax import lax
from jax.experimental import pallas as pl
from jax.experimental.pallas import tpu as pltpu
from jax.sharding import PartitionSpec as P

HM = 8
HEAD_SIZE = 32
CO = 32
MAXREL = 32
NBINS = 66


EPSILON = 1e-05


def layer_normalize(values):
    center = jnp.mean(values, axis=-1, keepdims=True)
    shifted = values - center
    spread = jnp.mean(shifted * shifted, axis=-1, keepdims=True)
    return shifted * lax.rsqrt(spread + EPSILON)


def triangle_inputs(pair_now, weight, gate_weight):
    normed = layer_normalize(pair_now).astype(jnp.bfloat16)
    combined = jnp.einsum("ijc,cf->fij", normed, weight, preferred_element_type=jnp.float32)
    hidden_width = weight.shape[1] // 4
    left_side = (
        jax.nn.sigmoid(combined[hidden_width : 2 * hidden_width]) * combined[:hidden_width]
    ).astype(jnp.bfloat16)
    right_side = (
        jax.nn.sigmoid(combined[3 * hidden_width :]) * combined[2 * hidden_width : 3 * hidden_width]
    ).astype(jnp.bfloat16)
    gating = jax.nn.sigmoid(
        jnp.einsum("ijc,cd->ijd", normed, gate_weight, preferred_element_type=jnp.float32)
    )
    return (left_side, right_side, gating)


def triangle_finish(pair_now, product, gating, final_weight):
    product = lax.optimization_barrier(product)
    normed = layer_normalize(product.transpose(1, 2, 0).astype(jnp.float32)).astype(jnp.bfloat16)
    return pair_now + gating * jnp.einsum(
        "ijc,cd->ijd", normed, final_weight, preferred_element_type=jnp.float32
    )


def by_channels(left_side, right_side, form):
    both = jnp.stack([left_side, right_side])
    both = lax.all_to_all(both, "dap", split_axis=1, concat_axis=2, tiled=True)
    partial_out = jnp.einsum(form, both[0], both[1], preferred_element_type=jnp.float32)
    return lax.all_to_all(
        partial_out.astype(jnp.bfloat16), "dap", split_axis=1, concat_axis=0, tiled=True
    )


def gather_doubling(block):
    shard_pieces = lax.axis_size("dap")
    place = lax.axis_index("dap")
    held = block
    depth = 0
    bit = shard_pieces // 2
    while bit:
        other = lax.ppermute(held, "dap", [(q, q ^ bit) for q in range(shard_pieces)])
        upper = (place & bit) != 0
        first = jnp.where(upper, other, held)
        second = jnp.where(upper, held, other)
        held = jnp.stack([first, second], axis=depth)
        depth += 1
        bit //= 2
    return held.reshape((shard_pieces,) + block.shape)


LANES = 128


def gate_curve(values):
    return 0.5 + 0.5 * jnp.tanh(0.5 * values)


def normalize_channels(values):
    center = jnp.mean(values, axis=0, keepdims=True)
    shifted = values - center
    spread = jnp.mean(shifted * shifted, axis=0, keepdims=True)
    return (shifted * lax.rsqrt(spread + EPSILON)).astype(jnp.bfloat16)


def mix(weight, values):
    return jnp.dot(weight, values, preferred_element_type=jnp.float32)


def fold_halves(first_even, second_even, first_odd, second_odd, low_half):
    straight = jnp.where(low_half, first_even, second_odd)
    crossed = jnp.where(low_half, second_even, first_odd)
    return straight + pltpu.roll(crossed, LANES // 2, 1)


def transpose_blocks(ref):
    rows, columns = ref.shape
    return jnp.concatenate(
        [
            jnp.concatenate(
                [
                    ref[a : a + LANES, b : b + LANES].astype(jnp.float32).T.astype(jnp.bfloat16)
                    for a in range(0, rows, LANES)
                ],
                axis=1,
            )
            for b in range(0, columns, LANES)
        ],
        axis=0,
    )


def start_copies(sources, landed, arrived):
    copies = [
        pltpu.make_async_copy(source, landed[k], arrived.at[k]) for k, source in enumerate(sources)
    ]
    for copy in copies:
        copy.start()
    return copies


FIRSTS = (0, 4, 2, 6)


def start_kernel(place_ref, live_ref, bins_ref, table_ref, *rest):
    part_refs, core_refs, pair_refs, sources = rest[:4], rest[4:8], rest[8:12], rest[12:15]
    pair_mid_ref, left_ref, gating_ref, right_ref = rest[15:19]
    wide_ref, right_cols_ref, mean_wide_ref, mean_weight_ref, table_wide_ref = rest[19:24]
    stack_refs, landed, arrived = rest[24:26], rest[26:29], rest[29]
    copies = start_copies(sources, landed, arrived)
    place = place_ref[0]
    inverse_live = 1.0 / jnp.sum(live_ref[...], axis=1, keepdims=True)
    half = LANES // 2
    channel = lax.broadcasted_iota(jnp.int32, (LANES, LANES), 0)
    table_wide_ref[...] = jnp.zeros_like(table_wide_ref)
    table_wide_ref[0:NBINS, :] = table_ref[...].astype(jnp.float32)
    table = table_wide_ref[...].T.astype(jnp.bfloat16)
    low_half = lax.broadcasted_iota(jnp.int32, (LANES, LANES), 1) < half

    for g in range(4):
        for m in range(2):
            device = place ^ FIRSTS[g] ^ (8 * m)
            for part, owner in ((part_refs[g], device), (core_refs[g], device ^ 1)):
                wide_ref[pl.ds(pl.multiple_of(owner * 128, 128), 128), :] = part[
                    m, 128:256, :
                ].astype(jnp.float32)
    for d in range(0, CO, 2):
        rows = [
            wide_ref[pl.ds(par * CO + d + e, 32, stride=2 * CO), :]
            for e in range(2)
            for par in range(2)
        ]
        right_cols_ref[:, d * half : d * half + LANES] = (
            jnp.concatenate(rows, axis=0).T.astype(jnp.bfloat16)
        )

    for copy in copies:
        copy.wait()
    mean_wide_ref[...] = landed[0][...].astype(jnp.float32)
    for e in range(2):
        for block in range(4):
            rows = [
                mean_wide_ref[pl.ds(2 * (4 * block + k) + e, CO, stride=CO), :] for k in range(4)
            ]
            mean_weight_ref[e * LANES : (e + 1) * LANES, block * LANES : (block + 1) * LANES] = (
                jnp.concatenate(rows, axis=0).T.astype(jnp.bfloat16)
            )
    out_mix = transpose_blocks(landed[1])
    out_gate = transpose_blocks(landed[2])

    for g in range(4):
        stack_ref = stack_refs[g % 2]
        left_rows = part_refs[g][:, 0:128, :].reshape(256, LANES)
        outer = mix(left_rows, right_cols_ref[...]).astype(jnp.bfloat16)
        for i in range(8):
            for d in range(16):
                stack_ref[d * 32 : (d + 1) * 32, i * LANES : (i + 1) * LANES] = outer[
                    i * 32 : (i + 1) * 32, d * LANES : (d + 1) * LANES
                ]
        mixed = mix(mean_weight_ref[...], stack_ref[...])
        slabs = []
        places = []
        devices = [place ^ FIRSTS[g] ^ (8 * m) for m in range(2)]
        one_hot = [
            (channel == bins_ref[pl.ds(2 * devices[q // 2] + q % 2, 1), :]).astype(jnp.float32)
            for q in range(4)
        ]
        embedding = mix(table, jnp.concatenate(one_hot, axis=1).astype(jnp.bfloat16))
        for q in range(4):
            device = devices[q // 2]
            here = 2 * (device // 2) + q % 2
            even = slice(2 * q * LANES, (2 * q + 1) * LANES)
            odd = slice((2 * q + 1) * LANES, (2 * q + 2) * LANES)
            outer_mean = fold_halves(
                mixed[0:128, even], mixed[0:128, odd], mixed[128:256, even], mixed[128:256, odd], low_half
            )
            start = pair_refs[g][q // 2, q % 2].astype(jnp.float32)
            start = start + embedding[:, q * LANES : (q + 1) * LANES]
            slab = start + outer_mean * inverse_live
            pair_mid_ref[here] = slab
            slabs.append(normalize_channels(slab))
            places.append(here)
        normed = jnp.concatenate(slabs, axis=1)
        combined = mix(out_mix, normed)
        left = gate_curve(combined[128:256]) * combined[0:128]
        right = gate_curve(combined[384:512]) * combined[256:384]
        gating = gate_curve(mix(out_gate, normed))
        for q in range(4):
            lanes = slice(q * LANES, (q + 1) * LANES)
            rows = pl.ds(pl.multiple_of(places[q] * 128, 128), 128)
            left_ref[rows, :] = left[:, lanes]
            right_ref[rows, :] = right[:, lanes].astype(jnp.bfloat16)
            gating_ref[places[q]] = gating[:, lanes]


def triangle_kernel(
    place_ref,
    pair_mid_ref,
    left_ref,
    gating_ref,
    right_own_ref,
    right_other_ref,
    *rest,
):
    sources, (own_pair_ref, own_part_ref, other_part_ref) = rest[:6], rest[6:9]
    narrow_ref, wide_out_ref = rest[9:11]
    right_ref, product_ref, pair_now_ref, chosen_ref, own_left_ref, own_product_ref = rest[11:17]
    landed, arrived = rest[17:23], rest[23]
    copies = start_copies(sources, landed, arrived)
    place = place_ref[0]
    core = place % 2
    half = LANES // 2
    low_half = lax.broadcasted_iota(jnp.int32, (LANES, LANES), 1) < half
    low_short = lax.broadcasted_iota(jnp.int32, (32, LANES), 1) < half
    for chip in range(8):
        for source, side in ((right_own_ref, core), (right_other_ref, 1 - core)):
            rows = pl.ds(pl.multiple_of((4 * chip + 2 * side) * 128, 256), 256)
            right_ref[rows, :] = source[chip * 256 : (chip + 1) * 256, :].astype(jnp.float32)

    nothing = jnp.zeros((32, LANES), jnp.bfloat16)

    def outgoing_channels(block, carry):
        for e in range(32):
            c = block * 32 + e
            left = left_ref[pl.ds(c, 16, stride=128), :].astype(jnp.bfloat16)
            right = right_ref[pl.ds(c, 32, stride=128), :]
            moved = pltpu.roll(right, half, 1).astype(jnp.bfloat16)
            right = right.astype(jnp.bfloat16)
            spread = jnp.concatenate(
                [
                    jnp.where(low_short, right, nothing),
                    jnp.where(low_short, moved, nothing),
                    jnp.where(low_short, nothing, moved),
                    jnp.where(low_short, nothing, right),
                ],
                axis=0,
            )
            product_ref[pl.ds(c, 16, stride=128), :] = contract_last(left, spread)
        return carry

    lax.fori_loop(0, 4, outgoing_channels, 0)

    for copy in copies:
        copy.wait()
    out_final = transpose_blocks(landed[0])
    in_mix = transpose_blocks(landed[1])
    narrow_ref[0:128, :] = transpose_blocks(landed[3])
    narrow_ref[128:256, :] = transpose_blocks(landed[2])
    narrow_ref[256:768, :] = transpose_blocks(landed[4])
    wide_out_ref[...] = transpose_blocks(landed[5])

    column = lax.broadcasted_iota(jnp.int32, (1, 256), 1)
    which = column // 16
    residue = which % 4
    device = place ^ ((which // 4) % 2)
    wanted = half * (which // 8) + 32 * (residue % 2) + 2 * device + residue // 2
    slab_of = column % 16
    source_lane = lax.broadcasted_iota(jnp.int32, (LANES, 256), 0)
    for g in range(4):
        products = [
            normalize_channels(product_ref[(4 * g + q) * 128 : (4 * g + q + 1) * 128, :])
            for q in range(4)
        ]
        finished = mix(out_final, jnp.concatenate(products, axis=1))
        slabs = []
        picks = []
        for q in range(4):
            h = 4 * g + q
            lanes = slice(q * LANES, (q + 1) * LANES)
            slab = pair_mid_ref[h] + gating_ref[h] * finished[:, lanes]
            pair_now_ref[h] = slab
            slabs.append(normalize_channels(slab))
            here = jnp.where(slab_of == h, wanted, -1)
            picks.append((source_lane == here).astype(jnp.float32).astype(jnp.bfloat16))
        normed = jnp.concatenate(slabs, axis=1)
        chosen = mix(normed, jnp.concatenate(picks, axis=0))
        if g:
            chosen_ref[...] += chosen
        else:
            chosen_ref[...] = chosen
        combined = mix(in_mix[256:512], normed)
        right = gate_curve(combined[128:256]) * combined[0:128]
        for q in range(4):
            right_ref[(4 * g + q) * 128 : (4 * g + q + 1) * 128, :] = right[
                :, q * LANES : (q + 1) * LANES
            ]
    for t in range(2):
        own_pair_ref[t] = pair_now_ref[2 * (place // 2) + t]

    combined = mix(in_mix[0:256], chosen_ref[...].astype(jnp.bfloat16))
    own_left = gate_curve(combined[128:256]) * combined[0:128]
    for m in range(16):
        part = own_left[:, (m // 8) * LANES : (m // 8 + 1) * LANES]
        if m % 8:
            part = pltpu.roll(part, LANES - 16 * (m % 8), 1)
        own_left_ref[m * 128 : (m + 1) * 128, :] = part

    def incoming_channels(block, carry):
        for e in range(32):
            c = block * 32 + e
            left = own_left_ref[pl.ds(c, 16, stride=128), :][:, 0:16].astype(jnp.bfloat16)
            right = right_ref[pl.ds(c, 16, stride=128), :].astype(jnp.bfloat16)
            own_product_ref[pl.ds(c, 16, stride=128), :] = mix(left, right)
        return carry

    lax.fori_loop(0, 4, incoming_channels, 0)

    def block_of(b, e, residue):
        m = 8 * b + 4 * e + residue
        return own_product_ref[m * 128 : (m + 1) * 128, :]

    for e, target in ((0, own_part_ref), (1, other_part_ref)):
        for t in range(2):
            target[t] = fold_halves(
                block_of(0, e, 2 * t),
                block_of(0, e, 2 * t + 1),
                block_of(1, e, 2 * t),
                block_of(1, e, 2 * t + 1),
                low_half,
            )


def finish_kernel(own_pair_ref, own_part_ref, other_part_ref, narrow_ref, down_ref, result_ref):
    products = [normalize_channels(own_part_ref[t] + other_part_ref[t]) for t in range(2)]
    finished = mix(narrow_ref[0:128, :], jnp.concatenate(products, axis=1))
    own_pair = jnp.concatenate([own_pair_ref[t] for t in range(2)], axis=1)
    gating = gate_curve(mix(narrow_ref[128:256, :], normalize_channels(own_pair)))
    own_pair = own_pair + gating * finished
    hidden = jnp.maximum(mix(narrow_ref[256:768, :], normalize_channels(own_pair)), 0.0)
    own_pair = own_pair + mix(down_ref[...], hidden.astype(jnp.bfloat16))
    own_pair = own_pair.astype(jnp.bfloat16)
    order = lane_order_matrix()
    for t in range(2):
        result_ref[t * 128 : (t + 1) * 128, :] = contract_last(
            order, own_pair[:, t * LANES : (t + 1) * LANES]
        ).astype(jnp.bfloat16)


def lane_order_matrix():
    half = LANES // 2
    member = lax.broadcasted_iota(jnp.int32, (LANES, LANES), 0)
    lane = lax.broadcasted_iota(jnp.int32, (LANES, LANES), 1)
    back = half * (member // half) + 32 * (member % 2) + (member % half) // 2
    return (lane == back).astype(jnp.float32).astype(jnp.bfloat16)


def contract_first(first, second):
    return lax.dot_general(
        first, second, (((0,), (0,)), ((), ())), preferred_element_type=jnp.float32
    )


def rows_kernel(rows_ref, pair_ref, blocks_ref, own_pair_ref, wide_ref):
    order = lane_order_matrix()
    for t in range(2):
        own_pair_ref[t] = contract_first(
            pair_ref[2 * t : 2 * t + 2].reshape(LANES, LANES), order
        ).astype(jnp.bfloat16)
    residues = rows_ref.shape[1]
    count = 8 * residues
    rows = rows_ref[...].astype(jnp.float32).reshape(count, 2 * LANES)
    for e in range(2):
        wide_ref[e * count : (e + 1) * count, :] = rows[:, e * LANES : (e + 1) * LANES]
    for p in range(16):
        for e in range(2):
            block = [
                wide_ref[pl.ds(e * count + 4 * p + i, 8, stride=residues), :] for i in range(4)
            ]
            blocks_ref[p, :, e * LANES : (e + 1) * LANES] = jnp.concatenate(block, axis=0).astype(
                jnp.bfloat16
            )


def normalize_rows(values):
    center = jnp.mean(values, axis=1, keepdims=True)
    shifted = values - center
    spread = jnp.mean(shifted * shifted, axis=1, keepdims=True)
    return (shifted * lax.rsqrt(spread + EPSILON)).astype(jnp.bfloat16)


def contract_last(first, second):
    return lax.dot_general(
        first, second, (((1,), (1,)), ((), ())), preferred_element_type=jnp.float32
    )


def msa_kernel(
    live_ref,
    blocks_ref,
    narrow_ref,
    up_ref,
    down_ref,
    outer_ref,
    result_ref,
    parts_ref,
    wide_ref,
    attended_ref,
    final_ref,
):
    for p in range(16):
        block = blocks_ref[p].astype(jnp.float32)
        for i in range(4):
            wide_ref[i * 128 + p * 8 : i * 128 + p * 8 + 8, :] = block[i * 8 : i * 8 + 8, :]
    live = live_ref[...]
    alive = live > 0.0
    width = HM * HEAD_SIZE
    head_of = lax.broadcasted_iota(jnp.int32, (128, width), 1) // HEAD_SIZE
    zero = jnp.zeros((128, width), jnp.bfloat16)
    one = jnp.ones((128, width), jnp.bfloat16)

    def by_head(values):
        return jnp.concatenate([jnp.where(head_of == h, values, zero) for h in range(HM)], axis=0)

    heads = by_head(one)
    normed = normalize_rows(wide_ref[...])
    query = (mix(normed, narrow_ref[:, :width]) * HEAD_SIZE ** (-0.5)).astype(jnp.bfloat16)
    key = mix(normed, narrow_ref[:, width : 2 * width]).astype(jnp.bfloat16)
    value_gate = mix(normed, narrow_ref[:, 2 * width : 4 * width])
    value = value_gate[:, :width].astype(jnp.bfloat16)
    for i in range(4):
        rows = slice(i * 128, (i + 1) * 128)
        scores = contract_last(query[rows], by_head(key[rows]))
        raised = []
        for h in range(HM):
            score = jnp.where(alive, scores[:, h * 128 : (h + 1) * 128], -1000000000.0)
            raised.append(jnp.exp(score - jnp.max(score, axis=1, keepdims=True)).astype(jnp.bfloat16))
        raised = jnp.concatenate(raised, axis=1)
        attended_ref[rows, :] = mix(raised, by_head(value[rows])) / mix(raised, heads)
    gated = (gate_curve(value_gate[:, width:]) * attended_ref[...]).astype(jnp.bfloat16)
    current = wide_ref[...] + mix(gated, narrow_ref[:, 4 * width :])
    hidden = jnp.maximum(mix(normalize_rows(current), up_ref[...]), 0.0).astype(jnp.bfloat16)
    final = (current + mix(hidden, down_ref[...])).astype(jnp.bfloat16).astype(jnp.float32)
    outer = contract_last(outer_ref[...], normalize_rows(final))
    for i in range(4):
        rows = slice(i * 128, (i + 1) * 128)
        part = (outer[:, rows] * live).astype(jnp.bfloat16)
        parts_ref[i * CO : (i + 1) * CO, :] = part[:CO, :]
        parts_ref[128 + i * CO : 128 + (i + 1) * CO, :] = part[CO:, :]
        final_ref[pl.ds(i, 128, stride=4), :] = final[rows, :128]
        final_ref[pl.ds(512 + i, 128, stride=4), :] = final[rows, 128:]
    result_ref[:, :128] = final_ref[:512, :].astype(jnp.bfloat16)
    result_ref[:, 128:] = final_ref[512:, :].astype(jnp.bfloat16)


def exchange(values, offset):
    pieces = lax.axis_size("dap")
    return lax.ppermute(values, "dap", [(q, q ^ offset) for q in range(pieces)])


def whole_block(
    alignment_input,
    pair_state_input,
    bin_all,
    live_row_float,
    relative_position_table,
    column_query_weight,
    column_key_weight,
    column_value_gate_weight,
    column_output_weight,
    alignment_transition_up,
    alignment_transition_down,
    outer_input_weight,
    *pair_weights,
):
    channels = alignment_input.shape[2]
    width = pair_state_input.shape[2]
    place = lax.axis_index("dap").astype(jnp.int32).reshape(1)
    vmem = pl.BlockSpec(memory_space=pltpu.VMEM)
    smem = pl.BlockSpec(memory_space=pltpu.SMEM)
    hbm = pl.BlockSpec(memory_space=pltpu.HBM)

    def array(*shape, dtype=jnp.bfloat16):
        return jax.ShapeDtypeStruct(shape, dtype)

    def wide(*shape):
        return jax.ShapeDtypeStruct(shape, jnp.float32)

    def limit(mebibytes):
        return pltpu.CompilerParams(vmem_limit_bytes=mebibytes * 1024 * 1024)

    blocks, own_pair = pl.pallas_call(
        rows_kernel,
        out_shape=[array(16, 32, channels), array(2, width, LANES)],
        in_specs=[vmem, vmem],
        out_specs=[vmem, vmem],
        scratch_shapes=[pltpu.VMEM((1024, LANES), jnp.float32)],
        compiler_params=limit(16),
        name="rows_by_device",
    )(alignment_input, pair_state_input)
    blocks = lax.all_to_all(blocks, "dap", split_axis=0, concat_axis=0, tiled=True)

    pair_first = jnp.stack([own_pair, exchange(own_pair, 8)])
    blocks, pair_first = lax.optimization_barrier((blocks, pair_first))
    pair_second = exchange(pair_first, 4)

    result, parts = pl.pallas_call(
        msa_kernel,
        out_shape=(array(512, channels), array(256, LANES)),
        in_specs=[vmem] * 6,
        out_specs=(vmem, vmem),
        scratch_shapes=[
            pltpu.VMEM((512, channels), jnp.float32),
            pltpu.VMEM((512, channels), jnp.float32),
            pltpu.VMEM((1024, LANES), jnp.float32),
        ],
        compiler_params=limit(32),
        cost_estimate=pl.CostEstimate(
            flops=2_000_000_000, bytes_accessed=10_000_000, transcendentals=1_000_000
        ),
        name="msa_whole",
    )(
        live_row_float.reshape(1, LANES),
        blocks,
        jnp.concatenate(
            [
                column_query_weight,
                column_key_weight,
                column_value_gate_weight,
                column_output_weight,
            ],
            axis=1,
        ),
        alignment_transition_up,
        alignment_transition_down,
        outer_input_weight.T,
    )
    parts, pair_second = lax.optimization_barrier((parts, pair_second))
    pair_pieces = [pair_first, pair_second, exchange(pair_first, 2), exchange(pair_second, 2)]
    first = jnp.stack([parts, exchange(parts, 8)])
    second = exchange(first, 4)
    pieces = [first, second, exchange(first, 2), exchange(second, 2)]
    core_pieces = [exchange(piece, 1) for piece in pieces]

    slabs = (16, 128, LANES)
    tall = (16 * 128, LANES)
    pair_mid, left, gating, right = pl.pallas_call(
        start_kernel,
        out_shape=[wide(*slabs), wide(*tall), wide(*slabs), array(*tall)],
        in_specs=[smem] + [vmem] * 15 + [hbm] * 3,
        out_specs=[vmem] * 4,
        scratch_shapes=[
            pltpu.VMEM((2048, LANES), jnp.float32),
            pltpu.VMEM((128, 2048), jnp.bfloat16),
            pltpu.VMEM((1024, LANES), jnp.float32),
            pltpu.VMEM((256, 512), jnp.bfloat16),
            pltpu.VMEM((LANES, LANES), jnp.float32),
            pltpu.VMEM((512, 1024), jnp.bfloat16),
            pltpu.VMEM((512, 1024), jnp.bfloat16),
        ]
        + [pltpu.VMEM(w.shape, jnp.bfloat16) for w in pair_weights[:3]]
        + [pltpu.SemaphoreType.DMA((3,))],
        compiler_params=limit(48),
        name="pair_start",
    )(
        place,
        live_row_float.reshape(1, LANES),
        lanes_order(bin_all).reshape(32, LANES),
        relative_position_table,
        *pieces,
        *core_pieces,
        *pair_pieces,
        *pair_weights[:3],
    )
    own_pair, own_part, other_part, narrow_weights, down_weight = pl.pallas_call(
        triangle_kernel,
        out_shape=[wide(2, 128, LANES)] * 3 + [array(768, LANES), array(128, 512)],
        in_specs=[smem] + [vmem] * 5 + [hbm] * 6,
        out_specs=[vmem] * 5,
        scratch_shapes=[
            pltpu.VMEM((32 * 128, LANES), jnp.float32),
            pltpu.VMEM(tall, jnp.float32),
            pltpu.VMEM(slabs, jnp.float32),
            pltpu.VMEM((128, 256), jnp.float32),
            pltpu.VMEM(tall, jnp.float32),
            pltpu.VMEM(tall, jnp.float32),
        ]
        + [pltpu.VMEM(w.shape, jnp.bfloat16) for w in pair_weights[3:]]
        + [pltpu.SemaphoreType.DMA((6,))],
        compiler_params=limit(48),
        name="pair_triangles",
    )(place, pair_mid, left, gating, right, exchange(right, 1), *pair_weights[3:])
    pair_output = pl.pallas_call(
        finish_kernel,
        out_shape=array(256, LANES),
        in_specs=[vmem] * 5,
        out_specs=vmem,
        compiler_params=limit(16),
        name="pair_finish",
    )(own_pair, own_part, exchange(other_part, 1), narrow_weights, down_weight)
    return result.reshape(128, 4, channels), pair_output.reshape(pair_state_input.shape)


def lanes_order(values):
    lead = values.shape[:-1]
    halves = values.reshape(lead + (values.shape[-1] // 2, 2))
    return jnp.swapaxes(halves, -1, -2).reshape(values.shape)


def local(
    alignment_input,
    pair_state_input,
    residue_number_index,
    chain_label,
    alignment_row_mask,
    relative_position_table,
    column_query_weight,
    column_key_weight,
    column_value_gate_weight,
    column_output_weight,
    alignment_transition_up,
    alignment_transition_down,
    outer_input_weight,
    outer_output_weight,
    outgoing_projection_weight,
    outgoing_output_gate,
    outgoing_output_weight,
    incoming_projection_weight,
    incoming_output_gate,
    incoming_output_weight,
    pair_transition_up,
    pair_transition_down,
):
    shard_pieces = lax.axis_size("dap")
    own_rows = pair_state_input.shape[0]
    residue_count = pair_state_input.shape[1]
    channel_count = alignment_input.shape[2]
    head_width = HM * HEAD_SIZE
    first_row = lax.axis_index("dap") * own_rows
    own_index = lax.dynamic_slice_in_dim(residue_number_index, first_row, own_rows)
    own_chain = lax.dynamic_slice_in_dim(chain_label, first_row, own_rows)

    def bins_of(index, chain):
        offset = index[:, None] - residue_number_index[None, :]
        return jnp.where(
            chain[:, None] == chain_label[None, :],
            jnp.clip(offset + MAXREL, 0, 2 * MAXREL),
            2 * MAXREL + 1,
        )

    bin_index = bins_of(own_index, own_chain)
    one_hot = (bin_index[:, :, None] == jnp.arange(NBINS, dtype=jnp.int32)[None, None, :]).astype(
        jnp.bfloat16
    )
    pair_start = pair_state_input.astype(jnp.float32) + jnp.einsum(
        "ijb,bc->ijc", one_hot, relative_position_table, preferred_element_type=jnp.float32
    )
    live_rows = alignment_row_mask > 0
    live_row_float = live_rows.astype(jnp.float32)

    if alignment_row_mask.shape[0] == LANES and 2 * residue_count == LANES and own_rows == 4:
        return whole_block(
            alignment_input,
            pair_state_input,
            bins_of(residue_number_index, chain_label),
            live_row_float,
            relative_position_table,
            column_query_weight,
            column_key_weight,
            column_value_gate_weight,
            column_output_weight,
            alignment_transition_up,
            alignment_transition_down,
            outer_input_weight,
            outer_output_weight,
            outgoing_projection_weight,
            outgoing_output_gate,
            outgoing_output_weight,
            incoming_projection_weight,
            incoming_output_gate,
            incoming_output_weight,
            pair_transition_up,
            pair_transition_down,
        )

    def attend_one(operands):
        query_col, key_col, value_col = operands
        scores = jnp.einsum("shd,thd->hst", query_col, key_col, preferred_element_type=jnp.float32)
        scores = jnp.where(live_rows[None, None, :], scores, -1000000000.0)
        row_top = jnp.max(scores, axis=-1, keepdims=True)
        raised = jnp.exp(scores - row_top)
        attention = (raised / jnp.sum(raised, axis=-1, keepdims=True)).astype(jnp.bfloat16)
        return jnp.einsum("hst,thd->shd", attention, value_col, preferred_element_type=jnp.float32)

    blocked_view = alignment_input.reshape(
        alignment_input.shape[0], shard_pieces, residue_count // shard_pieces, channel_count
    )
    block_in = lax.all_to_all(blocked_view, "dap", split_axis=1, concat_axis=0, tiled=True)
    depth_rows = block_in.shape[0]
    count_cols = block_in.shape[2]
    current = block_in.reshape(depth_rows, count_cols, channel_count).astype(jnp.float32)
    normed = layer_normalize(current).astype(jnp.bfloat16)
    query_rows = (
        jnp.einsum("sic,ce->sie", normed, column_query_weight, preferred_element_type=jnp.float32)
        * HEAD_SIZE ** (-0.5)
    ).astype(jnp.bfloat16)
    key_row_block = jnp.einsum(
        "sic,ce->sie", normed, column_key_weight, preferred_element_type=jnp.float32
    ).astype(jnp.bfloat16)
    value_gate_pair = jnp.einsum(
        "sic,ce->sie", normed, column_value_gate_weight, preferred_element_type=jnp.float32
    )
    value_rows = value_gate_pair[..., :head_width].astype(jnp.bfloat16)

    def by_column(values):
        return values.transpose(1, 0, 2).reshape(count_cols, depth_rows, HM, HEAD_SIZE)

    attended = lax.map(
        attend_one, (by_column(query_rows), by_column(key_row_block), by_column(value_rows))
    )
    attended = attended.reshape(count_cols, depth_rows, head_width).transpose(1, 0, 2)
    gated_out = (jax.nn.sigmoid(value_gate_pair[..., head_width:]) * attended).astype(jnp.bfloat16)
    current = current + jnp.einsum(
        "sie,ec->sic", gated_out, column_output_weight, preferred_element_type=jnp.float32
    )
    hidden = jax.nn.relu(
        jnp.einsum(
            "sic,cf->sif",
            layer_normalize(current).astype(jnp.bfloat16),
            alignment_transition_up,
            preferred_element_type=jnp.float32,
        )
    ).astype(jnp.bfloat16)
    current = current + jnp.einsum(
        "sif,fc->sic", hidden, alignment_transition_down, preferred_element_type=jnp.float32
    )
    result = current.astype(jnp.bfloat16)
    outer_product_input = jnp.einsum(
        "sic,cf->sif",
        layer_normalize(result.astype(jnp.float32)).astype(jnp.bfloat16),
        outer_input_weight,
        preferred_element_type=jnp.float32,
    )
    outer_product_input = outer_product_input * live_row_float[:, None, None]
    left_part = outer_product_input[..., :CO].astype(jnp.bfloat16)
    right_part = outer_product_input[..., CO:].astype(jnp.bfloat16)
    all_rows = result.shape[0]
    left_cols = left_part.transpose(1, 0, 2)
    right_cols = right_part.transpose(1, 0, 2).reshape(own_rows, all_rows * CO)
    live_count = jnp.sum(live_row_float)
    right_piece = gather_doubling(right_cols).reshape(-1, all_rows * CO)
    span_rows = right_piece.shape[0]
    products = jnp.einsum(
        "isc,jsd->ijcd",
        left_cols,
        right_piece.reshape(span_rows, all_rows, CO),
        preferred_element_type=jnp.float32,
    )
    products = products.astype(jnp.bfloat16).reshape(own_rows, span_rows, CO * CO)
    outer_mean = (
        jnp.einsum("ijf,fc->ijc", products, outer_output_weight, preferred_element_type=jnp.float32)
        / live_count
    )
    pair_mid = pair_start + outer_mean
    out_left, out_right, out_gating = triangle_inputs(
        pair_mid, outgoing_projection_weight, outgoing_output_gate
    )
    out_product = by_channels(out_left, out_right, "cik,cjk->cij")
    pair_after_out = triangle_finish(pair_mid, out_product, out_gating, outgoing_output_weight)
    in_left, in_right, in_gating = triangle_inputs(
        pair_after_out, incoming_projection_weight, incoming_output_gate
    )
    in_product = by_channels(in_left, in_right, "cki,ckj->cij")
    pair_after_in = triangle_finish(pair_after_out, in_product, in_gating, incoming_output_weight)
    pair_expanded = jax.nn.relu(
        jnp.einsum(
            "ijc,cf->ijf",
            layer_normalize(pair_after_in).astype(jnp.bfloat16),
            pair_transition_up,
            preferred_element_type=jnp.float32,
        )
    ).astype(jnp.bfloat16)
    pair_state_output = (
        pair_after_in
        + jnp.einsum(
            "ijf,fc->ijc", pair_expanded, pair_transition_down, preferred_element_type=jnp.float32
        )
    ).astype(jnp.bfloat16)
    return (result, pair_state_output)


def solution(mesh):
    in_specs = (
        P(("grp", "dap"), None, None),
        P(("grp", "dap"), None, None),
        P("grp"),
        P("grp"),
        P("grp"),
        P(),
        P(),
        P(),
        P(),
        P(),
        P(),
        P(),
        P(),
        P(),
        P(),
        P(),
        P(),
        P(),
        P(),
        P(),
        P(),
        P(),
    )
    out_specs = (P("grp", "dap", None), P(("grp", "dap"), None, None))
    return jax.shard_map(local, mesh=mesh, in_specs=in_specs, out_specs=out_specs, check_vma=False)
```

```python
import jax
import jax.numpy as jnp
from jax import lax
from jax.experimental import pallas as pl
from jax.experimental.pallas import tpu as pltpu
from jax.sharding import PartitionSpec as P

HM = 8
HEAD_SIZE = 32
CO = 32
MAXREL = 32
NBINS = 66


EPSILON = 1e-05


def layer_normalize(values):
    center = jnp.mean(values, axis=-1, keepdims=True)
    shifted = values - center
    spread = jnp.mean(shifted * shifted, axis=-1, keepdims=True)
    return shifted * lax.rsqrt(spread + EPSILON)


def triangle_inputs(pair_now, weight, gate_weight):
    normed = layer_normalize(pair_now).astype(jnp.bfloat16)
    combined = jnp.einsum("ijc,cf->fij", normed, weight, preferred_element_type=jnp.float32)
    hidden_width = weight.shape[1] // 4
    left_side = (
        jax.nn.sigmoid(combined[hidden_width : 2 * hidden_width]) * combined[:hidden_width]
    ).astype(jnp.bfloat16)
    right_side = (
        jax.nn.sigmoid(combined[3 * hidden_width :]) * combined[2 * hidden_width : 3 * hidden_width]
    ).astype(jnp.bfloat16)
    gating = jax.nn.sigmoid(
        jnp.einsum("ijc,cd->ijd", normed, gate_weight, preferred_element_type=jnp.float32)
    )
    return (left_side, right_side, gating)


def triangle_finish(pair_now, product, gating, final_weight):
    product = lax.optimization_barrier(product)
    normed = layer_normalize(product.transpose(1, 2, 0).astype(jnp.float32)).astype(jnp.bfloat16)
    return pair_now + gating * jnp.einsum(
        "ijc,cd->ijd", normed, final_weight, preferred_element_type=jnp.float32
    )


def by_channels(left_side, right_side, form):
    both = jnp.stack([left_side, right_side])
    both = lax.all_to_all(both, "dap", split_axis=1, concat_axis=2, tiled=True)
    partial_out = jnp.einsum(form, both[0], both[1], preferred_element_type=jnp.float32)
    return lax.all_to_all(
        partial_out.astype(jnp.bfloat16), "dap", split_axis=1, concat_axis=0, tiled=True
    )


def gather_doubling(block):
    shard_pieces = lax.axis_size("dap")
    place = lax.axis_index("dap")
    held = block
    depth = 0
    bit = shard_pieces // 2
    while bit:
        other = lax.ppermute(held, "dap", [(q, q ^ bit) for q in range(shard_pieces)])
        upper = (place & bit) != 0
        first = jnp.where(upper, other, held)
        second = jnp.where(upper, held, other)
        held = jnp.stack([first, second], axis=depth)
        depth += 1
        bit //= 2
    return held.reshape((shard_pieces,) + block.shape)


LANES = 128


def gate_curve(values):
    return 0.5 + 0.5 * jnp.tanh(0.5 * values)


def normalize_channels(values):
    center = jnp.mean(values, axis=0, keepdims=True)
    shifted = values - center
    spread = jnp.mean(shifted * shifted, axis=0, keepdims=True)
    return (shifted * lax.rsqrt(spread + EPSILON)).astype(jnp.bfloat16)


def mix(weight, values):
    return jnp.dot(weight, values, preferred_element_type=jnp.float32)


def fold_halves(first_even, second_even, first_odd, second_odd, low_half):
    straight = jnp.where(low_half, first_even, second_odd)
    crossed = jnp.where(low_half, second_even, first_odd)
    return straight + pltpu.roll(crossed, LANES // 2, 1)


def transpose_blocks(ref):
    rows, columns = ref.shape
    return jnp.concatenate(
        [
            jnp.concatenate(
                [
                    ref[a : a + LANES, b : b + LANES].astype(jnp.float32).T.astype(jnp.bfloat16)
                    for a in range(0, rows, LANES)
                ],
                axis=1,
            )
            for b in range(0, columns, LANES)
        ],
        axis=0,
    )


def start_copies(sources, landed, arrived):
    copies = [
        pltpu.make_async_copy(source, landed[k], arrived.at[k]) for k, source in enumerate(sources)
    ]
    for copy in copies:
        copy.start()
    return copies


FIRSTS = (0, 4, 2, 6)


def start_kernel(place_ref, live_ref, bins_ref, table_ref, *rest):
    part_refs, core_refs, pair_refs, sources = rest[:4], rest[4:8], rest[8:12], rest[12:15]
    pair_mid_ref, left_ref, gating_ref, right_ref = rest[15:19]
    wide_ref, right_cols_ref, mean_wide_ref, mean_weight_ref, table_wide_ref = rest[19:24]
    stack_refs, landed, arrived = rest[24:26], rest[26:29], rest[29]
    copies = start_copies(sources, landed, arrived)
    place = place_ref[0]
    inverse_live = 1.0 / jnp.sum(live_ref[...], axis=1, keepdims=True)
    half = LANES // 2
    channel = lax.broadcasted_iota(jnp.int32, (LANES, LANES), 0)
    table_wide_ref[...] = jnp.zeros_like(table_wide_ref)
    table_wide_ref[0:NBINS, :] = table_ref[...].astype(jnp.float32)
    table = table_wide_ref[...].T.astype(jnp.bfloat16)
    low_half = lax.broadcasted_iota(jnp.int32, (LANES, LANES), 1) < half

    for g in range(4):
        for m in range(2):
            device = place ^ FIRSTS[g] ^ (8 * m)
            for part, owner in ((part_refs[g], device), (core_refs[g], device ^ 1)):
                wide_ref[pl.ds(pl.multiple_of(owner * 128, 128), 128), :] = part[
                    m, 128:256, :
                ].astype(jnp.float32)
    for d in range(0, CO, 2):
        rows = [
            wide_ref[pl.ds(par * CO + d + e, 32, stride=2 * CO), :]
            for e in range(2)
            for par in range(2)
        ]
        right_cols_ref[:, d * half : d * half + LANES] = (
            jnp.concatenate(rows, axis=0).T.astype(jnp.bfloat16)
        )

    for copy in copies:
        copy.wait()
    mean_wide_ref[...] = landed[0][...].astype(jnp.float32)
    for e in range(2):
        for block in range(4):
            rows = [
                mean_wide_ref[pl.ds(2 * (4 * block + k) + e, CO, stride=CO), :] for k in range(4)
            ]
            mean_weight_ref[e * LANES : (e + 1) * LANES, block * LANES : (block + 1) * LANES] = (
                jnp.concatenate(rows, axis=0).T.astype(jnp.bfloat16)
            )
    out_mix = transpose_blocks(landed[1])
    out_gate = transpose_blocks(landed[2])

    for g in range(4):
        stack_ref = stack_refs[g % 2]
        left_rows = part_refs[g][:, 0:128, :].reshape(256, LANES)
        outer = mix(left_rows, right_cols_ref[...]).astype(jnp.bfloat16)
        for i in range(8):
            for d in range(16):
                stack_ref[d * 32 : (d + 1) * 32, i * LANES : (i + 1) * LANES] = outer[
                    i * 32 : (i + 1) * 32, d * LANES : (d + 1) * LANES
                ]
        mixed = mix(mean_weight_ref[...], stack_ref[...])
        slabs = []
        places = []
        devices = [place ^ FIRSTS[g] ^ (8 * m) for m in range(2)]
        one_hot = [
            (channel == bins_ref[pl.ds(2 * devices[q // 2] + q % 2, 1), :]).astype(jnp.float32)
            for q in range(4)
        ]
        embedding = mix(table, jnp.concatenate(one_hot, axis=1).astype(jnp.bfloat16))
        for q in range(4):
            device = devices[q // 2]
            here = 2 * (device // 2) + q % 2
            even = slice(2 * q * LANES, (2 * q + 1) * LANES)
            odd = slice((2 * q + 1) * LANES, (2 * q + 2) * LANES)
            outer_mean = fold_halves(
                mixed[0:128, even], mixed[0:128, odd], mixed[128:256, even], mixed[128:256, odd], low_half
            )
            start = pair_refs[g][q // 2, q % 2].astype(jnp.float32)
            start = start + embedding[:, q * LANES : (q + 1) * LANES]
            slab = start + outer_mean * inverse_live
            pair_mid_ref[here] = slab
            slabs.append(normalize_channels(slab))
            places.append(here)
        normed = jnp.concatenate(slabs, axis=1)
        combined = mix(out_mix, normed)
        left = gate_curve(combined[128:256]) * combined[0:128]
        right = gate_curve(combined[384:512]) * combined[256:384]
        gating = gate_curve(mix(out_gate, normed))
        for q in range(4):
            lanes = slice(q * LANES, (q + 1) * LANES)
            rows = pl.ds(pl.multiple_of(places[q] * 128, 128), 128)
            left_ref[rows, :] = left[:, lanes]
            right_ref[rows, :] = right[:, lanes].astype(jnp.bfloat16)
            gating_ref[places[q]] = gating[:, lanes]


def triangle_kernel(
    place_ref,
    pair_mid_ref,
    left_ref,
    gating_ref,
    right_own_ref,
    right_other_ref,
    *rest,
):
    sources, (own_pair_ref, own_part_ref, other_part_ref) = rest[:6], rest[6:9]
    narrow_ref, wide_out_ref = rest[9:11]
    right_ref, product_ref, pair_now_ref, chosen_ref, own_left_ref, own_product_ref = rest[11:17]
    landed, arrived = rest[17:23], rest[23]
    copies = start_copies(sources, landed, arrived)
    place = place_ref[0]
    core = place % 2
    half = LANES // 2
    low_half = lax.broadcasted_iota(jnp.int32, (LANES, LANES), 1) < half
    low_short = lax.broadcasted_iota(jnp.int32, (32, LANES), 1) < half
    for chip in range(8):
        for source, side in ((right_own_ref, core), (right_other_ref, 1 - core)):
            rows = pl.ds(pl.multiple_of((4 * chip + 2 * side) * 128, 256), 256)
            right_ref[rows, :] = source[chip * 256 : (chip + 1) * 256, :].astype(jnp.float32)

    nothing = jnp.zeros((32, LANES), jnp.bfloat16)

    def outgoing_channels(block, carry):
        for e in range(32):
            c = block * 32 + e
            left = left_ref[pl.ds(c, 16, stride=128), :].astype(jnp.bfloat16)
            right = right_ref[pl.ds(c, 32, stride=128), :]
            moved = pltpu.roll(right, half, 1).astype(jnp.bfloat16)
            right = right.astype(jnp.bfloat16)
            spread = jnp.concatenate(
                [
                    jnp.where(low_short, right, nothing),
                    jnp.where(low_short, moved, nothing),
                    jnp.where(low_short, nothing, moved),
                    jnp.where(low_short, nothing, right),
                ],
                axis=0,
            )
            product_ref[pl.ds(c, 16, stride=128), :] = contract_last(left, spread)
        return carry

    lax.fori_loop(0, 4, outgoing_channels, 0)

    for copy in copies:
        copy.wait()
    out_final = transpose_blocks(landed[0])
    in_mix = transpose_blocks(landed[1])
    narrow_ref[0:128, :] = transpose_blocks(landed[3])
    narrow_ref[128:256, :] = transpose_blocks(landed[2])
    narrow_ref[256:768, :] = transpose_blocks(landed[4])
    wide_out_ref[...] = transpose_blocks(landed[5])

    column = lax.broadcasted_iota(jnp.int32, (1, 256), 1)
    which = column // 16
    residue = which % 4
    device = place ^ ((which // 4) % 2)
    wanted = half * (which // 8) + 32 * (residue % 2) + 2 * device + residue // 2
    slab_of = column % 16
    source_lane = lax.broadcasted_iota(jnp.int32, (LANES, 256), 0)
    for g in range(4):
        products = [
            normalize_channels(product_ref[(4 * g + q) * 128 : (4 * g + q + 1) * 128, :])
            for q in range(4)
        ]
        finished = mix(out_final, jnp.concatenate(products, axis=1))
        slabs = []
        picks = []
        for q in range(4):
            h = 4 * g + q
            lanes = slice(q * LANES, (q + 1) * LANES)
            slab = pair_mid_ref[h] + gating_ref[h] * finished[:, lanes]
            pair_now_ref[h] = slab
            slabs.append(normalize_channels(slab))
            here = jnp.where(slab_of == h, wanted, -1)
            picks.append((source_lane == here).astype(jnp.float32).astype(jnp.bfloat16))
        normed = jnp.concatenate(slabs, axis=1)
        chosen = mix(normed, jnp.concatenate(picks, axis=0))
        if g:
            chosen_ref[...] += chosen
        else:
            chosen_ref[...] = chosen
        combined = mix(in_mix[256:512], normed)
        right = gate_curve(combined[128:256]) * combined[0:128]
        for q in range(4):
            right_ref[(4 * g + q) * 128 : (4 * g + q + 1) * 128, :] = right[
                :, q * LANES : (q + 1) * LANES
            ]
    for t in range(2):
        own_pair_ref[t] = pair_now_ref[2 * (place // 2) + t]

    combined = mix(in_mix[0:256], chosen_ref[...].astype(jnp.bfloat16))
    own_left = gate_curve(combined[128:256]) * combined[0:128]
    for m in range(16):
        part = own_left[:, (m // 8) * LANES : (m // 8 + 1) * LANES]
        if m % 8:
            part = pltpu.roll(part, LANES - 16 * (m % 8), 1)
        own_left_ref[m * 128 : (m + 1) * 128, :] = part

    def incoming_channels(block, carry):
        for e in range(32):
            c = block * 32 + e
            left = own_left_ref[pl.ds(c, 16, stride=128), :][:, 0:16].astype(jnp.bfloat16)
            right = right_ref[pl.ds(c, 16, stride=128), :].astype(jnp.bfloat16)
            own_product_ref[pl.ds(c, 16, stride=128), :] = mix(left, right)
        return carry

    lax.fori_loop(0, 4, incoming_channels, 0)

    def block_of(b, e, residue):
        m = 8 * b + 4 * e + residue
        return own_product_ref[m * 128 : (m + 1) * 128, :]

    for e, target in ((0, own_part_ref), (1, other_part_ref)):
        for t in range(2):
            target[t] = fold_halves(
                block_of(0, e, 2 * t),
                block_of(0, e, 2 * t + 1),
                block_of(1, e, 2 * t),
                block_of(1, e, 2 * t + 1),
                low_half,
            )


def finish_kernel(own_pair_ref, own_part_ref, other_part_ref, narrow_ref, down_ref, result_ref):
    products = [normalize_channels(own_part_ref[t] + other_part_ref[t]) for t in range(2)]
    finished = mix(narrow_ref[0:128, :], jnp.concatenate(products, axis=1))
    own_pair = jnp.concatenate([own_pair_ref[t] for t in range(2)], axis=1)
    gating = gate_curve(mix(narrow_ref[128:256, :], normalize_channels(own_pair)))
    own_pair = own_pair + gating * finished
    hidden = jnp.maximum(mix(narrow_ref[256:768, :], normalize_channels(own_pair)), 0.0)
    own_pair = own_pair + mix(down_ref[...], hidden.astype(jnp.bfloat16))
    own_pair = own_pair.astype(jnp.bfloat16)
    order = lane_order_matrix()
    for t in range(2):
        result_ref[t * 128 : (t + 1) * 128, :] = contract_last(
            order, own_pair[:, t * LANES : (t + 1) * LANES]
        ).astype(jnp.bfloat16)


def lane_order_matrix():
    half = LANES // 2
    member = lax.broadcasted_iota(jnp.int32, (LANES, LANES), 0)
    lane = lax.broadcasted_iota(jnp.int32, (LANES, LANES), 1)
    back = half * (member // half) + 32 * (member % 2) + (member % half) // 2
    return (lane == back).astype(jnp.float32).astype(jnp.bfloat16)


def contract_first(first, second):
    return lax.dot_general(
        first, second, (((0,), (0,)), ((), ())), preferred_element_type=jnp.float32
    )


def rows_kernel(rows_ref, pair_ref, blocks_ref, own_pair_ref, wide_ref):
    order = lane_order_matrix()
    for t in range(2):
        own_pair_ref[t] = contract_first(
            pair_ref[2 * t : 2 * t + 2].reshape(LANES, LANES), order
        ).astype(jnp.bfloat16)
    residues = rows_ref.shape[1]
    count = 8 * residues
    rows = rows_ref[...].astype(jnp.float32).reshape(count, 2 * LANES)
    for e in range(2):
        wide_ref[e * count : (e + 1) * count, :] = rows[:, e * LANES : (e + 1) * LANES]
    for p in range(16):
        for e in range(2):
            block = [
                wide_ref[pl.ds(e * count + 4 * p + i, 8, stride=residues), :] for i in range(4)
            ]
            blocks_ref[p, :, e * LANES : (e + 1) * LANES] = jnp.concatenate(block, axis=0).astype(
                jnp.bfloat16
            )


def normalize_rows(values):
    center = jnp.mean(values, axis=1, keepdims=True)
    shifted = values - center
    spread = jnp.mean(shifted * shifted, axis=1, keepdims=True)
    return (shifted * lax.rsqrt(spread + EPSILON)).astype(jnp.bfloat16)


def contract_last(first, second):
    return lax.dot_general(
        first, second, (((1,), (1,)), ((), ())), preferred_element_type=jnp.float32
    )


def msa_kernel(
    live_ref,
    blocks_ref,
    narrow_ref,
    up_ref,
    down_ref,
    outer_ref,
    result_ref,
    parts_ref,
    wide_ref,
    attended_ref,
    final_ref,
):
    for p in range(16):
        block = blocks_ref[p].astype(jnp.float32)
        for i in range(4):
            wide_ref[i * 128 + p * 8 : i * 128 + p * 8 + 8, :] = block[i * 8 : i * 8 + 8, :]
    live = live_ref[...]
    alive = live > 0.0
    width = HM * HEAD_SIZE
    head_of = lax.broadcasted_iota(jnp.int32, (128, width), 1) // HEAD_SIZE
    zero = jnp.zeros((128, width), jnp.bfloat16)
    one = jnp.ones((128, width), jnp.bfloat16)

    def by_head(values):
        return jnp.concatenate([jnp.where(head_of == h, values, zero) for h in range(HM)], axis=0)

    heads = by_head(one)
    normed = normalize_rows(wide_ref[...])
    query = (mix(normed, narrow_ref[:, :width]) * HEAD_SIZE ** (-0.5)).astype(jnp.bfloat16)
    key = mix(normed, narrow_ref[:, width : 2 * width]).astype(jnp.bfloat16)
    value_gate = mix(normed, narrow_ref[:, 2 * width : 4 * width])
    value = value_gate[:, :width].astype(jnp.bfloat16)
    for i in range(4):
        rows = slice(i * 128, (i + 1) * 128)
        scores = contract_last(query[rows], by_head(key[rows]))
        raised = []
        for h in range(HM):
            score = jnp.where(alive, scores[:, h * 128 : (h + 1) * 128], -1000000000.0)
            raised.append(jnp.exp(score - jnp.max(score, axis=1, keepdims=True)).astype(jnp.bfloat16))
        raised = jnp.concatenate(raised, axis=1)
        attended_ref[rows, :] = mix(raised, by_head(value[rows])) / mix(raised, heads)
    gated = (gate_curve(value_gate[:, width:]) * attended_ref[...]).astype(jnp.bfloat16)
    current = wide_ref[...] + mix(gated, narrow_ref[:, 4 * width :])
    hidden = jnp.maximum(mix(normalize_rows(current), up_ref[...]), 0.0).astype(jnp.bfloat16)
    final = (current + mix(hidden, down_ref[...])).astype(jnp.bfloat16).astype(jnp.float32)
    outer = contract_last(outer_ref[...], normalize_rows(final))
    for i in range(4):
        rows = slice(i * 128, (i + 1) * 128)
        part = (outer[:, rows] * live).astype(jnp.bfloat16)
        parts_ref[i * CO : (i + 1) * CO, :] = part[:CO, :]
        parts_ref[128 + i * CO : 128 + (i + 1) * CO, :] = part[CO:, :]
        final_ref[pl.ds(i, 128, stride=4), :] = final[rows, :128]
        final_ref[pl.ds(512 + i, 128, stride=4), :] = final[rows, 128:]
    result_ref[:, :128] = final_ref[:512, :].astype(jnp.bfloat16)
    result_ref[:, 128:] = final_ref[512:, :].astype(jnp.bfloat16)


def exchange(values, offset):
    pieces = lax.axis_size("dap")
    return lax.ppermute(values, "dap", [(q, q ^ offset) for q in range(pieces)])


def whole_block(
    alignment_input,
    pair_state_input,
    bin_all,
    live_row_float,
    relative_position_table,
    column_query_weight,
    column_key_weight,
    column_value_gate_weight,
    column_output_weight,
    alignment_transition_up,
    alignment_transition_down,
    outer_input_weight,
    *pair_weights,
):
    channels = alignment_input.shape[2]
    width = pair_state_input.shape[2]
    place = lax.axis_index("dap").astype(jnp.int32).reshape(1)
    vmem = pl.BlockSpec(memory_space=pltpu.VMEM)
    smem = pl.BlockSpec(memory_space=pltpu.SMEM)
    hbm = pl.BlockSpec(memory_space=pltpu.HBM)

    def array(*shape, dtype=jnp.bfloat16):
        return jax.ShapeDtypeStruct(shape, dtype)

    def wide(*shape):
        return jax.ShapeDtypeStruct(shape, jnp.float32)

    def limit(mebibytes):
        return pltpu.CompilerParams(vmem_limit_bytes=mebibytes * 1024 * 1024)

    blocks, own_pair = pl.pallas_call(
        rows_kernel,
        out_shape=[array(16, 32, channels), array(2, width, LANES)],
        in_specs=[vmem, vmem],
        out_specs=[vmem, vmem],
        scratch_shapes=[pltpu.VMEM((1024, LANES), jnp.float32)],
        compiler_params=limit(16),
        name="rows_by_device",
    )(alignment_input, pair_state_input)
    blocks = lax.all_to_all(blocks, "dap", split_axis=0, concat_axis=0, tiled=True)

    pair_first = jnp.stack([own_pair, exchange(own_pair, 8)])
    blocks, pair_first = lax.optimization_barrier((blocks, pair_first))
    pair_second = exchange(pair_first, 4)
    pair_across = exchange(pair_first, 2)

    result, parts = pl.pallas_call(
        msa_kernel,
        out_shape=(array(512, channels), array(256, LANES)),
        in_specs=[vmem] * 6,
        out_specs=(vmem, vmem),
        scratch_shapes=[
            pltpu.VMEM((512, channels), jnp.float32),
            pltpu.VMEM((512, channels), jnp.float32),
            pltpu.VMEM((1024, LANES), jnp.float32),
        ],
        compiler_params=limit(32),
        cost_estimate=pl.CostEstimate(
            flops=2_000_000_000, bytes_accessed=10_000_000, transcendentals=1_000_000
        ),
        name="msa_whole",
    )(
        live_row_float.reshape(1, LANES),
        blocks,
        jnp.concatenate(
            [
                column_query_weight,
                column_key_weight,
                column_value_gate_weight,
                column_output_weight,
            ],
            axis=1,
        ),
        alignment_transition_up,
        alignment_transition_down,
        outer_input_weight.T,
    )
    parts, pair_second, pair_across = lax.optimization_barrier((parts, pair_second, pair_across))
    far, pair_last = lax.optimization_barrier((exchange(parts, 8), exchange(pair_second, 2)))
    pair_pieces = [pair_first, pair_second, pair_across, pair_last]
    first = jnp.stack([parts, far])
    second = exchange(first, 4)
    pieces = [first, second, exchange(first, 2), exchange(second, 2)]
    core_pieces = [exchange(piece, 1) for piece in pieces]

    slabs = (16, 128, LANES)
    tall = (16 * 128, LANES)
    pair_mid, left, gating, right = pl.pallas_call(
        start_kernel,
        out_shape=[wide(*slabs), wide(*tall), wide(*slabs), array(*tall)],
        in_specs=[smem] + [vmem] * 15 + [hbm] * 3,
        out_specs=[vmem] * 4,
        scratch_shapes=[
            pltpu.VMEM((2048, LANES), jnp.float32),
            pltpu.VMEM((128, 2048), jnp.bfloat16),
            pltpu.VMEM((1024, LANES), jnp.float32),
            pltpu.VMEM((256, 512), jnp.bfloat16),
            pltpu.VMEM((LANES, LANES), jnp.float32),
            pltpu.VMEM((512, 1024), jnp.bfloat16),
            pltpu.VMEM((512, 1024), jnp.bfloat16),
        ]
        + [pltpu.VMEM(w.shape, jnp.bfloat16) for w in pair_weights[:3]]
        + [pltpu.SemaphoreType.DMA((3,))],
        compiler_params=limit(48),
        name="pair_start",
    )(
        place,
        live_row_float.reshape(1, LANES),
        lanes_order(bin_all).reshape(32, LANES),
        relative_position_table,
        *pieces,
        *core_pieces,
        *pair_pieces,
        *pair_weights[:3],
    )
    own_pair, own_part, other_part, narrow_weights, down_weight = pl.pallas_call(
        triangle_kernel,
        out_shape=[wide(2, 128, LANES)] * 3 + [array(768, LANES), array(128, 512)],
        in_specs=[smem] + [vmem] * 5 + [hbm] * 6,
        out_specs=[vmem] * 5,
        scratch_shapes=[
            pltpu.VMEM((32 * 128, LANES), jnp.float32),
            pltpu.VMEM(tall, jnp.float32),
            pltpu.VMEM(slabs, jnp.float32),
            pltpu.VMEM((128, 256), jnp.float32),
            pltpu.VMEM(tall, jnp.float32),
            pltpu.VMEM(tall, jnp.float32),
        ]
        + [pltpu.VMEM(w.shape, jnp.bfloat16) for w in pair_weights[3:]]
        + [pltpu.SemaphoreType.DMA((6,))],
        compiler_params=limit(48),
        name="pair_triangles",
    )(place, pair_mid, left, gating, right, exchange(right, 1), *pair_weights[3:])
    pair_output = pl.pallas_call(
        finish_kernel,
        out_shape=array(256, LANES),
        in_specs=[vmem] * 5,
        out_specs=vmem,
        compiler_params=limit(16),
        name="pair_finish",
    )(own_pair, own_part, exchange(other_part, 1), narrow_weights, down_weight)
    return result.reshape(128, 4, channels), pair_output.reshape(pair_state_input.shape)


def lanes_order(values):
    lead = values.shape[:-1]
    halves = values.reshape(lead + (values.shape[-1] // 2, 2))
    return jnp.swapaxes(halves, -1, -2).reshape(values.shape)


def local(
    alignment_input,
    pair_state_input,
    residue_number_index,
    chain_label,
    alignment_row_mask,
    relative_position_table,
    column_query_weight,
    column_key_weight,
    column_value_gate_weight,
    column_output_weight,
    alignment_transition_up,
    alignment_transition_down,
    outer_input_weight,
    outer_output_weight,
    outgoing_projection_weight,
    outgoing_output_gate,
    outgoing_output_weight,
    incoming_projection_weight,
    incoming_output_gate,
    incoming_output_weight,
    pair_transition_up,
    pair_transition_down,
):
    shard_pieces = lax.axis_size("dap")
    own_rows = pair_state_input.shape[0]
    residue_count = pair_state_input.shape[1]
    channel_count = alignment_input.shape[2]
    head_width = HM * HEAD_SIZE
    first_row = lax.axis_index("dap") * own_rows
    own_index = lax.dynamic_slice_in_dim(residue_number_index, first_row, own_rows)
    own_chain = lax.dynamic_slice_in_dim(chain_label, first_row, own_rows)

    def bins_of(index, chain):
        offset = index[:, None] - residue_number_index[None, :]
        return jnp.where(
            chain[:, None] == chain_label[None, :],
            jnp.clip(offset + MAXREL, 0, 2 * MAXREL),
            2 * MAXREL + 1,
        )

    bin_index = bins_of(own_index, own_chain)
    one_hot = (bin_index[:, :, None] == jnp.arange(NBINS, dtype=jnp.int32)[None, None, :]).astype(
        jnp.bfloat16
    )
    pair_start = pair_state_input.astype(jnp.float32) + jnp.einsum(
        "ijb,bc->ijc", one_hot, relative_position_table, preferred_element_type=jnp.float32
    )
    live_rows = alignment_row_mask > 0
    live_row_float = live_rows.astype(jnp.float32)

    if alignment_row_mask.shape[0] == LANES and 2 * residue_count == LANES and own_rows == 4:
        return whole_block(
            alignment_input,
            pair_state_input,
            bins_of(residue_number_index, chain_label),
            live_row_float,
            relative_position_table,
            column_query_weight,
            column_key_weight,
            column_value_gate_weight,
            column_output_weight,
            alignment_transition_up,
            alignment_transition_down,
            outer_input_weight,
            outer_output_weight,
            outgoing_projection_weight,
            outgoing_output_gate,
            outgoing_output_weight,
            incoming_projection_weight,
            incoming_output_gate,
            incoming_output_weight,
            pair_transition_up,
            pair_transition_down,
        )

    def attend_one(operands):
        query_col, key_col, value_col = operands
        scores = jnp.einsum("shd,thd->hst", query_col, key_col, preferred_element_type=jnp.float32)
        scores = jnp.where(live_rows[None, None, :], scores, -1000000000.0)
        row_top = jnp.max(scores, axis=-1, keepdims=True)
        raised = jnp.exp(scores - row_top)
        attention = (raised / jnp.sum(raised, axis=-1, keepdims=True)).astype(jnp.bfloat16)
        return jnp.einsum("hst,thd->shd", attention, value_col, preferred_element_type=jnp.float32)

    blocked_view = alignment_input.reshape(
        alignment_input.shape[0], shard_pieces, residue_count // shard_pieces, channel_count
    )
    block_in = lax.all_to_all(blocked_view, "dap", split_axis=1, concat_axis=0, tiled=True)
    depth_rows = block_in.shape[0]
    count_cols = block_in.shape[2]
    current = block_in.reshape(depth_rows, count_cols, channel_count).astype(jnp.float32)
    normed = layer_normalize(current).astype(jnp.bfloat16)
    query_rows = (
        jnp.einsum("sic,ce->sie", normed, column_query_weight, preferred_element_type=jnp.float32)
        * HEAD_SIZE ** (-0.5)
    ).astype(jnp.bfloat16)
    key_row_block = jnp.einsum(
        "sic,ce->sie", normed, column_key_weight, preferred_element_type=jnp.float32
    ).astype(jnp.bfloat16)
    value_gate_pair = jnp.einsum(
        "sic,ce->sie", normed, column_value_gate_weight, preferred_element_type=jnp.float32
    )
    value_rows = value_gate_pair[..., :head_width].astype(jnp.bfloat16)

    def by_column(values):
        return values.transpose(1, 0, 2).reshape(count_cols, depth_rows, HM, HEAD_SIZE)

    attended = lax.map(
        attend_one, (by_column(query_rows), by_column(key_row_block), by_column(value_rows))
    )
    attended = attended.reshape(count_cols, depth_rows, head_width).transpose(1, 0, 2)
    gated_out = (jax.nn.sigmoid(value_gate_pair[..., head_width:]) * attended).astype(jnp.bfloat16)
    current = current + jnp.einsum(
        "sie,ec->sic", gated_out, column_output_weight, preferred_element_type=jnp.float32
    )
    hidden = jax.nn.relu(
        jnp.einsum(
            "sic,cf->sif",
            layer_normalize(current).astype(jnp.bfloat16),
            alignment_transition_up,
            preferred_element_type=jnp.float32,
        )
    ).astype(jnp.bfloat16)
    current = current + jnp.einsum(
        "sif,fc->sic", hidden, alignment_transition_down, preferred_element_type=jnp.float32
    )
    result = current.astype(jnp.bfloat16)
    outer_product_input = jnp.einsum(
        "sic,cf->sif",
        layer_normalize(result.astype(jnp.float32)).astype(jnp.bfloat16),
        outer_input_weight,
        preferred_element_type=jnp.float32,
    )
    outer_product_input = outer_product_input * live_row_float[:, None, None]
    left_part = outer_product_input[..., :CO].astype(jnp.bfloat16)
    right_part = outer_product_input[..., CO:].astype(jnp.bfloat16)
    all_rows = result.shape[0]
    left_cols = left_part.transpose(1, 0, 2)
    right_cols = right_part.transpose(1, 0, 2).reshape(own_rows, all_rows * CO)
    live_count = jnp.sum(live_row_float)
    right_piece = gather_doubling(right_cols).reshape(-1, all_rows * CO)
    span_rows = right_piece.shape[0]
    products = jnp.einsum(
        "isc,jsd->ijcd",
        left_cols,
        right_piece.reshape(span_rows, all_rows, CO),
        preferred_element_type=jnp.float32,
    )
    products = products.astype(jnp.bfloat16).reshape(own_rows, span_rows, CO * CO)
    outer_mean = (
        jnp.einsum("ijf,fc->ijc", products, outer_output_weight, preferred_element_type=jnp.float32)
        / live_count
    )
    pair_mid = pair_start + outer_mean
    out_left, out_right, out_gating = triangle_inputs(
        pair_mid, outgoing_projection_weight, outgoing_output_gate
    )
    out_product = by_channels(out_left, out_right, "cik,cjk->cij")
    pair_after_out = triangle_finish(pair_mid, out_product, out_gating, outgoing_output_weight)
    in_left, in_right, in_gating = triangle_inputs(
        pair_after_out, incoming_projection_weight, incoming_output_gate
    )
    in_product = by_channels(in_left, in_right, "cki,ckj->cij")
    pair_after_in = triangle_finish(pair_after_out, in_product, in_gating, incoming_output_weight)
    pair_expanded = jax.nn.relu(
        jnp.einsum(
            "ijc,cf->ijf",
            layer_normalize(pair_after_in).astype(jnp.bfloat16),
            pair_transition_up,
            preferred_element_type=jnp.float32,
        )
    ).astype(jnp.bfloat16)
    pair_state_output = (
        pair_after_in
        + jnp.einsum(
            "ijf,fc->ijc", pair_expanded, pair_transition_down, preferred_element_type=jnp.float32
        )
    ).astype(jnp.bfloat16)
    return (result, pair_state_output)


def solution(mesh):
    in_specs = (
        P(("grp", "dap"), None, None),
        P(("grp", "dap"), None, None),
        P("grp"),
        P("grp"),
        P("grp"),
        P(),
        P(),
        P(),
        P(),
        P(),
        P(),
        P(),
        P(),
        P(),
        P(),
        P(),
        P(),
        P(),
        P(),
        P(),
        P(),
        P(),
    )
    out_specs = (P("grp", "dap", None), P(("grp", "dap"), None, None))
    return jax.shard_map(local, mesh=mesh, in_specs=in_specs, out_specs=out_specs, check_vma=False)
```

```python
import jax
import jax.numpy as jnp
from jax import lax
from jax.experimental import pallas as pl
from jax.experimental.pallas import tpu as pltpu
from jax.sharding import PartitionSpec as P

HM = 8
HEAD_SIZE = 32
CO = 32
MAXREL = 32
NBINS = 66


EPSILON = 1e-05


def layer_normalize(values):
    center = jnp.mean(values, axis=-1, keepdims=True)
    shifted = values - center
    spread = jnp.mean(shifted * shifted, axis=-1, keepdims=True)
    return shifted * lax.rsqrt(spread + EPSILON)


def triangle_inputs(pair_now, weight, gate_weight):
    normed = layer_normalize(pair_now).astype(jnp.bfloat16)
    combined = jnp.einsum("ijc,cf->fij", normed, weight, preferred_element_type=jnp.float32)
    hidden_width = weight.shape[1] // 4
    left_side = (
        jax.nn.sigmoid(combined[hidden_width : 2 * hidden_width]) * combined[:hidden_width]
    ).astype(jnp.bfloat16)
    right_side = (
        jax.nn.sigmoid(combined[3 * hidden_width :]) * combined[2 * hidden_width : 3 * hidden_width]
    ).astype(jnp.bfloat16)
    gating = jax.nn.sigmoid(
        jnp.einsum("ijc,cd->ijd", normed, gate_weight, preferred_element_type=jnp.float32)
    )
    return (left_side, right_side, gating)


def triangle_finish(pair_now, product, gating, final_weight):
    product = lax.optimization_barrier(product)
    normed = layer_normalize(product.transpose(1, 2, 0).astype(jnp.float32)).astype(jnp.bfloat16)
    return pair_now + gating * jnp.einsum(
        "ijc,cd->ijd", normed, final_weight, preferred_element_type=jnp.float32
    )


def by_channels(left_side, right_side, form):
    both = jnp.stack([left_side, right_side])
    both = lax.all_to_all(both, "dap", split_axis=1, concat_axis=2, tiled=True)
    partial_out = jnp.einsum(form, both[0], both[1], preferred_element_type=jnp.float32)
    return lax.all_to_all(
        partial_out.astype(jnp.bfloat16), "dap", split_axis=1, concat_axis=0, tiled=True
    )


def gather_doubling(block):
    shard_pieces = lax.axis_size("dap")
    place = lax.axis_index("dap")
    held = block
    depth = 0
    bit = shard_pieces // 2
    while bit:
        other = lax.ppermute(held, "dap", [(q, q ^ bit) for q in range(shard_pieces)])
        upper = (place & bit) != 0
        first = jnp.where(upper, other, held)
        second = jnp.where(upper, held, other)
        held = jnp.stack([first, second], axis=depth)
        depth += 1
        bit //= 2
    return held.reshape((shard_pieces,) + block.shape)


LANES = 128


def gate_curve(values):
    return 0.5 + 0.5 * jnp.tanh(0.5 * values)


def normalize_channels(values):
    center = jnp.mean(values, axis=0, keepdims=True)
    shifted = values - center
    spread = jnp.mean(shifted * shifted, axis=0, keepdims=True)
    return (shifted * lax.rsqrt(spread + EPSILON)).astype(jnp.bfloat16)


def mix(weight, values):
    return jnp.dot(weight, values, preferred_element_type=jnp.float32)


def fold_halves(first_even, second_even, first_odd, second_odd, low_half):
    straight = jnp.where(low_half, first_even, second_odd)
    crossed = jnp.where(low_half, second_even, first_odd)
    return straight + pltpu.roll(crossed, LANES // 2, 1)


def transpose_blocks(ref):
    rows, columns = ref.shape
    return jnp.concatenate(
        [
            jnp.concatenate(
                [
                    ref[a : a + LANES, b : b + LANES].astype(jnp.float32).T.astype(jnp.bfloat16)
                    for a in range(0, rows, LANES)
                ],
                axis=1,
            )
            for b in range(0, columns, LANES)
        ],
        axis=0,
    )


def start_copies(sources, landed, arrived):
    copies = [
        pltpu.make_async_copy(source, landed[k], arrived.at[k]) for k, source in enumerate(sources)
    ]
    for copy in copies:
        copy.start()
    return copies


FIRSTS = (0, 4, 2, 6)


def start_kernel(place_ref, live_ref, bins_ref, table_ref, *rest):
    part_refs, core_refs, pair_refs, sources = rest[:4], rest[4:8], rest[8:12], rest[12:15]
    pair_mid_ref, normed_ref, mix_ref, right_ref = rest[15:19]
    wide_ref, right_cols_ref, mean_wide_ref, mean_weight_ref, table_wide_ref = rest[19:24]
    stack_refs, landed, arrived = rest[24:26], rest[26:29], rest[29]
    copies = start_copies(sources, landed, arrived)
    place = place_ref[0]
    inverse_live = 1.0 / jnp.sum(live_ref[...], axis=1, keepdims=True)
    half = LANES // 2
    channel = lax.broadcasted_iota(jnp.int32, (LANES, LANES), 0)
    table_wide_ref[...] = jnp.zeros_like(table_wide_ref)
    table_wide_ref[0:NBINS, :] = table_ref[...].astype(jnp.float32)
    table = table_wide_ref[...].T.astype(jnp.bfloat16)
    low_half = lax.broadcasted_iota(jnp.int32, (LANES, LANES), 1) < half

    for g in range(4):
        for m in range(2):
            device = place ^ FIRSTS[g] ^ (8 * m)
            for part, owner in ((part_refs[g], device), (core_refs[g], device ^ 1)):
                wide_ref[pl.ds(pl.multiple_of(owner * 128, 128), 128), :] = part[
                    m, 128:256, :
                ].astype(jnp.float32)
    for d in range(0, CO, 2):
        rows = [
            wide_ref[pl.ds(par * CO + d + e, 32, stride=2 * CO), :]
            for e in range(2)
            for par in range(2)
        ]
        right_cols_ref[:, d * half : d * half + LANES] = (
            jnp.concatenate(rows, axis=0).T.astype(jnp.bfloat16)
        )

    for copy in copies:
        copy.wait()
    mean_wide_ref[...] = landed[0][...].astype(jnp.float32)
    for e in range(2):
        for block in range(4):
            rows = [
                mean_wide_ref[pl.ds(2 * (4 * block + k) + e, CO, stride=CO), :] for k in range(4)
            ]
            mean_weight_ref[e * LANES : (e + 1) * LANES, block * LANES : (block + 1) * LANES] = (
                jnp.concatenate(rows, axis=0).T.astype(jnp.bfloat16)
            )
    out_mix = transpose_blocks(landed[1])
    out_gate = transpose_blocks(landed[2])

    for g in range(4):
        stack_ref = stack_refs[g % 2]
        left_rows = part_refs[g][:, 0:128, :].reshape(256, LANES)
        outer = mix(left_rows, right_cols_ref[...]).astype(jnp.bfloat16)
        for i in range(8):
            for d in range(16):
                stack_ref[d * 32 : (d + 1) * 32, i * LANES : (i + 1) * LANES] = outer[
                    i * 32 : (i + 1) * 32, d * LANES : (d + 1) * LANES
                ]
        mixed = mix(mean_weight_ref[...], stack_ref[...])
        slabs = []
        places = []
        devices = [place ^ FIRSTS[g] ^ (8 * m) for m in range(2)]
        one_hot = [
            (channel == bins_ref[pl.ds(2 * devices[q // 2] + q % 2, 1), :]).astype(jnp.float32)
            for q in range(4)
        ]
        embedding = mix(table, jnp.concatenate(one_hot, axis=1).astype(jnp.bfloat16))
        for q in range(4):
            device = devices[q // 2]
            here = 2 * (device // 2) + q % 2
            even = slice(2 * q * LANES, (2 * q + 1) * LANES)
            odd = slice((2 * q + 1) * LANES, (2 * q + 2) * LANES)
            outer_mean = fold_halves(
                mixed[0:128, even], mixed[0:128, odd], mixed[128:256, even], mixed[128:256, odd], low_half
            )
            start = pair_refs[g][q // 2, q % 2].astype(jnp.float32)
            start = start + embedding[:, q * LANES : (q + 1) * LANES]
            slab = start + outer_mean * inverse_live
            pair_mid_ref[here] = slab
            slabs.append(normalize_channels(slab))
            places.append(here)
        normed = jnp.concatenate(slabs, axis=1)
        combined = mix(out_mix[256:512], normed)
        right = gate_curve(combined[128:256]) * combined[0:128]
        for q in range(4):
            lanes = slice(q * LANES, (q + 1) * LANES)
            rows = pl.ds(pl.multiple_of(places[q] * 128, 128), 128)
            right_ref[rows, :] = right[:, lanes].astype(jnp.bfloat16)
            normed_ref[places[q]] = normed[:, lanes]
    mix_ref[0:256, :] = out_mix[0:256]
    mix_ref[256:384, :] = out_gate


def gates_kernel(normed_ref, mix_ref, left_ref, gating_ref):
    for g in range(4):
        normed = jnp.concatenate([normed_ref[4 * g + q] for q in range(4)], axis=1)
        combined = mix(mix_ref[...], normed)
        left = gate_curve(combined[128:256]) * combined[0:128]
        gating = gate_curve(combined[256:384])
        for q in range(4):
            h = 4 * g + q
            lanes = slice(q * LANES, (q + 1) * LANES)
            left_ref[h * 128 : (h + 1) * 128, :] = left[:, lanes]
            gating_ref[h] = gating[:, lanes]


def triangle_kernel(
    place_ref,
    pair_mid_ref,
    left_ref,
    gating_ref,
    right_own_ref,
    right_other_ref,
    *rest,
):
    sources, (own_pair_ref, own_part_ref, other_part_ref) = rest[:6], rest[6:9]
    narrow_ref, wide_out_ref = rest[9:11]
    right_ref, product_ref, pair_now_ref, chosen_ref, own_left_ref, own_product_ref = rest[11:17]
    landed, arrived = rest[17:23], rest[23]
    copies = start_copies(sources, landed, arrived)
    place = place_ref[0]
    core = place % 2
    half = LANES // 2
    low_half = lax.broadcasted_iota(jnp.int32, (LANES, LANES), 1) < half
    low_short = lax.broadcasted_iota(jnp.int32, (32, LANES), 1) < half
    for chip in range(8):
        for source, side in ((right_own_ref, core), (right_other_ref, 1 - core)):
            rows = pl.ds(pl.multiple_of((4 * chip + 2 * side) * 128, 256), 256)
            right_ref[rows, :] = source[chip * 256 : (chip + 1) * 256, :].astype(jnp.float32)

    nothing = jnp.zeros((32, LANES), jnp.bfloat16)

    def outgoing_channels(block, carry):
        for e in range(32):
            c = block * 32 + e
            left = left_ref[pl.ds(c, 16, stride=128), :].astype(jnp.bfloat16)
            right = right_ref[pl.ds(c, 32, stride=128), :]
            moved = pltpu.roll(right, half, 1).astype(jnp.bfloat16)
            right = right.astype(jnp.bfloat16)
            spread = jnp.concatenate(
                [
                    jnp.where(low_short, right, nothing),
                    jnp.where(low_short, moved, nothing),
                    jnp.where(low_short, nothing, moved),
                    jnp.where(low_short, nothing, right),
                ],
                axis=0,
            )
            product_ref[pl.ds(c, 16, stride=128), :] = contract_last(left, spread)
        return carry

    lax.fori_loop(0, 4, outgoing_channels, 0)

    for copy in copies:
        copy.wait()
    out_final = transpose_blocks(landed[0])
    in_mix = transpose_blocks(landed[1])
    narrow_ref[0:128, :] = transpose_blocks(landed[3])
    narrow_ref[128:256, :] = transpose_blocks(landed[2])
    narrow_ref[256:768, :] = transpose_blocks(landed[4])
    wide_out_ref[...] = transpose_blocks(landed[5])

    column = lax.broadcasted_iota(jnp.int32, (1, 256), 1)
    which = column // 16
    residue = which % 4
    device = place ^ ((which // 4) % 2)
    wanted = half * (which // 8) + 32 * (residue % 2) + 2 * device + residue // 2
    slab_of = column % 16
    source_lane = lax.broadcasted_iota(jnp.int32, (LANES, 256), 0)
    for g in range(4):
        products = [
            normalize_channels(product_ref[(4 * g + q) * 128 : (4 * g + q + 1) * 128, :])
            for q in range(4)
        ]
        finished = mix(out_final, jnp.concatenate(products, axis=1))
        slabs = []
        picks = []
        for q in range(4):
            h = 4 * g + q
            lanes = slice(q * LANES, (q + 1) * LANES)
            slab = pair_mid_ref[h] + gating_ref[h] * finished[:, lanes]
            pair_now_ref[h] = slab
            slabs.append(normalize_channels(slab))
            here = jnp.where(slab_of == h, wanted, -1)
            picks.append((source_lane == here).astype(jnp.float32).astype(jnp.bfloat16))
        normed = jnp.concatenate(slabs, axis=1)
        chosen = mix(normed, jnp.concatenate(picks, axis=0))
        if g:
            chosen_ref[...] += chosen
        else:
            chosen_ref[...] = chosen
        combined = mix(in_mix[256:512], normed)
        right = gate_curve(combined[128:256]) * combined[0:128]
        for q in range(4):
            right_ref[(4 * g + q) * 128 : (4 * g + q + 1) * 128, :] = right[
                :, q * LANES : (q + 1) * LANES
            ]
    for t in range(2):
        own_pair_ref[t] = pair_now_ref[2 * (place // 2) + t]

    combined = mix(in_mix[0:256], chosen_ref[...].astype(jnp.bfloat16))
    own_left = gate_curve(combined[128:256]) * combined[0:128]
    for m in range(16):
        part = own_left[:, (m // 8) * LANES : (m // 8 + 1) * LANES]
        if m % 8:
            part = pltpu.roll(part, LANES - 16 * (m % 8), 1)
        own_left_ref[m * 128 : (m + 1) * 128, :] = part

    def incoming_channels(block, carry):
        for e in range(32):
            c = block * 32 + e
            left = own_left_ref[pl.ds(c, 16, stride=128), :][:, 0:16].astype(jnp.bfloat16)
            right = right_ref[pl.ds(c, 16, stride=128), :].astype(jnp.bfloat16)
            own_product_ref[pl.ds(c, 16, stride=128), :] = mix(left, right)
        return carry

    lax.fori_loop(0, 4, incoming_channels, 0)

    def block_of(b, e, residue):
        m = 8 * b + 4 * e + residue
        return own_product_ref[m * 128 : (m + 1) * 128, :]

    for e, target in ((0, own_part_ref), (1, other_part_ref)):
        for t in range(2):
            target[t] = fold_halves(
                block_of(0, e, 2 * t),
                block_of(0, e, 2 * t + 1),
                block_of(1, e, 2 * t),
                block_of(1, e, 2 * t + 1),
                low_half,
            )


def finish_kernel(own_pair_ref, own_part_ref, other_part_ref, narrow_ref, down_ref, result_ref):
    products = [normalize_channels(own_part_ref[t] + other_part_ref[t]) for t in range(2)]
    finished = mix(narrow_ref[0:128, :], jnp.concatenate(products, axis=1))
    own_pair = jnp.concatenate([own_pair_ref[t] for t in range(2)], axis=1)
    gating = gate_curve(mix(narrow_ref[128:256, :], normalize_channels(own_pair)))
    own_pair = own_pair + gating * finished
    hidden = jnp.maximum(mix(narrow_ref[256:768, :], normalize_channels(own_pair)), 0.0)
    own_pair = own_pair + mix(down_ref[...], hidden.astype(jnp.bfloat16))
    own_pair = own_pair.astype(jnp.bfloat16)
    order = lane_order_matrix()
    for t in range(2):
        result_ref[t * 128 : (t + 1) * 128, :] = contract_last(
            order, own_pair[:, t * LANES : (t + 1) * LANES]
        ).astype(jnp.bfloat16)


def lane_order_matrix():
    half = LANES // 2
    member = lax.broadcasted_iota(jnp.int32, (LANES, LANES), 0)
    lane = lax.broadcasted_iota(jnp.int32, (LANES, LANES), 1)
    back = half * (member // half) + 32 * (member % 2) + (member % half) // 2
    return (lane == back).astype(jnp.float32).astype(jnp.bfloat16)


def contract_first(first, second):
    return lax.dot_general(
        first, second, (((0,), (0,)), ((), ())), preferred_element_type=jnp.float32
    )


def rows_kernel(rows_ref, pair_ref, blocks_ref, own_pair_ref, wide_ref):
    order = lane_order_matrix()
    for t in range(2):
        own_pair_ref[t] = contract_first(
            pair_ref[2 * t : 2 * t + 2].reshape(LANES, LANES), order
        ).astype(jnp.bfloat16)
    residues = rows_ref.shape[1]
    count = 8 * residues
    rows = rows_ref[...].astype(jnp.float32).reshape(count, 2 * LANES)
    for e in range(2):
        wide_ref[e * count : (e + 1) * count, :] = rows[:, e * LANES : (e + 1) * LANES]
    for p in range(16):
        for e in range(2):
            block = [
                wide_ref[pl.ds(e * count + 4 * p + i, 8, stride=residues), :] for i in range(4)
            ]
            blocks_ref[p, :, e * LANES : (e + 1) * LANES] = jnp.concatenate(block, axis=0).astype(
                jnp.bfloat16
            )


def normalize_rows(values):
    center = jnp.mean(values, axis=1, keepdims=True)
    shifted = values - center
    spread = jnp.mean(shifted * shifted, axis=1, keepdims=True)
    return (shifted * lax.rsqrt(spread + EPSILON)).astype(jnp.bfloat16)


def contract_last(first, second):
    return lax.dot_general(
        first, second, (((1,), (1,)), ((), ())), preferred_element_type=jnp.float32
    )


def msa_kernel(
    live_ref,
    blocks_ref,
    narrow_ref,
    up_ref,
    down_ref,
    outer_ref,
    result_ref,
    parts_ref,
    wide_ref,
    attended_ref,
    final_ref,
):
    for p in range(16):
        block = blocks_ref[p].astype(jnp.float32)
        for i in range(4):
            wide_ref[i * 128 + p * 8 : i * 128 + p * 8 + 8, :] = block[i * 8 : i * 8 + 8, :]
    live = live_ref[...]
    alive = live > 0.0
    width = HM * HEAD_SIZE
    head_of = lax.broadcasted_iota(jnp.int32, (128, width), 1) // HEAD_SIZE
    zero = jnp.zeros((128, width), jnp.bfloat16)
    one = jnp.ones((128, width), jnp.bfloat16)

    def by_head(values):
        return jnp.concatenate([jnp.where(head_of == h, values, zero) for h in range(HM)], axis=0)

    heads = by_head(one)
    normed = normalize_rows(wide_ref[...])
    query = (mix(normed, narrow_ref[:, :width]) * HEAD_SIZE ** (-0.5)).astype(jnp.bfloat16)
    key = mix(normed, narrow_ref[:, width : 2 * width]).astype(jnp.bfloat16)
    value_gate = mix(normed, narrow_ref[:, 2 * width : 4 * width])
    value = value_gate[:, :width].astype(jnp.bfloat16)
    for i in range(4):
        rows = slice(i * 128, (i + 1) * 128)
        scores = contract_last(query[rows], by_head(key[rows]))
        raised = []
        for h in range(HM):
            score = jnp.where(alive, scores[:, h * 128 : (h + 1) * 128], -1000000000.0)
            raised.append(jnp.exp(score - jnp.max(score, axis=1, keepdims=True)).astype(jnp.bfloat16))
        raised = jnp.concatenate(raised, axis=1)
        attended_ref[rows, :] = mix(raised, by_head(value[rows])) / mix(raised, heads)
    gated = (gate_curve(value_gate[:, width:]) * attended_ref[...]).astype(jnp.bfloat16)
    current = wide_ref[...] + mix(gated, narrow_ref[:, 4 * width :])
    hidden = jnp.maximum(mix(normalize_rows(current), up_ref[...]), 0.0).astype(jnp.bfloat16)
    final = (current + mix(hidden, down_ref[...])).astype(jnp.bfloat16).astype(jnp.float32)
    outer = contract_last(outer_ref[...], normalize_rows(final))
    for i in range(4):
        rows = slice(i * 128, (i + 1) * 128)
        part = (outer[:, rows] * live).astype(jnp.bfloat16)
        parts_ref[i * CO : (i + 1) * CO, :] = part[:CO, :]
        parts_ref[128 + i * CO : 128 + (i + 1) * CO, :] = part[CO:, :]
        final_ref[pl.ds(i, 128, stride=4), :] = final[rows, :128]
        final_ref[pl.ds(512 + i, 128, stride=4), :] = final[rows, 128:]
    result_ref[:, :128] = final_ref[:512, :].astype(jnp.bfloat16)
    result_ref[:, 128:] = final_ref[512:, :].astype(jnp.bfloat16)


def exchange(values, offset):
    pieces = lax.axis_size("dap")
    return lax.ppermute(values, "dap", [(q, q ^ offset) for q in range(pieces)])


def whole_block(
    alignment_input,
    pair_state_input,
    bin_all,
    live_row_float,
    relative_position_table,
    column_query_weight,
    column_key_weight,
    column_value_gate_weight,
    column_output_weight,
    alignment_transition_up,
    alignment_transition_down,
    outer_input_weight,
    *pair_weights,
):
    channels = alignment_input.shape[2]
    width = pair_state_input.shape[2]
    place = lax.axis_index("dap").astype(jnp.int32).reshape(1)
    vmem = pl.BlockSpec(memory_space=pltpu.VMEM)
    smem = pl.BlockSpec(memory_space=pltpu.SMEM)
    hbm = pl.BlockSpec(memory_space=pltpu.HBM)

    def array(*shape, dtype=jnp.bfloat16):
        return jax.ShapeDtypeStruct(shape, dtype)

    def wide(*shape):
        return jax.ShapeDtypeStruct(shape, jnp.float32)

    def limit(mebibytes):
        return pltpu.CompilerParams(vmem_limit_bytes=mebibytes * 1024 * 1024)

    blocks, own_pair = pl.pallas_call(
        rows_kernel,
        out_shape=[array(16, 32, channels), array(2, width, LANES)],
        in_specs=[vmem, vmem],
        out_specs=[vmem, vmem],
        scratch_shapes=[pltpu.VMEM((1024, LANES), jnp.float32)],
        compiler_params=limit(16),
        name="rows_by_device",
    )(alignment_input, pair_state_input)
    blocks = lax.all_to_all(blocks, "dap", split_axis=0, concat_axis=0, tiled=True)

    pair_first = jnp.stack([own_pair, exchange(own_pair, 8)])
    blocks, pair_first = lax.optimization_barrier((blocks, pair_first))
    pair_second = exchange(pair_first, 4)

    result, parts = pl.pallas_call(
        msa_kernel,
        out_shape=(array(512, channels), array(256, LANES)),
        in_specs=[vmem] * 6,
        out_specs=(vmem, vmem),
        scratch_shapes=[
            pltpu.VMEM((512, channels), jnp.float32),
            pltpu.VMEM((512, channels), jnp.float32),
            pltpu.VMEM((1024, LANES), jnp.float32),
        ],
        compiler_params=limit(32),
        cost_estimate=pl.CostEstimate(
            flops=2_000_000_000, bytes_accessed=10_000_000, transcendentals=1_000_000
        ),
        name="msa_whole",
    )(
        live_row_float.reshape(1, LANES),
        blocks,
        jnp.concatenate(
            [
                column_query_weight,
                column_key_weight,
                column_value_gate_weight,
                column_output_weight,
            ],
            axis=1,
        ),
        alignment_transition_up,
        alignment_transition_down,
        outer_input_weight.T,
    )
    parts, pair_second = lax.optimization_barrier((parts, pair_second))
    pair_pieces = [pair_first, pair_second, exchange(pair_first, 2), exchange(pair_second, 2)]
    first = jnp.stack([parts, exchange(parts, 8)])
    second = exchange(first, 4)
    pieces = [first, second, exchange(first, 2), exchange(second, 2)]
    core_pieces = [exchange(piece, 1) for piece in pieces]

    slabs = (16, 128, LANES)
    tall = (16 * 128, LANES)
    pair_mid, normed, mix_weights, right = pl.pallas_call(
        start_kernel,
        out_shape=[wide(*slabs), array(*slabs), array(384, LANES), array(*tall)],
        in_specs=[smem] + [vmem] * 15 + [hbm] * 3,
        out_specs=[vmem] * 4,
        scratch_shapes=[
            pltpu.VMEM((2048, LANES), jnp.float32),
            pltpu.VMEM((128, 2048), jnp.bfloat16),
            pltpu.VMEM((1024, LANES), jnp.float32),
            pltpu.VMEM((256, 512), jnp.bfloat16),
            pltpu.VMEM((LANES, LANES), jnp.float32),
            pltpu.VMEM((512, 1024), jnp.bfloat16),
            pltpu.VMEM((512, 1024), jnp.bfloat16),
        ]
        + [pltpu.VMEM(w.shape, jnp.bfloat16) for w in pair_weights[:3]]
        + [pltpu.SemaphoreType.DMA((3,))],
        compiler_params=limit(48),
        name="pair_start",
    )(
        place,
        live_row_float.reshape(1, LANES),
        lanes_order(bin_all).reshape(32, LANES),
        relative_position_table,
        *pieces,
        *core_pieces,
        *pair_pieces,
        *pair_weights[:3],
    )
    other_right = exchange(right, 1)
    left, gating = pl.pallas_call(
        gates_kernel,
        out_shape=[wide(*tall), wide(*slabs)],
        in_specs=[vmem] * 2,
        out_specs=[vmem] * 2,
        compiler_params=limit(16),
        cost_estimate=pl.CostEstimate(
            flops=1_000_000_000, bytes_accessed=6_000_000, transcendentals=500_000
        ),
        name="pair_gates",
    )(normed, mix_weights)
    own_pair, own_part, other_part, narrow_weights, down_weight = pl.pallas_call(
        triangle_kernel,
        out_shape=[wide(2, 128, LANES)] * 3 + [array(768, LANES), array(128, 512)],
        in_specs=[smem] + [vmem] * 5 + [hbm] * 6,
        out_specs=[vmem] * 5,
        scratch_shapes=[
            pltpu.VMEM((32 * 128, LANES), jnp.float32),
            pltpu.VMEM(tall, jnp.float32),
            pltpu.VMEM(slabs, jnp.float32),
            pltpu.VMEM((128, 256), jnp.float32),
            pltpu.VMEM(tall, jnp.float32),
            pltpu.VMEM(tall, jnp.float32),
        ]
        + [pltpu.VMEM(w.shape, jnp.bfloat16) for w in pair_weights[3:]]
        + [pltpu.SemaphoreType.DMA((6,))],
        compiler_params=limit(48),
        name="pair_triangles",
    )(place, pair_mid, left, gating, right, other_right, *pair_weights[3:])
    pair_output = pl.pallas_call(
        finish_kernel,
        out_shape=array(256, LANES),
        in_specs=[vmem] * 5,
        out_specs=vmem,
        compiler_params=limit(16),
        name="pair_finish",
    )(own_pair, own_part, exchange(other_part, 1), narrow_weights, down_weight)
    return result.reshape(128, 4, channels), pair_output.reshape(pair_state_input.shape)


def lanes_order(values):
    lead = values.shape[:-1]
    halves = values.reshape(lead + (values.shape[-1] // 2, 2))
    return jnp.swapaxes(halves, -1, -2).reshape(values.shape)


def local(
    alignment_input,
    pair_state_input,
    residue_number_index,
    chain_label,
    alignment_row_mask,
    relative_position_table,
    column_query_weight,
    column_key_weight,
    column_value_gate_weight,
    column_output_weight,
    alignment_transition_up,
    alignment_transition_down,
    outer_input_weight,
    outer_output_weight,
    outgoing_projection_weight,
    outgoing_output_gate,
    outgoing_output_weight,
    incoming_projection_weight,
    incoming_output_gate,
    incoming_output_weight,
    pair_transition_up,
    pair_transition_down,
):
    shard_pieces = lax.axis_size("dap")
    own_rows = pair_state_input.shape[0]
    residue_count = pair_state_input.shape[1]
    channel_count = alignment_input.shape[2]
    head_width = HM * HEAD_SIZE
    first_row = lax.axis_index("dap") * own_rows
    own_index = lax.dynamic_slice_in_dim(residue_number_index, first_row, own_rows)
    own_chain = lax.dynamic_slice_in_dim(chain_label, first_row, own_rows)

    def bins_of(index, chain):
        offset = index[:, None] - residue_number_index[None, :]
        return jnp.where(
            chain[:, None] == chain_label[None, :],
            jnp.clip(offset + MAXREL, 0, 2 * MAXREL),
            2 * MAXREL + 1,
        )

    bin_index = bins_of(own_index, own_chain)
    one_hot = (bin_index[:, :, None] == jnp.arange(NBINS, dtype=jnp.int32)[None, None, :]).astype(
        jnp.bfloat16
    )
    pair_start = pair_state_input.astype(jnp.float32) + jnp.einsum(
        "ijb,bc->ijc", one_hot, relative_position_table, preferred_element_type=jnp.float32
    )
    live_rows = alignment_row_mask > 0
    live_row_float = live_rows.astype(jnp.float32)

    if alignment_row_mask.shape[0] == LANES and 2 * residue_count == LANES and own_rows == 4:
        return whole_block(
            alignment_input,
            pair_state_input,
            bins_of(residue_number_index, chain_label),
            live_row_float,
            relative_position_table,
            column_query_weight,
            column_key_weight,
            column_value_gate_weight,
            column_output_weight,
            alignment_transition_up,
            alignment_transition_down,
            outer_input_weight,
            outer_output_weight,
            outgoing_projection_weight,
            outgoing_output_gate,
            outgoing_output_weight,
            incoming_projection_weight,
            incoming_output_gate,
            incoming_output_weight,
            pair_transition_up,
            pair_transition_down,
        )

    def attend_one(operands):
        query_col, key_col, value_col = operands
        scores = jnp.einsum("shd,thd->hst", query_col, key_col, preferred_element_type=jnp.float32)
        scores = jnp.where(live_rows[None, None, :], scores, -1000000000.0)
        row_top = jnp.max(scores, axis=-1, keepdims=True)
        raised = jnp.exp(scores - row_top)
        attention = (raised / jnp.sum(raised, axis=-1, keepdims=True)).astype(jnp.bfloat16)
        return jnp.einsum("hst,thd->shd", attention, value_col, preferred_element_type=jnp.float32)

    blocked_view = alignment_input.reshape(
        alignment_input.shape[0], shard_pieces, residue_count // shard_pieces, channel_count
    )
    block_in = lax.all_to_all(blocked_view, "dap", split_axis=1, concat_axis=0, tiled=True)
    depth_rows = block_in.shape[0]
    count_cols = block_in.shape[2]
    current = block_in.reshape(depth_rows, count_cols, channel_count).astype(jnp.float32)
    normed = layer_normalize(current).astype(jnp.bfloat16)
    query_rows = (
        jnp.einsum("sic,ce->sie", normed, column_query_weight, preferred_element_type=jnp.float32)
        * HEAD_SIZE ** (-0.5)
    ).astype(jnp.bfloat16)
    key_row_block = jnp.einsum(
        "sic,ce->sie", normed, column_key_weight, preferred_element_type=jnp.float32
    ).astype(jnp.bfloat16)
    value_gate_pair = jnp.einsum(
        "sic,ce->sie", normed, column_value_gate_weight, preferred_element_type=jnp.float32
    )
    value_rows = value_gate_pair[..., :head_width].astype(jnp.bfloat16)

    def by_column(values):
        return values.transpose(1, 0, 2).reshape(count_cols, depth_rows, HM, HEAD_SIZE)

    attended = lax.map(
        attend_one, (by_column(query_rows), by_column(key_row_block), by_column(value_rows))
    )
    attended = attended.reshape(count_cols, depth_rows, head_width).transpose(1, 0, 2)
    gated_out = (jax.nn.sigmoid(value_gate_pair[..., head_width:]) * attended).astype(jnp.bfloat16)
    current = current + jnp.einsum(
        "sie,ec->sic", gated_out, column_output_weight, preferred_element_type=jnp.float32
    )
    hidden = jax.nn.relu(
        jnp.einsum(
            "sic,cf->sif",
            layer_normalize(current).astype(jnp.bfloat16),
            alignment_transition_up,
            preferred_element_type=jnp.float32,
        )
    ).astype(jnp.bfloat16)
    current = current + jnp.einsum(
        "sif,fc->sic", hidden, alignment_transition_down, preferred_element_type=jnp.float32
    )
    result = current.astype(jnp.bfloat16)
    outer_product_input = jnp.einsum(
        "sic,cf->sif",
        layer_normalize(result.astype(jnp.float32)).astype(jnp.bfloat16),
        outer_input_weight,
        preferred_element_type=jnp.float32,
    )
    outer_product_input = outer_product_input * live_row_float[:, None, None]
    left_part = outer_product_input[..., :CO].astype(jnp.bfloat16)
    right_part = outer_product_input[..., CO:].astype(jnp.bfloat16)
    all_rows = result.shape[0]
    left_cols = left_part.transpose(1, 0, 2)
    right_cols = right_part.transpose(1, 0, 2).reshape(own_rows, all_rows * CO)
    live_count = jnp.sum(live_row_float)
    right_piece = gather_doubling(right_cols).reshape(-1, all_rows * CO)
    span_rows = right_piece.shape[0]
    products = jnp.einsum(
        "isc,jsd->ijcd",
        left_cols,
        right_piece.reshape(span_rows, all_rows, CO),
        preferred_element_type=jnp.float32,
    )
    products = products.astype(jnp.bfloat16).reshape(own_rows, span_rows, CO * CO)
    outer_mean = (
        jnp.einsum("ijf,fc->ijc", products, outer_output_weight, preferred_element_type=jnp.float32)
        / live_count
    )
    pair_mid = pair_start + outer_mean
    out_left, out_right, out_gating = triangle_inputs(
        pair_mid, outgoing_projection_weight, outgoing_output_gate
    )
    out_product = by_channels(out_left, out_right, "cik,cjk->cij")
    pair_after_out = triangle_finish(pair_mid, out_product, out_gating, outgoing_output_weight)
    in_left, in_right, in_gating = triangle_inputs(
        pair_after_out, incoming_projection_weight, incoming_output_gate
    )
    in_product = by_channels(in_left, in_right, "cki,ckj->cij")
    pair_after_in = triangle_finish(pair_after_out, in_product, in_gating, incoming_output_weight)
    pair_expanded = jax.nn.relu(
        jnp.einsum(
            "ijc,cf->ijf",
            layer_normalize(pair_after_in).astype(jnp.bfloat16),
            pair_transition_up,
            preferred_element_type=jnp.float32,
        )
    ).astype(jnp.bfloat16)
    pair_state_output = (
        pair_after_in
        + jnp.einsum(
            "ijf,fc->ijc", pair_expanded, pair_transition_down, preferred_element_type=jnp.float32
        )
    ).astype(jnp.bfloat16)
    return (result, pair_state_output)


def solution(mesh):
    in_specs = (
        P(("grp", "dap"), None, None),
        P(("grp", "dap"), None, None),
        P("grp"),
        P("grp"),
        P("grp"),
        P(),
        P(),
        P(),
        P(),
        P(),
        P(),
        P(),
        P(),
        P(),
        P(),
        P(),
        P(),
        P(),
        P(),
        P(),
        P(),
        P(),
    )
    out_specs = (P("grp", "dap", None), P(("grp", "dap"), None, None))
    return jax.shard_map(local, mesh=mesh, in_specs=in_specs, out_specs=out_specs, check_vma=False)
```
